32 devices in a mesh: head: 4 (over y, core), seq: 8 (over z, x).
Axes of the slice: x: 2, y: 2, z: 4, core: 2. Of those that a mesh axis runs over, the one named last changes fastest.
Arguments:
- queries: bfloat16 [4, 1024, 256], P('head', 'seq'), may hold values from -6 to 6
- key_rows: bfloat16 [4, 1024, 256], P('head', 'seq'), may hold values from -6 to 6
- value_rows: bfloat16 [4, 1024, 256], P('head', 'seq'), may hold values from -6 to 6
- out_grad: bfloat16 [4, 1024, 256], P('head', 'seq'), may hold values from -6 to 6
- step_sizes: float32 [4, 1024], P('head', 'seq'), may hold values from 0.0001 to 0.0004
- norm_gain: float32 [4, 256], P('head'), may hold values from 0.1 to 1.9
- gate_init: bfloat16 [4, 256, 768], P('head', 'seq'), may hold values from -0.90625 to 0.90625
- up_init: bfloat16 [4, 256, 768], P('head', 'seq'), may hold values from -0.90625 to 0.90625
- down_init: bfloat16 [4, 256, 768], P('head', 'seq'), may hold values from -0.90625 to 0.90625
- gate_saved: bfloat16 [4, 256, 768], P('head', 'seq'), may hold values from -0.90625 to 0.90625
- up_saved: bfloat16 [4, 256, 768], P('head', 'seq'), may hold values from -0.90625 to 0.90625
- down_saved: bfloat16 [4, 256, 768], P('head', 'seq'), may hold values from -0.90625 to 0.90625
Outputs:
- grad_queries: bfloat16 [4, 1024, 256], P('head', 'seq')
- grad_keys: bfloat16 [4, 1024, 256], P('head', 'seq')
- grad_values: bfloat16 [4, 1024, 256], P('head', 'seq')
- grad_gate: float32 [4, 256, 768], P('head', 'seq')
- grad_up: float32 [4, 256, 768], P('head', 'seq')
- grad_down: float32 [4, 256, 768], P('head', 'seq')
The draws below stay inside these ranges and needn't reach their ends.
All inputs are finite; a program needn't handle non-finite values.
Results may differ from the reference program's by a relative error of at most 0.0085.
The reference program's roundings to bfloat16 on the way (of `normed`, `q_hidden`, `out_delta`, `delta_gate`, `cot_bf`, `scaled_values`, `k_hidden` and `back_proj`) count: a program that leaves them out, or rounds other values in their place, can miss the bound.
Values may be sent and summed in bfloat16 or wider, within the bound.
No kernel may reach another device: no remote copies, remote signals or barrier semaphores. Data moves between devices by JAX's collectives and lax.ppermute only.
A program may use at most 64 MiB of HBM per device.

```python
import math
import jax
import jax.numpy as jnp
from jax import lax

HEADS = 4
HD = 256
HID = 768
TOKENS = 1024


def fast_weights(key, salt):
    row_key = jax.random.fold_in(jax.random.fold_in(key, 7), 0)
    col_key = jax.random.fold_in(jax.random.fold_in(key, 9), salt)
    base_key = jax.random.fold_in(jax.random.fold_in(key, salt), 0)
    place = jnp.arange(HD, dtype=jnp.float32) / max(HD - 1, 1)
    row_scale = 10.0 ** place[None, :, None] * jnp.exp(jax.random.uniform(row_key, (HEADS, HD, 1), minval=-0.35, maxval=0.35))
    col_scale = jnp.exp(jax.random.uniform(col_key, (HEADS, 1, HID), minval=0.0, maxval=0.3))
    base = jnp.clip(jax.random.normal(base_key, (HEADS, HD, HID)), -4.0, 4.0)
    return (base * row_scale * col_scale / (5.3 * math.sqrt(HD))).astype(jnp.bfloat16)


def draw_gate_init(key, part):
    return fast_weights(key, 11)


def draw_up_init(key, part):
    return fast_weights(key, 12)


def draw_down_init(key, part):
    return fast_weights(key, 13)


def draw_gate_saved(key, part):
    return fast_weights(key, 21)


def draw_up_saved(key, part):
    return fast_weights(key, 22)


def draw_down_saved(key, part):
    return fast_weights(key, 23)


def block_levels(rng, extent, cuts, low, top_value):
    def one(dim, blocks):
        heights = jax.random.uniform(jax.random.fold_in(jax.random.fold_in(rng, 6), dim), (blocks,), jnp.float32, low / len(cuts), top_value / len(cuts))
        return jnp.repeat(jnp.exp(heights), extent[dim] // blocks).reshape((-1,) + (1,) * (len(extent) - dim - 1))

    level = one(*cuts[0])
    for cut in cuts[1:]:
        level = level * one(*cut)
    return level


def scatter_about(stream_key, shape, scale, reach, cuts=(), kind=jnp.bfloat16):
    values = scale * jax.random.normal(stream_key, shape, jnp.float32)
    if cuts:
        values = values * block_levels(stream_key, shape, cuts, -0.22, 0.18)
    return jnp.clip(values, -reach, reach).astype(kind)


def setup_inputs(seed: int = 0) -> dict:
    key_of = jax.random.split(jax.random.key(seed), 13)
    return {
        "queries": scatter_about(key_of[0], (HEADS, TOKENS, HD), 1.0, 6.0, ((0, 4), (1, 8))),
        "key_rows": scatter_about(key_of[1], (HEADS, TOKENS, HD), 1.0, 6.0, ((0, 4), (1, 8))),
        "value_rows": scatter_about(key_of[2], (HEADS, TOKENS, HD), 1.0, 6.0, ((0, 4), (1, 8))),
        "out_grad": scatter_about(key_of[3], (HEADS, TOKENS, HD), 1.0, 6.0, ((0, 4), (1, 8))),
        "step_sizes": jnp.clip(jnp.exp(math.log(0.0004) - 1.3862944 * jax.random.uniform(key_of[4], (HEADS, TOKENS), jnp.float32) ** block_levels(key_of[4], (HEADS, TOKENS), ((0, 4), (1, 8)), -0.2, 0.2)), 0.0001, 0.0004),
        "norm_gain": jnp.clip(1.0 + 0.18 * jax.random.normal(key_of[5], (HEADS, HD), jnp.float32), 0.1, 1.9),
        "gate_init": draw_gate_init(jax.random.fold_in(key_of[12], 71), 0),
        "up_init": draw_up_init(jax.random.fold_in(key_of[12], 71), 0),
        "down_init": draw_down_init(jax.random.fold_in(key_of[12], 71), 0),
        "gate_saved": draw_gate_saved(jax.random.fold_in(key_of[12], 71), 0),
        "up_saved": draw_up_saved(jax.random.fold_in(key_of[12], 71), 0),
        "down_saved": draw_down_saved(jax.random.fold_in(key_of[12], 71), 0),
    }


def silu_parts(pre_act):
    sigmoid_val = jax.nn.sigmoid(pre_act)
    silu_val = pre_act * sigmoid_val
    silu_slope = sigmoid_val * (1.0 + pre_act * (1.0 - sigmoid_val))
    silu_bend = sigmoid_val * (1.0 - sigmoid_val) * (2.0 + pre_act * (1.0 - 2.0 * sigmoid_val))
    return (silu_val, silu_slope, silu_bend)

def column_norm(weight):
    return jnp.sqrt(lax.optimization_barrier(jnp.sum(jnp.square(weight.astype(jnp.float32)), axis=0)) + 1e-06)

def matmul_f32(left_op, right_op):
    return jnp.dot(left_op, right_op, preferred_element_type=jnp.float32)

def normed_set(inits, saveds):
    norm_init = [column_norm(weight) for weight in inits]
    norm_saved = [column_norm(weight) for weight in saveds]
    normed = [(saveds[which].astype(jnp.float32) * (norm_init[which] / norm_saved[which])).astype(jnp.bfloat16) for which in range(3)]
    return (normed, norm_init, norm_saved)

def query_forward(parts):
    queries_h, gate_i, up_i, down_i, gate_s, up_s, down_s = parts
    normed, norm_init, norm_saved = normed_set((gate_i, up_i, down_i), (gate_s, up_s, down_s))
    q_gate = matmul_f32(queries_h, normed[0])
    q_up = matmul_f32(queries_h, normed[1])
    q_hidden = (silu_parts(q_gate)[0] * q_up).astype(jnp.bfloat16)
    return matmul_f32(q_hidden, normed[2].T)

def head_backward(parts):
    queries_h, keys_h, values_h, rates_h, delta_h, gate_i, up_i, down_i, gate_s, up_s, down_s = parts
    inits = (gate_i, up_i, down_i)
    saveds = (gate_s, up_s, down_s)
    normed, norm_init, norm_saved = normed_set(inits, saveds)
    q_gate = matmul_f32(queries_h, normed[0])
    q_up = matmul_f32(queries_h, normed[1])
    gate_act, gate_slope, gate_bend = silu_parts(q_gate)
    q_hidden = (gate_act * q_up).astype(jnp.bfloat16)
    delta_hidden = matmul_f32(delta_h, normed[2])
    delta_gate = (delta_hidden * q_up * gate_slope).astype(jnp.bfloat16)
    delta_up = (delta_hidden * gate_act).astype(jnp.bfloat16)
    grad_q = (matmul_f32(delta_gate, normed[0].T) + matmul_f32(delta_up, normed[1].T)).astype(jnp.bfloat16)
    apply_grad = (matmul_f32(queries_h.T, delta_gate), matmul_f32(queries_h.T, delta_up), matmul_f32(delta_h.T, q_hidden))
    col_dot = [lax.optimization_barrier(jnp.sum(saveds[which].astype(jnp.float32) * apply_grad[which], axis=0)) for which in range(3)]
    cot = [apply_grad[which] * (norm_init[which] / norm_saved[which]) - saveds[which].astype(jnp.float32) * (col_dot[which] * norm_init[which] / norm_saved[which] ** 3) for which in range(3)]
    cot_bf = [piece.astype(jnp.bfloat16) for piece in cot]
    direct = [cot[which] + inits[which].astype(jnp.float32) * (col_dot[which] / (norm_init[which] * norm_saved[which])) for which in range(3)]
    k_gate = matmul_f32(keys_h, gate_i)
    k_up = matmul_f32(keys_h, up_i)
    k_act, k_slope, k_bend = silu_parts(k_gate)
    scaled_values = (rates_h[:, None] * values_h.astype(jnp.float32)).astype(jnp.bfloat16)
    k_proj = matmul_f32(scaled_values, down_i)
    k_hidden = (k_act * k_up).astype(jnp.bfloat16)
    rise_gate = (k_proj * k_up * k_slope).astype(jnp.bfloat16)
    rise_up = (k_proj * k_act).astype(jnp.bfloat16)
    back_gate = matmul_f32(keys_h, cot_bf[0])
    back_up = matmul_f32(keys_h, cot_bf[1])
    back_hidden = matmul_f32(scaled_values, cot_bf[2])
    back_proj = (back_gate * k_up * k_slope + back_up * k_act).astype(jnp.bfloat16)
    back_kup = (back_gate * k_proj * k_slope + back_hidden * k_act).astype(jnp.bfloat16)
    back_kgate = (back_gate * k_proj * k_up * k_bend + (back_up * k_proj + back_hidden * k_up) * k_slope).astype(jnp.bfloat16)
    grad_k = (matmul_f32(rise_gate, cot_bf[0].T) + matmul_f32(rise_up, cot_bf[1].T) + matmul_f32(back_kgate, gate_i.T) + matmul_f32(back_kup, up_i.T)).astype(jnp.bfloat16)
    grad_v = (rates_h[:, None] * (matmul_f32(k_hidden, cot_bf[2].T) + matmul_f32(back_proj, down_i.T))).astype(jnp.bfloat16)
    grad_g = direct[0] + matmul_f32(keys_h.T, back_kgate)
    grad_u = direct[1] + matmul_f32(keys_h.T, back_kup)
    grad_d = direct[2] + matmul_f32(scaled_values.T, back_proj)
    return (grad_q, grad_k, grad_v, grad_g, grad_u, grad_d)

def reference(queries, key_rows, value_rows, out_grad, step_sizes, norm_gain, gate_init, up_init, down_init, gate_saved, up_saved, down_saved):
    apply_out = lax.map(query_forward, (queries, gate_init, up_init, down_init, gate_saved, up_saved, down_saved))
    full_width = HEADS * HD
    gain_rows = norm_gain[:, None, :]
    grad_f32 = out_grad.astype(jnp.float32)
    mean_square = lax.optimization_barrier(jnp.sum(jnp.square(apply_out), axis=(0, 2))) / full_width
    gain_dot = lax.optimization_barrier(jnp.sum(apply_out * gain_rows * grad_f32, axis=(0, 2))) / full_width
    root = jnp.sqrt(mean_square + 1e-05)[None, :, None]
    out_delta = (gain_rows * grad_f32 / root - apply_out * gain_dot[None, :, None] / root ** 3).astype(jnp.bfloat16)
    results = lax.map(head_backward, (queries, key_rows, value_rows, step_sizes, out_delta, gate_init, up_init, down_init, gate_saved, up_saved, down_saved))
    return (results[0], results[1], results[2], results[3], results[4], results[5])
```

```python
import jax
import jax.numpy as jnp
from jax import lax
from jax.sharding import PartitionSpec as P

EPS_COL = 1e-06
EPS_ROOT = 1e-05
BF = jnp.bfloat16
F32 = jnp.float32


def silu_parts(pre_act):
    sigmoid_val = jax.nn.sigmoid(pre_act)
    silu_val = pre_act * sigmoid_val
    silu_slope = sigmoid_val * (1.0 + pre_act * (1.0 - sigmoid_val))
    silu_bend = sigmoid_val * (1.0 - sigmoid_val) * (2.0 + pre_act * (1.0 - 2.0 * sigmoid_val))
    return (silu_val, silu_slope, silu_bend)


def mm(left_op, right_op):
    return jnp.dot(left_op, right_op, preferred_element_type=F32)


def mm_nt(left_op, right_op):
    return lax.dot_general(left_op, right_op, (((1,), (1,)), ((), ())), preferred_element_type=F32)


def mm_tn(left_op, right_op):
    return lax.dot_general(left_op, right_op, (((0,), (0,)), ((), ())), preferred_element_type=F32)


def column_norm(weight):
    return jnp.sqrt(jnp.sum(jnp.square(weight.astype(F32)), axis=0, keepdims=True) + EPS_COL)


def send(block, axis, size, dist):
    if dist == 0:
        return block
    return lax.ppermute(block, axis, [(i, i ^ dist) for i in range(size)])


def make_local(seq_n, head_n, group):
    def local(q, k, v, og, rates, gains, gi, ui, di, gs, us, ds):
        q, k, v, og, rates = q[0], k[0], v[0], og[0], rates[0]
        hidden = gi.shape[2]
        slab = hidden // group
        rows = gi.shape[1]
        feat = q.shape[1]
        width = head_n * feat
        me = lax.axis_index("seq")
        mine = lax.rem(me, group)
        near = range(group)
        every = range(seq_n)

        sv = (rates[:, None] * v.astype(F32)).astype(BF)
        packed = jnp.stack([w[0].reshape(rows, group, slab) for w in (gs, us, ds, gi, ui, di)], axis=2)
        packed = packed.reshape(rows, group, 6 * slab).transpose(1, 0, 2)
        wsend = [lax.dynamic_index_in_dim(packed, mine ^ d, 0, keepdims=False) for d in near]
        wrecv = [send(wsend[d % group], "seq", seq_n, d) for d in every]
        qs = [send(q, "seq", seq_n, d) for d in near]
        ks = [send(k, "seq", seq_n, d) for d in near]
        vs = [send(sv, "seq", seq_n, d) for d in near]
        qs += [send(q, "seq", seq_n, d) for d in every[group:]]

        wall = jnp.zeros((seq_n * rows, 6 * slab), BF)
        for d in every:
            wall = lax.dynamic_update_slice_in_dim(wall, wrecv[d], (me ^ d) * rows, 0)
        saved = [wall[:, i * slab : (i + 1) * slab] for i in range(3)]
        init = [wall[:, (i + 3) * slab : (i + 4) * slab] for i in range(3)]
        norm_init = [column_norm(w) for w in init]
        norm_saved = [column_norm(w) for w in saved]
        ratio = [norm_init[i] / norm_saved[i] for i in range(3)]
        normed = [(saved[i].astype(F32) * ratio[i]).astype(BF) for i in range(3)]

        qall = jnp.concatenate(qs, axis=0)
        q_gate = mm(qall, normed[0])
        q_up = mm(qall, normed[1])
        act, slope, _ = silu_parts(q_gate)
        q_hidden = (act * q_up).astype(BF)
        own_tok = q.shape[0]
        near_tok = group * own_tok
        part = mm_nt(q_hidden[:near_tok], normed[2]).astype(BF)
        parts = [send(part[d * own_tok : (d + 1) * own_tok], "seq", seq_n, d) for d in near]
        apply_out = sum(p.astype(F32) for p in parts)

        gg = gains * og.astype(F32)
        sums = lax.psum(
            jnp.stack((jnp.sum(apply_out * apply_out, axis=1), jnp.sum(apply_out * gg, axis=1))), "head"
        )
        root = jnp.sqrt(sums[0] / width + EPS_ROOT)[:, None]
        gain_dot = (sums[1] / width)[:, None]
        out_delta = (gg / root - apply_out * gain_dot / root**3).astype(BF)
        odall = jnp.concatenate([send(out_delta, "seq", seq_n, d) for d in every], axis=0)

        delta_hidden = mm(odall, normed[2])
        delta_gate = (delta_hidden * q_up * slope).astype(BF)
        delta_up = (delta_hidden * act).astype(BF)
        gq = (mm_nt(delta_gate[:near_tok], normed[0]) + mm_nt(delta_up[:near_tok], normed[1])).astype(BF)
        apply_grad = (mm_tn(qall, delta_gate), mm_tn(qall, delta_up), mm_tn(odall, q_hidden))
        saved_f = [w.astype(F32) for w in saved]
        col_dot = [jnp.sum(saved_f[i] * apply_grad[i], axis=0, keepdims=True) for i in range(3)]
        cot = [
            apply_grad[i] * ratio[i] - saved_f[i] * (col_dot[i] * norm_init[i] / norm_saved[i] ** 3)
            for i in range(3)
        ]
        cb = [c.astype(BF) for c in cot]
        direct = [
            cot[i] + init[i].astype(F32) * (col_dot[i] / (norm_init[i] * norm_saved[i])) for i in range(3)
        ]

        kall = jnp.concatenate(ks, axis=0)
        vall = jnp.concatenate(vs, axis=0)
        k_gate = mm(kall, init[0])
        k_up = mm(kall, init[1])
        k_proj = mm(vall, init[2])
        k_act, k_slope, k_bend = silu_parts(k_gate)
        k_hidden = (k_act * k_up).astype(BF)
        rise_gate = (k_proj * k_up * k_slope).astype(BF)
        rise_up = (k_proj * k_act).astype(BF)
        back_gate = mm(kall, cb[0])
        back_up = mm(kall, cb[1])
        back_hidden = mm(vall, cb[2])
        back_proj = (back_gate * k_up * k_slope + back_up * k_act).astype(BF)
        back_kup = (back_gate * k_proj * k_slope + back_hidden * k_act).astype(BF)
        back_kgate = (
            back_gate * k_proj * k_up * k_bend + (back_up * k_proj + back_hidden * k_up) * k_slope
        ).astype(BF)
        gk = (
            mm_nt(rise_gate, cb[0]) + mm_nt(rise_up, cb[1]) + mm_nt(back_kgate, init[0]) + mm_nt(back_kup, init[1])
        ).astype(BF)
        gv = (mm_nt(k_hidden, cb[2]) + mm_nt(back_proj, init[2])).astype(BF)
        first = me < group
        inner = [mm_tn(kall, back_kgate), mm_tn(kall, back_kup), mm_tn(vall, back_proj)]
        inner = jnp.concatenate(
            [inner[i] + jnp.where(first, direct[i], 0.0) for i in range(3)], axis=1
        ).astype(BF)

        def home(x):
            return sum(
                send(x[d * own_tok : (d + 1) * own_tok], "seq", seq_n, d).astype(F32) for d in near
            )

        grad_q = home(gq).astype(BF)
        grad_k = home(gk).astype(BF)
        grad_v = (rates[:, None] * home(gv)).astype(BF)
        got = [
            send(lax.dynamic_slice_in_dim(inner, (me ^ d) * rows, rows, 0), "seq", seq_n, d) for d in every
        ]
        total = jnp.stack([sum(got[d].astype(F32) for d in every[e::group]) for e in near])
        cols = [lax.dynamic_index_in_dim(total, mine ^ j, 0, keepdims=False) for j in near]
        grads = [
            jnp.concatenate([c[:, i * slab : (i + 1) * slab] for c in cols], axis=1)[None] for i in range(3)
        ]
        return (grad_q[None], grad_k[None], grad_v[None], *grads)

    return local


def solution(mesh):
    seq_n = mesh.shape["seq"]
    head_n = mesh.shape["head"]
    group = min(4, seq_n)
    tok = P("head", "seq", None)
    return jax.shard_map(
        make_local(seq_n, head_n, group),
        mesh=mesh,
        in_specs=(tok, tok, tok, tok, P("head", "seq"), P("head", None), tok, tok, tok, tok, tok, tok),
        out_specs=(tok, tok, tok, tok, tok, tok),
        check_vma=False,
    )
```

```python
import jax
import jax.numpy as jnp
from jax import lax
from jax.sharding import PartitionSpec as P

EPS_COL = 1e-06
EPS_ROOT = 1e-05
BF = jnp.bfloat16
F32 = jnp.float32


def silu_parts(pre_act):
    sigmoid_val = jax.nn.sigmoid(pre_act)
    silu_val = pre_act * sigmoid_val
    silu_slope = sigmoid_val * (1.0 + pre_act * (1.0 - sigmoid_val))
    silu_bend = sigmoid_val * (1.0 - sigmoid_val) * (2.0 + pre_act * (1.0 - 2.0 * sigmoid_val))
    return (silu_val, silu_slope, silu_bend)


def mm(left_op, right_op):
    return jnp.dot(left_op, right_op, preferred_element_type=F32)


def mm_nt(left_op, right_op):
    return lax.dot_general(left_op, right_op, (((1,), (1,)), ((), ())), preferred_element_type=F32)


def mm_tn(left_op, right_op):
    return lax.dot_general(left_op, right_op, (((0,), (0,)), ((), ())), preferred_element_type=F32)


def column_norm(weight):
    return jnp.sqrt(jnp.sum(jnp.square(weight.astype(F32)), axis=0, keepdims=True) + EPS_COL)


def swap(blocks, groups=None):
    return lax.all_to_all(blocks, "seq", 0, 0, axis_index_groups=groups, tiled=True)


def share(block, size, groups=None):
    return swap(jnp.broadcast_to(block[None], (size,) + block.shape), groups)


def make_local(seq_n, head_n, group):
    def local(q, k, v, og, rates, gains, gi, ui, di, gs, us, ds):
        q, k, v, og, rates = q[0], k[0], v[0], og[0], rates[0]
        hidden = gi.shape[2]
        slab = hidden // group
        rows = gi.shape[1]
        feat = q.shape[1]
        width = head_n * feat
        me = lax.axis_index("seq")
        near = range(group)
        tok_groups = seq_n // group
        groups = [[t * group + j for j in near] for t in range(tok_groups)]
        own_tok = q.shape[0]
        near_tok = group * own_tok
        start = lax.div(me, group) * near_tok

        def mine(x):
            return lax.dynamic_slice_in_dim(x, start, near_tok, 0)

        sv = (rates[:, None] * v.astype(F32)).astype(BF)
        packed = jnp.stack([w[0].reshape(rows, group, slab) for w in (gs, us, ds, gi, ui, di)], axis=2)
        packed = packed.reshape(rows, group, 6 * slab).transpose(1, 0, 2)
        wall = swap(jnp.tile(packed, (tok_groups, 1, 1))).reshape(seq_n * rows, 6 * slab)
        qall = share(q, seq_n).reshape(seq_n * own_tok, feat)
        kvall = share(jnp.concatenate((k, sv), axis=1), group, groups).reshape(near_tok, 2 * feat)
        kall, vall = kvall[:, :feat], kvall[:, feat:]
        saved = [wall[:, i * slab : (i + 1) * slab] for i in range(3)]
        init = [wall[:, (i + 3) * slab : (i + 4) * slab] for i in range(3)]
        norm_init = [column_norm(w) for w in init]
        norm_saved = [column_norm(w) for w in saved]
        ratio = [norm_init[i] / norm_saved[i] for i in range(3)]
        normed = [(saved[i].astype(F32) * ratio[i]).astype(BF) for i in range(3)]

        q_gate = mm(qall, normed[0])
        q_up = mm(qall, normed[1])
        act, slope, _ = silu_parts(q_gate)
        q_hidden = (act * q_up).astype(BF)
        part = mm_nt(mine(q_hidden), normed[2]).astype(BF)
        apply_out = jnp.sum(swap(part.reshape(group, own_tok, feat), groups).astype(F32), axis=0)

        gg = gains * og.astype(F32)
        sums = lax.psum(
            jnp.stack((jnp.sum(apply_out * apply_out, axis=1), jnp.sum(apply_out * gg, axis=1))), "head"
        )
        root = jnp.sqrt(sums[0] / width + EPS_ROOT)[:, None]
        gain_dot = (sums[1] / width)[:, None]
        out_delta = (gg / root - apply_out * gain_dot / root**3).astype(BF)
        odall = share(out_delta, seq_n).reshape(seq_n * own_tok, feat)

        delta_hidden = mm(odall, normed[2])
        delta_gate = (delta_hidden * q_up * slope).astype(BF)
        delta_up = (delta_hidden * act).astype(BF)
        gq = (mm_nt(mine(delta_gate), normed[0]) + mm_nt(mine(delta_up), normed[1])).astype(BF)
        apply_grad = (mm_tn(qall, delta_gate), mm_tn(qall, delta_up), mm_tn(odall, q_hidden))
        saved_f = [w.astype(F32) for w in saved]
        col_dot = [jnp.sum(saved_f[i] * apply_grad[i], axis=0, keepdims=True) for i in range(3)]
        cot = [
            apply_grad[i] * ratio[i] - saved_f[i] * (col_dot[i] * norm_init[i] / norm_saved[i] ** 3)
            for i in range(3)
        ]
        cb = [c.astype(BF) for c in cot]
        direct = [
            cot[i] + init[i].astype(F32) * (col_dot[i] / (norm_init[i] * norm_saved[i])) for i in range(3)
        ]

        k_gate = mm(kall, init[0])
        k_up = mm(kall, init[1])
        k_proj = mm(vall, init[2])
        k_act, k_slope, k_bend = silu_parts(k_gate)
        k_hidden = (k_act * k_up).astype(BF)
        rise_gate = (k_proj * k_up * k_slope).astype(BF)
        rise_up = (k_proj * k_act).astype(BF)
        back_gate = mm(kall, cb[0])
        back_up = mm(kall, cb[1])
        back_hidden = mm(vall, cb[2])
        back_proj = (back_gate * k_up * k_slope + back_up * k_act).astype(BF)
        back_kup = (back_gate * k_proj * k_slope + back_hidden * k_act).astype(BF)
        back_kgate = (
            back_gate * k_proj * k_up * k_bend + (back_up * k_proj + back_hidden * k_up) * k_slope
        ).astype(BF)
        gk = (
            mm_nt(rise_gate, cb[0]) + mm_nt(rise_up, cb[1]) + mm_nt(back_kgate, init[0]) + mm_nt(back_kup, init[1])
        ).astype(BF)
        gv = (mm_nt(k_hidden, cb[2]) + mm_nt(back_proj, init[2])).astype(BF)
        first = me < group
        inner = [mm_tn(kall, back_kgate), mm_tn(kall, back_kup), mm_tn(vall, back_proj)]
        inner = jnp.concatenate(
            [inner[i] + jnp.where(first, direct[i], 0.0) for i in range(3)], axis=1
        ).astype(BF)

        tokens = jnp.concatenate((gq, gk, gv), axis=1).reshape(group, own_tok, 3 * feat)
        tokens = jnp.sum(swap(tokens, groups).astype(F32), axis=0)
        grad_q = tokens[:, :feat].astype(BF)
        grad_k = tokens[:, feat : 2 * feat].astype(BF)
        grad_v = (rates[:, None] * tokens[:, 2 * feat :]).astype(BF)
        got = swap(inner.reshape(seq_n, rows, 3 * slab)).reshape(tok_groups, group, rows, 3, slab)
        got = jnp.sum(got.astype(F32), axis=0).transpose(2, 1, 0, 3).reshape(3, rows, hidden)
        grads = [got[i][None] for i in range(3)]
        return (grad_q[None], grad_k[None], grad_v[None], *grads)

    return local


def solution(mesh):
    seq_n = mesh.shape["seq"]
    head_n = mesh.shape["head"]
    group = min(4, seq_n)
    tok = P("head", "seq", None)
    return jax.shard_map(
        make_local(seq_n, head_n, group),
        mesh=mesh,
        in_specs=(tok, tok, tok, tok, P("head", "seq"), P("head", None), tok, tok, tok, tok, tok, tok),
        out_specs=(tok, tok, tok, tok, tok, tok),
        check_vma=False,
    )
```

```python
import functools

import jax
import jax.numpy as jnp
from jax import lax
from jax.experimental import pallas as pl
from jax.experimental.pallas import tpu as pltpu
from jax.sharding import PartitionSpec as P

EPS_COL = 1e-06
EPS_ROOT = 1e-05
BF = jnp.bfloat16
F32 = jnp.float32
VMEM = pl.BlockSpec(memory_space=pltpu.VMEM)
SMEM = pl.BlockSpec(memory_space=pltpu.SMEM)


def silu_parts(pre_act):
    sigmoid_val = jax.nn.sigmoid(pre_act)
    silu_val = pre_act * sigmoid_val
    silu_slope = sigmoid_val * (1.0 + pre_act * (1.0 - sigmoid_val))
    silu_bend = sigmoid_val * (1.0 - sigmoid_val) * (2.0 + pre_act * (1.0 - 2.0 * sigmoid_val))
    return (silu_val, silu_slope, silu_bend)


def mm(left_op, right_op):
    return jnp.dot(left_op, right_op, preferred_element_type=F32)


def mm_nt(left_op, right_op):
    return lax.dot_general(left_op, right_op, (((1,), (1,)), ((), ())), preferred_element_type=F32)


def mm_tn(left_op, right_op):
    return lax.dot_general(left_op, right_op, (((0,), (0,)), ((), ())), preferred_element_type=F32)


def column_norm(weight):
    return jnp.sqrt(jnp.sum(weight * weight, axis=0, keepdims=True) + EPS_COL)


def flat(x):
    return x.reshape(-1, x.shape[-1])


def call(kernel, outs, args, flops, mib, smem=0):
    moved = sum(x.size * x.dtype.itemsize for x in (*args, *outs))
    return pl.pallas_call(
        kernel,
        out_shape=outs,
        in_specs=[SMEM] * smem + [VMEM] * (len(args) - smem),
        out_specs=[VMEM] * len(outs),
        compiler_params=pltpu.CompilerParams(vmem_limit_bytes=mib << 20),
        cost_estimate=pl.CostEstimate(flops=flops, bytes_accessed=moved, transcendentals=0),
    )(*args)


def arr(shape, dtype):
    return jax.ShapeDtypeStruct(shape, dtype)


def pack_kernel(group, slab, q, gs, us, ds, gi, ui, di, w_out, q_out):
    for j in range(group):
        cols = pl.ds(j * slab, slab)
        block = jnp.concatenate([w[0, :, cols] for w in (gs, us, ds, gi, ui, di)], axis=1)
        for p in range(j, w_out.shape[0], group):
            w_out[p] = block
        q_out[j] = q[0]


def spread_kernel(k, v, rates, *rest):
    far, out = rest[:-1], rest[-1]
    tokens, feat = k.shape[1:]
    rate = jnp.broadcast_to(rates[...], (feat, tokens)).T
    sv = (rate * v[0].astype(F32)).astype(BF)
    for j in range(out.shape[0]):
        out[j, 0] = k[0]
        out[j, 1] = sv
        for e, block in enumerate(far):
            out[j, 2 + e] = block[0]


def normalized(w, slab):
    parts = [w[:, pl.ds(i * slab, slab)].astype(F32) for i in range(6)]
    saved, init = parts[:3], parts[3:]
    norm_init = [column_norm(x) for x in init]
    norm_saved = [column_norm(x) for x in saved]
    ratio = [norm_init[i] / norm_saved[i] for i in range(3)]
    normed = [(saved[i] * ratio[i]).astype(BF) for i in range(3)]
    return saved, init, norm_init, norm_saved, ratio, normed


def forward_kernel(slab, w, q, out):
    normed = normalized(w, slab)[-1]
    rows = flat(q[...])
    hidden = (silu_parts(mm(rows, normed[0]))[0] * mm(rows, normed[1])).astype(BF)
    out[...] = mm_nt(hidden, normed[2]).astype(BF).reshape(out.shape)


def delta_kernel(width, sums, apply_out, gg, out):
    tokens, feat = apply_out.shape
    square = jnp.broadcast_to(sums[0:1, :], (feat, tokens)).T
    gain = jnp.broadcast_to(sums[1:2, :], (feat, tokens)).T
    root = jnp.sqrt(square / width + EPS_ROOT)
    delta = (gg[...] / root - apply_out[...] * (gain / width) / (root * root * root)).astype(BF)
    for p in range(out.shape[0]):
        out[p] = delta


def backward_kernel(slab, group, place, w, q, kvq, od, tok_out, inner_out, ag, au, ad):
    mine = place[0]
    saved, init, norm_init, norm_saved, ratio, normed = normalized(w, slab)
    feat = q.shape[-1]

    def query_side(rows, delta):
        q_gate = mm(rows, normed[0])
        q_up = mm(rows, normed[1])
        act, slope, _ = silu_parts(q_gate)
        hidden = (act * q_up).astype(BF)
        delta_hidden = mm(delta, normed[2])
        delta_gate = (delta_hidden * q_up * slope).astype(BF)
        delta_up = (delta_hidden * act).astype(BF)
        grads = (mm_tn(rows, delta_gate), mm_tn(rows, delta_up), mm_tn(delta, hidden))
        return delta_gate, delta_up, grads

    delta_gate, delta_up, grads = query_side(flat(q[...]), flat(od[pl.ds(mine * group, group)]))
    grad_q = mm_nt(delta_gate, normed[0]) + mm_nt(delta_up, normed[1])
    tok_out[:, :, 0:feat] = grad_q.astype(BF).reshape(group, -1, feat)
    ag[...], au[...], ad[...] = grads

    def other(e, carry):
        rows = flat(kvq[:, 1 + e])
        more = query_side(rows, flat(od[pl.ds((mine ^ e) * group, group)]))[2]
        ag[...] += more[0]
        au[...] += more[1]
        ad[...] += more[2]
        return carry

    lax.fori_loop(1, od.shape[0] // group, other, 0)

    apply_grad = (ag[...], au[...], ad[...])
    cots, direct = [], []
    share = jnp.where(mine == 0, 1.0, 0.0)
    for i in range(3):
        col_dot = jnp.sum(saved[i] * apply_grad[i], axis=0, keepdims=True)
        cot = apply_grad[i] * ratio[i] - saved[i] * (
            col_dot * norm_init[i] / (norm_saved[i] * norm_saved[i] * norm_saved[i])
        )
        cots.append(cot.astype(BF))
        direct.append((cot + init[i] * (col_dot / (norm_init[i] * norm_saved[i]))) * share)

    init_bf = [w[:, pl.ds((3 + i) * slab, slab)] for i in range(3)]
    keys = flat(kvq[:, 0])
    values = flat(kvq[:, 1])
    k_gate = mm(keys, init_bf[0])
    k_up = mm(keys, init_bf[1])
    k_proj = mm(values, init_bf[2])
    k_act, k_slope, k_bend = silu_parts(k_gate)
    k_hidden = (k_act * k_up).astype(BF)
    rise_gate = (k_proj * k_up * k_slope).astype(BF)
    rise_up = (k_proj * k_act).astype(BF)
    back_gate = mm(keys, cots[0])
    back_up = mm(keys, cots[1])
    back_hidden = mm(values, cots[2])
    back_proj = (back_gate * k_up * k_slope + back_up * k_act).astype(BF)
    back_kup = (back_gate * k_proj * k_slope + back_hidden * k_act).astype(BF)
    back_kgate = (
        back_gate * k_proj * k_up * k_bend + (back_up * k_proj + back_hidden * k_up) * k_slope
    ).astype(BF)
    grad_k = (
        mm_nt(rise_gate, cots[0])
        + mm_nt(rise_up, cots[1])
        + mm_nt(back_kgate, init_bf[0])
        + mm_nt(back_kup, init_bf[1])
    )
    grad_v = mm_nt(k_hidden, cots[2]) + mm_nt(back_proj, init_bf[2])
    tok_out[:, :, feat : 2 * feat] = grad_k.astype(BF).reshape(group, -1, feat)
    tok_out[:, :, 2 * feat : 3 * feat] = grad_v.astype(BF).reshape(group, -1, feat)
    inner = (mm_tn(keys, back_kgate), mm_tn(keys, back_kup), mm_tn(values, back_proj))
    inner_out[...] = jnp.concatenate([inner[i] + direct[i] for i in range(3)], axis=1).astype(BF)


def tokens_kernel(rates, got, gq, gk, gv):
    tokens, feat = gq.shape[1:]
    total = got[0].astype(F32)
    for j in range(1, got.shape[0]):
        total += got[j].astype(F32)
    gq[0] = total[:, 0:feat].astype(BF)
    gk[0] = total[:, feat : 2 * feat].astype(BF)
    rate = jnp.broadcast_to(rates[...], (feat, tokens)).T
    gv[0] = (rate * total[:, 2 * feat : 3 * feat]).astype(BF)


def weights_kernel(group, slab, got, *outs):
    cols = []
    for j in range(group):
        total = got[j].astype(F32)
        for p in range(j + group, got.shape[0], group):
            total += got[p].astype(F32)
        cols.append(total)
    for i in range(3):
        outs[i][0] = jnp.concatenate([c[:, i * slab : (i + 1) * slab] for c in cols], axis=1)


def make_local(seq_n, head_n, group):
    tok_groups = seq_n // group
    groups = [[t * group + j for j in range(group)] for t in range(tok_groups)]

    def swap(blocks, axis_groups=None):
        return lax.all_to_all(blocks, "seq", 0, 0, axis_index_groups=axis_groups, tiled=True)

    def local(q, k, v, og, rates, gains, gi, ui, di, gs, us, ds):
        _, rows, hidden = gi.shape
        _, own, feat = q.shape
        slab = hidden // group
        near = group * own
        place = lax.div(lax.axis_index("seq"), group).astype(jnp.int32)[None]

        packed, queries = call(
            functools.partial(pack_kernel, group, slab),
            (arr((seq_n, rows, 6 * slab), BF), arr((group, own, feat), BF)),
            (q, gs, us, ds, gi, ui, di),
            0,
            16,
        )
        wall = swap(packed).reshape(seq_n * rows, 6 * slab)
        queries = swap(queries, groups)
        far = [
            lax.ppermute(q, "seq", [(i, i ^ (e * group)) for i in range(seq_n)]) for e in range(1, tok_groups)
        ]
        (kvq,) = call(
            spread_kernel, (arr((group, 1 + tok_groups, own, feat), BF),), (k, v, rates, *far), 0, 24
        )
        kvq = swap(kvq, groups)

        (part,) = call(
            functools.partial(forward_kernel, slab),
            (arr((group, own, feat), BF),),
            (wall, queries),
            6 * near * feat * slab,
            24,
        )
        apply_out = jnp.sum(swap(part, groups).astype(F32), axis=0)
        gg = gains * og[0].astype(F32)
        sums = lax.psum(
            jnp.stack((jnp.sum(apply_out * apply_out, axis=1), jnp.sum(apply_out * gg, axis=1))), "head"
        )
        (od,) = call(
            functools.partial(delta_kernel, head_n * feat),
            (arr((seq_n, own, feat), BF),),
            (sums, apply_out, gg),
            0,
            16,
        )
        od = swap(od)

        tok, inner = pl.pallas_call(
            functools.partial(backward_kernel, slab, group),
            out_shape=(arr((group, own, 3 * feat), BF), arr((seq_n * rows, 3 * slab), BF)),
            in_specs=[SMEM, VMEM, VMEM, VMEM, VMEM],
            out_specs=[VMEM, VMEM],
            scratch_shapes=[pltpu.VMEM((seq_n * rows, slab), F32)] * 3,
            compiler_params=pltpu.CompilerParams(vmem_limit_bytes=40 << 20),
            cost_estimate=pl.CostEstimate(
                flops=66 * near * feat * slab, bytes_accessed=8 * near * feat, transcendentals=0
            ),
        )(place, wall, queries, kvq, od)
        inner = swap(inner.reshape(seq_n, rows, 3 * slab))
        tok = swap(tok, groups)
        out_tok = arr((1, own, feat), BF)
        grads_t = call(tokens_kernel, (out_tok, out_tok, out_tok), (rates, tok), 0, 16)
        grad_w = arr((1, rows, hidden), F32)
        grads_w = call(
            functools.partial(weights_kernel, group, slab), (grad_w, grad_w, grad_w), (inner,), 0, 16
        )
        return (*grads_t, *grads_w)

    return local


def solution(mesh):
    seq_n = mesh.shape["seq"]
    head_n = mesh.shape["head"]
    group = min(4, seq_n)
    tok = P("head", "seq", None)
    return jax.shard_map(
        make_local(seq_n, head_n, group),
        mesh=mesh,
        in_specs=(tok, tok, tok, tok, P("head", "seq"), P("head", None), tok, tok, tok, tok, tok, tok),
        out_specs=(tok, tok, tok, tok, tok, tok),
        check_vma=False,
    )
```

```python
import functools

import jax
import jax.numpy as jnp
from jax import lax
from jax.experimental import pallas as pl
from jax.experimental.pallas import tpu as pltpu
from jax.sharding import PartitionSpec as P

EPS_COL = 1e-06
EPS_ROOT = 1e-05
BF = jnp.bfloat16
F32 = jnp.float32
VMEM = pl.BlockSpec(memory_space=pltpu.VMEM)
SMEM = pl.BlockSpec(memory_space=pltpu.SMEM)


def silu_parts(pre_act):
    sigmoid_val = jax.nn.sigmoid(pre_act)
    silu_val = pre_act * sigmoid_val
    silu_slope = sigmoid_val * (1.0 + pre_act * (1.0 - sigmoid_val))
    silu_bend = sigmoid_val * (1.0 - sigmoid_val) * (2.0 + pre_act * (1.0 - 2.0 * sigmoid_val))
    return (silu_val, silu_slope, silu_bend)


def mm(left_op, right_op):
    return jnp.dot(left_op, right_op, preferred_element_type=F32)


def mm_nt(left_op, right_op):
    return lax.dot_general(left_op, right_op, (((1,), (1,)), ((), ())), preferred_element_type=F32)


def mm_tn(left_op, right_op):
    return lax.dot_general(left_op, right_op, (((0,), (0,)), ((), ())), preferred_element_type=F32)


def column_norm(weight):
    return jnp.sqrt(jnp.sum(weight * weight, axis=0, keepdims=True) + EPS_COL)


def flat(x):
    return x.reshape(-1, x.shape[-1])


def call(kernel, outs, args, flops, mib, smem=0):
    moved = sum(x.size * x.dtype.itemsize for x in (*args, *outs))
    return pl.pallas_call(
        kernel,
        out_shape=outs,
        in_specs=[SMEM] * smem + [VMEM] * (len(args) - smem),
        out_specs=[VMEM] * len(outs),
        compiler_params=pltpu.CompilerParams(vmem_limit_bytes=mib << 20),
        cost_estimate=pl.CostEstimate(flops=flops, bytes_accessed=moved, transcendentals=0),
    )(*args)


def copying_call(kernel, outs, args, buffers):
    return pl.pallas_call(
        kernel,
        out_shape=outs,
        in_specs=[pl.BlockSpec(memory_space=pl.ANY)] * len(args),
        out_specs=[VMEM] * len(outs),
        scratch_shapes=[*buffers, pltpu.SemaphoreType.DMA((len(args),))],
        compiler_params=pltpu.CompilerParams(vmem_limit_bytes=16 << 20),
    )(*args)


def arr(shape, dtype):
    return jax.ShapeDtypeStruct(shape, dtype)


def fetch(sources, buffers, sems):
    copies = [pltpu.make_async_copy(s, b, sems.at[i]) for i, (s, b) in enumerate(zip(sources, buffers))]
    for copy in copies:
        copy.start()
    for copy in copies:
        copy.wait()


def pack_kernel(group, slab, gs, us, ds, gi, ui, di, w_out, buf, sems):
    fetch((gs, us, ds, gi, ui, di), [buf.at[pl.ds(i, 1)] for i in range(6)], sems)
    for j in range(group):
        cols = pl.ds(j * slab, slab)
        block = jnp.concatenate([buf[i, :, cols] for i in range(6)], axis=1)
        for p in range(j, w_out.shape[0], group):
            w_out[p] = block


def tokens_in_kernel(k, v, og, rates, gains, kv_out, gg_out, kb, vb, ob, rb, gb, sems):
    fetch((k, v, og, rates, gains), (kb, vb, ob, rb, gb), sems)
    tokens, feat = gg_out.shape
    rate = jnp.broadcast_to(rb[...], (feat, tokens)).T
    kv_out[:, 0:feat] = kb[0]
    kv_out[:, feat : 2 * feat] = (rate * vb[0].astype(F32)).astype(BF)
    gg_out[...] = gb[...] * ob[0].astype(F32)


def normalized(w, slab):
    parts = [w[:, pl.ds(i * slab, slab)].astype(F32) for i in range(6)]
    saved, init = parts[:3], parts[3:]
    norm_init = [column_norm(x) for x in init]
    norm_saved = [column_norm(x) for x in saved]
    ratio = [norm_init[i] / norm_saved[i] for i in range(3)]
    normed = [(saved[i] * ratio[i]).astype(BF) for i in range(3)]
    return saved, init, norm_init, norm_saved, ratio, normed


def forward_kernel(slab, w, q, out):
    normed = normalized(w, slab)[-1]
    rows = flat(q[...])
    hidden = (silu_parts(mm(rows, normed[0]))[0] * mm(rows, normed[1])).astype(BF)
    out[...] = mm_nt(hidden, normed[2]).astype(BF).reshape(out.shape)


def delta_kernel(width, sums, apply_out, gg, out):
    tokens, feat = apply_out.shape
    square = jnp.broadcast_to(sums[0:1, :], (feat, tokens)).T
    gain = jnp.broadcast_to(sums[1:2, :], (feat, tokens)).T
    root = jnp.sqrt(square / width + EPS_ROOT)
    delta = (gg[...] / root - apply_out[...] * (gain / width) / (root * root * root)).astype(BF)
    for p in range(out.shape[0]):
        out[p] = delta


def backward_kernel(slab, group, place, w, q, kv, od, *rest):
    outs, (inner_out, tok, ag, au, ad) = rest[:group], rest[group:]
    mine, rank = place[0], place[1]
    saved, init, norm_init, norm_saved, ratio, normed = normalized(w, slab)
    feat = q.shape[-1]

    def query_side(rows, delta):
        q_gate = mm(rows, normed[0])
        q_up = mm(rows, normed[1])
        act, slope, _ = silu_parts(q_gate)
        hidden = (act * q_up).astype(BF)
        delta_hidden = mm(delta, normed[2])
        delta_gate = (delta_hidden * q_up * slope).astype(BF)
        delta_up = (delta_hidden * act).astype(BF)
        grads = (mm_tn(rows, delta_gate), mm_tn(rows, delta_up), mm_tn(delta, hidden))
        return delta_gate, delta_up, grads

    def take(ref, e):
        return flat(ref[pl.ds((mine ^ e) * group, group)])

    delta_gate, delta_up, grads = query_side(take(q, 0), take(od, 0))
    grad_q = mm_nt(delta_gate, normed[0]) + mm_nt(delta_up, normed[1])
    tok[:, :, 0:feat] = grad_q.astype(BF).reshape(group, -1, feat)
    ag[...], au[...], ad[...] = grads

    def other(e, carry):
        more = query_side(take(q, e), take(od, e))[2]
        ag[...] += more[0]
        au[...] += more[1]
        ad[...] += more[2]
        return carry

    lax.fori_loop(1, od.shape[0] // group, other, 0)

    apply_grad = (ag[...], au[...], ad[...])
    cots, direct = [], []
    share = jnp.where(mine == 0, 1.0, 0.0)
    for i in range(3):
        col_dot = jnp.sum(saved[i] * apply_grad[i], axis=0, keepdims=True)
        cot = apply_grad[i] * ratio[i] - saved[i] * (
            col_dot * norm_init[i] / (norm_saved[i] * norm_saved[i] * norm_saved[i])
        )
        cots.append(cot.astype(BF))
        direct.append((cot + init[i] * (col_dot / (norm_init[i] * norm_saved[i]))) * share)

    init_bf = [w[:, pl.ds((3 + i) * slab, slab)] for i in range(3)]
    keys = flat(kv[:, :, 0:feat])
    values = flat(kv[:, :, feat : 2 * feat])
    k_gate = mm(keys, init_bf[0])
    k_up = mm(keys, init_bf[1])
    k_proj = mm(values, init_bf[2])
    k_act, k_slope, k_bend = silu_parts(k_gate)
    k_hidden = (k_act * k_up).astype(BF)
    rise_gate = (k_proj * k_up * k_slope).astype(BF)
    rise_up = (k_proj * k_act).astype(BF)
    back_gate = mm(keys, cots[0])
    back_up = mm(keys, cots[1])
    back_hidden = mm(values, cots[2])
    back_proj = (back_gate * k_up * k_slope + back_up * k_act).astype(BF)
    back_kup = (back_gate * k_proj * k_slope + back_hidden * k_act).astype(BF)
    back_kgate = (
        back_gate * k_proj * k_up * k_bend + (back_up * k_proj + back_hidden * k_up) * k_slope
    ).astype(BF)
    grad_k = (
        mm_nt(rise_gate, cots[0])
        + mm_nt(rise_up, cots[1])
        + mm_nt(back_kgate, init_bf[0])
        + mm_nt(back_kup, init_bf[1])
    )
    grad_v = mm_nt(k_hidden, cots[2]) + mm_nt(back_proj, init_bf[2])
    tok[:, :, feat : 2 * feat] = grad_k.astype(BF).reshape(group, -1, feat)
    tok[:, :, 2 * feat : 3 * feat] = grad_v.astype(BF).reshape(group, -1, feat)
    inner = (mm_tn(keys, back_kgate), mm_tn(keys, back_kup), mm_tn(values, back_proj))
    inner_out[...] = jnp.concatenate([inner[i] + direct[i] for i in range(3)], axis=1).astype(BF)
    for d in range(group):
        outs[d][...] = tok[rank ^ d]


def tokens_kernel(rates, *refs):
    got, (gq, gk, gv) = refs[:-3], refs[-3:]
    tokens, feat = gq.shape[1:]
    total = got[0][...].astype(F32)
    for block in got[1:]:
        total += block[...].astype(F32)
    gq[0] = total[:, 0:feat].astype(BF)
    gk[0] = total[:, feat : 2 * feat].astype(BF)
    rate = jnp.broadcast_to(rates[...], (feat, tokens)).T
    gv[0] = (rate * total[:, 2 * feat : 3 * feat]).astype(BF)


def weights_kernel(group, slab, got, *outs):
    cols = []
    for j in range(group):
        total = got[j].astype(F32)
        for p in range(j + group, got.shape[0], group):
            total += got[p].astype(F32)
        cols.append(total)
    for i in range(3):
        outs[i][0] = jnp.concatenate([c[:, i * slab : (i + 1) * slab] for c in cols], axis=1)


def make_local(seq_n, head_n, group):
    tok_groups = seq_n // group
    groups = [[t * group + j for j in range(group)] for t in range(tok_groups)]

    def swap(blocks, axis_groups=None):
        return lax.all_to_all(blocks, "seq", 0, 0, axis_index_groups=axis_groups, tiled=True)

    def local(q, k, v, og, rates, gains, gi, ui, di, gs, us, ds):
        _, rows, hidden = gi.shape
        _, own, feat = q.shape
        slab = hidden // group
        near = group * own
        me = lax.axis_index("seq")
        place = jnp.stack((lax.div(me, group), lax.rem(me, group))).astype(jnp.int32)

        queries = lax.all_gather(q[0], "seq", axis_index_groups=groups)
        (packed,) = copying_call(
            functools.partial(pack_kernel, group, slab),
            (arr((seq_n, rows, 6 * slab), BF),),
            (gs, us, ds, gi, ui, di),
            [pltpu.VMEM((6, rows, hidden), BF)],
        )
        kv, gg = copying_call(
            tokens_in_kernel,
            (arr((own, 2 * feat), BF), arr((own, feat), F32)),
            (k, v, og, rates, gains),
            [pltpu.VMEM(x.shape, x.dtype) for x in (k, v, og, rates, gains)],
        )
        wall = swap(packed).reshape(seq_n * rows, 6 * slab)
        kv = lax.all_gather(kv, "seq", axis_index_groups=groups)
        q_all = lax.all_gather(q[0], "seq")

        (part,) = call(
            functools.partial(forward_kernel, slab),
            (arr((group, own, feat), BF),),
            (wall, queries),
            6 * near * feat * slab,
            24,
        )
        apply_out = jnp.sum(swap(part, groups).astype(F32), axis=0)
        sums = lax.psum(
            jnp.stack((jnp.sum(apply_out * apply_out, axis=1), jnp.sum(apply_out * gg, axis=1))), "head"
        )
        (od,) = call(
            functools.partial(delta_kernel, head_n * feat),
            (arr((seq_n, own, feat), BF),),
            (sums, apply_out, gg),
            0,
            16,
        )
        od = swap(od)

        *tok, inner = pl.pallas_call(
            functools.partial(backward_kernel, slab, group),
            out_shape=(*[arr((own, 3 * feat), BF)] * group, arr((seq_n * rows, 3 * slab), BF)),
            in_specs=[SMEM, VMEM, VMEM, VMEM, VMEM],
            out_specs=[VMEM] * (group + 1),
            scratch_shapes=[
                pltpu.VMEM((group, own, 3 * feat), BF),
                *[pltpu.VMEM((seq_n * rows, slab), F32)] * 3,
            ],
            compiler_params=pltpu.CompilerParams(vmem_limit_bytes=40 << 20),
            cost_estimate=pl.CostEstimate(
                flops=66 * near * feat * slab, bytes_accessed=8 * near * feat, transcendentals=0
            ),
        )(place, wall, q_all, kv, od)
        inner = swap(inner.reshape(seq_n, rows, 3 * slab))
        tok = [tok[0]] + [
            lax.ppermute(tok[d], "seq", [(i, i ^ d) for i in range(seq_n)]) for d in range(1, group)
        ]
        out_tok = arr((1, own, feat), BF)
        grads_t = call(tokens_kernel, (out_tok, out_tok, out_tok), (rates, *tok), 0, 16)
        grad_w = arr((1, rows, hidden), F32)
        grads_w = call(
            functools.partial(weights_kernel, group, slab), (grad_w, grad_w, grad_w), (inner,), 0, 16
        )
        return (*grads_t, *grads_w)

    return local


def solution(mesh):
    seq_n = mesh.shape["seq"]
    head_n = mesh.shape["head"]
    group = min(4, seq_n)
    tok = P("head", "seq", None)
    return jax.shard_map(
        make_local(seq_n, head_n, group),
        mesh=mesh,
        in_specs=(tok, tok, tok, tok, P("head", "seq"), P("head", None), tok, tok, tok, tok, tok, tok),
        out_specs=(tok, tok, tok, tok, tok, tok),
        check_vma=False,
    )
```

```python
import functools

import jax
import jax.numpy as jnp
from jax import lax
from jax.experimental import pallas as pl
from jax.experimental.pallas import tpu as pltpu
from jax.sharding import PartitionSpec as P

EPS_COL = 1e-06
EPS_ROOT = 1e-05
BF = jnp.bfloat16
F32 = jnp.float32
VMEM = pl.BlockSpec(memory_space=pltpu.VMEM)
SMEM = pl.BlockSpec(memory_space=pltpu.SMEM)


def silu_parts(pre_act):
    sigmoid_val = jax.nn.sigmoid(pre_act)
    silu_val = pre_act * sigmoid_val
    silu_slope = sigmoid_val * (1.0 + pre_act * (1.0 - sigmoid_val))
    silu_bend = sigmoid_val * (1.0 - sigmoid_val) * (2.0 + pre_act * (1.0 - 2.0 * sigmoid_val))
    return (silu_val, silu_slope, silu_bend)


def mm(left_op, right_op):
    return jnp.dot(left_op, right_op, preferred_element_type=F32)


def mm_nt(left_op, right_op):
    return lax.dot_general(left_op, right_op, (((1,), (1,)), ((), ())), preferred_element_type=F32)


def mm_tn(left_op, right_op):
    return lax.dot_general(left_op, right_op, (((0,), (0,)), ((), ())), preferred_element_type=F32)


def column_norm(weight):
    return jnp.sqrt(jnp.sum(weight * weight, axis=0, keepdims=True) + EPS_COL)


def flat(x):
    return x.reshape(-1, x.shape[-1])


def call(kernel, outs, args, flops, mib, smem=0):
    moved = sum(x.size * x.dtype.itemsize for x in (*args, *outs))
    return pl.pallas_call(
        kernel,
        out_shape=outs,
        in_specs=[SMEM] * smem + [VMEM] * (len(args) - smem),
        out_specs=[VMEM] * len(outs),
        compiler_params=pltpu.CompilerParams(vmem_limit_bytes=mib << 20),
        cost_estimate=pl.CostEstimate(flops=flops, bytes_accessed=moved, transcendentals=0),
    )(*args)


def copying_call(kernel, outs, args, buffers):
    return pl.pallas_call(
        kernel,
        out_shape=outs,
        in_specs=[pl.BlockSpec(memory_space=pltpu.HBM)] * len(args),
        out_specs=[VMEM] * len(outs),
        scratch_shapes=[*buffers, pltpu.SemaphoreType.DMA((len(args),))],
        compiler_params=pltpu.CompilerParams(vmem_limit_bytes=16 << 20),
    )(*args)


def arr(shape, dtype):
    return jax.ShapeDtypeStruct(shape, dtype)


def fetch(sources, buffers, sems):
    copies = [pltpu.make_async_copy(s, b, sems.at[i]) for i, (s, b) in enumerate(zip(sources, buffers))]
    for copy in copies:
        copy.start()
    for copy in copies:
        copy.wait()


def pack_kernel(group, slab, *refs):
    args, (w_out, tok_out, q_out, gg_out, buf, qb, kb, vb, ob, rb, gb, sems) = refs[:12], refs[12:]
    fetch(args, [buf.at[pl.ds(i, 1)] for i in range(6)] + [qb, kb, vb, ob, rb, gb], sems)
    for j in range(group):
        cols = pl.ds(j * slab, slab)
        block = jnp.concatenate([buf[i, :, cols] for i in range(6)], axis=1)
        for p in range(j, w_out.shape[0], group):
            w_out[p] = block
    tokens, feat = gg_out.shape
    rate = jnp.broadcast_to(rb[...], (feat, tokens)).T
    tok_out[:, 0:feat] = qb[0]
    tok_out[:, feat : 2 * feat] = kb[0]
    tok_out[:, 2 * feat : 3 * feat] = (rate * vb[0].astype(F32)).astype(BF)
    q_out[...] = qb[0]
    gg_out[...] = gb[...] * ob[0].astype(F32)


def normalized(w, slab):
    parts = [w[:, pl.ds(i * slab, slab)].astype(F32) for i in range(6)]
    saved, init = parts[:3], parts[3:]
    norm_init = [column_norm(x) for x in init]
    norm_saved = [column_norm(x) for x in saved]
    ratio = [norm_init[i] / norm_saved[i] for i in range(3)]
    normed = [(saved[i] * ratio[i]).astype(BF) for i in range(3)]
    return saved, init, norm_init, norm_saved, ratio, normed


def forward_kernel(slab, group, place, w, *refs):
    toks, (out, part) = refs[:group], refs[group:]
    rank = place[1]
    feat = out.shape[-1]
    normed = normalized(w, slab)[-1]
    rows = jnp.concatenate([t[:, 0:feat] for t in toks], axis=0)
    hidden = (silu_parts(mm(rows, normed[0]))[0] * mm(rows, normed[1])).astype(BF)
    part[...] = mm_nt(hidden, normed[2]).astype(BF).reshape(part.shape)
    for d in range(group):
        out[rank ^ d] = part[d]


def delta_kernel(width, sums, apply_out, gg, out):
    tokens, feat = apply_out.shape
    square = jnp.broadcast_to(sums[0:1, :], (feat, tokens)).T
    gain = jnp.broadcast_to(sums[1:2, :], (feat, tokens)).T
    root = jnp.sqrt(square / width + EPS_ROOT)
    delta = (gg[...] / root - apply_out[...] * (gain / width) / (root * root * root)).astype(BF)
    for p in range(out.shape[0]):
        out[p] = delta


def backward_kernel(slab, group, tok_groups, place, w, *refs):
    toks, refs = refs[:group], refs[group:]
    far, refs = refs[: (tok_groups - 1) * group], refs[(tok_groups - 1) * group :]
    od, *refs = refs
    outs, (inner_out, q, tok, ag, au, ad) = refs[:group], refs[group:]
    mine, rank = place[0], place[1]
    saved, init, norm_init, norm_saved, ratio, normed = normalized(w, slab)
    own, feat = od.shape[1:]
    for d in range(group):
        q[0, rank ^ d] = toks[d][:, 0:feat]
        for e in range(1, tok_groups):
            q[e, rank ^ d] = far[(e - 1) * group + d][...]

    def query_side(rows, delta):
        q_gate = mm(rows, normed[0])
        q_up = mm(rows, normed[1])
        act, slope, _ = silu_parts(q_gate)
        hidden = (act * q_up).astype(BF)
        delta_hidden = mm(delta, normed[2])
        delta_gate = (delta_hidden * q_up * slope).astype(BF)
        delta_up = (delta_hidden * act).astype(BF)
        grads = (mm_tn(rows, delta_gate), mm_tn(rows, delta_up), mm_tn(delta, hidden))
        return delta_gate, delta_up, grads

    def take(e):
        return flat(q[e]), flat(od[pl.ds((mine ^ e) * group, group)])

    delta_gate, delta_up, grads = query_side(*take(0))
    grad_q = mm_nt(delta_gate, normed[0]) + mm_nt(delta_up, normed[1])
    tok[...] = grad_q.astype(BF).reshape(tok.shape)
    ag[...], au[...], ad[...] = grads

    def other(e, carry):
        more = query_side(*take(e))[2]
        ag[...] += more[0]
        au[...] += more[1]
        ad[...] += more[2]
        return carry

    lax.fori_loop(1, od.shape[0] // group, other, 0)

    apply_grad = (ag[...], au[...], ad[...])
    cots, direct = [], []
    share = jnp.where(mine == 0, 1.0, 0.0)
    for i in range(3):
        col_dot = jnp.sum(saved[i] * apply_grad[i], axis=0, keepdims=True)
        cot = apply_grad[i] * ratio[i] - saved[i] * (
            col_dot * norm_init[i] / (norm_saved[i] * norm_saved[i] * norm_saved[i])
        )
        cots.append(cot.astype(BF))
        direct.append((cot + init[i] * (col_dot / (norm_init[i] * norm_saved[i]))) * share)

    init_bf = [w[:, pl.ds((3 + i) * slab, slab)] for i in range(3)]
    keys = jnp.concatenate([t[:, feat : 2 * feat] for t in toks], axis=0)
    values = jnp.concatenate([t[:, 2 * feat : 3 * feat] for t in toks], axis=0)
    k_gate = mm(keys, init_bf[0])
    k_up = mm(keys, init_bf[1])
    k_proj = mm(values, init_bf[2])
    k_act, k_slope, k_bend = silu_parts(k_gate)
    k_hidden = (k_act * k_up).astype(BF)
    rise_gate = (k_proj * k_up * k_slope).astype(BF)
    rise_up = (k_proj * k_act).astype(BF)
    back_gate = mm(keys, cots[0])
    back_up = mm(keys, cots[1])
    back_hidden = mm(values, cots[2])
    back_proj = (back_gate * k_up * k_slope + back_up * k_act).astype(BF)
    back_kup = (back_gate * k_proj * k_slope + back_hidden * k_act).astype(BF)
    back_kgate = (
        back_gate * k_proj * k_up * k_bend + (back_up * k_proj + back_hidden * k_up) * k_slope
    ).astype(BF)
    grad_k = (
        mm_nt(rise_gate, cots[0])
        + mm_nt(rise_up, cots[1])
        + mm_nt(back_kgate, init_bf[0])
        + mm_nt(back_kup, init_bf[1])
    )
    grad_v = mm_nt(k_hidden, cots[2]) + mm_nt(back_proj, init_bf[2])
    grad_k = grad_k.astype(BF)
    grad_v = grad_v.astype(BF)
    for d in range(group):
        outs[d][:, 0:feat] = tok[rank ^ d]
        outs[d][:, feat : 2 * feat] = grad_k[d * own : (d + 1) * own]
        outs[d][:, 2 * feat : 3 * feat] = grad_v[d * own : (d + 1) * own]
    inner = (mm_tn(keys, back_kgate), mm_tn(keys, back_kup), mm_tn(values, back_proj))
    inner_out[...] = jnp.concatenate([inner[i] + direct[i] for i in range(3)], axis=1).astype(BF)


def tokens_kernel(rates, *refs):
    got, (gq, gk, gv) = refs[:-3], refs[-3:]
    tokens, feat = gq.shape[1:]
    total = got[0][...].astype(F32)
    for block in got[1:]:
        total += block[...].astype(F32)
    gq[0] = total[:, 0:feat].astype(BF)
    gk[0] = total[:, feat : 2 * feat].astype(BF)
    rate = jnp.broadcast_to(rates[...], (feat, tokens)).T
    gv[0] = (rate * total[:, 2 * feat : 3 * feat]).astype(BF)


def weights_kernel(group, slab, got, *outs):
    cols = []
    for j in range(group):
        total = got[j].astype(F32)
        for p in range(j + group, got.shape[0], group):
            total += got[p].astype(F32)
        cols.append(total)
    for i in range(3):
        outs[i][0] = jnp.concatenate([c[:, i * slab : (i + 1) * slab] for c in cols], axis=1)


def make_local(seq_n, head_n, group):
    tok_groups = seq_n // group
    groups = [[t * group + j for j in range(group)] for t in range(tok_groups)]

    def swap(blocks, axis_groups=None):
        return lax.all_to_all(blocks, "seq", 0, 0, axis_index_groups=axis_groups, tiled=True)

    def local(q, k, v, og, rates, gains, gi, ui, di, gs, us, ds):
        _, rows, hidden = gi.shape
        _, own, feat = q.shape
        slab = hidden // group
        near = group * own
        me = lax.axis_index("seq")
        place = jnp.stack((lax.div(me, group), lax.rem(me, group))).astype(jnp.int32)

        def near_all(x):
            return [x] + [lax.ppermute(x, "seq", [(i, i ^ d) for i in range(seq_n)]) for d in range(1, group)]

        args = (gs, us, ds, gi, ui, di, q, k, v, og, rates, gains)
        packed, tokens, queries, gg = copying_call(
            functools.partial(pack_kernel, group, slab),
            (
                arr((seq_n, rows, 6 * slab), BF),
                arr((own, 3 * feat), BF),
                arr((own, feat), BF),
                arr((own, feat), F32),
            ),
            args,
            [pltpu.VMEM((6, rows, hidden), BF), *[pltpu.VMEM(x.shape, x.dtype) for x in args[6:]]],
        )
        wall = swap(packed).reshape(seq_n * rows, 6 * slab)
        tokens = near_all(tokens)
        mirrored = [
            lax.ppermute(queries, "seq", [(i, i ^ (e * group)) for i in range(seq_n)])
            for e in range(1, tok_groups)
        ]

        (part,) = pl.pallas_call(
            functools.partial(forward_kernel, slab, group),
            out_shape=(arr((group, own, feat), BF),),
            in_specs=[SMEM] + [VMEM] * (group + 1),
            out_specs=[VMEM],
            scratch_shapes=[pltpu.VMEM((group, own, feat), BF)],
            compiler_params=pltpu.CompilerParams(vmem_limit_bytes=24 << 20),
            cost_estimate=pl.CostEstimate(
                flops=6 * near * feat * slab, bytes_accessed=4 * near * feat, transcendentals=0
            ),
        )(place, wall, *tokens)
        apply_out = jnp.sum(swap(part, groups).astype(F32), axis=0)
        sums = lax.psum(
            jnp.stack((jnp.sum(apply_out * apply_out, axis=1), jnp.sum(apply_out * gg, axis=1))), "head"
        )
        (od,) = call(
            functools.partial(delta_kernel, head_n * feat),
            (arr((seq_n, own, feat), BF),),
            (sums, apply_out, gg),
            0,
            16,
        )
        od, *mirrored = lax.optimization_barrier((od, *mirrored))
        od = swap(od)
        far = [block for m in mirrored for block in near_all(m)]

        *tok, inner = pl.pallas_call(
            functools.partial(backward_kernel, slab, group, tok_groups),
            out_shape=(*[arr((own, 3 * feat), BF)] * group, arr((seq_n * rows, 3 * slab), BF)),
            in_specs=[SMEM] + [VMEM] * (2 + group * tok_groups),
            out_specs=[VMEM] * (group + 1),
            scratch_shapes=[
                pltpu.VMEM((tok_groups, group, own, feat), BF),
                pltpu.VMEM((group, own, feat), BF),
                *[pltpu.VMEM((seq_n * rows, slab), F32)] * 3,
            ],
            compiler_params=pltpu.CompilerParams(vmem_limit_bytes=40 << 20),
            cost_estimate=pl.CostEstimate(
                flops=66 * near * feat * slab, bytes_accessed=8 * near * feat, transcendentals=0
            ),
        )(place, wall, *tokens, *far, od)
        inner = swap(inner.reshape(seq_n, rows, 3 * slab))
        tok = [tok[0]] + [
            lax.ppermute(tok[d], "seq", [(i, i ^ d) for i in range(seq_n)]) for d in range(1, group)
        ]
        out_tok = arr((1, own, feat), BF)
        grads_t = call(tokens_kernel, (out_tok, out_tok, out_tok), (rates, *tok), 0, 16)
        grad_w = arr((1, rows, hidden), F32)
        grads_w = call(
            functools.partial(weights_kernel, group, slab), (grad_w, grad_w, grad_w), (inner,), 0, 16
        )
        return (*grads_t, *grads_w)

    return local


def solution(mesh):
    seq_n = mesh.shape["seq"]
    head_n = mesh.shape["head"]
    group = min(4, seq_n)
    tok = P("head", "seq", None)
    return jax.shard_map(
        make_local(seq_n, head_n, group),
        mesh=mesh,
        in_specs=(tok, tok, tok, tok, P("head", "seq"), P("head", None), tok, tok, tok, tok, tok, tok),
        out_specs=(tok, tok, tok, tok, tok, tok),
        check_vma=False,
    )
```

```python
import functools

import jax
import jax.numpy as jnp
from jax import lax
from jax.experimental import pallas as pl
from jax.experimental.pallas import tpu as pltpu
from jax.sharding import PartitionSpec as P

EPS_COL = 1e-06
EPS_ROOT = 1e-05
BF = jnp.bfloat16
F32 = jnp.float32
VMEM = pl.BlockSpec(memory_space=pltpu.VMEM)
SMEM = pl.BlockSpec(memory_space=pltpu.SMEM)


def silu_parts(pre_act):
    sigmoid_val = jax.nn.sigmoid(pre_act)
    silu_val = pre_act * sigmoid_val
    silu_slope = sigmoid_val * (1.0 + pre_act * (1.0 - sigmoid_val))
    silu_bend = sigmoid_val * (1.0 - sigmoid_val) * (2.0 + pre_act * (1.0 - 2.0 * sigmoid_val))
    return (silu_val, silu_slope, silu_bend)


def mm(left_op, right_op):
    return jnp.dot(left_op, right_op, preferred_element_type=F32)


def mm_nt(left_op, right_op):
    return lax.dot_general(left_op, right_op, (((1,), (1,)), ((), ())), preferred_element_type=F32)


def mm_tn(left_op, right_op):
    return lax.dot_general(left_op, right_op, (((0,), (0,)), ((), ())), preferred_element_type=F32)


def column_norm(weight):
    return jnp.sqrt(jnp.sum(weight * weight, axis=0, keepdims=True) + EPS_COL)


def flat(x):
    return x.reshape(-1, x.shape[-1])


def call(kernel, outs, args, mib, smem=0, flops=0, scratch=()):
    moved = sum(x.size * x.dtype.itemsize for x in (*args, *outs))
    return pl.pallas_call(
        kernel,
        out_shape=outs,
        in_specs=[SMEM] * smem + [VMEM] * (len(args) - smem),
        out_specs=[VMEM] * len(outs),
        scratch_shapes=scratch,
        compiler_params=pltpu.CompilerParams(vmem_limit_bytes=mib << 20),
        cost_estimate=pl.CostEstimate(flops=flops, bytes_accessed=moved, transcendentals=0),
    )(*args)


def copying_call(kernel, outs, args, buffers):
    return pl.pallas_call(
        kernel,
        out_shape=outs,
        in_specs=[pl.BlockSpec(memory_space=pltpu.HBM)] * len(args),
        out_specs=[VMEM] * len(outs),
        scratch_shapes=[*buffers, pltpu.SemaphoreType.DMA((len(args),))],
        compiler_params=pltpu.CompilerParams(vmem_limit_bytes=56 << 20),
    )(*args)


def arr(shape, dtype):
    return jax.ShapeDtypeStruct(shape, dtype)


def fetch(sources, buffers, sems):
    copies = [pltpu.make_async_copy(s, b, sems.at[i]) for i, (s, b) in enumerate(zip(sources, buffers))]
    for copy in copies:
        copy.start()
    for copy in copies:
        copy.wait()


def token_pack_kernel(*refs):
    args, (tok_out, gg_out, qb, kb, vb, ob, rb, gb, sems) = refs[:6], refs[6:]
    fetch(args, (qb, kb, vb, ob, rb, gb), sems)
    tokens, feat = gg_out.shape
    rate = jnp.broadcast_to(rb[...], (feat, tokens)).T
    tok_out[:, 0:feat] = qb[0]
    tok_out[:, feat : 2 * feat] = kb[0]
    tok_out[:, 2 * feat : 3 * feat] = (rate * vb[0].astype(F32)).astype(BF)
    gg_out[...] = gb[...] * ob[0].astype(F32)


def weight_pack_kernel(group, slab, *refs):
    args, (w_out, buf, sems) = refs[:6], refs[6:]
    fetch(args, [buf.at[pl.ds(i, 1)] for i in range(6)], sems)
    for j in range(group):
        cols = pl.ds(j * slab, slab)
        block = jnp.concatenate([buf[i, :, cols] for i in range(6)], axis=1)
        for p in range(j, w_out.shape[0], group):
            w_out[p] = block


def normalized(w, slab):
    parts = [w[:, pl.ds(i * slab, slab)].astype(F32) for i in range(6)]
    saved, init = parts[:3], parts[3:]
    norm_init = [column_norm(x) for x in init]
    norm_saved = [column_norm(x) for x in saved]
    ratio = [norm_init[i] / norm_saved[i] for i in range(3)]
    normed = [(saved[i] * ratio[i]).astype(BF) for i in range(3)]
    return saved, init, norm_init, norm_saved, ratio, normed


def stack(refs, cols=slice(None)):
    return jnp.concatenate([r[:, cols] for r in refs], axis=0)


def forward_kernel(slab, group, w, *refs):
    tokens, mirrored, parts = refs[:group], refs[group:-group], refs[-group:]
    own, feat = parts[0].shape[0], parts[0].shape[1] // (1 + len(mirrored))
    normed = normalized(w, slab)[-1]
    rows = stack(tokens, slice(0, feat))
    hidden = (silu_parts(mm(rows, normed[0]))[0] * mm(rows, normed[1])).astype(BF)
    out = mm_nt(hidden, normed[2]).astype(BF)
    for d in range(group):
        parts[d][:, 0:feat] = out[d * own : (d + 1) * own]
        for e, queries in enumerate(mirrored):
            parts[d][:, (1 + e) * feat : (2 + e) * feat] = queries[...]


def reduce_kernel(gg, *refs):
    parts, (apply_out, sums) = refs[:-2], refs[-2:]
    feat = apply_out.shape[1]
    total = parts[0][:, 0:feat].astype(F32)
    for part in parts[1:]:
        total += part[:, 0:feat].astype(F32)
    apply_out[...] = total
    sums[0:1, :] = jnp.sum((total * total).T, axis=0, keepdims=True)
    sums[1:2, :] = jnp.sum((total * gg[...]).T, axis=0, keepdims=True)


def delta_kernel(width, apply_out, gg, *refs):
    sums, out = refs[:-1], refs[-1]
    tokens, feat = apply_out.shape
    total = sums[0][...]
    for more in sums[1:]:
        total += more[...]
    square = jnp.broadcast_to(total[0:1, :], (feat, tokens)).T
    gain = jnp.broadcast_to(total[1:2, :], (feat, tokens)).T
    root = jnp.sqrt(square / width + EPS_ROOT)
    out[...] = (gg[...] / root - apply_out[...] * (gain / width) / (root * root * root)).astype(BF)


def backward_kernel(slab, group, tok_groups, place, w, *refs):
    lists = []
    for count in (group, group, group, group * (tok_groups - 1), group, group * tok_groups):
        lists.append(refs[:count])
        refs = refs[count:]
    tokens, parts, od_near, od_far, outs, inner_outs = lists
    far_q, far_od, inner_all, ag, au, ad = refs
    mine, me = place[0], place[2]
    saved, init, norm_init, norm_saved, ratio, normed = normalized(w, slab)
    own, feat = od_near[0].shape
    for e in range(1, tok_groups):
        for d in range(group):
            far_q[e - 1, d] = parts[d][:, e * feat : (e + 1) * feat]
            far_od[e - 1, d] = od_far[(e - 1) * group + d][...]

    def query_side(rows, delta):
        q_gate = mm(rows, normed[0])
        q_up = mm(rows, normed[1])
        act, slope, _ = silu_parts(q_gate)
        hidden = (act * q_up).astype(BF)
        delta_hidden = mm(delta, normed[2])
        delta_gate = (delta_hidden * q_up * slope).astype(BF)
        delta_up = (delta_hidden * act).astype(BF)
        grads = (mm_tn(rows, delta_gate), mm_tn(rows, delta_up), mm_tn(delta, hidden))
        return delta_gate, delta_up, grads

    delta_gate, delta_up, grads = query_side(stack(tokens, slice(0, feat)), stack(od_near))
    grad_q = (mm_nt(delta_gate, normed[0]) + mm_nt(delta_up, normed[1])).astype(BF)
    ag[...], au[...], ad[...] = grads

    def other(e, carry):
        more = query_side(flat(far_q[e]), flat(far_od[e]))[2]
        ag[...] += more[0]
        au[...] += more[1]
        ad[...] += more[2]
        return carry

    lax.fori_loop(0, tok_groups - 1, other, 0)

    apply_grad = (ag[...], au[...], ad[...])
    cots, direct = [], []
    share = jnp.where(mine == 0, 1.0, 0.0)
    for i in range(3):
        col_dot = jnp.sum(saved[i] * apply_grad[i], axis=0, keepdims=True)
        cot = apply_grad[i] * ratio[i] - saved[i] * (
            col_dot * norm_init[i] / (norm_saved[i] * norm_saved[i] * norm_saved[i])
        )
        cots.append(cot.astype(BF))
        direct.append((cot + init[i] * (col_dot / (norm_init[i] * norm_saved[i]))) * share)

    init_bf = [w[:, pl.ds((3 + i) * slab, slab)] for i in range(3)]
    keys = stack(tokens, slice(feat, 2 * feat))
    values = stack(tokens, slice(2 * feat, 3 * feat))
    k_gate = mm(keys, init_bf[0])
    k_up = mm(keys, init_bf[1])
    k_proj = mm(values, init_bf[2])
    k_act, k_slope, k_bend = silu_parts(k_gate)
    k_hidden = (k_act * k_up).astype(BF)
    rise_gate = (k_proj * k_up * k_slope).astype(BF)
    rise_up = (k_proj * k_act).astype(BF)
    back_gate = mm(keys, cots[0])
    back_up = mm(keys, cots[1])
    back_hidden = mm(values, cots[2])
    back_proj = (back_gate * k_up * k_slope + back_up * k_act).astype(BF)
    back_kup = (back_gate * k_proj * k_slope + back_hidden * k_act).astype(BF)
    back_kgate = (
        back_gate * k_proj * k_up * k_bend + (back_up * k_proj + back_hidden * k_up) * k_slope
    ).astype(BF)
    grad_k = (
        mm_nt(rise_gate, cots[0])
        + mm_nt(rise_up, cots[1])
        + mm_nt(back_kgate, init_bf[0])
        + mm_nt(back_kup, init_bf[1])
    )
    grad_v = mm_nt(k_hidden, cots[2]) + mm_nt(back_proj, init_bf[2])
    grad_k = grad_k.astype(BF)
    grad_v = grad_v.astype(BF)
    for d in range(group):
        outs[d][:, 0:feat] = grad_q[d * own : (d + 1) * own]
        outs[d][:, feat : 2 * feat] = grad_k[d * own : (d + 1) * own]
        outs[d][:, 2 * feat : 3 * feat] = grad_v[d * own : (d + 1) * own]
    inner = (mm_tn(keys, back_kgate), mm_tn(keys, back_kup), mm_tn(values, back_proj))
    total = jnp.concatenate([inner[i] + direct[i] for i in range(3)], axis=1)
    rows = inner_all.shape[1]
    for p in range(inner_all.shape[0]):
        inner_all[p] = total[p * rows : (p + 1) * rows]
    for d, out in enumerate(inner_outs):
        out[...] = inner_all[me ^ d].astype(BF)


def tokens_kernel(rates, *refs):
    got, (gq, gk, gv) = refs[:-3], refs[-3:]
    tokens, feat = gq.shape[1:]
    total = got[0][...].astype(F32)
    for block in got[1:]:
        total += block[...].astype(F32)
    gq[0] = total[:, 0:feat].astype(BF)
    gk[0] = total[:, feat : 2 * feat].astype(BF)
    rate = jnp.broadcast_to(rates[...], (feat, tokens)).T
    gv[0] = (rate * total[:, 2 * feat : 3 * feat]).astype(BF)


def weights_kernel(group, slab, place, *refs):
    got, outs, total = refs[:-4], refs[-4:-1], refs[-1]
    for d in range(group):
        block = got[d][...].astype(F32)
        for more in got[d + group :: group]:
            block += more[...].astype(F32)
        total[d] = block
    cols = [total[place[1] ^ j] for j in range(group)]
    for i in range(3):
        outs[i][0] = jnp.concatenate([c[:, i * slab : (i + 1) * slab] for c in cols], axis=1)


def make_local(seq_n, head_n, group):
    tok_groups = seq_n // group

    def move(x, dist, axis="seq", size=seq_n):
        return lax.ppermute(x, axis, [(i, i ^ dist) for i in range(size)])

    def near_all(x):
        return [x] + [move(x, d) for d in range(1, group)]

    def mirror(x):
        return [move(x, e * group) for e in range(1, tok_groups)]

    def local(q, k, v, og, rates, gains, gi, ui, di, gs, us, ds):
        _, rows, hidden = gi.shape
        _, own, feat = q.shape
        slab = hidden // group
        near = group * own
        me = lax.axis_index("seq")
        place = jnp.stack((lax.div(me, group), lax.rem(me, group), me)).astype(jnp.int32)

        q_mirror = mirror(q[0])
        tok_args = (q, k, v, og, rates, gains)
        tokens, gg = copying_call(
            token_pack_kernel,
            (arr((own, 3 * feat), BF), arr((own, feat), F32)),
            tok_args,
            [pltpu.VMEM(x.shape, x.dtype) for x in tok_args],
        )
        tokens = near_all(tokens)
        (packed,) = copying_call(
            functools.partial(weight_pack_kernel, group, slab),
            (arr((seq_n, rows, 6 * slab), BF),),
            (gs, us, ds, gi, ui, di),
            [pltpu.VMEM((6, rows, hidden), BF)],
        )
        wall = lax.all_to_all(packed, "seq", 0, 0, tiled=True).reshape(seq_n * rows, 6 * slab)

        block = arr((own, feat), BF)
        parts = call(
            functools.partial(forward_kernel, slab, group),
            (arr((own, feat * tok_groups), BF),) * group,
            (wall, *tokens, *q_mirror),
            24,
            flops=6 * near * feat * slab,
        )
        parts = [parts[0]] + [move(parts[d], d) for d in range(1, group)]
        apply_out, sums = call(
            reduce_kernel, (arr((own, feat), F32), arr((2, own), F32)), (gg, *parts), 16
        )
        sums = [sums] + [move(sums, d, "head", head_n) for d in range(1, head_n)]
        (od,) = call(functools.partial(delta_kernel, head_n * feat), (block,), (apply_out, gg, *sums), 16)
        od_mirror = mirror(od)
        od_near = near_all(od)
        od_far = [x for m in od_mirror for x in near_all(m)]

        far = pltpu.VMEM((max(tok_groups - 1, 1), group, own, feat), BF)
        result = call(
            functools.partial(backward_kernel, slab, group, tok_groups),
            (arr((own, 3 * feat), BF),) * group + (arr((rows, 3 * slab), BF),) * seq_n,
            (place, wall, *tokens, *parts, *od_near, *od_far),
            40,
            smem=1,
            flops=66 * near * feat * slab,
            scratch=[
                far,
                far,
                pltpu.VMEM((seq_n, rows, 3 * slab), F32),
                *[pltpu.VMEM((seq_n * rows, slab), F32)] * 3,
            ],
        )
        tok, inner = result[:group], result[group:]
        tok = [tok[0]] + [move(tok[d], d) for d in range(1, group)]
        inner = [inner[0]] + [move(inner[d], d) for d in range(1, seq_n)]
        out_tok = arr((1, own, feat), BF)
        grad_w = arr((1, rows, hidden), F32)
        grads_t = call(tokens_kernel, (out_tok,) * 3, (rates, *tok), 16)
        grads_w = call(
            functools.partial(weights_kernel, group, slab),
            (grad_w,) * 3,
            (place, *inner),
            16,
            smem=1,
            scratch=[pltpu.VMEM((group, rows, 3 * slab), F32)],
        )
        return (*grads_t, *grads_w)

    return local


def solution(mesh):
    seq_n = mesh.shape["seq"]
    head_n = mesh.shape["head"]
    group = min(4, seq_n)
    tok = P("head", "seq", None)
    return jax.shard_map(
        make_local(seq_n, head_n, group),
        mesh=mesh,
        in_specs=(tok, tok, tok, tok, P("head", "seq"), P("head", None), tok, tok, tok, tok, tok, tok),
        out_specs=(tok, tok, tok, tok, tok, tok),
        check_vma=False,
    )
```

```python
import functools

import jax
import jax.numpy as jnp
from jax import lax
from jax.experimental import pallas as pl
from jax.experimental.pallas import tpu as pltpu
from jax.sharding import PartitionSpec as P

EPS_COL = 1e-06
EPS_ROOT = 1e-05
BF = jnp.bfloat16
F32 = jnp.float32
VMEM = pl.BlockSpec(memory_space=pltpu.VMEM)
SMEM = pl.BlockSpec(memory_space=pltpu.SMEM)


def silu_parts(pre_act):
    sigmoid_val = jax.nn.sigmoid(pre_act)
    silu_val = pre_act * sigmoid_val
    silu_slope = sigmoid_val * (1.0 + pre_act * (1.0 - sigmoid_val))
    silu_bend = sigmoid_val * (1.0 - sigmoid_val) * (2.0 + pre_act * (1.0 - 2.0 * sigmoid_val))
    return (silu_val, silu_slope, silu_bend)


def mm(left_op, right_op):
    return jnp.dot(left_op, right_op, preferred_element_type=F32)


def mm_nt(left_op, right_op):
    return lax.dot_general(left_op, right_op, (((1,), (1,)), ((), ())), preferred_element_type=F32)


def mm_tn(left_op, right_op):
    return lax.dot_general(left_op, right_op, (((0,), (0,)), ((), ())), preferred_element_type=F32)


def column_norm(weight):
    return jnp.sqrt(jnp.sum(weight * weight, axis=0, keepdims=True) + EPS_COL)


def flat(x):
    return x.reshape(-1, x.shape[-1])


def call(kernel, outs, args, mib, smem=0, flops=0, scratch=()):
    moved = sum(x.size * x.dtype.itemsize for x in (*args, *outs))
    return pl.pallas_call(
        kernel,
        out_shape=outs,
        in_specs=[SMEM] * smem + [VMEM] * (len(args) - smem),
        out_specs=[VMEM] * len(outs),
        scratch_shapes=scratch,
        compiler_params=pltpu.CompilerParams(vmem_limit_bytes=mib << 20),
        cost_estimate=pl.CostEstimate(flops=flops, bytes_accessed=moved, transcendentals=0),
    )(*args)


def copying_call(kernel, outs, args, buffers):
    return pl.pallas_call(
        kernel,
        out_shape=outs,
        in_specs=[pl.BlockSpec(memory_space=pltpu.HBM)] * len(args),
        out_specs=[VMEM] * len(outs),
        scratch_shapes=[*buffers, pltpu.SemaphoreType.DMA((len(args),))],
        compiler_params=pltpu.CompilerParams(vmem_limit_bytes=56 << 20),
    )(*args)


def arr(shape, dtype):
    return jax.ShapeDtypeStruct(shape, dtype)


def fetch(sources, buffers, sems):
    copies = [pltpu.make_async_copy(s, b, sems.at[i]) for i, (s, b) in enumerate(zip(sources, buffers))]
    for copy in copies:
        copy.start()
    for copy in copies:
        copy.wait()


def token_pack_kernel(k, v, og, rates, gains, kv_out, gg_out, rate_out):
    tokens, feat = gg_out.shape
    rate = jnp.broadcast_to(rates[...], (feat, tokens)).T
    kv_out[:, 0:feat] = k[0]
    kv_out[:, feat : 2 * feat] = (rate * v[0].astype(F32)).astype(BF)
    gg_out[...] = gains[...] * og[0].astype(F32)
    rate_out[...] = rate


def weight_pack_kernel(group, slab, *refs):
    args, (w_out, buf, sems) = refs[:6], refs[6:]
    fetch(args, [buf.at[pl.ds(i, 1)] for i in range(6)], sems)
    for j in range(group):
        cols = pl.ds(j * slab, slab)
        block = jnp.concatenate([buf[i, :, cols] for i in range(6)], axis=1)
        for p in range(j, w_out.shape[0], group):
            w_out[p] = block


def normalized(w, slab):
    parts = [w[:, pl.ds(i * slab, slab)].astype(F32) for i in range(6)]
    saved, init = parts[:3], parts[3:]
    norm_init = [column_norm(x) for x in init]
    norm_saved = [column_norm(x) for x in saved]
    ratio = [norm_init[i] / norm_saved[i] for i in range(3)]
    normed = [(saved[i] * ratio[i]).astype(BF) for i in range(3)]
    return saved, init, norm_init, norm_saved, ratio, normed


def stack(refs, cols=slice(None)):
    return jnp.concatenate([r[:, cols] for r in refs], axis=0)


def forward_kernel(slab, group, w, *refs):
    queries, parts = refs[:group], refs[group:]
    normed = normalized(w, slab)[-1]
    rows = stack(queries)
    hidden = (silu_parts(mm(rows, normed[0]))[0] * mm(rows, normed[1])).astype(BF)
    out = mm_nt(hidden, normed[2]).astype(BF)
    own = rows.shape[0] // group
    for d in range(group):
        parts[d][...] = out[d * own : (d + 1) * own]


def reduce_kernel(gg, *refs):
    parts, (apply_out, sums) = refs[:-2], refs[-2:]
    total = parts[0][...].astype(F32)
    for part in parts[1:]:
        total += part[...].astype(F32)
    apply_out[...] = total
    sums[0:1, :] = jnp.sum((total * total).T, axis=0, keepdims=True)
    sums[1:2, :] = jnp.sum((total * gg[...]).T, axis=0, keepdims=True)


def delta_kernel(width, apply_out, gg, kv, *refs):
    sums, (od_out, out) = refs[:-2], refs[-2:]
    tokens, feat = apply_out.shape
    total = sums[0][...]
    for more in sums[1:]:
        total += more[...]
    square = jnp.broadcast_to(total[0:1, :], (feat, tokens)).T
    gain = jnp.broadcast_to(total[1:2, :], (feat, tokens)).T
    root = jnp.sqrt(square / width + EPS_ROOT)
    delta = (gg[...] / root - apply_out[...] * (gain / width) / (root * root * root)).astype(BF)
    od_out[...] = delta
    out[:, 0:feat] = delta
    out[:, feat : 3 * feat] = kv[...]


def backward_kernel(slab, group, tok_groups, place, w, *refs):
    far = group * (tok_groups - 1)
    lists = []
    for count in (group, far, group, far, group, tok_groups):
        lists.append(refs[:count])
        refs = refs[count:]
    q_near, q_far, tokens, od_far, outs, homes = lists
    far_q, far_od, home, ag, au, ad = refs
    mine = place[0]
    saved, init, norm_init, norm_saved, ratio, normed = normalized(w, slab)
    own, feat = q_near[0].shape
    for i in range(far):
        far_q[i // group, i % group] = q_far[i][...]
        far_od[i // group, i % group] = od_far[i][...]

    def query_side(rows, delta):
        q_gate = mm(rows, normed[0])
        q_up = mm(rows, normed[1])
        act, slope, _ = silu_parts(q_gate)
        hidden = (act * q_up).astype(BF)
        delta_hidden = mm(delta, normed[2])
        delta_gate = (delta_hidden * q_up * slope).astype(BF)
        delta_up = (delta_hidden * act).astype(BF)
        grads = (mm_tn(rows, delta_gate), mm_tn(rows, delta_up), mm_tn(delta, hidden))
        return delta_gate, delta_up, grads

    delta_gate, delta_up, grads = query_side(stack(q_near), stack(tokens, slice(0, feat)))
    grad_q = (mm_nt(delta_gate, normed[0]) + mm_nt(delta_up, normed[1])).astype(BF)
    ag[...], au[...], ad[...] = grads

    def other(e, carry):
        more = query_side(flat(far_q[e]), flat(far_od[e]))[2]
        ag[...] += more[0]
        au[...] += more[1]
        ad[...] += more[2]
        return carry

    lax.fori_loop(0, tok_groups - 1, other, 0)

    apply_grad = (ag[...], au[...], ad[...])
    cots, direct = [], []
    share = jnp.where(mine == 0, 1.0, 0.0)
    for i in range(3):
        col_dot = jnp.sum(saved[i] * apply_grad[i], axis=0, keepdims=True)
        cot = apply_grad[i] * ratio[i] - saved[i] * (
            col_dot * norm_init[i] / (norm_saved[i] * norm_saved[i] * norm_saved[i])
        )
        cots.append(cot.astype(BF))
        direct.append((cot + init[i] * (col_dot / (norm_init[i] * norm_saved[i]))) * share)

    init_bf = [w[:, pl.ds((3 + i) * slab, slab)] for i in range(3)]
    keys = stack(tokens, slice(feat, 2 * feat))
    values = stack(tokens, slice(2 * feat, 3 * feat))
    k_gate = mm(keys, init_bf[0])
    k_up = mm(keys, init_bf[1])
    k_proj = mm(values, init_bf[2])
    k_act, k_slope, k_bend = silu_parts(k_gate)
    k_hidden = (k_act * k_up).astype(BF)
    rise_gate = (k_proj * k_up * k_slope).astype(BF)
    rise_up = (k_proj * k_act).astype(BF)
    back_gate = mm(keys, cots[0])
    back_up = mm(keys, cots[1])
    back_hidden = mm(values, cots[2])
    back_proj = (back_gate * k_up * k_slope + back_up * k_act).astype(BF)
    back_kup = (back_gate * k_proj * k_slope + back_hidden * k_act).astype(BF)
    back_kgate = (
        back_gate * k_proj * k_up * k_bend + (back_up * k_proj + back_hidden * k_up) * k_slope
    ).astype(BF)
    grad_k = (
        mm_nt(rise_gate, cots[0])
        + mm_nt(rise_up, cots[1])
        + mm_nt(back_kgate, init_bf[0])
        + mm_nt(back_kup, init_bf[1])
    )
    grad_v = mm_nt(k_hidden, cots[2]) + mm_nt(back_proj, init_bf[2])
    grad_k = grad_k.astype(BF)
    grad_v = grad_v.astype(BF)
    for d in range(group):
        outs[d][:, 0:feat] = grad_q[d * own : (d + 1) * own]
        outs[d][:, feat : 2 * feat] = grad_k[d * own : (d + 1) * own]
        outs[d][:, 2 * feat : 3 * feat] = grad_v[d * own : (d + 1) * own]
    inner = (mm_tn(keys, back_kgate), mm_tn(keys, back_kup), mm_tn(values, back_proj))
    total = jnp.concatenate([inner[i] + direct[i] for i in range(3)], axis=1)
    rows = home.shape[1]
    for t in range(tok_groups):
        home[t] = total[t * rows : (t + 1) * rows]
    for e, out in enumerate(homes):
        out[...] = home[mine ^ e].astype(out.dtype)


def home_kernel(group, place, *refs):
    blocks, outs, total = refs[: -group - 1], refs[-group - 1 : -1], refs[-1]
    whole = blocks[0][...]
    for block in blocks[1:]:
        whole += block[...].astype(F32)
    rows = total.shape[1]
    for j in range(group):
        total[j] = whole[j * rows : (j + 1) * rows]
    for d in range(group):
        outs[d][...] = total[place[1] ^ d].astype(BF)


def tokens_kernel(rate, *refs):
    got, (gq, gk, gv) = refs[:-3], refs[-3:]
    feat = gq.shape[2]
    total = got[0][...].astype(F32)
    for block in got[1:]:
        total += block[...].astype(F32)
    gq[0] = total[:, 0:feat].astype(BF)
    gk[0] = total[:, feat : 2 * feat].astype(BF)
    gv[0] = (rate[...] * total[:, 2 * feat : 3 * feat]).astype(BF)


def weights_kernel(group, slab, place, *refs):
    got, outs, total = refs[:-4], refs[-4:-1], refs[-1]
    for d in range(group):
        total[d] = got[d][...].astype(F32)
    cols = [total[place[1] ^ j] for j in range(group)]
    for i in range(3):
        outs[i][0] = jnp.concatenate([c[:, i * slab : (i + 1) * slab] for c in cols], axis=1)


def make_local(seq_n, head_n, group):
    tok_groups = seq_n // group

    def move(x, dist, axis="seq", size=seq_n):
        return lax.ppermute(x, axis, [(i, i ^ dist) for i in range(size)])

    def near_all(x):
        return [x] + [move(x, d) for d in range(1, group)]

    def mirror(x):
        return [move(x, e * group) for e in range(1, tok_groups)]

    def local(q, k, v, og, rates, gains, gi, ui, di, gs, us, ds):
        _, rows, hidden = gi.shape
        _, own, feat = q.shape
        slab = hidden // group
        near = group * own
        me = lax.axis_index("seq")
        place = jnp.stack((lax.div(me, group), lax.rem(me, group), me)).astype(jnp.int32)

        (packed,) = copying_call(
            functools.partial(weight_pack_kernel, group, slab),
            (arr((seq_n, rows, 6 * slab), BF),),
            (gs, us, ds, gi, ui, di),
            [pltpu.VMEM((6, rows, hidden), BF)],
        )
        packed, queries = lax.optimization_barrier((packed, q[0]))
        wall = lax.all_to_all(packed, "seq", 0, 0, tiled=True).reshape(seq_n * rows, 6 * slab)
        q_near = near_all(queries)
        q_far = [x for m in mirror(queries) for x in near_all(m)]
        kv, gg, rate = call(
            token_pack_kernel,
            (arr((own, 2 * feat), BF), arr((own, feat), F32), arr((own, feat), F32)),
            (k, v, og, rates, gains),
            8,
        )
        wall, kv, *q_far = lax.optimization_barrier((wall, kv, *q_far))

        block = arr((own, feat), BF)
        parts = call(
            functools.partial(forward_kernel, slab, group),
            (block,) * group,
            (wall, *q_near),
            24,
            flops=6 * near * feat * slab,
        )
        parts = [parts[0]] + [move(parts[d], d) for d in range(1, group)]
        apply_out, sums = call(
            reduce_kernel, (arr((own, feat), F32), arr((2, own), F32)), (gg, *parts), 16
        )
        sums = [sums] + [move(sums, d, "head", head_n) for d in range(1, head_n)]
        od, tokens = call(
            functools.partial(delta_kernel, head_n * feat),
            (block, arr((own, 3 * feat), BF)),
            (apply_out, gg, kv, *sums),
            16,
        )
        od_mirror = mirror(od)
        tokens = near_all(tokens)
        od_far = [x for m in od_mirror for x in near_all(m)]

        far = pltpu.VMEM((max(tok_groups - 1, 1), group, own, feat), BF)
        home = (group * rows, 3 * slab)
        result = call(
            functools.partial(backward_kernel, slab, group, tok_groups),
            (
                *(arr((own, 3 * feat), BF),) * group,
                arr(home, F32),
                *(arr(home, BF),) * (tok_groups - 1),
            ),
            (place, wall, *q_near, *q_far, *tokens, *od_far),
            40,
            smem=1,
            flops=66 * near * feat * slab,
            scratch=[
                far,
                far,
                pltpu.VMEM((tok_groups, *home), F32),
                *[pltpu.VMEM((seq_n * rows, slab), F32)] * 3,
            ],
        )
        tok, inner = result[:group], result[group:]
        inner = [inner[0]] + [move(inner[e], e * group) for e in range(1, tok_groups)]
        tok = [tok[0]] + [move(tok[d], d) for d in range(1, group)]
        inner = call(
            functools.partial(home_kernel, group),
            (arr((rows, 3 * slab), BF),) * group,
            (place, *inner),
            16,
            smem=1,
            scratch=[pltpu.VMEM((group, rows, 3 * slab), F32)],
        )
        inner = [inner[0]] + [move(inner[d], d) for d in range(1, group)]
        out_tok = arr((1, own, feat), BF)
        grad_w = arr((1, rows, hidden), F32)
        grads_t = call(tokens_kernel, (out_tok,) * 3, (rate, *tok), 16)
        grads_w = call(
            functools.partial(weights_kernel, group, slab),
            (grad_w,) * 3,
            (place, *inner),
            16,
            smem=1,
            scratch=[pltpu.VMEM((group, rows, 3 * slab), F32)],
        )
        return (*grads_t, *grads_w)

    return local


def solution(mesh):
    seq_n = mesh.shape["seq"]
    head_n = mesh.shape["head"]
    group = min(4, seq_n)
    tok = P("head", "seq", None)
    return jax.shard_map(
        make_local(seq_n, head_n, group),
        mesh=mesh,
        in_specs=(tok, tok, tok, tok, P("head", "seq"), P("head", None), tok, tok, tok, tok, tok, tok),
        out_specs=(tok, tok, tok, tok, tok, tok),
        check_vma=False,
    )
```

```python
import functools

import jax
import jax.numpy as jnp
from jax import lax
from jax.experimental import pallas as pl
from jax.experimental.pallas import tpu as pltpu
from jax.sharding import PartitionSpec as P

EPS_COL = 1e-06
EPS_ROOT = 1e-05
BF = jnp.bfloat16
F32 = jnp.float32
VMEM = pl.BlockSpec(memory_space=pltpu.VMEM)
SMEM = pl.BlockSpec(memory_space=pltpu.SMEM)


def silu_parts(pre_act):
    sigmoid_val = jax.nn.sigmoid(pre_act)
    silu_val = pre_act * sigmoid_val
    silu_slope = sigmoid_val * (1.0 + pre_act * (1.0 - sigmoid_val))
    silu_bend = sigmoid_val * (1.0 - sigmoid_val) * (2.0 + pre_act * (1.0 - 2.0 * sigmoid_val))
    return (silu_val, silu_slope, silu_bend)


def mm(left_op, right_op):
    return jnp.dot(left_op, right_op, preferred_element_type=F32)


def mm_nt(left_op, right_op):
    return lax.dot_general(left_op, right_op, (((1,), (1,)), ((), ())), preferred_element_type=F32)


def mm_tn(left_op, right_op):
    return lax.dot_general(left_op, right_op, (((0,), (0,)), ((), ())), preferred_element_type=F32)


def column_norm(weight):
    return jnp.sqrt(jnp.sum(weight * weight, axis=0, keepdims=True) + EPS_COL)


def flat(x):
    return x.reshape(-1, x.shape[-1])


def call(kernel, outs, args, mib, smem=0, flops=0, scratch=()):
    moved = sum(x.size * x.dtype.itemsize for x in (*args, *outs))
    return pl.pallas_call(
        kernel,
        out_shape=outs,
        in_specs=[SMEM] * smem + [VMEM] * (len(args) - smem),
        out_specs=[VMEM] * len(outs),
        scratch_shapes=scratch,
        compiler_params=pltpu.CompilerParams(vmem_limit_bytes=mib << 20),
        cost_estimate=pl.CostEstimate(flops=flops, bytes_accessed=moved, transcendentals=0),
    )(*args)


def copying_call(kernel, outs, args, buffers):
    return pl.pallas_call(
        kernel,
        out_shape=outs,
        in_specs=[pl.BlockSpec(memory_space=pltpu.HBM)] * len(args),
        out_specs=[VMEM] * len(outs),
        scratch_shapes=[*buffers, pltpu.SemaphoreType.DMA((len(args),))],
        compiler_params=pltpu.CompilerParams(vmem_limit_bytes=56 << 20),
    )(*args)


def arr(shape, dtype):
    return jax.ShapeDtypeStruct(shape, dtype)


def fetch(sources, buffers, sems):
    copies = [pltpu.make_async_copy(s, b, sems.at[i]) for i, (s, b) in enumerate(zip(sources, buffers))]
    for copy in copies:
        copy.start()
    for copy in copies:
        copy.wait()


def token_pack_kernel(k, v, og, rates, gains, kv_out, gg_out, rate_out):
    tokens, feat = gg_out.shape
    rate = jnp.broadcast_to(rates[...], (feat, tokens)).T
    values = (rate * v[0].astype(F32)).astype(BF)
    for j in range(kv_out.shape[0]):
        kv_out[j, :, 0:feat] = k[0]
        kv_out[j, :, feat : 2 * feat] = values
    gg_out[...] = gains[...] * og[0].astype(F32)
    rate_out[...] = rate


def weight_pack_kernel(group, slab, *refs):
    args, (w_out, buf, sems) = refs[:6], refs[6:]
    fetch(args, [buf.at[pl.ds(i, 1)] for i in range(6)], sems)
    for j in range(group):
        cols = pl.ds(j * slab, slab)
        block = jnp.concatenate([buf[i, :, cols] for i in range(6)], axis=1)
        for p in range(j, w_out.shape[0], group):
            w_out[p] = block


def normalized(w, slab):
    parts = [w[:, pl.ds(i * slab, slab)].astype(F32) for i in range(6)]
    saved, init = parts[:3], parts[3:]
    norm_init = [column_norm(x) for x in init]
    norm_saved = [column_norm(x) for x in saved]
    ratio = [norm_init[i] / norm_saved[i] for i in range(3)]
    normed = [(saved[i] * ratio[i]).astype(BF) for i in range(3)]
    return saved, init, norm_init, norm_saved, ratio, normed


def stack(refs, cols=slice(None)):
    return jnp.concatenate([r[:, cols] for r in refs], axis=0)


def forward_kernel(slab, group, w, *refs):
    queries, parts = refs[:group], refs[group:]
    normed = normalized(w, slab)[-1]
    rows = stack(queries)
    hidden = (silu_parts(mm(rows, normed[0]))[0] * mm(rows, normed[1])).astype(BF)
    out = mm_nt(hidden, normed[2]).astype(BF)
    own = rows.shape[0] // group
    for d in range(group):
        parts[d][...] = out[d * own : (d + 1) * own]


def reduce_kernel(gg, *refs):
    parts, (apply_out, sums) = refs[:-2], refs[-2:]
    total = parts[0][...].astype(F32)
    for part in parts[1:]:
        total += part[...].astype(F32)
    apply_out[...] = total
    sums[0:1, :] = jnp.sum((total * total).T, axis=0, keepdims=True)
    sums[1:2, :] = jnp.sum((total * gg[...]).T, axis=0, keepdims=True)


def delta_kernel(width, apply_out, gg, *refs):
    sums, out = refs[:-1], refs[-1]
    tokens, feat = apply_out.shape
    total = sums[0][...]
    for more in sums[1:]:
        total += more[...]
    square = jnp.broadcast_to(total[0:1, :], (feat, tokens)).T
    gain = jnp.broadcast_to(total[1:2, :], (feat, tokens)).T
    root = jnp.sqrt(square / width + EPS_ROOT)
    out[...] = (gg[...] / root - apply_out[...] * (gain / width) / (root * root * root)).astype(BF)


def pair_kernel(left, right, out):
    feat = left.shape[1]
    out[:, 0:feat] = left[...]
    out[:, feat : 2 * feat] = right[...]


def backward_kernel(slab, group, tok_groups, place, w, kv, *refs):
    far = group * (tok_groups - 1)
    lists = []
    for count in (group, group, far, group, tok_groups):
        lists.append(refs[:count])
        refs = refs[count:]
    q_near, od_near, pairs, outs, homes = lists
    far_q, far_od, home, ag, au, ad = refs
    mine = place[0]
    saved, init, norm_init, norm_saved, ratio, normed = normalized(w, slab)
    own, feat = q_near[0].shape
    for i in range(far):
        far_od[i // group, i % group] = pairs[i][:, 0:feat]
        far_q[i // group, i % group] = pairs[i][:, feat : 2 * feat]

    def query_side(rows, delta):
        q_gate = mm(rows, normed[0])
        q_up = mm(rows, normed[1])
        act, slope, _ = silu_parts(q_gate)
        hidden = (act * q_up).astype(BF)
        delta_hidden = mm(delta, normed[2])
        delta_gate = (delta_hidden * q_up * slope).astype(BF)
        delta_up = (delta_hidden * act).astype(BF)
        grads = (mm_tn(rows, delta_gate), mm_tn(rows, delta_up), mm_tn(delta, hidden))
        return delta_gate, delta_up, grads

    delta_gate, delta_up, grads = query_side(stack(q_near), stack(od_near))
    grad_q = (mm_nt(delta_gate, normed[0]) + mm_nt(delta_up, normed[1])).astype(BF)
    ag[...], au[...], ad[...] = grads

    def other(e, carry):
        more = query_side(flat(far_q[e]), flat(far_od[e]))[2]
        ag[...] += more[0]
        au[...] += more[1]
        ad[...] += more[2]
        return carry

    lax.fori_loop(0, tok_groups - 1, other, 0)

    apply_grad = (ag[...], au[...], ad[...])
    cots, direct = [], []
    share = jnp.where(mine == 0, 1.0, 0.0)
    for i in range(3):
        col_dot = jnp.sum(saved[i] * apply_grad[i], axis=0, keepdims=True)
        cot = apply_grad[i] * ratio[i] - saved[i] * (
            col_dot * norm_init[i] / (norm_saved[i] * norm_saved[i] * norm_saved[i])
        )
        cots.append(cot.astype(BF))
        direct.append((cot + init[i] * (col_dot / (norm_init[i] * norm_saved[i]))) * share)

    init_bf = [w[:, pl.ds((3 + i) * slab, slab)] for i in range(3)]
    rank = place[1]
    keys = jnp.concatenate([kv[rank ^ d, :, 0:feat] for d in range(group)], axis=0)
    values = jnp.concatenate([kv[rank ^ d, :, feat : 2 * feat] for d in range(group)], axis=0)
    k_gate = mm(keys, init_bf[0])
    k_up = mm(keys, init_bf[1])
    k_proj = mm(values, init_bf[2])
    k_act, k_slope, k_bend = silu_parts(k_gate)
    k_hidden = (k_act * k_up).astype(BF)
    rise_gate = (k_proj * k_up * k_slope).astype(BF)
    rise_up = (k_proj * k_act).astype(BF)
    back_gate = mm(keys, cots[0])
    back_up = mm(keys, cots[1])
    back_hidden = mm(values, cots[2])
    back_proj = (back_gate * k_up * k_slope + back_up * k_act).astype(BF)
    back_kup = (back_gate * k_proj * k_slope + back_hidden * k_act).astype(BF)
    back_kgate = (
        back_gate * k_proj * k_up * k_bend + (back_up * k_proj + back_hidden * k_up) * k_slope
    ).astype(BF)
    grad_k = (
        mm_nt(rise_gate, cots[0])
        + mm_nt(rise_up, cots[1])
        + mm_nt(back_kgate, init_bf[0])
        + mm_nt(back_kup, init_bf[1])
    )
    grad_v = mm_nt(k_hidden, cots[2]) + mm_nt(back_proj, init_bf[2])
    grad_k = grad_k.astype(BF)
    grad_v = grad_v.astype(BF)
    for d in range(group):
        outs[d][:, 0:feat] = grad_q[d * own : (d + 1) * own]
        outs[d][:, feat : 2 * feat] = grad_k[d * own : (d + 1) * own]
        outs[d][:, 2 * feat : 3 * feat] = grad_v[d * own : (d + 1) * own]
    inner = (mm_tn(keys, back_kgate), mm_tn(keys, back_kup), mm_tn(values, back_proj))
    total = jnp.concatenate([inner[i] + direct[i] for i in range(3)], axis=1)
    rows = home.shape[1]
    for t in range(tok_groups):
        home[t] = total[t * rows : (t + 1) * rows]
    for e, out in enumerate(homes):
        out[...] = home[mine ^ e].astype(out.dtype)


def home_kernel(group, place, *refs):
    blocks, outs, total = refs[: -group - 1], refs[-group - 1 : -1], refs[-1]
    whole = blocks[0][...]
    for block in blocks[1:]:
        whole += block[...].astype(F32)
    rows = total.shape[1]
    for j in range(group):
        total[j] = whole[j * rows : (j + 1) * rows]
    for d in range(group):
        outs[d][...] = total[place[1] ^ d].astype(BF)


def tokens_kernel(rate, *refs):
    got, (gq, gk, gv) = refs[:-3], refs[-3:]
    feat = gq.shape[2]
    total = got[0][...].astype(F32)
    for block in got[1:]:
        total += block[...].astype(F32)
    gq[0] = total[:, 0:feat].astype(BF)
    gk[0] = total[:, feat : 2 * feat].astype(BF)
    gv[0] = (rate[...] * total[:, 2 * feat : 3 * feat]).astype(BF)


def weights_kernel(group, slab, place, *refs):
    got, outs, total = refs[:-4], refs[-4:-1], refs[-1]
    for d in range(group):
        total[d] = got[d][...].astype(F32)
    cols = [total[place[1] ^ j] for j in range(group)]
    for i in range(3):
        outs[i][0] = jnp.concatenate([c[:, i * slab : (i + 1) * slab] for c in cols], axis=1)


def make_local(seq_n, head_n, group):
    tok_groups = seq_n // group
    groups = [[t * group + j for j in range(group)] for t in range(tok_groups)]

    def move(x, dist, axis="seq", size=seq_n):
        return lax.ppermute(x, axis, [(i, i ^ dist) for i in range(size)])

    def near_all(x):
        return [x] + [move(x, d) for d in range(1, group)]

    def mirror(x):
        return [move(x, e * group) for e in range(1, tok_groups)]

    def local(q, k, v, og, rates, gains, gi, ui, di, gs, us, ds):
        _, rows, hidden = gi.shape
        _, own, feat = q.shape
        slab = hidden // group
        near = group * own
        me = lax.axis_index("seq")
        place = jnp.stack((lax.div(me, group), lax.rem(me, group), me)).astype(jnp.int32)

        (packed,) = copying_call(
            functools.partial(weight_pack_kernel, group, slab),
            (arr((seq_n, rows, 6 * slab), BF),),
            (gs, us, ds, gi, ui, di),
            [pltpu.VMEM((6, rows, hidden), BF)],
        )
        packed, queries = lax.optimization_barrier((packed, q[0]))
        wall = lax.all_to_all(packed, "seq", 0, 0, tiled=True).reshape(seq_n * rows, 6 * slab)
        q_near = near_all(queries)
        kv, gg, rate = call(
            token_pack_kernel,
            (arr((group, own, 2 * feat), BF), arr((own, feat), F32), arr((own, feat), F32)),
            (k, v, og, rates, gains),
            8,
        )
        wall, kv = lax.optimization_barrier((wall, kv))

        block = arr((own, feat), BF)
        parts = call(
            functools.partial(forward_kernel, slab, group),
            (block,) * group,
            (wall, *q_near),
            24,
            flops=6 * near * feat * slab,
        )
        *parts, queries = lax.optimization_barrier((*parts, queries))
        parts = [parts[0]] + [move(parts[d], d) for d in range(1, group)]
        q_mirror = mirror(queries)
        parts[1], kv = lax.optimization_barrier((parts[1], kv))
        kv = lax.all_to_all(kv, "seq", 0, 0, axis_index_groups=groups, tiled=True)
        apply_out, sums = call(
            reduce_kernel, (arr((own, feat), F32), arr((2, own), F32)), (gg, *parts), 16
        )
        sums = [sums] + [move(sums, d, "head", head_n) for d in range(1, head_n)]
        (od,) = call(functools.partial(delta_kernel, head_n * feat), (block,), (apply_out, gg, *sums), 16)
        od_mirror = mirror(od)
        od_near = near_all(od)
        kv, *od_mirror = lax.optimization_barrier((kv, *od_mirror))
        pairs = [
            call(pair_kernel, (arr((own, 2 * feat), BF),), pair, 16)[0] for pair in zip(od_mirror, q_mirror)
        ]
        pairs = [x for m in pairs for x in near_all(m)]

        far = pltpu.VMEM((max(tok_groups - 1, 1), group, own, feat), BF)
        home = (group * rows, 3 * slab)
        result = call(
            functools.partial(backward_kernel, slab, group, tok_groups),
            (
                *(arr((own, 3 * feat), BF),) * group,
                arr(home, F32),
                *(arr(home, BF),) * (tok_groups - 1),
            ),
            (place, wall, kv, *q_near, *od_near, *pairs),
            40,
            smem=1,
            flops=66 * near * feat * slab,
            scratch=[
                far,
                far,
                pltpu.VMEM((tok_groups, *home), F32),
                *[pltpu.VMEM((seq_n * rows, slab), F32)] * 3,
            ],
        )
        tok, inner = result[:group], result[group:]
        inner = [inner[0]] + [move(inner[e], e * group) for e in range(1, tok_groups)]
        tok = [tok[0]] + [move(tok[d], d) for d in range(1, group)]
        inner = call(
            functools.partial(home_kernel, group),
            (arr((rows, 3 * slab), BF),) * group,
            (place, *inner),
            16,
            smem=1,
            scratch=[pltpu.VMEM((group, rows, 3 * slab), F32)],
        )
        *inner, tok[1] = lax.optimization_barrier((*inner, tok[1]))
        inner = [inner[0]] + [move(inner[d], d) for d in range(1, group)]
        out_tok = arr((1, own, feat), BF)
        grad_w = arr((1, rows, hidden), F32)
        grads_t = call(tokens_kernel, (out_tok,) * 3, (rate, *tok), 16)
        grads_w = call(
            functools.partial(weights_kernel, group, slab),
            (grad_w,) * 3,
            (place, *inner),
            16,
            smem=1,
            scratch=[pltpu.VMEM((group, rows, 3 * slab), F32)],
        )
        return (*grads_t, *grads_w)

    return local


def solution(mesh):
    seq_n = mesh.shape["seq"]
    head_n = mesh.shape["head"]
    group = min(4, seq_n)
    tok = P("head", "seq", None)
    return jax.shard_map(
        make_local(seq_n, head_n, group),
        mesh=mesh,
        in_specs=(tok, tok, tok, tok, P("head", "seq"), P("head", None), tok, tok, tok, tok, tok, tok),
        out_specs=(tok, tok, tok, tok, tok, tok),
        check_vma=False,
    )
```

```python
import functools

import jax
import jax.numpy as jnp
from jax import lax
from jax.experimental import pallas as pl
from jax.experimental.pallas import tpu as pltpu
from jax.sharding import PartitionSpec as P

EPS_COL = 1e-06
EPS_ROOT = 1e-05
BF = jnp.bfloat16
F32 = jnp.float32
VMEM = pl.BlockSpec(memory_space=pltpu.VMEM)
SMEM = pl.BlockSpec(memory_space=pltpu.SMEM)


def silu_parts(pre_act):
    sigmoid_val = jax.nn.sigmoid(pre_act)
    silu_val = pre_act * sigmoid_val
    silu_slope = sigmoid_val * (1.0 + pre_act * (1.0 - sigmoid_val))
    silu_bend = sigmoid_val * (1.0 - sigmoid_val) * (2.0 + pre_act * (1.0 - 2.0 * sigmoid_val))
    return (silu_val, silu_slope, silu_bend)


def mm(left_op, right_op):
    return jnp.dot(left_op, right_op, preferred_element_type=F32)


def mm_nt(left_op, right_op):
    return lax.dot_general(left_op, right_op, (((1,), (1,)), ((), ())), preferred_element_type=F32)


def mm_tn(left_op, right_op):
    return lax.dot_general(left_op, right_op, (((0,), (0,)), ((), ())), preferred_element_type=F32)


def column_norm(weight):
    return jnp.sqrt(jnp.sum(weight * weight, axis=0, keepdims=True) + EPS_COL)


def flat(x):
    return x.reshape(-1, x.shape[-1])


def call(kernel, outs, args, mib, smem=0, flops=0, scratch=()):
    moved = sum(x.size * x.dtype.itemsize for x in (*args, *outs))
    return pl.pallas_call(
        kernel,
        out_shape=outs,
        in_specs=[SMEM] * smem + [VMEM] * (len(args) - smem),
        out_specs=[VMEM] * len(outs),
        scratch_shapes=scratch,
        compiler_params=pltpu.CompilerParams(vmem_limit_bytes=mib << 20),
        cost_estimate=pl.CostEstimate(flops=flops, bytes_accessed=moved, transcendentals=0),
    )(*args)


def copying_call(kernel, outs, args, buffers):
    return pl.pallas_call(
        kernel,
        out_shape=outs,
        in_specs=[pl.BlockSpec(memory_space=pltpu.HBM)] * len(args),
        out_specs=[VMEM] * len(outs),
        scratch_shapes=[*buffers, pltpu.SemaphoreType.DMA((len(args),))],
        compiler_params=pltpu.CompilerParams(vmem_limit_bytes=56 << 20),
    )(*args)


def arr(shape, dtype):
    return jax.ShapeDtypeStruct(shape, dtype)


def fetch(sources, buffers, sems):
    copies = [pltpu.make_async_copy(s, b, sems.at[i]) for i, (s, b) in enumerate(zip(sources, buffers))]
    for copy in copies:
        copy.start()
    for copy in copies:
        copy.wait()


def token_pack_kernel(q, k, v, og, rates, gains, all_out, kv_out, gg_out, rate_out):
    tokens, feat = gg_out.shape
    rate = jnp.broadcast_to(rates[...], (feat, tokens)).T
    values = (rate * v[0].astype(F32)).astype(BF)
    all_out[:, 0:feat] = q[0]
    all_out[:, feat : 2 * feat] = k[0]
    all_out[:, 2 * feat : 3 * feat] = values
    kv_out[:, 0:feat] = k[0]
    kv_out[:, feat : 2 * feat] = values
    gg_out[...] = gains[...] * og[0].astype(F32)
    rate_out[...] = rate


def weight_pack_kernel(group, slab, *refs):
    args, (w_out, buf, sems) = refs[:6], refs[6:]
    fetch(args, [buf.at[pl.ds(i, 1)] for i in range(6)], sems)
    for j in range(group):
        cols = pl.ds(j * slab, slab)
        block = jnp.concatenate([buf[i, :, cols] for i in range(6)], axis=1)
        for p in range(j, w_out.shape[0], group):
            w_out[p] = block


def columns(w, slab):
    parts = [w[:, pl.ds(i * slab, slab)].astype(F32) for i in range(6)]
    saved, init = parts[:3], parts[3:]
    return saved, init, [column_norm(x) for x in init], [column_norm(x) for x in saved]


def stack(refs, cols=slice(None)):
    return jnp.concatenate([r[:, cols] for r in refs], axis=0)


def thirds(x, slab):
    return [x[:, pl.ds(i * slab, slab)] for i in range(3)]


def forward_kernel(slab, group, w, *refs):
    queries, parts, normed_out = refs[:group], refs[group:-1], refs[-1]
    own, feat = parts[0].shape
    saved, init, norm_init, norm_saved = columns(w, slab)
    normed = [(saved[i] * (norm_init[i] / norm_saved[i])).astype(BF) for i in range(3)]
    rows = stack(queries, slice(0, feat))
    hidden = (silu_parts(mm(rows, normed[0]))[0] * mm(rows, normed[1])).astype(BF)
    out = mm_nt(hidden, normed[2]).astype(BF)
    for d in range(group):
        parts[d][...] = out[d * own : (d + 1) * own]
    normed_out[...] = jnp.concatenate(normed, axis=1)


def reduce_kernel(gg, *refs):
    parts, (apply_out, sums) = refs[:-2], refs[-2:]
    total = total_of(parts)
    apply_out[...] = total
    sums[0:1, :] = jnp.sum((total * total).T, axis=0, keepdims=True)
    sums[1:2, :] = jnp.sum((total * gg[...]).T, axis=0, keepdims=True)


def delta_kernel(width, apply_out, gg, *refs):
    sums, out = refs[:-1], refs[-1]
    tokens, feat = apply_out.shape
    total = sums[0][...]
    for more in sums[1:]:
        total += more[...]
    square = jnp.broadcast_to(total[0:1, :], (feat, tokens)).T
    gain = jnp.broadcast_to(total[1:2, :], (feat, tokens)).T
    root = jnp.sqrt(square / width + EPS_ROOT)
    out[...] = (gg[...] / root - apply_out[...] * (gain / width) / (root * root * root)).astype(BF)


def pair_kernel(left, right, out):
    feat = left.shape[1]
    out[:, 0:feat] = left[...]
    out[:, feat : 2 * feat] = right[...]


def query_side(rows, delta, normed):
    q_gate = mm(rows, normed[0])
    q_up = mm(rows, normed[1])
    act, slope, _ = silu_parts(q_gate)
    hidden = (act * q_up).astype(BF)
    delta_hidden = mm(delta, normed[2])
    delta_gate = (delta_hidden * q_up * slope).astype(BF)
    delta_up = (delta_hidden * act).astype(BF)
    grads = (mm_tn(rows, delta_gate), mm_tn(rows, delta_up), mm_tn(delta, hidden))
    return delta_gate, delta_up, grads


def near_kernel(slab, group, normed_ref, *refs):
    q_near, od_near, outs, grads_out = refs[:group], refs[group : 2 * group], refs[2 * group : -1], refs[-1]
    own, feat = od_near[0].shape
    normed = thirds(normed_ref, slab)
    delta_gate, delta_up, grads = query_side(stack(q_near, slice(0, feat)), stack(od_near), normed)
    grad_q = (mm_nt(delta_gate, normed[0]) + mm_nt(delta_up, normed[1])).astype(BF)
    for d in range(group):
        outs[d][...] = grad_q[d * own : (d + 1) * own]
    for i in range(3):
        grads_out[i] = grads[i]


def key_kernel(slab, group, w, *refs):
    kvs, (factors, rises) = refs[:group], refs[group:]
    feat = w.shape[0]
    init = [w[:, pl.ds((3 + i) * slab, slab)] for i in range(3)]
    keys = stack(kvs, slice(-2 * feat, -feat))
    values = stack(kvs, slice(-feat, None))
    k_gate = mm(keys, init[0])
    k_up = mm(keys, init[1])
    k_proj = mm(values, init[2])
    k_act, k_slope, k_bend = silu_parts(k_gate)
    rises[0] = (k_act * k_up).astype(BF)
    rises[1] = (k_proj * k_up * k_slope).astype(BF)
    rises[2] = (k_proj * k_act).astype(BF)
    factors[0] = k_act
    factors[1] = k_up * k_slope
    factors[2] = k_proj * k_slope
    factors[3] = k_proj * k_up * k_bend


def backward_kernel(slab, group, tok_groups, place, w, normed_ref, grads, factors, rises, *refs):
    far = group * (tok_groups - 1)
    kvs, pairs, outs, refs = refs[:group], refs[group : group + far], refs[group + far : -4], refs[-4:]
    inner_out, far_od, far_q, sums = refs
    feat = w.shape[0]
    own = outs[0].shape[0]
    for i in range(far):
        far_od[i // group, i % group] = pairs[i][:, 0:feat]
        far_q[i // group, i % group] = pairs[i][:, feat : 2 * feat]
    normed = thirds(normed_ref, slab)
    sums[...] = grads[...]

    def other(e, carry):
        more = query_side(flat(far_q[e]), flat(far_od[e]), normed)[2]
        for i in range(3):
            sums[i] += more[i]
        return carry

    lax.fori_loop(0, tok_groups - 1, other, 0)

    saved, init, norm_init, norm_saved = columns(w, slab)
    cots, direct = [], []
    once = jnp.where(place[0] == 0, 1.0, 0.0)
    for i in range(3):
        apply_grad = sums[i]
        col_dot = jnp.sum(saved[i] * apply_grad, axis=0, keepdims=True)
        cot = apply_grad * (norm_init[i] / norm_saved[i]) - saved[i] * (
            col_dot * norm_init[i] / (norm_saved[i] * norm_saved[i] * norm_saved[i])
        )
        cots.append(cot.astype(BF))
        direct.append((cot + init[i] * (col_dot / (norm_init[i] * norm_saved[i]))) * once)

    init_bf = [w[:, pl.ds((3 + i) * slab, slab)] for i in range(3)]
    keys = stack(kvs, slice(-2 * feat, -feat))
    values = stack(kvs, slice(-feat, None))
    back_gate = mm(keys, cots[0])
    back_up = mm(keys, cots[1])
    back_hidden = mm(values, cots[2])
    back_proj = (back_gate * factors[1] + back_up * factors[0]).astype(BF)
    back_kup = (back_gate * factors[2] + back_hidden * factors[0]).astype(BF)
    back_kgate = (back_gate * factors[3] + (back_up * factors[2] + back_hidden * factors[1])).astype(BF)
    grad_k = (
        mm_nt(rises[1], cots[0])
        + mm_nt(rises[2], cots[1])
        + mm_nt(back_kgate, init_bf[0])
        + mm_nt(back_kup, init_bf[1])
    ).astype(BF)
    grad_v = (mm_nt(rises[0], cots[2]) + mm_nt(back_proj, init_bf[2])).astype(BF)
    for d in range(group):
        outs[d][:, 0:feat] = grad_k[d * own : (d + 1) * own]
        outs[d][:, feat : 2 * feat] = grad_v[d * own : (d + 1) * own]
    inner = (mm_tn(keys, back_kgate), mm_tn(keys, back_kup), mm_tn(values, back_proj))
    inner_out[...] = jnp.concatenate([inner[i] + direct[i] for i in range(3)], axis=1).astype(BF)


def total_of(refs):
    total = refs[0][...].astype(F32)
    for block in refs[1:]:
        total += block[...].astype(F32)
    return total


def tokens_kernel(group, rate, *refs):
    queries, got, (gq, gk, gv) = refs[:group], refs[group:-3], refs[-3:]
    feat = gq.shape[2]
    gq[0] = total_of(queries).astype(BF)
    total = total_of(got)
    gk[0] = total[:, 0:feat].astype(BF)
    gv[0] = (rate[...] * total[:, feat : 2 * feat]).astype(BF)


def weights_kernel(group, slab, got, *outs):
    cols = []
    for j in range(group):
        total = got[j].astype(F32)
        for p in range(j + group, got.shape[0], group):
            total += got[p].astype(F32)
        cols.append(total)
    for i in range(3):
        outs[i][0] = jnp.concatenate([c[:, i * slab : (i + 1) * slab] for c in cols], axis=1)


def make_local(seq_n, head_n, group):
    tok_groups = seq_n // group

    def move(x, dist, axis="seq", size=seq_n):
        return lax.ppermute(x, axis, [(i, i ^ dist) for i in range(size)])

    def near_all(x):
        return [x] + [move(x, d) for d in range(1, group)]

    def mirror(x):
        return [move(x, e * group) for e in range(1, tok_groups)]

    def local(q, k, v, og, rates, gains, gi, ui, di, gs, us, ds):
        _, rows, hidden = gi.shape
        _, own, feat = q.shape
        slab = hidden // group
        near = group * own
        me = lax.axis_index("seq")
        place = jnp.stack((lax.div(me, group), lax.rem(me, group), me)).astype(jnp.int32)

        (packed,) = copying_call(
            functools.partial(weight_pack_kernel, group, slab),
            (arr((seq_n, rows, 6 * slab), BF),),
            (gs, us, ds, gi, ui, di),
            [pltpu.VMEM((6, rows, hidden), BF)],
        )
        packed, queries = lax.optimization_barrier((packed, q[0]))
        wall = lax.all_to_all(packed, "seq", 0, 0, tiled=True).reshape(seq_n * rows, 6 * slab)
        tokens, kv, gg, rate = call(
            token_pack_kernel,
            (arr((own, 3 * feat), BF), arr((own, 2 * feat), BF), arr((own, feat), F32), arr((own, feat), F32)),
            (q, k, v, og, rates, gains),
            8,
        )
        beside = move(tokens, 1) if group > 1 else None
        rest = range(2, group)
        q_near = [queries, beside][:group] + [move(queries, d) for d in rest]
        kv_near = [kv, beside][:group] + [move(kv, d) for d in rest]

        block = arr((own, feat), BF)
        mflop = 2 * near * feat * slab
        *parts, normed = call(
            functools.partial(forward_kernel, slab, group),
            (*(block,) * group, arr((seq_n * rows, 3 * slab), BF)),
            (wall, *q_near),
            24,
            flops=3 * mflop,
        )
        parts = [parts[0]] + [move(parts[d], d) for d in range(1, group)]
        *parts, kv_near = lax.optimization_barrier((*parts, kv_near))
        apply_out, sums = call(
            reduce_kernel, (arr((own, feat), F32), arr((2, own), F32)), (gg, *parts), 16
        )
        sums, queries = lax.optimization_barrier((sums, queries))
        sums = [sums] + [move(sums, d, "head", head_n) for d in range(1, head_n)]
        q_mirror = mirror(queries)
        (od,) = call(functools.partial(delta_kernel, head_n * feat), (block,), (apply_out, gg, *sums), 16)
        od_mirror = mirror(od)
        od_near = near_all(od)
        factors, rises = call(
            functools.partial(key_kernel, slab, group),
            (arr((4, near, slab), F32), arr((3, near, slab), BF)),
            (wall, *kv_near),
            24,
            flops=12 * mflop,
        )
        pairs = [
            call(pair_kernel, (arr((own, 2 * feat), BF),), pair, 16)[0] for pair in zip(od_mirror, q_mirror)
        ]
        pairs = [x for m in pairs for x in near_all(m)]
        *grad_q, grads = call(
            functools.partial(near_kernel, slab, group),
            (*(block,) * group, arr((3, seq_n * rows, slab), F32)),
            (normed, *q_near, *od_near),
            24,
            flops=12 * mflop,
        )
        grad_q = [grad_q[0]] + [move(grad_q[d], d) for d in range(1, group)]

        far = pltpu.VMEM((max(tok_groups - 1, 1), group, own, feat), BF)
        *tok, inner = call(
            functools.partial(backward_kernel, slab, group, tok_groups),
            (*(arr((own, 2 * feat), BF),) * group, arr((seq_n * rows, 3 * slab), BF)),
            (place, wall, normed, grads, factors, rises, *kv_near, *pairs),
            32,
            smem=1,
            flops=24 * mflop,
            scratch=[far, far, pltpu.VMEM((3, seq_n * rows, slab), F32)],
        )
        inner = lax.all_to_all(inner.reshape(seq_n, rows, 3 * slab), "seq", 0, 0, tiled=True)
        tok = [tok[0]] + [move(tok[d], d) for d in range(1, group)]
        out_tok = arr((1, own, feat), BF)
        grad_w = arr((1, rows, hidden), F32)
        grads_t = call(
            functools.partial(tokens_kernel, group), (out_tok,) * 3, (rate, *grad_q, *tok), 16
        )
        grads_w = call(functools.partial(weights_kernel, group, slab), (grad_w,) * 3, (inner,), 16)
        return (*grads_t, *grads_w)

    return local


def solution(mesh):
    seq_n = mesh.shape["seq"]
    head_n = mesh.shape["head"]
    group = min(4, seq_n)
    tok = P("head", "seq", None)
    return jax.shard_map(
        make_local(seq_n, head_n, group),
        mesh=mesh,
        in_specs=(tok, tok, tok, tok, P("head", "seq"), P("head", None), tok, tok, tok, tok, tok, tok),
        out_specs=(tok, tok, tok, tok, tok, tok),
        check_vma=False,
    )
```

```python
import functools

import jax
import jax.numpy as jnp
from jax import lax
from jax.experimental import pallas as pl
from jax.experimental.pallas import tpu as pltpu
from jax.sharding import PartitionSpec as P

EPS_COL = 1e-06
EPS_ROOT = 1e-05
BF = jnp.bfloat16
F32 = jnp.float32
LANES = 128
VMEM = pl.BlockSpec(memory_space=pltpu.VMEM)
SMEM = pl.BlockSpec(memory_space=pltpu.SMEM)


def silu_parts(pre_act):
    sigmoid_val = jax.nn.sigmoid(pre_act)
    silu_val = pre_act * sigmoid_val
    silu_slope = sigmoid_val * (1.0 + pre_act * (1.0 - sigmoid_val))
    silu_bend = sigmoid_val * (1.0 - sigmoid_val) * (2.0 + pre_act * (1.0 - 2.0 * sigmoid_val))
    return (silu_val, silu_slope, silu_bend)


def mm(left_op, right_op):
    return jnp.dot(left_op, right_op, preferred_element_type=F32)


def mm_nt(left_op, right_op):
    return lax.dot_general(left_op, right_op, (((1,), (1,)), ((), ())), preferred_element_type=F32)


def mm_tn(left_op, right_op):
    return lax.dot_general(left_op, right_op, (((0,), (0,)), ((), ())), preferred_element_type=F32)


def column_norm(weight):
    return jnp.sqrt(jnp.sum(weight * weight, axis=0, keepdims=True) + EPS_COL)


def flat(x):
    return x.reshape(-1, x.shape[-1])


def call(kernel, outs, args, mib, smem=0, flops=0, scratch=()):
    moved = sum(x.size * x.dtype.itemsize for x in (*args, *outs))
    return pl.pallas_call(
        kernel,
        out_shape=outs,
        in_specs=[SMEM] * smem + [VMEM] * (len(args) - smem),
        out_specs=[VMEM] * len(outs),
        scratch_shapes=scratch,
        compiler_params=pltpu.CompilerParams(vmem_limit_bytes=mib << 20),
        cost_estimate=pl.CostEstimate(flops=flops, bytes_accessed=moved, transcendentals=0),
    )(*args)


def copying_call(kernel, outs, place, args, buffers):
    return pl.pallas_call(
        kernel,
        out_shape=outs,
        in_specs=[SMEM] + [pl.BlockSpec(memory_space=pltpu.HBM)] * len(args),
        out_specs=[VMEM] * len(outs),
        scratch_shapes=[*buffers, pltpu.SemaphoreType.DMA((len(args),))],
        compiler_params=pltpu.CompilerParams(vmem_limit_bytes=56 << 20),
    )(place, *args)


def arr(shape, dtype):
    return jax.ShapeDtypeStruct(shape, dtype)


def fetch(sources, buffers, sems):
    copies = [pltpu.make_async_copy(s, b, sems.at[i]) for i, (s, b) in enumerate(zip(sources, buffers))]
    for copy in copies:
        copy.start()
    for copy in copies:
        copy.wait()


def padded(rows):
    return -(-rows // 16) * 16


def tiles(cols):
    return -(-cols // LANES)


def put(out, at, value):
    rows, cols = value.shape
    for t in range(tiles(cols)):
        wide = min(LANES, cols - t * LANES)
        out[at : at + rows, 0:wide] = value[:, t * LANES : t * LANES + wide]
        at += padded(rows)
    return at


def get(ref, at, rows, cols):
    parts = []
    for t in range(tiles(cols)):
        wide = min(LANES, cols - t * LANES)
        parts.append(ref[at : at + rows, 0:wide])
        at += padded(rows)
    return jnp.concatenate(parts, axis=1), at


def message(*blocks):
    return arr((sum(tiles(cols) * padded(rows) for rows, cols in blocks), LANES), BF)


def pack_kernel(group, slab, place, *refs):
    args, refs = refs[:12], refs[12:]
    w_outs, near_outs, (kv_out, gg_out, rate_out), refs = (
        refs[:group],
        refs[group : 2 * group - 1],
        refs[2 * group - 1 : 2 * group + 2],
        refs[2 * group + 2 :],
    )
    buf, qb, kb, vb, ob, rb, gb, slabs, sems = refs
    fetch(args, [buf.at[pl.ds(i, 1)] for i in range(6)] + [qb, kb, vb, ob, rb, gb], sems)
    rank = place[1]
    for j in range(group):
        cols = pl.ds(j * slab, slab)
        slabs[j] = jnp.concatenate([buf[i, :, cols] for i in range(6)], axis=1)
    tokens, feat = gg_out.shape
    rate = jnp.broadcast_to(rb[...], (feat, tokens)).T
    values = (rate * vb[0].astype(F32)).astype(BF)
    for d in range(group):
        block = slabs[rank ^ d]
        w_outs[d][...] = block
        if d:
            out = near_outs[d - 1]
            at = put(out, put(out, 0, block), qb[0])
            if d == 1:
                put(out, put(out, at, kb[0]), values)
    kv_out[:, 0:feat] = kb[0]
    kv_out[:, feat : 2 * feat] = values
    gg_out[...] = gb[...] * ob[0].astype(F32)
    rate_out[...] = rate


def columns(w, slab):
    parts = [w[:, pl.ds(i * slab, slab)].astype(F32) for i in range(6)]
    saved, init = parts[:3], parts[3:]
    return saved, init, [column_norm(x) for x in init], [column_norm(x) for x in saved]


def stack(refs, cols=slice(None)):
    return jnp.concatenate([r[:, cols] for r in refs], axis=0)


def thirds(x, slab):
    return [x[:, pl.ds(i * slab, slab)] for i in range(3)]


def forward_kernel(slab, group, place, q, *refs):
    blocks, refs = refs[: -group - 4], refs[-group - 4 :]
    parts, (normed_out, w, kv_out, buf) = refs[:group], refs[group:]
    own, feat = parts[0].shape
    me, (_, rows, cols) = place[2], buf.shape
    queries = [q[...]]
    for d, block in enumerate(blocks):
        if 0 < d < group:
            value, at = get(block, 0, rows, cols)
            tokens, at = get(block, at, own, feat)
            queries.append(tokens)
            if d == 1:
                kv_out[...] = get(block, at, own, 2 * feat)[0]
        else:
            value = block[...]
        buf[me ^ d] = value
    if rows % 16:
        w[...] = jnp.concatenate([buf[p].astype(F32) for p in range(buf.shape[0])], axis=0).astype(BF)
    else:
        w[...] = flat(buf[...])
    saved, init, norm_init, norm_saved = columns(w, slab)
    normed = [(saved[i] * (norm_init[i] / norm_saved[i])).astype(BF) for i in range(3)]
    rows = jnp.concatenate(queries, axis=0)
    hidden = (silu_parts(mm(rows, normed[0]))[0] * mm(rows, normed[1])).astype(BF)
    out = mm_nt(hidden, normed[2]).astype(BF)
    for d in range(group):
        parts[d][...] = out[d * own : (d + 1) * own]
    normed_out[...] = jnp.concatenate(normed, axis=1)


def reduce_kernel(gg, *refs):
    parts, (apply_out, sums) = refs[:-2], refs[-2:]
    total = total_of(parts)
    apply_out[...] = total
    sums[0:1, :] = jnp.sum((total * total).T, axis=0, keepdims=True)
    sums[1:2, :] = jnp.sum((total * gg[...]).T, axis=0, keepdims=True)


def delta_kernel(width, apply_out, gg, *refs):
    sums, out = refs[:-1], refs[-1]
    tokens, feat = apply_out.shape
    total = sums[0][...]
    for more in sums[1:]:
        total += more[...]
    square = jnp.broadcast_to(total[0:1, :], (feat, tokens)).T
    gain = jnp.broadcast_to(total[1:2, :], (feat, tokens)).T
    root = jnp.sqrt(square / width + EPS_ROOT)
    out[...] = (gg[...] / root - apply_out[...] * (gain / width) / (root * root * root)).astype(BF)


def pair_kernel(left, right, out):
    feat = left.shape[1]
    out[:, 0:feat] = left[...]
    out[:, feat : 2 * feat] = right[...]


def query_side(rows, delta, normed):
    q_gate = mm(rows, normed[0])
    q_up = mm(rows, normed[1])
    act, slope, _ = silu_parts(q_gate)
    hidden = (act * q_up).astype(BF)
    delta_hidden = mm(delta, normed[2])
    delta_gate = (delta_hidden * q_up * slope).astype(BF)
    delta_up = (delta_hidden * act).astype(BF)
    grads = (mm_tn(rows, delta_gate), mm_tn(rows, delta_up), mm_tn(delta, hidden))
    return delta_gate, delta_up, grads


def near_kernel(slab, group, rows_of_w, normed_ref, *refs):
    msgs, od_near, outs, grads_out = refs[:group], refs[group : 2 * group], refs[2 * group : -1], refs[-1]
    own, feat = od_near[0].shape
    normed = thirds(normed_ref, slab)
    at = tiles(6 * slab) * padded(rows_of_w)
    queries = [msgs[0][...]] + [get(m, at, own, feat)[0] for m in msgs[1:]]
    delta_gate, delta_up, grads = query_side(jnp.concatenate(queries, axis=0), stack(od_near), normed)
    grad_q = (mm_nt(delta_gate, normed[0]) + mm_nt(delta_up, normed[1])).astype(BF)
    for d in range(group):
        outs[d][...] = grad_q[d * own : (d + 1) * own]
    for i in range(3):
        grads_out[i] = grads[i]


def key_kernel(slab, group, w, *refs):
    kvs, (factors, rises) = refs[:group], refs[group:]
    feat = w.shape[0]
    init = [w[:, pl.ds((3 + i) * slab, slab)] for i in range(3)]
    keys = stack(kvs, slice(0, feat))
    values = stack(kvs, slice(feat, 2 * feat))
    k_gate = mm(keys, init[0])
    k_up = mm(keys, init[1])
    k_proj = mm(values, init[2])
    k_act, k_slope, k_bend = silu_parts(k_gate)
    rises[0] = (k_act * k_up).astype(BF)
    rises[1] = (k_proj * k_up * k_slope).astype(BF)
    rises[2] = (k_proj * k_act).astype(BF)
    factors[0] = k_act
    factors[1] = k_up * k_slope
    factors[2] = k_proj * k_slope
    factors[3] = k_proj * k_up * k_bend


def backward_kernel(slab, group, tok_groups, place, w, normed_ref, grads, factors, rises, *refs):
    far = group * (tok_groups - 1)
    kvs, pairs, outs, (inner_buf, sums) = refs[:group], refs[group : group + far], refs[group + far : -2], refs[-2:]
    feat = w.shape[0]
    tok_out, outs = outs[0], outs[1:]
    own = tok_out.shape[0]
    normed = thirds(normed_ref, slab)
    total = [grads[i] for i in range(3)]
    for e in range(tok_groups - 1):
        these = pairs[e * group : (e + 1) * group]
        more = query_side(stack(these, slice(feat, 2 * feat)), stack(these, slice(0, feat)), normed)[2]
        total = [total[i] + more[i] for i in range(3)]
        if tok_groups > 2:
            for i in range(3):
                sums[i] = total[i]
            total = [sums[i] for i in range(3)]

    saved, init, norm_init, norm_saved = columns(w, slab)
    cots, direct = [], []
    once = jnp.where(place[0] == 0, 1.0, 0.0)
    for i in range(3):
        apply_grad = total[i]
        col_dot = jnp.sum(saved[i] * apply_grad, axis=0, keepdims=True)
        cot = apply_grad * (norm_init[i] / norm_saved[i]) - saved[i] * (
            col_dot * norm_init[i] / (norm_saved[i] * norm_saved[i] * norm_saved[i])
        )
        cots.append(cot.astype(BF))
        direct.append((cot + init[i] * (col_dot / (norm_init[i] * norm_saved[i]))) * once)

    init_bf = [w[:, pl.ds((3 + i) * slab, slab)] for i in range(3)]
    keys = stack(kvs, slice(0, feat))
    values = stack(kvs, slice(feat, 2 * feat))
    back_gate = mm(keys, cots[0])
    back_up = mm(keys, cots[1])
    back_hidden = mm(values, cots[2])
    back_proj = (back_gate * factors[1] + back_up * factors[0]).astype(BF)
    back_kup = (back_gate * factors[2] + back_hidden * factors[0]).astype(BF)
    back_kgate = (back_gate * factors[3] + (back_up * factors[2] + back_hidden * factors[1])).astype(BF)
    grad_k = (
        mm_nt(rises[1], cots[0])
        + mm_nt(rises[2], cots[1])
        + mm_nt(back_kgate, init_bf[0])
        + mm_nt(back_kup, init_bf[1])
    ).astype(BF)
    grad_v = (mm_nt(rises[0], cots[2]) + mm_nt(back_proj, init_bf[2])).astype(BF)
    inner = (mm_tn(keys, back_kgate), mm_tn(keys, back_kup), mm_tn(values, back_proj))
    whole = jnp.concatenate([inner[i] + direct[i] for i in range(3)], axis=1)
    rows = inner_buf.shape[1]
    for p in range(inner_buf.shape[0]):
        inner_buf[p] = whole[p * rows : (p + 1) * rows]
    tok_out[:, 0:feat] = grad_k[0:own]
    tok_out[:, feat : 2 * feat] = grad_v[0:own]
    for d in range(inner_buf.shape[0]):
        block = inner_buf[place[2] ^ d].astype(BF)
        if 0 < d < group:
            out = outs[d]
            at = put(out, 0, grad_k[d * own : (d + 1) * own])
            put(out, put(out, at, grad_v[d * own : (d + 1) * own]), block)
        else:
            outs[d][...] = block


def total_of(refs):
    total = refs[0][...].astype(F32)
    for block in refs[1:]:
        total += block[...].astype(F32)
    return total


def final_kernel(group, slab, place, rate, tok, *refs):
    queries, blocks, (gq, gk, gv, *outs, buf) = refs[:group], refs[group:-7], refs[-7:]
    _, own, feat = gq.shape
    rows = buf.shape[1]
    gq[0] = total_of(queries).astype(BF)
    keys = tok[:, 0:feat].astype(F32)
    values = tok[:, feat : 2 * feat].astype(F32)
    for d in range(group):
        if d:
            more, at = get(blocks[d], 0, own, feat)
            keys += more.astype(F32)
            more, at = get(blocks[d], at, own, feat)
            values += more.astype(F32)
            block = get(blocks[d], at, rows, 3 * slab)[0]
        else:
            block = blocks[d][...]
        buf[d] = block.astype(F32)
        for other in blocks[d + group :: group]:
            buf[d] += other[...].astype(F32)
    gk[0] = keys.astype(BF)
    gv[0] = (rate[...] * values).astype(BF)
    cols = [buf[place[1] ^ j] for j in range(group)]
    for i in range(3):
        outs[i][0] = jnp.concatenate([c[:, i * slab : (i + 1) * slab] for c in cols], axis=1)


def mixed(seq_n, group, lead):
    near, far = list(range(1, group)), list(range(group, seq_n))
    first, second = (far, near) if lead == 2 else (near, far)
    order = first[:2]
    first = first[2:]
    while first or second:
        order += second[:1] + first[:1]
        first, second = first[1:], second[1:]
    return order


def make_local(seq_n, head_n, group):
    tok_groups = seq_n // group

    def move(x, dist, axis="seq", size=seq_n):
        return lax.ppermute(x, axis, [(i, i ^ dist) for i in range(size)])

    def near_all(x):
        return [x] + [move(x, d) for d in range(1, group)]

    def mirror(x):
        return [move(x, e * group) for e in range(1, tok_groups)]

    def local(q, k, v, og, rates, gains, gi, ui, di, gs, us, ds):
        _, rows, hidden = gi.shape
        _, own, feat = q.shape
        slab = hidden // group
        near = group * own
        me = lax.axis_index("seq")
        place = jnp.stack((lax.div(me, group), lax.rem(me, group), me)).astype(jnp.int32)

        w_block, q_block = (rows, 6 * slab), (own, feat)
        near_msgs = [
            message(w_block, q_block, *((q_block, q_block) if d == 1 else ())) for d in range(1, group)
        ]
        args = (gs, us, ds, gi, ui, di, q, k, v, og, rates, gains)
        packed = copying_call(
            functools.partial(pack_kernel, group, slab),
            (
                *(arr(w_block, BF),) * group,
                *near_msgs,
                arr((own, 2 * feat), BF),
                arr(q_block, F32),
                arr(q_block, F32),
            ),
            place,
            args,
            [
                pltpu.VMEM((6, rows, hidden), BF),
                *[pltpu.VMEM(x.shape, x.dtype) for x in args[6:]],
                pltpu.VMEM((group, rows, 6 * slab), BF),
            ],
        )
        w_blocks, near_blocks, (kv, gg, rate) = packed[:group], packed[group:-3], packed[-3:]
        sends = {d: w_blocks[d % group] for d in range(group, seq_n)}
        sends.update({d: near_blocks[d - 1] for d in range(1, group)})
        got = {0: w_blocks[0]}
        for d in mixed(seq_n, group, 2):
            got[d] = move(sends[d], d)
        kv_far = [move(kv, d) for d in range(2, group)]
        queries = q[0]

        block = arr(q_block, BF)
        mflop = 2 * near * feat * slab
        *parts, normed, wall, kv_one = call(
            functools.partial(forward_kernel, slab, group),
            (
                *(block,) * group,
                arr((seq_n * rows, 3 * slab), BF),
                arr((seq_n * rows, 6 * slab), BF),
                arr((own, 2 * feat), BF),
            ),
            (place, queries, *[got[d] for d in range(seq_n)]),
            24,
            smem=1,
            flops=3 * mflop,
            scratch=[pltpu.VMEM((seq_n, rows, 6 * slab), BF)],
        )
        kv_near = [kv, kv_one, *kv_far][:group]
        q_near = [queries] + [got[d] for d in range(1, group)]
        parts = [parts[0]] + [move(parts[d], d) for d in range(1, group)]
        *parts, kv_near = lax.optimization_barrier((*parts, kv_near))
        apply_out, sums = call(
            reduce_kernel, (arr((own, feat), F32), arr((2, own), F32)), (gg, *parts), 16
        )
        sums, queries = lax.optimization_barrier((sums, queries))
        sums = [sums] + [move(sums, d, "head", head_n) for d in range(1, head_n)]
        q_mirror = mirror(queries)
        (od,) = call(functools.partial(delta_kernel, head_n * feat), (block,), (apply_out, gg, *sums), 16)
        od_mirror = mirror(od)
        od_near = near_all(od)
        factors, rises = call(
            functools.partial(key_kernel, slab, group),
            (arr((4, near, slab), F32), arr((3, near, slab), BF)),
            (wall, *kv_near),
            24,
            flops=12 * mflop,
        )
        pairs = [
            call(pair_kernel, (arr((own, 2 * feat), BF),), pair, 16)[0] for pair in zip(od_mirror, q_mirror)
        ]
        pairs = [x for m in pairs for x in near_all(m)]
        *grad_q, grads = call(
            functools.partial(near_kernel, slab, group, rows),
            (*(block,) * group, arr((3, seq_n * rows, slab), F32)),
            (normed, *q_near, *od_near),
            24,
            flops=12 * mflop,
        )
        grad_q = [grad_q[0]] + [move(grad_q[d], d) for d in range(1, group)]

        pairs = list(pairs)
        *tok_inner, = call(
            functools.partial(backward_kernel, slab, group, tok_groups),
            (
                arr((own, 2 * feat), BF),
                *[
                    message(q_block, q_block, (rows, 3 * slab)) if 0 < d < group else arr((rows, 3 * slab), BF)
                    for d in range(seq_n)
                ],
            ),
            (place, wall, normed, grads, factors, rises, *kv_near, *pairs),
            40,
            smem=1,
            flops=24 * mflop,
            scratch=[
                pltpu.VMEM((seq_n, rows, 3 * slab), F32),
                pltpu.VMEM((3, seq_n * rows, slab), F32),
            ],
        )
        tok_inner, grad_q = lax.optimization_barrier((tok_inner, grad_q))
        tok, sends = tok_inner[0], tok_inner[1:]
        got = {0: sends[0]}
        for d in mixed(seq_n, group, 1):
            got[d] = move(sends[d], d)
        out_tok = arr((1, own, feat), BF)
        grad_w = arr((1, rows, hidden), F32)
        return call(
            functools.partial(final_kernel, group, slab),
            (*(out_tok,) * 3, *(grad_w,) * 3),
            (place, rate, tok, *grad_q, *[got[d] for d in range(seq_n)]),
            16,
            smem=1,
            scratch=[pltpu.VMEM((group, rows, 3 * slab), F32)],
        )

    return local


def solution(mesh):
    seq_n = mesh.shape["seq"]
    head_n = mesh.shape["head"]
    group = min(4, seq_n)
    tok = P("head", "seq", None)
    return jax.shard_map(
        make_local(seq_n, head_n, group),
        mesh=mesh,
        in_specs=(tok, tok, tok, tok, P("head", "seq"), P("head", None), tok, tok, tok, tok, tok, tok),
        out_specs=(tok, tok, tok, tok, tok, tok),
        check_vma=False,
    )
```

```python
import functools

import jax
import jax.numpy as jnp
from jax import lax
from jax.experimental import pallas as pl
from jax.experimental.pallas import tpu as pltpu
from jax.sharding import PartitionSpec as P

EPS_COL = 1e-06
EPS_ROOT = 1e-05
BF = jnp.bfloat16
F32 = jnp.float32
LANES = 128
VMEM = pl.BlockSpec(memory_space=pltpu.VMEM)
SMEM = pl.BlockSpec(memory_space=pltpu.SMEM)


def silu_parts(pre_act):
    sigmoid_val = jax.nn.sigmoid(pre_act)
    silu_val = pre_act * sigmoid_val
    silu_slope = sigmoid_val * (1.0 + pre_act * (1.0 - sigmoid_val))
    silu_bend = sigmoid_val * (1.0 - sigmoid_val) * (2.0 + pre_act * (1.0 - 2.0 * sigmoid_val))
    return (silu_val, silu_slope, silu_bend)


def mm(left_op, right_op):
    return jnp.dot(left_op, right_op, preferred_element_type=F32)


def mm_nt(left_op, right_op):
    return lax.dot_general(left_op, right_op, (((1,), (1,)), ((), ())), preferred_element_type=F32)


def mm_tn(left_op, right_op):
    return lax.dot_general(left_op, right_op, (((0,), (0,)), ((), ())), preferred_element_type=F32)


def column_norm(weight):
    return jnp.sqrt(jnp.sum(weight * weight, axis=0, keepdims=True) + EPS_COL)


def flat(x):
    return x.reshape(-1, x.shape[-1])


def call(kernel, outs, args, mib, smem=0, flops=0, scratch=()):
    moved = sum(x.size * x.dtype.itemsize for x in (*args, *outs))
    return pl.pallas_call(
        kernel,
        out_shape=outs,
        in_specs=[SMEM] * smem + [VMEM] * (len(args) - smem),
        out_specs=[VMEM] * len(outs),
        scratch_shapes=scratch,
        compiler_params=pltpu.CompilerParams(vmem_limit_bytes=mib << 20),
        cost_estimate=pl.CostEstimate(flops=flops, bytes_accessed=moved, transcendentals=0),
    )(*args)


def copying_call(kernel, outs, args, buffers):
    return pl.pallas_call(
        kernel,
        out_shape=outs,
        in_specs=[pl.BlockSpec(memory_space=pltpu.HBM)] * len(args),
        out_specs=[VMEM] * len(outs),
        scratch_shapes=[*buffers, pltpu.SemaphoreType.DMA((len(args),))],
        compiler_params=pltpu.CompilerParams(vmem_limit_bytes=56 << 20),
    )(*args)


def arr(shape, dtype):
    return jax.ShapeDtypeStruct(shape, dtype)


def fetch(sources, buffers, sems):
    copies = [pltpu.make_async_copy(s, b, sems.at[i]) for i, (s, b) in enumerate(zip(sources, buffers))]
    for copy in copies:
        copy.start()
    for copy in copies:
        copy.wait()


def padded(rows):
    return -(-rows // 16) * 16


def tiles(cols):
    return -(-cols // LANES)


def put(out, at, value):
    rows, cols = value.shape
    for t in range(tiles(cols)):
        wide = min(LANES, cols - t * LANES)
        out[at : at + rows, 0:wide] = value[:, t * LANES : t * LANES + wide]
        at += padded(rows)
    return at


def get(ref, at, rows, cols):
    parts = []
    for t in range(tiles(cols)):
        wide = min(LANES, cols - t * LANES)
        parts.append(ref[at : at + rows, 0:wide])
        at += padded(rows)
    return jnp.concatenate(parts, axis=1), at


def message(*blocks):
    return arr((sum(tiles(cols) * padded(rows) for rows, cols in blocks), LANES), BF)


def token_pack_kernel(q, k, v, og, rates, gains, all_out, kv_out, gg_out, rate_out):
    tokens, feat = gg_out.shape
    rate = jnp.broadcast_to(rates[...], (feat, tokens)).T
    values = (rate * v[0].astype(F32)).astype(BF)
    all_out[:, 0:feat] = q[0]
    all_out[:, feat : 2 * feat] = k[0]
    all_out[:, 2 * feat : 3 * feat] = values
    kv_out[:, 0:feat] = k[0]
    kv_out[:, feat : 2 * feat] = values
    gg_out[...] = gains[...] * og[0].astype(F32)
    rate_out[...] = rate


def weight_pack_kernel(group, slab, *refs):
    args, (w_out, buf, sems) = refs[:6], refs[6:]
    fetch(args, [buf.at[pl.ds(i, 1)] for i in range(6)], sems)
    for j in range(group):
        cols = pl.ds(j * slab, slab)
        block = jnp.concatenate([buf[i, :, cols] for i in range(6)], axis=1)
        for p in range(j, w_out.shape[0], group):
            w_out[p] = block


def columns(w, slab):
    parts = [w[:, pl.ds(i * slab, slab)].astype(F32) for i in range(6)]
    saved, init = parts[:3], parts[3:]
    return saved, init, [column_norm(x) for x in init], [column_norm(x) for x in saved]


def stack(refs, cols=slice(None)):
    return jnp.concatenate([r[:, cols] for r in refs], axis=0)


def thirds(x, slab):
    return [x[:, pl.ds(i * slab, slab)] for i in range(3)]


def forward_kernel(slab, group, w, *refs):
    queries, parts, normed_out = refs[:group], refs[group:-1], refs[-1]
    own, feat = parts[0].shape
    saved, init, norm_init, norm_saved = columns(w, slab)
    normed = [(saved[i] * (norm_init[i] / norm_saved[i])).astype(BF) for i in range(3)]
    rows = stack(queries, slice(0, feat))
    hidden = (silu_parts(mm(rows, normed[0]))[0] * mm(rows, normed[1])).astype(BF)
    out = mm_nt(hidden, normed[2]).astype(BF)
    for d in range(group):
        parts[d][...] = out[d * own : (d + 1) * own]
    normed_out[...] = jnp.concatenate(normed, axis=1)


def reduce_kernel(gg, *refs):
    parts, (apply_out, sums) = refs[:-2], refs[-2:]
    total = total_of(parts)
    apply_out[...] = total
    sums[0:1, :] = jnp.sum((total * total).T, axis=0, keepdims=True)
    sums[1:2, :] = jnp.sum((total * gg[...]).T, axis=0, keepdims=True)


def delta_kernel(width, apply_out, gg, *refs):
    sums, out = refs[:-1], refs[-1]
    tokens, feat = apply_out.shape
    total = sums[0][...]
    for more in sums[1:]:
        total += more[...]
    square = jnp.broadcast_to(total[0:1, :], (feat, tokens)).T
    gain = jnp.broadcast_to(total[1:2, :], (feat, tokens)).T
    root = jnp.sqrt(square / width + EPS_ROOT)
    out[...] = (gg[...] / root - apply_out[...] * (gain / width) / (root * root * root)).astype(BF)


def pair_kernel(left, right, out):
    feat = left.shape[1]
    out[:, 0:feat] = left[...]
    out[:, feat : 2 * feat] = right[...]


def query_side(rows, delta, normed):
    q_gate = mm(rows, normed[0])
    q_up = mm(rows, normed[1])
    act, slope, _ = silu_parts(q_gate)
    hidden = (act * q_up).astype(BF)
    delta_hidden = mm(delta, normed[2])
    delta_gate = (delta_hidden * q_up * slope).astype(BF)
    delta_up = (delta_hidden * act).astype(BF)
    grads = (mm_tn(rows, delta_gate), mm_tn(rows, delta_up), mm_tn(delta, hidden))
    return delta_gate, delta_up, grads


def near_kernel(slab, group, normed_ref, *refs):
    q_near, od_near, (grad_q, grads_out) = refs[:group], refs[group : 2 * group], refs[2 * group :]
    feat = od_near[0].shape[1]
    normed = thirds(normed_ref, slab)
    delta_gate, delta_up, grads = query_side(stack(q_near, slice(0, feat)), stack(od_near), normed)
    grad_q[...] = (mm_nt(delta_gate, normed[0]) + mm_nt(delta_up, normed[1])).astype(BF)
    for i in range(3):
        grads_out[i] = grads[i]


def key_kernel(slab, group, w, *refs):
    kvs, (factors, rises) = refs[:group], refs[group:]
    feat = w.shape[0]
    init = [w[:, pl.ds((3 + i) * slab, slab)] for i in range(3)]
    keys = stack(kvs, slice(-2 * feat, -feat))
    values = stack(kvs, slice(-feat, None))
    k_gate = mm(keys, init[0])
    k_up = mm(keys, init[1])
    k_proj = mm(values, init[2])
    k_act, k_slope, k_bend = silu_parts(k_gate)
    rises[0] = (k_act * k_up).astype(BF)
    rises[1] = (k_proj * k_up * k_slope).astype(BF)
    rises[2] = (k_proj * k_act).astype(BF)
    factors[0] = k_act
    factors[1] = k_up * k_slope
    factors[2] = k_proj * k_slope
    factors[3] = k_proj * k_up * k_bend


def backward_kernel(slab, group, tok_groups, place, w, normed_ref, grad_q, grads, factors, rises, *refs):
    far = group * (tok_groups - 1)
    kvs, pairs, outs, (inner_buf, sums) = refs[:group], refs[group : group + far], refs[group + far : -2], refs[-2:]
    feat = w.shape[0]
    tok_out, outs = outs[0], outs[1:]
    own = tok_out.shape[0]
    normed = thirds(normed_ref, slab)
    total = [grads[i] for i in range(3)]
    for e in range(tok_groups - 1):
        these = pairs[e * group : (e + 1) * group]
        more = query_side(stack(these, slice(feat, 2 * feat)), stack(these, slice(0, feat)), normed)[2]
        total = [total[i] + more[i] for i in range(3)]
        if tok_groups > 2:
            for i in range(3):
                sums[i] = total[i]
            total = [sums[i] for i in range(3)]

    saved, init, norm_init, norm_saved = columns(w, slab)
    cots, direct = [], []
    once = jnp.where(place[0] == 0, 1.0, 0.0)
    for i in range(3):
        apply_grad = total[i]
        col_dot = jnp.sum(saved[i] * apply_grad, axis=0, keepdims=True)
        cot = apply_grad * (norm_init[i] / norm_saved[i]) - saved[i] * (
            col_dot * norm_init[i] / (norm_saved[i] * norm_saved[i] * norm_saved[i])
        )
        cots.append(cot.astype(BF))
        direct.append((cot + init[i] * (col_dot / (norm_init[i] * norm_saved[i]))) * once)

    init_bf = [w[:, pl.ds((3 + i) * slab, slab)] for i in range(3)]
    keys = stack(kvs, slice(-2 * feat, -feat))
    values = stack(kvs, slice(-feat, None))
    back_gate = mm(keys, cots[0])
    back_up = mm(keys, cots[1])
    back_hidden = mm(values, cots[2])
    back_proj = (back_gate * factors[1] + back_up * factors[0]).astype(BF)
    back_kup = (back_gate * factors[2] + back_hidden * factors[0]).astype(BF)
    back_kgate = (back_gate * factors[3] + (back_up * factors[2] + back_hidden * factors[1])).astype(BF)
    grad_k = (
        mm_nt(rises[1], cots[0])
        + mm_nt(rises[2], cots[1])
        + mm_nt(back_kgate, init_bf[0])
        + mm_nt(back_kup, init_bf[1])
    ).astype(BF)
    grad_v = (mm_nt(rises[0], cots[2]) + mm_nt(back_proj, init_bf[2])).astype(BF)
    inner = (mm_tn(keys, back_kgate), mm_tn(keys, back_kup), mm_tn(values, back_proj))
    whole = jnp.concatenate([inner[i] + direct[i] for i in range(3)], axis=1)
    rows = inner_buf.shape[1]
    for p in range(inner_buf.shape[0]):
        inner_buf[p] = whole[p * rows : (p + 1) * rows]
    tok_out[:, 0:feat] = grad_q[0:own, :]
    tok_out[:, feat : 2 * feat] = grad_k[0:own]
    tok_out[:, 2 * feat : 3 * feat] = grad_v[0:own]
    for d in range(inner_buf.shape[0]):
        block = inner_buf[place[2] ^ d].astype(BF)
        if 0 < d < group:
            out = outs[d]
            at = 0
            for tok in (grad_q, grad_k, grad_v):
                at = put(out, at, tok[d * own : (d + 1) * own, :])
            put(out, at, block)
        else:
            outs[d][...] = block


def total_of(refs):
    total = refs[0][...].astype(F32)
    for block in refs[1:]:
        total += block[...].astype(F32)
    return total


def final_kernel(group, order, slab, place, rate, tok, *refs):
    given, (gq, gk, gv, *outs, buf) = refs[:-7], refs[-7:]
    blocks = dict(zip(order, given))
    _, own, feat = gq.shape
    rows = buf.shape[1]
    sums = [tok[:, i * feat : (i + 1) * feat].astype(F32) for i in range(3)]
    for d in range(group):
        block = blocks[d]
        at = 0
        if d:
            for i in range(3):
                more, at = get(block, at, own, feat)
                sums[i] += more.astype(F32)
            value = get(block, at, rows, 3 * slab)[0]
        else:
            value = block[...]
        buf[d] = value.astype(F32)
        for other in range(d + group, len(order), group):
            buf[d] += blocks[other][...].astype(F32)
    gq[0] = sums[0].astype(BF)
    gk[0] = sums[1].astype(BF)
    gv[0] = (rate[...] * sums[2]).astype(BF)
    cols = [buf[place[1] ^ j] for j in range(group)]
    for i in range(3):
        outs[i][0] = jnp.concatenate([c[:, i * slab : (i + 1) * slab] for c in cols], axis=1)


def make_local(seq_n, head_n, group):
    tok_groups = seq_n // group

    def move(x, dist, axis="seq", size=seq_n):
        return lax.ppermute(x, axis, [(i, i ^ dist) for i in range(size)])

    def near_all(x):
        return [x] + [move(x, d) for d in range(1, group)]

    def mirror(x):
        return [move(x, e * group) for e in range(1, tok_groups)]

    def local(q, k, v, og, rates, gains, gi, ui, di, gs, us, ds):
        _, rows, hidden = gi.shape
        _, own, feat = q.shape
        slab = hidden // group
        near = group * own
        me = lax.axis_index("seq")
        place = jnp.stack((lax.div(me, group), lax.rem(me, group), me)).astype(jnp.int32)

        (packed,) = copying_call(
            functools.partial(weight_pack_kernel, group, slab),
            (arr((seq_n, rows, 6 * slab), BF),),
            (gs, us, ds, gi, ui, di),
            [pltpu.VMEM((6, rows, hidden), BF)],
        )
        packed, queries = lax.optimization_barrier((packed, q[0]))
        wall = lax.all_to_all(packed, "seq", 0, 0, tiled=True).reshape(seq_n * rows, 6 * slab)
        tokens, kv, gg, rate = call(
            token_pack_kernel,
            (arr((own, 3 * feat), BF), arr((own, 2 * feat), BF), arr((own, feat), F32), arr((own, feat), F32)),
            (q, k, v, og, rates, gains),
            8,
        )
        beside = move(tokens, 1) if group > 1 else None
        rest = range(2, group)
        q_near = [queries, beside][:group] + [move(queries, d) for d in rest]
        kv_near = [kv, beside][:group] + [move(kv, d) for d in rest]

        block = arr((own, feat), BF)
        mflop = 2 * near * feat * slab
        *parts, normed = call(
            functools.partial(forward_kernel, slab, group),
            (*(block,) * group, arr((seq_n * rows, 3 * slab), BF)),
            (wall, *q_near),
            24,
            flops=3 * mflop,
        )
        parts = [parts[0]] + [move(parts[d], d) for d in (*range(2, group), *range(1, min(2, group)))]
        *parts, kv_near = lax.optimization_barrier((*parts, kv_near))
        apply_out, sums = call(
            reduce_kernel, (arr((own, feat), F32), arr((2, own), F32)), (gg, *parts), 16
        )
        sums, queries = lax.optimization_barrier((sums, queries))
        sums = [sums] + [move(sums, d, "head", head_n) for d in range(1, head_n)]
        q_mirror = mirror(queries)
        (od,) = call(functools.partial(delta_kernel, head_n * feat), (block,), (apply_out, gg, *sums), 16)
        od_mirror = mirror(od)
        od_near = near_all(od)
        factors, rises = call(
            functools.partial(key_kernel, slab, group),
            (arr((4, near, slab), F32), arr((3, near, slab), BF)),
            (wall, *kv_near),
            24,
            flops=12 * mflop,
        )
        pairs = [
            call(pair_kernel, (arr((own, 2 * feat), BF),), pair, 16)[0] for pair in zip(od_mirror, q_mirror)
        ]
        pairs = [x for m in pairs for x in near_all(m)]
        grad_q, grads = call(
            functools.partial(near_kernel, slab, group),
            (arr((near, feat), BF), arr((3, seq_n * rows, slab), F32)),
            (normed, *q_near, *od_near),
            24,
            flops=12 * mflop,
        )

        q_block = (own, feat)
        tok, *sends = call(
            functools.partial(backward_kernel, slab, group, tok_groups),
            (
                arr((own, 3 * feat), BF),
                *[
                    message(*(q_block,) * 3, (rows, 3 * slab)) if 0 < d < group else arr((rows, 3 * slab), BF)
                    for d in range(seq_n)
                ],
            ),
            (place, wall, normed, grad_q, grads, factors, rises, *kv_near, *pairs),
            40,
            smem=1,
            flops=24 * mflop,
            scratch=[
                pltpu.VMEM((seq_n, rows, 3 * slab), F32),
                pltpu.VMEM((3, seq_n * rows, slab), F32),
            ],
        )
        far = list(range(group, seq_n))
        order = [0, *far[:2], *range(2, group), *range(1, min(2, group)), *far[2:]]
        got = [move(sends[d], d) if d else sends[d] for d in order]
        out_tok = arr((1, own, feat), BF)
        grad_w = arr((1, rows, hidden), F32)
        return call(
            functools.partial(final_kernel, group, order, slab),
            (*(out_tok,) * 3, *(grad_w,) * 3),
            (place, rate, tok, *got),
            16,
            smem=1,
            scratch=[pltpu.VMEM((group, rows, 3 * slab), F32)],
        )

    return local


def solution(mesh):
    seq_n = mesh.shape["seq"]
    head_n = mesh.shape["head"]
    group = min(4, seq_n)
    tok = P("head", "seq", None)
    return jax.shard_map(
        make_local(seq_n, head_n, group),
        mesh=mesh,
        in_specs=(tok, tok, tok, tok, P("head", "seq"), P("head", None), tok, tok, tok, tok, tok, tok),
        out_specs=(tok, tok, tok, tok, tok, tok),
        check_vma=False,
    )
```

```python
import functools

import jax
import jax.numpy as jnp
from jax import lax
from jax.experimental import pallas as pl
from jax.experimental.pallas import tpu as pltpu
from jax.sharding import PartitionSpec as P

EPS_COL = 1e-06
EPS_ROOT = 1e-05
BF = jnp.bfloat16
F32 = jnp.float32
VMEM = pl.BlockSpec(memory_space=pltpu.VMEM)
SMEM = pl.BlockSpec(memory_space=pltpu.SMEM)


def silu_parts(pre_act):
    sigmoid_val = jax.nn.sigmoid(pre_act)
    silu_val = pre_act * sigmoid_val
    silu_slope = sigmoid_val * (1.0 + pre_act * (1.0 - sigmoid_val))
    silu_bend = sigmoid_val * (1.0 - sigmoid_val) * (2.0 + pre_act * (1.0 - 2.0 * sigmoid_val))
    return (silu_val, silu_slope, silu_bend)


def mm(left_op, right_op):
    return jnp.dot(left_op, right_op, preferred_element_type=F32)


def mm_nt(left_op, right_op):
    return lax.dot_general(left_op, right_op, (((1,), (1,)), ((), ())), preferred_element_type=F32)


def mm_tn(left_op, right_op):
    return lax.dot_general(left_op, right_op, (((0,), (0,)), ((), ())), preferred_element_type=F32)


def column_norm(weight):
    return jnp.sqrt(jnp.sum(weight * weight, axis=0, keepdims=True) + EPS_COL)


def flat(x):
    return x.reshape(-1, x.shape[-1])


def call(kernel, outs, args, mib, smem=0, flops=0, scratch=()):
    moved = sum(x.size * x.dtype.itemsize for x in (*args, *outs))
    return pl.pallas_call(
        kernel,
        out_shape=outs,
        in_specs=[SMEM] * smem + [VMEM] * (len(args) - smem),
        out_specs=[VMEM] * len(outs),
        scratch_shapes=scratch,
        compiler_params=pltpu.CompilerParams(vmem_limit_bytes=mib << 20),
        cost_estimate=pl.CostEstimate(flops=flops, bytes_accessed=moved, transcendentals=0),
    )(*args)


def copying_call(kernel, outs, args, buffers):
    return pl.pallas_call(
        kernel,
        out_shape=outs,
        in_specs=[pl.BlockSpec(memory_space=pltpu.HBM)] * len(args),
        out_specs=[VMEM] * len(outs),
        scratch_shapes=[*buffers, pltpu.SemaphoreType.DMA((len(args),))],
        compiler_params=pltpu.CompilerParams(vmem_limit_bytes=56 << 20),
    )(*args)


def arr(shape, dtype):
    return jax.ShapeDtypeStruct(shape, dtype)


def fetch(sources, buffers, sems):
    copies = [pltpu.make_async_copy(s, b, sems.at[i]) for i, (s, b) in enumerate(zip(sources, buffers))]
    for copy in copies:
        copy.start()
    for copy in copies:
        copy.wait()


def token_pack_kernel(q, k, v, og, rates, gains, all_out, kv_out, gg_out, rate_out):
    tokens, feat = gg_out.shape
    rate = jnp.broadcast_to(rates[...], (feat, tokens)).T
    values = (rate * v[0].astype(F32)).astype(BF)
    all_out[:, 0:feat] = q[0]
    all_out[:, feat : 2 * feat] = k[0]
    all_out[:, 2 * feat : 3 * feat] = values
    kv_out[:, 0:feat] = k[0]
    kv_out[:, feat : 2 * feat] = values
    gg_out[...] = gains[...] * og[0].astype(F32)
    rate_out[...] = rate


def weight_pack_kernel(group, slab, *refs):
    args, (w_out, buf, sems) = refs[:6], refs[6:]
    fetch(args, [buf.at[pl.ds(i, 1)] for i in range(6)], sems)
    for j in range(group):
        cols = pl.ds(j * slab, slab)
        block = jnp.concatenate([buf[i, :, cols] for i in range(6)], axis=1)
        for p in range(j, w_out.shape[0], group):
            w_out[p] = block


def columns(w, slab):
    parts = [w[:, pl.ds(i * slab, slab)].astype(F32) for i in range(6)]
    saved, init = parts[:3], parts[3:]
    return saved, init, [column_norm(x) for x in init], [column_norm(x) for x in saved]


def stack(refs, cols=slice(None)):
    return jnp.concatenate([r[:, cols] for r in refs], axis=0)


def thirds(x, slab):
    return [x[:, pl.ds(i * slab, slab)] for i in range(3)]


def forward_kernel(slab, group, w, *refs):
    queries, parts, normed_out = refs[:group], refs[group:-1], refs[-1]
    own, feat = parts[0].shape
    saved, init, norm_init, norm_saved = columns(w, slab)
    normed = [(saved[i] * (norm_init[i] / norm_saved[i])).astype(BF) for i in range(3)]
    rows = stack(queries, slice(0, feat))
    hidden = (silu_parts(mm(rows, normed[0]))[0] * mm(rows, normed[1])).astype(BF)
    out = mm_nt(hidden, normed[2]).astype(BF)
    for d in range(group):
        parts[d][...] = out[d * own : (d + 1) * own]
    normed_out[...] = jnp.concatenate(normed, axis=1)


def reduce_kernel(gg, *refs):
    parts, (apply_out, sums) = refs[:-2], refs[-2:]
    total = total_of(parts)
    apply_out[...] = total
    sums[0:1, :] = jnp.sum((total * total).T, axis=0, keepdims=True)
    sums[1:2, :] = jnp.sum((total * gg[...]).T, axis=0, keepdims=True)


def delta_kernel(width, apply_out, gg, *refs):
    sums, out = refs[:-1], refs[-1]
    tokens, feat = apply_out.shape
    total = sums[0][...]
    for more in sums[1:]:
        total += more[...]
    square = jnp.broadcast_to(total[0:1, :], (feat, tokens)).T
    gain = jnp.broadcast_to(total[1:2, :], (feat, tokens)).T
    root = jnp.sqrt(square / width + EPS_ROOT)
    out[...] = (gg[...] / root - apply_out[...] * (gain / width) / (root * root * root)).astype(BF)


def pair_kernel(left, right, out):
    feat = left.shape[1]
    out[:, 0:feat] = left[...]
    out[:, feat : 2 * feat] = right[...]


def query_side(rows, delta, normed):
    q_gate = mm(rows, normed[0])
    q_up = mm(rows, normed[1])
    act, slope, _ = silu_parts(q_gate)
    hidden = (act * q_up).astype(BF)
    delta_hidden = mm(delta, normed[2])
    delta_gate = (delta_hidden * q_up * slope).astype(BF)
    delta_up = (delta_hidden * act).astype(BF)
    grads = (mm_tn(rows, delta_gate), mm_tn(rows, delta_up), mm_tn(delta, hidden))
    return delta_gate, delta_up, grads


def near_kernel(slab, group, normed_ref, *refs):
    q_near, od_near, (grad_q, grads_out) = refs[:group], refs[group : 2 * group], refs[2 * group :]
    feat = od_near[0].shape[1]
    normed = thirds(normed_ref, slab)
    delta_gate, delta_up, grads = query_side(stack(q_near, slice(0, feat)), stack(od_near), normed)
    grad_q[...] = (mm_nt(delta_gate, normed[0]) + mm_nt(delta_up, normed[1])).astype(BF)
    for i in range(3):
        grads_out[i] = grads[i]


def key_kernel(slab, group, w, *refs):
    kvs, (factors, rises, ratio, minus, plus) = refs[:group], refs[group:]
    feat = w.shape[0]
    saved, start, norm_init, norm_saved = columns(w, slab)
    for i in range(3):
        ratio[i : i + 1, :] = norm_init[i] / norm_saved[i]
        minus[i] = saved[i] * (norm_init[i] / (norm_saved[i] * norm_saved[i] * norm_saved[i]))
        plus[i] = start[i] / (norm_init[i] * norm_saved[i])
    init = [w[:, pl.ds((3 + i) * slab, slab)] for i in range(3)]
    keys = stack(kvs, slice(-2 * feat, -feat))
    values = stack(kvs, slice(-feat, None))
    k_gate = mm(keys, init[0])
    k_up = mm(keys, init[1])
    k_proj = mm(values, init[2])
    k_act, k_slope, k_bend = silu_parts(k_gate)
    rises[0] = (k_act * k_up).astype(BF)
    rises[1] = (k_proj * k_up * k_slope).astype(BF)
    rises[2] = (k_proj * k_act).astype(BF)
    factors[0] = k_act
    factors[1] = k_up * k_slope
    factors[2] = k_proj * k_slope
    factors[3] = k_proj * k_up * k_bend


def backward_kernel(
    slab, group, tok_groups, place, w, normed_ref, grad_q, grads, factors, rises, ratio, minus, plus, *refs
):
    far = group * (tok_groups - 1)
    kvs, pairs, outs, (home, sums) = refs[:group], refs[group : group + far], refs[group + far : -2], refs[-2:]
    feat = w.shape[0]
    outs, homes = outs[:group], outs[group:]
    own = outs[0].shape[0]
    normed = thirds(normed_ref, slab)
    total = [grads[i] for i in range(3)]
    for e in range(tok_groups - 1):
        these = pairs[e * group : (e + 1) * group]
        more = query_side(stack(these, slice(feat, 2 * feat)), stack(these, slice(0, feat)), normed)[2]
        total = [total[i] + more[i] for i in range(3)]
        if tok_groups > 2:
            for i in range(3):
                sums[i] = total[i]
            total = [sums[i] for i in range(3)]

    cots, direct = [], []
    once = jnp.where(place[0] == 0, 1.0, 0.0)
    for i in range(3):
        saved = w[:, pl.ds(i * slab, slab)].astype(F32)
        col_dot = jnp.sum(saved * total[i], axis=0, keepdims=True)
        cot = total[i] * ratio[i : i + 1, :] - minus[i] * col_dot
        cots.append(cot.astype(BF))
        direct.append((cot + plus[i] * col_dot) * once)

    init_bf = [w[:, pl.ds((3 + i) * slab, slab)] for i in range(3)]
    keys = stack(kvs, slice(-2 * feat, -feat))
    values = stack(kvs, slice(-feat, None))
    back_gate = mm(keys, cots[0])
    back_up = mm(keys, cots[1])
    back_hidden = mm(values, cots[2])
    back_proj = (back_gate * factors[1] + back_up * factors[0]).astype(BF)
    back_kup = (back_gate * factors[2] + back_hidden * factors[0]).astype(BF)
    back_kgate = (back_gate * factors[3] + (back_up * factors[2] + back_hidden * factors[1])).astype(BF)
    grad_k = (
        mm_nt(rises[1], cots[0])
        + mm_nt(rises[2], cots[1])
        + mm_nt(back_kgate, init_bf[0])
        + mm_nt(back_kup, init_bf[1])
    ).astype(BF)
    grad_v = (mm_nt(rises[0], cots[2]) + mm_nt(back_proj, init_bf[2])).astype(BF)
    inner = (mm_tn(keys, back_kgate), mm_tn(keys, back_kup), mm_tn(values, back_proj))
    whole = jnp.concatenate([inner[i] + direct[i] for i in range(3)], axis=1)
    rows = home.shape[1]
    for t in range(tok_groups):
        home[t] = whole[t * rows : (t + 1) * rows]
    for e, out in enumerate(homes):
        out[...] = home[place[0] ^ e].astype(out.dtype)
    for d in range(group):
        outs[d][:, 0:feat] = grad_q[d * own : (d + 1) * own, :]
        outs[d][:, feat : 2 * feat] = grad_k[d * own : (d + 1) * own]
        outs[d][:, 2 * feat : 3 * feat] = grad_v[d * own : (d + 1) * own]


def home_kernel(*refs):
    blocks, out = refs[:-1], refs[-1]
    group, rows, _ = out.shape
    whole = total_of(blocks).astype(BF)
    for j in range(group):
        out[j] = whole[j * rows : (j + 1) * rows]


def total_of(refs):
    total = refs[0][...].astype(F32)
    for block in refs[1:]:
        total += block[...].astype(F32)
    return total


def tokens_kernel(rate, *refs):
    got, (gq, gk, gv) = refs[:-3], refs[-3:]
    feat = gq.shape[2]
    total = total_of(got)
    gq[0] = total[:, 0:feat].astype(BF)
    gk[0] = total[:, feat : 2 * feat].astype(BF)
    gv[0] = (rate[...] * total[:, 2 * feat : 3 * feat]).astype(BF)


def weights_kernel(slab, got, *outs):
    for i in range(3):
        cols = [got[j, :, i * slab : (i + 1) * slab].astype(F32) for j in range(got.shape[0])]
        outs[i][0] = jnp.concatenate(cols, axis=1)


def make_local(seq_n, head_n, group):
    tok_groups = seq_n // group
    groups = [[t * group + j for j in range(group)] for t in range(tok_groups)]

    def move(x, dist, axis="seq", size=seq_n):
        return lax.ppermute(x, axis, [(i, i ^ dist) for i in range(size)])

    def near_all(x):
        return [x] + [move(x, d) for d in range(1, group)]

    def mirror(x):
        return [move(x, e * group) for e in range(1, tok_groups)]

    def local(q, k, v, og, rates, gains, gi, ui, di, gs, us, ds):
        _, rows, hidden = gi.shape
        _, own, feat = q.shape
        slab = hidden // group
        near = group * own
        me = lax.axis_index("seq")
        place = jnp.stack((lax.div(me, group), lax.rem(me, group), me)).astype(jnp.int32)

        (packed,) = copying_call(
            functools.partial(weight_pack_kernel, group, slab),
            (arr((seq_n, rows, 6 * slab), BF),),
            (gs, us, ds, gi, ui, di),
            [pltpu.VMEM((6, rows, hidden), BF)],
        )
        packed, queries = lax.optimization_barrier((packed, q[0]))
        wall = lax.all_to_all(packed, "seq", 0, 0, tiled=True).reshape(seq_n * rows, 6 * slab)
        tokens, kv, gg, rate = call(
            token_pack_kernel,
            (arr((own, 3 * feat), BF), arr((own, 2 * feat), BF), arr((own, feat), F32), arr((own, feat), F32)),
            (q, k, v, og, rates, gains),
            8,
        )
        beside = move(tokens, 1) if group > 1 else None
        rest = range(2, group)
        q_near = [queries, beside][:group] + [move(queries, d) for d in rest]
        kv_near = [kv, beside][:group] + [move(kv, d) for d in rest]

        block = arr((own, feat), BF)
        mflop = 2 * near * feat * slab
        *parts, normed = call(
            functools.partial(forward_kernel, slab, group),
            (*(block,) * group, arr((seq_n * rows, 3 * slab), BF)),
            (wall, *q_near),
            24,
            flops=3 * mflop,
        )
        parts = [parts[0]] + [move(parts[d], d) for d in (*range(2, group), *range(1, min(2, group)))]
        *parts, kv_near = lax.optimization_barrier((*parts, kv_near))
        apply_out, sums = call(
            reduce_kernel, (arr((own, feat), F32), arr((2, own), F32)), (gg, *parts), 16
        )
        sums, queries = lax.optimization_barrier((sums, queries))
        sums = [sums] + [move(sums, d, "head", head_n) for d in range(1, head_n)]
        q_mirror = mirror(queries)
        (od,) = call(functools.partial(delta_kernel, head_n * feat), (block,), (apply_out, gg, *sums), 16)
        od_mirror = mirror(od)
        od_near = near_all(od)
        column = arr((3, seq_n * rows, slab), F32)
        factors, rises, *stats = call(
            functools.partial(key_kernel, slab, group),
            (arr((4, near, slab), F32), arr((3, near, slab), BF), arr((3, slab), F32), column, column),
            (wall, *kv_near),
            24,
            flops=12 * mflop,
        )
        pairs = [
            call(pair_kernel, (arr((own, 2 * feat), BF),), pair, 16)[0] for pair in zip(od_mirror, q_mirror)
        ]
        pairs = [x for m in pairs for x in near_all(m)]
        grad_q, grads = call(
            functools.partial(near_kernel, slab, group),
            (arr((near, feat), BF), arr((3, seq_n * rows, slab), F32)),
            (normed, *q_near, *od_near),
            24,
            flops=12 * mflop,
        )

        home = (group * rows, 3 * slab)
        result = call(
            functools.partial(backward_kernel, slab, group, tok_groups),
            (
                *(arr((own, 3 * feat), BF),) * group,
                arr(home, F32),
                *(arr(home, BF),) * (tok_groups - 1),
            ),
            (place, wall, normed, grad_q, grads, factors, rises, *stats, *kv_near, *pairs),
            40,
            smem=1,
            flops=24 * mflop,
            scratch=[
                pltpu.VMEM((tok_groups, *home), F32),
                pltpu.VMEM((3, seq_n * rows, slab), F32),
            ],
        )
        tok, inner = result[:group], result[group:]
        inner = [inner[0]] + [move(inner[e], e * group) for e in range(1, tok_groups)]
        tok = [tok[0]] + [move(tok[d], d) for d in (*range(2, group), *range(1, min(2, group)))]
        (inner,) = call(home_kernel, (arr((group, rows, 3 * slab), BF),), inner, 16)
        inner = lax.all_to_all(inner, "seq", 0, 0, axis_index_groups=groups, tiled=True)
        out_tok = arr((1, own, feat), BF)
        grad_w = arr((1, rows, hidden), F32)
        grads_t = call(tokens_kernel, (out_tok,) * 3, (rate, *tok), 16)
        grads_w = call(functools.partial(weights_kernel, slab), (grad_w,) * 3, (inner,), 16)
        return (*grads_t, *grads_w)

    return local


def solution(mesh):
    seq_n = mesh.shape["seq"]
    head_n = mesh.shape["head"]
    group = min(4, seq_n)
    tok = P("head", "seq", None)
    return jax.shard_map(
        make_local(seq_n, head_n, group),
        mesh=mesh,
        in_specs=(tok, tok, tok, tok, P("head", "seq"), P("head", None), tok, tok, tok, tok, tok, tok),
        out_specs=(tok, tok, tok, tok, tok, tok),
        check_vma=False,
    )
```

```python
import functools

import jax
import jax.numpy as jnp
from jax import lax
from jax.experimental import pallas as pl
from jax.experimental.pallas import tpu as pltpu
from jax.sharding import PartitionSpec as P

EPS_COL = 1e-06
EPS_ROOT = 1e-05
BF = jnp.bfloat16
F32 = jnp.float32
LANES = 128
VMEM = pl.BlockSpec(memory_space=pltpu.VMEM)
SMEM = pl.BlockSpec(memory_space=pltpu.SMEM)


def silu_parts(pre_act):
    sigmoid_val = jax.nn.sigmoid(pre_act)
    silu_val = pre_act * sigmoid_val
    silu_slope = sigmoid_val * (1.0 + pre_act * (1.0 - sigmoid_val))
    silu_bend = sigmoid_val * (1.0 - sigmoid_val) * (2.0 + pre_act * (1.0 - 2.0 * sigmoid_val))
    return (silu_val, silu_slope, silu_bend)


def mm(left_op, right_op):
    return jnp.dot(left_op, right_op, preferred_element_type=F32)


def mm_nt(left_op, right_op):
    return lax.dot_general(left_op, right_op, (((1,), (1,)), ((), ())), preferred_element_type=F32)


def mm_tn(left_op, right_op):
    return lax.dot_general(left_op, right_op, (((0,), (0,)), ((), ())), preferred_element_type=F32)


def column_norm(weight):
    return jnp.sqrt(jnp.sum(weight * weight, axis=0, keepdims=True) + EPS_COL)


def flat(x):
    return x.reshape(-1, x.shape[-1])


def call(kernel, outs, args, mib, smem=0, flops=0, scratch=()):
    moved = sum(x.size * x.dtype.itemsize for x in (*args, *outs))
    return pl.pallas_call(
        kernel,
        out_shape=outs,
        in_specs=[SMEM] * smem + [VMEM] * (len(args) - smem),
        out_specs=[VMEM] * len(outs),
        scratch_shapes=scratch,
        compiler_params=pltpu.CompilerParams(vmem_limit_bytes=mib << 20),
        cost_estimate=pl.CostEstimate(flops=flops, bytes_accessed=moved, transcendentals=0),
    )(*args)


def copying_call(kernel, outs, args, buffers):
    return pl.pallas_call(
        kernel,
        out_shape=outs,
        in_specs=[pl.BlockSpec(memory_space=pltpu.HBM)] * len(args),
        out_specs=[VMEM] * len(outs),
        scratch_shapes=[*buffers, pltpu.SemaphoreType.DMA((len(args),))],
        compiler_params=pltpu.CompilerParams(vmem_limit_bytes=56 << 20),
    )(*args)


def arr(shape, dtype):
    return jax.ShapeDtypeStruct(shape, dtype)


def fetch(sources, buffers, sems):
    copies = [pltpu.make_async_copy(s, b, sems.at[i]) for i, (s, b) in enumerate(zip(sources, buffers))]
    for copy in copies:
        copy.start()
    for copy in copies:
        copy.wait()


def padded(rows):
    return -(-rows // 16) * 16


def tiles(cols):
    return -(-cols // LANES)


def put(out, at, value):
    rows, cols = value.shape
    for t in range(tiles(cols)):
        wide = min(LANES, cols - t * LANES)
        out[at : at + rows, 0:wide] = value[:, t * LANES : t * LANES + wide]
        at += padded(rows)
    return at


def get(ref, at, rows, cols):
    parts = []
    for t in range(tiles(cols)):
        wide = min(LANES, cols - t * LANES)
        parts.append(ref[at : at + rows, 0:wide])
        at += padded(rows)
    return jnp.concatenate(parts, axis=1), at


def message(*blocks):
    return arr((sum(tiles(cols) * padded(rows) for rows, cols in blocks), LANES), BF)


def token_pack_kernel(q, k, v, og, rates, gains, all_out, kv_out, gg_out, rate_out):
    tokens, feat = gg_out.shape
    rate = jnp.broadcast_to(rates[...], (feat, tokens)).T
    values = (rate * v[0].astype(F32)).astype(BF)
    all_out[:, 0:feat] = q[0]
    all_out[:, feat : 2 * feat] = k[0]
    all_out[:, 2 * feat : 3 * feat] = values
    kv_out[:, 0:feat] = k[0]
    kv_out[:, feat : 2 * feat] = values
    gg_out[...] = gains[...] * og[0].astype(F32)
    rate_out[...] = rate


def weight_pack_kernel(group, slab, *refs):
    args, (w_out, buf, sems) = refs[:6], refs[6:]
    fetch(args, [buf.at[pl.ds(i, 1)] for i in range(6)], sems)
    for j in range(group):
        cols = pl.ds(j * slab, slab)
        block = jnp.concatenate([buf[i, :, cols] for i in range(6)], axis=1)
        for p in range(j, w_out.shape[0], group):
            w_out[p] = block


def columns(w, slab):
    parts = [w[:, pl.ds(i * slab, slab)].astype(F32) for i in range(6)]
    saved, init = parts[:3], parts[3:]
    return saved, init, [column_norm(x) for x in init], [column_norm(x) for x in saved]


def stack(refs, cols=slice(None)):
    return jnp.concatenate([r[:, cols] for r in refs], axis=0)


def thirds(x, slab):
    return [x[:, pl.ds(i * slab, slab)] for i in range(3)]


def forward_kernel(slab, group, w, *refs):
    queries, parts, normed_out = refs[:group], refs[group:-1], refs[-1]
    own, feat = parts[0].shape
    saved, init, norm_init, norm_saved = columns(w, slab)
    normed = [(saved[i] * (norm_init[i] / norm_saved[i])).astype(BF) for i in range(3)]
    rows = stack(queries, slice(0, feat))
    hidden = (silu_parts(mm(rows, normed[0]))[0] * mm(rows, normed[1])).astype(BF)
    out = mm_nt(hidden, normed[2]).astype(BF)
    for d in range(group):
        parts[d][...] = out[d * own : (d + 1) * own]
    normed_out[...] = jnp.concatenate(normed, axis=1)


def reduce_kernel(gg, *refs):
    parts, (apply_out, sums) = refs[:-2], refs[-2:]
    total = total_of(parts)
    apply_out[...] = total
    sums[0:1, :] = jnp.sum((total * total).T, axis=0, keepdims=True)
    sums[1:2, :] = jnp.sum((total * gg[...]).T, axis=0, keepdims=True)


def delta_kernel(width, apply_out, gg, *refs):
    sums, out = refs[:-1], refs[-1]
    tokens, feat = apply_out.shape
    total = sums[0][...]
    for more in sums[1:]:
        total += more[...]
    square = jnp.broadcast_to(total[0:1, :], (feat, tokens)).T
    gain = jnp.broadcast_to(total[1:2, :], (feat, tokens)).T
    root = jnp.sqrt(square / width + EPS_ROOT)
    out[...] = (gg[...] / root - apply_out[...] * (gain / width) / (root * root * root)).astype(BF)


def pair_kernel(left, right, out):
    feat = left.shape[1]
    out[:, 0:feat] = left[...]
    out[:, feat : 2 * feat] = right[...]


def query_side(rows, delta, normed):
    q_gate = mm(rows, normed[0])
    q_up = mm(rows, normed[1])
    act, slope, _ = silu_parts(q_gate)
    hidden = (act * q_up).astype(BF)
    delta_hidden = mm(delta, normed[2])
    delta_gate = (delta_hidden * q_up * slope).astype(BF)
    delta_up = (delta_hidden * act).astype(BF)
    grads = (mm_tn(rows, delta_gate), mm_tn(rows, delta_up), mm_tn(delta, hidden))
    return delta_gate, delta_up, grads


def near_kernel(slab, group, normed_ref, *refs):
    q_near, od_near, (grad_q, grads_out) = refs[:group], refs[group : 2 * group], refs[2 * group :]
    feat = od_near[0].shape[1]
    normed = thirds(normed_ref, slab)
    delta_gate, delta_up, grads = query_side(stack(q_near, slice(0, feat)), stack(od_near), normed)
    grad_q[...] = (mm_nt(delta_gate, normed[0]) + mm_nt(delta_up, normed[1])).astype(BF)
    for i in range(3):
        grads_out[i] = grads[i]


def key_kernel(slab, group, w, *refs):
    kvs, (factors, rises, ratio, minus, plus) = refs[:group], refs[group:]
    feat = w.shape[0]
    saved, start, norm_init, norm_saved = columns(w, slab)
    for i in range(3):
        ratio[i : i + 1, :] = norm_init[i] / norm_saved[i]
        minus[i] = saved[i] * (norm_init[i] / (norm_saved[i] * norm_saved[i] * norm_saved[i]))
        plus[i] = start[i] / (norm_init[i] * norm_saved[i])
    init = [w[:, pl.ds((3 + i) * slab, slab)] for i in range(3)]
    keys = stack(kvs, slice(-2 * feat, -feat))
    values = stack(kvs, slice(-feat, None))
    k_gate = mm(keys, init[0])
    k_up = mm(keys, init[1])
    k_proj = mm(values, init[2])
    k_act, k_slope, k_bend = silu_parts(k_gate)
    rises[0] = (k_act * k_up).astype(BF)
    rises[1] = (k_proj * k_up * k_slope).astype(BF)
    rises[2] = (k_proj * k_act).astype(BF)
    factors[0] = k_act
    factors[1] = k_up * k_slope
    factors[2] = k_proj * k_slope
    factors[3] = k_proj * k_up * k_bend


def backward_kernel(
    slab, group, tok_groups, place, w, normed_ref, grad_q, grads, factors, rises, ratio, minus, plus, *refs
):
    far = group * (tok_groups - 1)
    kvs, pairs, outs, (inner_buf, sums) = refs[:group], refs[group : group + far], refs[group + far : -2], refs[-2:]
    feat = w.shape[0]
    tok_out, outs = outs[0], outs[1:]
    own = tok_out.shape[0]
    normed = thirds(normed_ref, slab)
    total = [grads[i] for i in range(3)]
    for e in range(tok_groups - 1):
        these = pairs[e * group : (e + 1) * group]
        more = query_side(stack(these, slice(feat, 2 * feat)), stack(these, slice(0, feat)), normed)[2]
        total = [total[i] + more[i] for i in range(3)]
        if tok_groups > 2:
            for i in range(3):
                sums[i] = total[i]
            total = [sums[i] for i in range(3)]

    cots, direct = [], []
    once = jnp.where(place[0] == 0, 1.0, 0.0)
    for i in range(3):
        saved = w[:, pl.ds(i * slab, slab)].astype(F32)
        col_dot = jnp.sum(saved * total[i], axis=0, keepdims=True)
        cot = total[i] * ratio[i : i + 1, :] - minus[i] * col_dot
        cots.append(cot.astype(BF))
        direct.append((cot + plus[i] * col_dot) * once)

    init_bf = [w[:, pl.ds((3 + i) * slab, slab)] for i in range(3)]
    keys = stack(kvs, slice(-2 * feat, -feat))
    values = stack(kvs, slice(-feat, None))
    back_gate = mm(keys, cots[0])
    back_up = mm(keys, cots[1])
    back_hidden = mm(values, cots[2])
    back_proj = (back_gate * factors[1] + back_up * factors[0]).astype(BF)
    back_kup = (back_gate * factors[2] + back_hidden * factors[0]).astype(BF)
    back_kgate = (back_gate * factors[3] + (back_up * factors[2] + back_hidden * factors[1])).astype(BF)
    grad_k = (
        mm_nt(rises[1], cots[0])
        + mm_nt(rises[2], cots[1])
        + mm_nt(back_kgate, init_bf[0])
        + mm_nt(back_kup, init_bf[1])
    ).astype(BF)
    grad_v = (mm_nt(rises[0], cots[2]) + mm_nt(back_proj, init_bf[2])).astype(BF)
    inner = (mm_tn(keys, back_kgate), mm_tn(keys, back_kup), mm_tn(values, back_proj))
    whole = jnp.concatenate([inner[i] + direct[i] for i in range(3)], axis=1)
    rows = inner_buf.shape[1]
    for p in range(inner_buf.shape[0]):
        inner_buf[p] = whole[p * rows : (p + 1) * rows]
    tok_out[:, 0:feat] = grad_q[0:own, :]
    tok_out[:, feat : 2 * feat] = grad_k[0:own]
    tok_out[:, 2 * feat : 3 * feat] = grad_v[0:own]
    outs[0][...] = inner_buf[place[2]].astype(BF)
    for d in range(1, group):
        out, at = outs[d], 0
        for tok in (grad_q, grad_k, grad_v):
            at = put(out, at, tok[d * own : (d + 1) * own, :])
        put(out, at, inner_buf[place[2] ^ d].astype(BF))
    for dist, out in zip(far_distances(group, tok_groups), outs[group:]):
        for i in range(2):
            out[i * padded(rows) : i * padded(rows) + rows, :] = inner_buf[place[2] ^ dist ^ i].astype(BF)


def relay_kernel(rows, *refs):
    out, step = refs[-1], padded(rows)
    for i, block in enumerate(refs[:-1]):
        out[i * step : i * step + rows, :] = block[step : step + rows, :]


def far_distances(group, tok_groups):
    return [e * group + d for e in range(1, tok_groups) for d in range(0, group, 2)]


def total_of(refs):
    total = refs[0][...].astype(F32)
    for block in refs[1:]:
        total += block[...].astype(F32)
    return total


def tokens_kernel(rate, tok, *refs):
    blocks, (gq, gk, gv) = refs[:-3], refs[-3:]
    _, own, feat = gq.shape
    sums = [tok[:, i * feat : (i + 1) * feat].astype(F32) for i in range(3)]
    for block in blocks:
        at = 0
        for i in range(3):
            more, at = get(block, at, own, feat)
            sums[i] += more.astype(F32)
    gq[0] = sums[0].astype(BF)
    gk[0] = sums[1].astype(BF)
    gv[0] = (rate[...] * sums[2]).astype(BF)


def weights_kernel(group, tok_groups, slab, at, place, relayed, inner, *refs):
    blocks, (*outs, buf) = refs[:-4], refs[-4:]
    _, rows, cols = buf.shape
    step = padded(rows)
    buf[0] = inner[...].astype(F32)
    for d in range(1, group):
        buf[d] = get(blocks[d - 1], at, rows, cols)[0].astype(F32)
    for i, dist in enumerate(far_distances(group, tok_groups)):
        d = dist % group
        buf[d] += blocks[group - 1 + i][0:rows, :].astype(F32)
        buf[d ^ 1] += relayed[i * step : i * step + rows, :].astype(F32)
    total = [buf[place[1] ^ j] for j in range(group)]
    for i in range(3):
        outs[i][0] = jnp.concatenate([t[:, i * slab : (i + 1) * slab] for t in total], axis=1)


def make_local(seq_n, head_n, group):
    tok_groups = seq_n // group

    def move(x, dist, axis="seq", size=seq_n):
        return lax.ppermute(x, axis, [(i, i ^ dist) for i in range(size)])

    def near_all(x):
        return [x] + [move(x, d) for d in range(1, group)]

    def mirror(x):
        return [move(x, e * group) for e in range(1, tok_groups)]

    def local(q, k, v, og, rates, gains, gi, ui, di, gs, us, ds):
        _, rows, hidden = gi.shape
        _, own, feat = q.shape
        slab = hidden // group
        near = group * own
        me = lax.axis_index("seq")
        place = jnp.stack((lax.div(me, group), lax.rem(me, group), me)).astype(jnp.int32)

        (packed,) = copying_call(
            functools.partial(weight_pack_kernel, group, slab),
            (arr((seq_n, rows, 6 * slab), BF),),
            (gs, us, ds, gi, ui, di),
            [pltpu.VMEM((6, rows, hidden), BF)],
        )
        packed, queries = lax.optimization_barrier((packed, q[0]))
        wall = lax.all_to_all(packed, "seq", 0, 0, tiled=True).reshape(seq_n * rows, 6 * slab)
        tokens, kv, gg, rate = call(
            token_pack_kernel,
            (arr((own, 3 * feat), BF), arr((own, 2 * feat), BF), arr((own, feat), F32), arr((own, feat), F32)),
            (q, k, v, og, rates, gains),
            8,
        )
        beside = move(tokens, 1) if group > 1 else None
        rest = range(2, group)
        q_near = [queries, beside][:group] + [move(queries, d) for d in rest]
        kv_near = [kv, beside][:group] + [move(kv, d) for d in rest]

        block = arr((own, feat), BF)
        mflop = 2 * near * feat * slab
        *parts, normed = call(
            functools.partial(forward_kernel, slab, group),
            (*(block,) * group, arr((seq_n * rows, 3 * slab), BF)),
            (wall, *q_near),
            24,
            flops=3 * mflop,
        )
        parts = [parts[0]] + [move(parts[d], d) for d in (*range(2, group), *range(1, min(2, group)))]
        *parts, kv_near = lax.optimization_barrier((*parts, kv_near))
        apply_out, sums = call(
            reduce_kernel, (arr((own, feat), F32), arr((2, own), F32)), (gg, *parts), 16
        )
        sums, queries = lax.optimization_barrier((sums, queries))
        sums = [sums] + [move(sums, d, "head", head_n) for d in range(1, head_n)]
        q_mirror = mirror(queries)
        (od,) = call(functools.partial(delta_kernel, head_n * feat), (block,), (apply_out, gg, *sums), 16)
        od_mirror = mirror(od)
        od_near = near_all(od)
        column = arr((3, seq_n * rows, slab), F32)
        factors, rises, *stats = call(
            functools.partial(key_kernel, slab, group),
            (arr((4, near, slab), F32), arr((3, near, slab), BF), arr((3, slab), F32), column, column),
            (wall, *kv_near),
            24,
            flops=12 * mflop,
        )
        pairs = [
            call(pair_kernel, (arr((own, 2 * feat), BF),), pair, 16)[0] for pair in zip(od_mirror, q_mirror)
        ]
        pairs = [x for m in pairs for x in near_all(m)]
        grad_q, grads = call(
            functools.partial(near_kernel, slab, group),
            (arr((near, feat), BF), arr((3, seq_n * rows, slab), F32)),
            (normed, *q_near, *od_near),
            24,
            flops=12 * mflop,
        )

        q_block = (own, feat)
        far = far_distances(group, tok_groups)
        tok, inner, *sends = call(
            functools.partial(backward_kernel, slab, group, tok_groups),
            (
                arr((own, 3 * feat), BF),
                arr((rows, 3 * slab), BF),
                *(message(*(q_block,) * 3, (rows, 3 * slab)),) * (group - 1),
                *(arr((2 * padded(rows), 3 * slab), BF),) * len(far),
            ),
            (place, wall, normed, grad_q, grads, factors, rises, *stats, *kv_near, *pairs),
            40,
            smem=1,
            flops=24 * mflop,
            scratch=[
                pltpu.VMEM((seq_n, rows, 3 * slab), F32),
                pltpu.VMEM((3, seq_n * rows, slab), F32),
            ],
        )
        near_got = {d: move(sends[d - 1], d) for d in (*range(2, group), *range(1, min(2, group)))}
        near_got = [near_got[d] for d in range(1, group)]
        far_got = [move(x, d) for x, d in zip(sends[group - 1 :], far)]
        (relayed,) = call(
            functools.partial(relay_kernel, rows),
            (arr((len(far) * padded(rows), 3 * slab), BF),),
            far_got,
            16,
        )
        relayed = move(relayed, 1)
        out_tok = arr((1, own, feat), BF)
        grad_w = arr((1, rows, hidden), F32)
        grads_t = call(tokens_kernel, (out_tok,) * 3, (rate, tok, *near_got), 16)
        at = 3 * tiles(feat) * padded(own)
        grads_w = call(
            functools.partial(weights_kernel, group, tok_groups, slab, at),
            (grad_w,) * 3,
            (place, relayed, inner, *near_got, *far_got),
            16,
            smem=1,
            scratch=[pltpu.VMEM((group, rows, 3 * slab), F32)],
        )
        return (*grads_t, *grads_w)

    return local


def solution(mesh):
    seq_n = mesh.shape["seq"]
    head_n = mesh.shape["head"]
    group = min(4, seq_n)
    tok = P("head", "seq", None)
    return jax.shard_map(
        make_local(seq_n, head_n, group),
        mesh=mesh,
        in_specs=(tok, tok, tok, tok, P("head", "seq"), P("head", None), tok, tok, tok, tok, tok, tok),
        out_specs=(tok, tok, tok, tok, tok, tok),
        check_vma=False,
    )
```

```python
import functools

import jax
import jax.numpy as jnp
from jax import lax
from jax.experimental import pallas as pl
from jax.experimental.pallas import tpu as pltpu
from jax.sharding import PartitionSpec as P

EPS_COL = 1e-06
EPS_ROOT = 1e-05
BF = jnp.bfloat16
F32 = jnp.float32
LANES = 128
VMEM = pl.BlockSpec(memory_space=pltpu.VMEM)
SMEM = pl.BlockSpec(memory_space=pltpu.SMEM)


def silu_parts(pre_act):
    sigmoid_val = jax.nn.sigmoid(pre_act)
    silu_val = pre_act * sigmoid_val
    silu_slope = sigmoid_val * (1.0 + pre_act * (1.0 - sigmoid_val))
    silu_bend = sigmoid_val * (1.0 - sigmoid_val) * (2.0 + pre_act * (1.0 - 2.0 * sigmoid_val))
    return (silu_val, silu_slope, silu_bend)


def mm(left_op, right_op):
    return jnp.dot(left_op, right_op, preferred_element_type=F32)


def mm_nt(left_op, right_op):
    return lax.dot_general(left_op, right_op, (((1,), (1,)), ((), ())), preferred_element_type=F32)


def mm_tn(left_op, right_op):
    return lax.dot_general(left_op, right_op, (((0,), (0,)), ((), ())), preferred_element_type=F32)


def column_norm(weight):
    return jnp.sqrt(jnp.sum(weight * weight, axis=0, keepdims=True) + EPS_COL)


def flat(x):
    return x.reshape(-1, x.shape[-1])


def call(kernel, outs, args, mib, smem=0, flops=0, scratch=()):
    moved = sum(x.size * x.dtype.itemsize for x in (*args, *outs))
    return pl.pallas_call(
        kernel,
        out_shape=outs,
        in_specs=[SMEM] * smem + [VMEM] * (len(args) - smem),
        out_specs=[VMEM] * len(outs),
        scratch_shapes=scratch,
        compiler_params=pltpu.CompilerParams(vmem_limit_bytes=mib << 20),
        cost_estimate=pl.CostEstimate(flops=flops, bytes_accessed=moved, transcendentals=0),
    )(*args)


def copying_call(kernel, outs, args, buffers):
    return pl.pallas_call(
        kernel,
        out_shape=outs,
        in_specs=[pl.BlockSpec(memory_space=pltpu.HBM)] * len(args),
        out_specs=[VMEM] * len(outs),
        scratch_shapes=[*buffers, pltpu.SemaphoreType.DMA((len(args),))],
        compiler_params=pltpu.CompilerParams(vmem_limit_bytes=56 << 20),
    )(*args)


def arr(shape, dtype):
    return jax.ShapeDtypeStruct(shape, dtype)


def fetch(sources, buffers, sems):
    copies = [pltpu.make_async_copy(s, b, sems.at[i]) for i, (s, b) in enumerate(zip(sources, buffers))]
    for copy in copies:
        copy.start()
    for copy in copies:
        copy.wait()


def padded(rows):
    return -(-rows // 16) * 16


def tiles(cols):
    return -(-cols // LANES)


def put(out, at, value):
    rows, cols = value.shape
    for t in range(tiles(cols)):
        wide = min(LANES, cols - t * LANES)
        out[at : at + rows, 0:wide] = value[:, t * LANES : t * LANES + wide]
        at += padded(rows)
    return at


def get(ref, at, rows, cols):
    parts = []
    for t in range(tiles(cols)):
        wide = min(LANES, cols - t * LANES)
        parts.append(ref[at : at + rows, 0:wide])
        at += padded(rows)
    return jnp.concatenate(parts, axis=1), at


def message(*blocks):
    return arr((sum(tiles(cols) * padded(rows) for rows, cols in blocks), LANES), BF)


def token_pack_kernel(q, k, v, og, rates, gains, all_out, kv_out, gg_out, rate_out):
    tokens, feat = gg_out.shape
    rate = jnp.broadcast_to(rates[...], (feat, tokens)).T
    values = (rate * v[0].astype(F32)).astype(BF)
    all_out[:, 0:feat] = q[0]
    all_out[:, feat : 2 * feat] = k[0]
    all_out[:, 2 * feat : 3 * feat] = values
    kv_out[:, 0:feat] = k[0]
    kv_out[:, feat : 2 * feat] = values
    gg_out[...] = gains[...] * og[0].astype(F32)
    rate_out[...] = rate


def weight_pack_kernel(group, slab, *refs):
    args, (w_out, buf, sems) = refs[:6], refs[6:]
    fetch(args, [buf.at[pl.ds(i, 1)] for i in range(6)], sems)
    for j in range(group):
        cols = pl.ds(j * slab, slab)
        block = jnp.concatenate([buf[i, :, cols] for i in range(6)], axis=1)
        for p in range(j, w_out.shape[0], group):
            w_out[p] = block


def columns(w, slab):
    parts = [w[:, pl.ds(i * slab, slab)].astype(F32) for i in range(6)]
    saved, init = parts[:3], parts[3:]
    return saved, init, [column_norm(x) for x in init], [column_norm(x) for x in saved]


def stack(refs, cols=slice(None)):
    return jnp.concatenate([r[:, cols] for r in refs], axis=0)


def thirds(x, slab):
    return [x[:, pl.ds(i * slab, slab)] for i in range(3)]


def forward_kernel(slab, group, w, *refs):
    queries, parts, normed_out = refs[:group], refs[group:-1], refs[-1]
    own, feat = parts[0].shape
    saved, init, norm_init, norm_saved = columns(w, slab)
    normed = [(saved[i] * (norm_init[i] / norm_saved[i])).astype(BF) for i in range(3)]
    rows = stack(queries, slice(0, feat))
    hidden = (silu_parts(mm(rows, normed[0]))[0] * mm(rows, normed[1])).astype(BF)
    out = mm_nt(hidden, normed[2]).astype(BF)
    for d in range(group):
        parts[d][...] = out[d * own : (d + 1) * own]
    normed_out[...] = jnp.concatenate(normed, axis=1)


def reduce_kernel(gg, *refs):
    parts, (apply_out, sums) = refs[:-2], refs[-2:]
    total = total_of(parts)
    apply_out[...] = total
    sums[0:1, :] = jnp.sum((total * total).T, axis=0, keepdims=True)
    sums[1:2, :] = jnp.sum((total * gg[...]).T, axis=0, keepdims=True)


def delta_kernel(width, apply_out, gg, *refs):
    sums, out = refs[:-1], refs[-1]
    tokens, feat = apply_out.shape
    total = sums[0][...]
    for more in sums[1:]:
        total += more[...]
    square = jnp.broadcast_to(total[0:1, :], (feat, tokens)).T
    gain = jnp.broadcast_to(total[1:2, :], (feat, tokens)).T
    root = jnp.sqrt(square / width + EPS_ROOT)
    out[...] = (gg[...] / root - apply_out[...] * (gain / width) / (root * root * root)).astype(BF)


def pair_kernel(left, right, out):
    feat = left.shape[1]
    out[:, 0:feat] = left[...]
    out[:, feat : 2 * feat] = right[...]


def query_side(rows, delta, normed):
    q_gate = mm(rows, normed[0])
    q_up = mm(rows, normed[1])
    act, slope, _ = silu_parts(q_gate)
    hidden = (act * q_up).astype(BF)
    delta_hidden = mm(delta, normed[2])
    delta_gate = (delta_hidden * q_up * slope).astype(BF)
    delta_up = (delta_hidden * act).astype(BF)
    grads = (mm_tn(rows, delta_gate), mm_tn(rows, delta_up), mm_tn(delta, hidden))
    return delta_gate, delta_up, grads


def near_kernel(slab, group, place, normed_ref, *refs):
    q_near, od_near, (grad_q, grads_out) = refs[:group], refs[group : 2 * group], refs[2 * group :]
    own = od_near[0].shape[0]
    normed = thirds(normed_ref, slab)
    delta_gate, delta_up, grads = query_side(stack(q_near, slice(0, od_near[0].shape[1])), stack(od_near), normed)
    found = (mm_nt(delta_gate, normed[0]) + mm_nt(delta_up, normed[1])).astype(BF)
    for d in range(group):
        grad_q[place[1] ^ d] = found[d * own : (d + 1) * own]
    for i in range(3):
        grads_out[i] = grads[i]


def key_kernel(slab, group, w, *refs):
    kvs, (factors, rises, ratio, minus, plus) = refs[:group], refs[group:]
    feat = w.shape[0]
    saved, start, norm_init, norm_saved = columns(w, slab)
    for i in range(3):
        ratio[i : i + 1, :] = norm_init[i] / norm_saved[i]
        minus[i] = saved[i] * (norm_init[i] / (norm_saved[i] * norm_saved[i] * norm_saved[i]))
        plus[i] = start[i] / (norm_init[i] * norm_saved[i])
    init = [w[:, pl.ds((3 + i) * slab, slab)] for i in range(3)]
    keys = stack(kvs, slice(-2 * feat, -feat))
    values = stack(kvs, slice(-feat, None))
    k_gate = mm(keys, init[0])
    k_up = mm(keys, init[1])
    k_proj = mm(values, init[2])
    k_act, k_slope, k_bend = silu_parts(k_gate)
    rises[0] = (k_act * k_up).astype(BF)
    rises[1] = (k_proj * k_up * k_slope).astype(BF)
    rises[2] = (k_proj * k_act).astype(BF)
    factors[0] = k_act
    factors[1] = k_up * k_slope
    factors[2] = k_proj * k_slope
    factors[3] = k_proj * k_up * k_bend


def backward_kernel(
    slab, group, tok_groups, place, w, normed_ref, grads, factors, rises, ratio, minus, plus, *refs
):
    far = group * (tok_groups - 1)
    kvs, pairs, outs, (inner_buf, sums) = refs[:group], refs[group : group + far], refs[group + far : -2], refs[-2:]
    feat = w.shape[0]
    tok_out, outs = outs[0], outs[1:]
    own = tok_out.shape[0]
    normed = thirds(normed_ref, slab)
    total = [grads[i] for i in range(3)]
    for e in range(tok_groups - 1):
        these = pairs[e * group : (e + 1) * group]
        more = query_side(stack(these, slice(feat, 2 * feat)), stack(these, slice(0, feat)), normed)[2]
        total = [total[i] + more[i] for i in range(3)]
        if tok_groups > 2:
            for i in range(3):
                sums[i] = total[i]
            total = [sums[i] for i in range(3)]

    cots, direct = [], []
    once = jnp.where(place[0] == 0, 1.0, 0.0)
    for i in range(3):
        saved = w[:, pl.ds(i * slab, slab)].astype(F32)
        col_dot = jnp.sum(saved * total[i], axis=0, keepdims=True)
        cot = total[i] * ratio[i : i + 1, :] - minus[i] * col_dot
        cots.append(cot.astype(BF))
        direct.append((cot + plus[i] * col_dot) * once)

    init_bf = [w[:, pl.ds((3 + i) * slab, slab)] for i in range(3)]
    keys = stack(kvs, slice(-2 * feat, -feat))
    values = stack(kvs, slice(-feat, None))
    back_gate = mm(keys, cots[0])
    back_up = mm(keys, cots[1])
    back_hidden = mm(values, cots[2])
    back_proj = (back_gate * factors[1] + back_up * factors[0]).astype(BF)
    back_kup = (back_gate * factors[2] + back_hidden * factors[0]).astype(BF)
    back_kgate = (back_gate * factors[3] + (back_up * factors[2] + back_hidden * factors[1])).astype(BF)
    grad_k = (
        mm_nt(rises[1], cots[0])
        + mm_nt(rises[2], cots[1])
        + mm_nt(back_kgate, init_bf[0])
        + mm_nt(back_kup, init_bf[1])
    ).astype(BF)
    grad_v = (mm_nt(rises[0], cots[2]) + mm_nt(back_proj, init_bf[2])).astype(BF)
    inner = (mm_tn(keys, back_kgate), mm_tn(keys, back_kup), mm_tn(values, back_proj))
    whole = jnp.concatenate([inner[i] + direct[i] for i in range(3)], axis=1)
    rows = inner_buf.shape[1]
    for p in range(inner_buf.shape[0]):
        inner_buf[p] = whole[p * rows : (p + 1) * rows]
    tok_out[:, 0:feat] = grad_k[0:own]
    tok_out[:, feat : 2 * feat] = grad_v[0:own]
    outs[0][...] = inner_buf[place[2]].astype(BF)
    for d in range(1, group):
        out, at = outs[d], 0
        for tok in (grad_k, grad_v):
            at = put(out, at, tok[d * own : (d + 1) * own, :])
        put(out, at, inner_buf[place[2] ^ d].astype(BF))
    for dist in range(group, inner_buf.shape[0]):
        outs[dist][...] = inner_buf[place[2] ^ dist].astype(BF)


def total_of(refs):
    total = refs[0][...].astype(F32)
    for block in refs[1:]:
        total += block[...].astype(F32)
    return total


def tokens_kernel(rate, queries, tok, *refs):
    blocks, (gq, gk, gv) = refs[:-3], refs[-3:]
    _, own, feat = gq.shape
    total = queries[0].astype(F32)
    for j in range(1, queries.shape[0]):
        total += queries[j].astype(F32)
    gq[0] = total.astype(BF)
    sums = [tok[:, i * feat : (i + 1) * feat].astype(F32) for i in range(2)]
    for block in blocks:
        at = 0
        for i in range(2):
            more, at = get(block, at, own, feat)
            sums[i] += more.astype(F32)
    gk[0] = sums[0].astype(BF)
    gv[0] = (rate[...] * sums[1]).astype(BF)


def weights_kernel(group, slab, at, place, inner, *refs):
    blocks, (*outs, buf) = refs[:-4], refs[-4:]
    _, rows, cols = buf.shape
    for d in range(group):
        total = (get(blocks[d - 1], at, rows, cols)[0] if d else inner[...]).astype(F32)
        for far in blocks[group - 1 + d :: group]:
            total += far[...].astype(F32)
        buf[d] = total
    total = [buf[place[1] ^ j] for j in range(group)]
    for i in range(3):
        outs[i][0] = jnp.concatenate([t[:, i * slab : (i + 1) * slab] for t in total], axis=1)


def make_local(seq_n, head_n, group):
    tok_groups = seq_n // group
    groups = [[t * group + j for j in range(group)] for t in range(tok_groups)]

    def move(x, dist, axis="seq", size=seq_n):
        return lax.ppermute(x, axis, [(i, i ^ dist) for i in range(size)])

    def near_all(x):
        return [x] + [move(x, d) for d in range(1, group)]

    def mirror(x):
        return [move(x, e * group) for e in range(1, tok_groups)]

    def local(q, k, v, og, rates, gains, gi, ui, di, gs, us, ds):
        _, rows, hidden = gi.shape
        _, own, feat = q.shape
        slab = hidden // group
        near = group * own
        me = lax.axis_index("seq")
        place = jnp.stack((lax.div(me, group), lax.rem(me, group), me)).astype(jnp.int32)

        (packed,) = copying_call(
            functools.partial(weight_pack_kernel, group, slab),
            (arr((seq_n, rows, 6 * slab), BF),),
            (gs, us, ds, gi, ui, di),
            [pltpu.VMEM((6, rows, hidden), BF)],
        )
        packed, queries = lax.optimization_barrier((packed, q[0]))
        wall = lax.all_to_all(packed, "seq", 0, 0, tiled=True).reshape(seq_n * rows, 6 * slab)
        tokens, kv, gg, rate = call(
            token_pack_kernel,
            (arr((own, 3 * feat), BF), arr((own, 2 * feat), BF), arr((own, feat), F32), arr((own, feat), F32)),
            (q, k, v, og, rates, gains),
            8,
        )
        beside = move(tokens, 1) if group > 1 else None
        rest = range(2, group)
        q_near = [queries, beside][:group] + [move(queries, d) for d in rest]
        kv_near = [kv, beside][:group] + [move(kv, d) for d in rest]

        block = arr((own, feat), BF)
        mflop = 2 * near * feat * slab
        *parts, normed = call(
            functools.partial(forward_kernel, slab, group),
            (*(block,) * group, arr((seq_n * rows, 3 * slab), BF)),
            (wall, *q_near),
            24,
            flops=3 * mflop,
        )
        parts = [parts[0]] + [move(parts[d], d) for d in (*range(2, group), *range(1, min(2, group)))]
        *parts, kv_near = lax.optimization_barrier((*parts, kv_near))
        apply_out, sums = call(
            reduce_kernel, (arr((own, feat), F32), arr((2, own), F32)), (gg, *parts), 16
        )
        sums, queries = lax.optimization_barrier((sums, queries))
        sums = [sums] + [move(sums, d, "head", head_n) for d in range(1, head_n)]
        q_mirror = mirror(queries)
        (od,) = call(functools.partial(delta_kernel, head_n * feat), (block,), (apply_out, gg, *sums), 16)
        od_mirror = mirror(od)
        od_near = near_all(od)
        column = arr((3, seq_n * rows, slab), F32)
        factors, rises, *stats = call(
            functools.partial(key_kernel, slab, group),
            (arr((4, near, slab), F32), arr((3, near, slab), BF), arr((3, slab), F32), column, column),
            (wall, *kv_near),
            24,
            flops=12 * mflop,
        )
        pairs = [
            call(pair_kernel, (arr((own, 2 * feat), BF),), pair, 16)[0] for pair in zip(od_mirror, q_mirror)
        ]
        pairs = [x for m in pairs for x in near_all(m)]
        grad_q, grads = call(
            functools.partial(near_kernel, slab, group),
            (arr((group, own, feat), BF), arr((3, seq_n * rows, slab), F32)),
            (place, normed, *q_near, *od_near),
            24,
            smem=1,
            flops=12 * mflop,
        )

        q_block = (own, feat)
        grad_q = lax.all_to_all(grad_q, "seq", 0, 0, axis_index_groups=groups, tiled=True)
        tok, inner, *sends = call(
            functools.partial(backward_kernel, slab, group, tok_groups),
            (
                arr((own, 2 * feat), BF),
                arr((rows, 3 * slab), BF),
                *(message(*(q_block,) * 2, (rows, 3 * slab)),) * (group - 1),
                *(arr((rows, 3 * slab), BF),) * (seq_n - group),
            ),
            (place, wall, normed, grads, factors, rises, *stats, *kv_near, *pairs),
            40,
            smem=1,
            flops=24 * mflop,
            scratch=[
                pltpu.VMEM((seq_n, rows, 3 * slab), F32),
                pltpu.VMEM((3, seq_n * rows, slab), F32),
            ],
        )
        sends, grad_q = lax.optimization_barrier((sends, grad_q))
        near_got = {d: move(sends[d - 1], d) for d in (*range(2, group), *range(1, min(2, group)))}
        near_got = [near_got[d] for d in range(1, group)]
        far_got = [move(sends[d - 1], d) for d in range(group, seq_n)]
        out_tok = arr((1, own, feat), BF)
        grad_w = arr((1, rows, hidden), F32)
        grads_t = call(tokens_kernel, (out_tok,) * 3, (rate, grad_q, tok, *near_got), 16)
        at = 2 * tiles(feat) * padded(own)
        grads_w = call(
            functools.partial(weights_kernel, group, slab, at),
            (grad_w,) * 3,
            (place, inner, *near_got, *far_got),
            16,
            smem=1,
            scratch=[pltpu.VMEM((group, rows, 3 * slab), F32)],
        )
        return (*grads_t, *grads_w)

    return local


def solution(mesh):
    seq_n = mesh.shape["seq"]
    head_n = mesh.shape["head"]
    group = min(4, seq_n)
    tok = P("head", "seq", None)
    return jax.shard_map(
        make_local(seq_n, head_n, group),
        mesh=mesh,
        in_specs=(tok, tok, tok, tok, P("head", "seq"), P("head", None), tok, tok, tok, tok, tok, tok),
        out_specs=(tok, tok, tok, tok, tok, tok),
        check_vma=False,
    )
```

```python
import functools

import jax
import jax.numpy as jnp
from jax import lax
from jax.experimental import pallas as pl
from jax.experimental.pallas import tpu as pltpu
from jax.sharding import PartitionSpec as P

EPS_COL = 1e-06
EPS_ROOT = 1e-05
BF = jnp.bfloat16
F32 = jnp.float32
LANES = 128
VMEM = pl.BlockSpec(memory_space=pltpu.VMEM)
SMEM = pl.BlockSpec(memory_space=pltpu.SMEM)


def silu_parts(pre_act):
    sigmoid_val = jax.nn.sigmoid(pre_act)
    silu_val = pre_act * sigmoid_val
    silu_slope = sigmoid_val * (1.0 + pre_act * (1.0 - sigmoid_val))
    silu_bend = sigmoid_val * (1.0 - sigmoid_val) * (2.0 + pre_act * (1.0 - 2.0 * sigmoid_val))
    return (silu_val, silu_slope, silu_bend)


def mm(left_op, right_op):
    return jnp.dot(left_op, right_op, preferred_element_type=F32)


def mm_nt(left_op, right_op):
    return lax.dot_general(left_op, right_op, (((1,), (1,)), ((), ())), preferred_element_type=F32)


def mm_tn(left_op, right_op):
    return lax.dot_general(left_op, right_op, (((0,), (0,)), ((), ())), preferred_element_type=F32)


def column_norm(weight):
    return jnp.sqrt(jnp.sum(weight * weight, axis=0, keepdims=True) + EPS_COL)


def flat(x):
    return x.reshape(-1, x.shape[-1])


def call(kernel, outs, args, mib, smem=0, flops=0, scratch=()):
    moved = sum(x.size * x.dtype.itemsize for x in (*args, *outs))
    return pl.pallas_call(
        kernel,
        out_shape=outs,
        in_specs=[SMEM] * smem + [VMEM] * (len(args) - smem),
        out_specs=[VMEM] * len(outs),
        scratch_shapes=scratch,
        compiler_params=pltpu.CompilerParams(vmem_limit_bytes=mib << 20),
        cost_estimate=pl.CostEstimate(flops=flops, bytes_accessed=moved, transcendentals=0),
    )(*args)


def copying_call(kernel, outs, args, buffers):
    return pl.pallas_call(
        kernel,
        out_shape=outs,
        in_specs=[pl.BlockSpec(memory_space=pltpu.HBM)] * len(args),
        out_specs=[VMEM] * len(outs),
        scratch_shapes=[*buffers, pltpu.SemaphoreType.DMA((len(args),))],
        compiler_params=pltpu.CompilerParams(vmem_limit_bytes=56 << 20),
    )(*args)


def arr(shape, dtype):
    return jax.ShapeDtypeStruct(shape, dtype)


def fetch(sources, buffers, sems):
    copies = [pltpu.make_async_copy(s, b, sems.at[i]) for i, (s, b) in enumerate(zip(sources, buffers))]
    for copy in copies:
        copy.start()
    for copy in copies:
        copy.wait()


def padded(rows):
    return -(-rows // 16) * 16


def tiles(cols):
    return -(-cols // LANES)


def put(out, at, value):
    rows, cols = value.shape
    for t in range(tiles(cols)):
        wide = min(LANES, cols - t * LANES)
        out[at : at + rows, 0:wide] = value[:, t * LANES : t * LANES + wide]
        at += padded(rows)
    return at


def get(ref, at, rows, cols):
    parts = []
    for t in range(tiles(cols)):
        wide = min(LANES, cols - t * LANES)
        parts.append(ref[at : at + rows, 0:wide])
        at += padded(rows)
    return jnp.concatenate(parts, axis=1), at


def message(*blocks):
    return arr((sum(tiles(cols) * padded(rows) for rows, cols in blocks), LANES), BF)


def token_pack_kernel(q, k, v, og, rates, gains, all_out, kv_out, gg_out, rate_out):
    tokens, feat = gg_out.shape
    rate = jnp.broadcast_to(rates[...], (feat, tokens)).T
    values = (rate * v[0].astype(F32)).astype(BF)
    all_out[:, 0:feat] = q[0]
    all_out[:, feat : 2 * feat] = k[0]
    all_out[:, 2 * feat : 3 * feat] = values
    kv_out[:, 0:feat] = k[0]
    kv_out[:, feat : 2 * feat] = values
    gg_out[...] = gains[...] * og[0].astype(F32)
    rate_out[...] = rate


def weight_pack_kernel(group, slab, *refs):
    args, (w_out, buf, sems) = refs[:6], refs[6:]
    fetch(args, [buf.at[pl.ds(i, 1)] for i in range(6)], sems)
    for j in range(group):
        cols = pl.ds(j * slab, slab)
        block = jnp.concatenate([buf[i, :, cols] for i in range(6)], axis=1)
        for p in range(j, w_out.shape[0], group):
            w_out[p] = block


def columns(w, slab):
    parts = [w[:, pl.ds(i * slab, slab)].astype(F32) for i in range(6)]
    saved, init = parts[:3], parts[3:]
    return saved, init, [column_norm(x) for x in init], [column_norm(x) for x in saved]


def stack(refs, cols=slice(None)):
    return jnp.concatenate([r[:, cols] for r in refs], axis=0)


def thirds(x, slab):
    return [x[:, pl.ds(i * slab, slab)] for i in range(3)]


def forward_kernel(slab, group, w, *refs):
    queries, parts, normed_out = refs[:group], refs[group:-1], refs[-1]
    own, feat = parts[0].shape
    saved, init, norm_init, norm_saved = columns(w, slab)
    normed = [(saved[i] * (norm_init[i] / norm_saved[i])).astype(BF) for i in range(3)]
    rows = stack(queries, slice(0, feat))
    hidden = (silu_parts(mm(rows, normed[0]))[0] * mm(rows, normed[1])).astype(BF)
    out = mm_nt(hidden, normed[2]).astype(BF)
    for d in range(group):
        parts[d][...] = out[d * own : (d + 1) * own]
    normed_out[...] = jnp.concatenate(normed, axis=1)


def reduce_kernel(gg, *refs):
    parts, (apply_out, sums) = refs[:-2], refs[-2:]
    total = total_of(parts)
    apply_out[...] = total
    sums[0:1, :] = jnp.sum((total * total).T, axis=0, keepdims=True)
    sums[1:2, :] = jnp.sum((total * gg[...]).T, axis=0, keepdims=True)


def delta_kernel(width, apply_out, gg, *refs):
    sums, out = refs[:-1], refs[-1]
    tokens, feat = apply_out.shape
    total = sums[0][...]
    for more in sums[1:]:
        total += more[...]
    square = jnp.broadcast_to(total[0:1, :], (feat, tokens)).T
    gain = jnp.broadcast_to(total[1:2, :], (feat, tokens)).T
    root = jnp.sqrt(square / width + EPS_ROOT)
    out[...] = (gg[...] / root - apply_out[...] * (gain / width) / (root * root * root)).astype(BF)


def pair_kernel(left, right, out):
    feat = left.shape[1]
    out[:, 0:feat] = left[...]
    out[:, feat : 2 * feat] = right[...]


def query_side(rows, delta, normed):
    q_gate = mm(rows, normed[0])
    q_up = mm(rows, normed[1])
    act, slope, _ = silu_parts(q_gate)
    hidden = (act * q_up).astype(BF)
    delta_hidden = mm(delta, normed[2])
    delta_gate = (delta_hidden * q_up * slope).astype(BF)
    delta_up = (delta_hidden * act).astype(BF)
    grads = (mm_tn(rows, delta_gate), mm_tn(rows, delta_up), mm_tn(delta, hidden))
    return delta_gate, delta_up, grads


def near_kernel(slab, group, place, normed_ref, *refs):
    q_near, od_near, (grad_q, grads_out) = refs[:group], refs[group : 2 * group], refs[2 * group :]
    own = od_near[0].shape[0]
    normed = thirds(normed_ref, slab)
    delta_gate, delta_up, grads = query_side(stack(q_near, slice(0, od_near[0].shape[1])), stack(od_near), normed)
    found = (mm_nt(delta_gate, normed[0]) + mm_nt(delta_up, normed[1])).astype(BF)
    for d in range(group):
        grad_q[place[1] ^ d] = found[d * own : (d + 1) * own]
    for i in range(3):
        grads_out[i] = grads[i]


def key_kernel(slab, group, w, *refs):
    kvs, (factors, rises, ratio, minus, plus) = refs[:group], refs[group:]
    feat = w.shape[0]
    saved, start, norm_init, norm_saved = columns(w, slab)
    for i in range(3):
        ratio[i : i + 1, :] = norm_init[i] / norm_saved[i]
        minus[i] = saved[i] * (norm_init[i] / (norm_saved[i] * norm_saved[i] * norm_saved[i]))
        plus[i] = start[i] / (norm_init[i] * norm_saved[i])
    init = [w[:, pl.ds((3 + i) * slab, slab)] for i in range(3)]
    keys = stack(kvs, slice(-2 * feat, -feat))
    values = stack(kvs, slice(-feat, None))
    k_gate = mm(keys, init[0])
    k_up = mm(keys, init[1])
    k_proj = mm(values, init[2])
    k_act, k_slope, k_bend = silu_parts(k_gate)
    rises[0] = (k_act * k_up).astype(BF)
    rises[1] = (k_proj * k_up * k_slope).astype(BF)
    rises[2] = (k_proj * k_act).astype(BF)
    factors[0] = k_act
    factors[1] = k_up * k_slope
    factors[2] = k_proj * k_slope
    factors[3] = k_proj * k_up * k_bend


def backward_kernel(
    slab, group, tok_groups, place, w, normed_ref, grads, factors, rises, ratio, minus, plus, *refs
):
    far = group * (tok_groups - 1)
    kvs, pairs, outs, (inner_buf, sums) = refs[:group], refs[group : group + far], refs[group + far : -2], refs[-2:]
    feat = w.shape[0]
    tok_out, outs = outs[0], outs[1:]
    own = tok_out.shape[0]
    normed = thirds(normed_ref, slab)
    total = [grads[i] for i in range(3)]
    for e in range(tok_groups - 1):
        these = pairs[e * group : (e + 1) * group]
        more = query_side(stack(these, slice(feat, 2 * feat)), stack(these, slice(0, feat)), normed)[2]
        total = [total[i] + more[i] for i in range(3)]
        if tok_groups > 2:
            for i in range(3):
                sums[i] = total[i]
            total = [sums[i] for i in range(3)]

    cots, direct = [], []
    once = jnp.where(place[0] == 0, 1.0, 0.0)
    for i in range(3):
        saved = w[:, pl.ds(i * slab, slab)].astype(F32)
        col_dot = jnp.sum(saved * total[i], axis=0, keepdims=True)
        cot = total[i] * ratio[i : i + 1, :] - minus[i] * col_dot
        cots.append(cot.astype(BF))
        direct.append((cot + plus[i] * col_dot) * once)

    init_bf = [w[:, pl.ds((3 + i) * slab, slab)] for i in range(3)]
    keys = stack(kvs, slice(-2 * feat, -feat))
    values = stack(kvs, slice(-feat, None))
    back_gate = mm(keys, cots[0])
    back_up = mm(keys, cots[1])
    back_hidden = mm(values, cots[2])
    back_proj = (back_gate * factors[1] + back_up * factors[0]).astype(BF)
    back_kup = (back_gate * factors[2] + back_hidden * factors[0]).astype(BF)
    back_kgate = (back_gate * factors[3] + (back_up * factors[2] + back_hidden * factors[1])).astype(BF)
    grad_k = (
        mm_nt(rises[1], cots[0])
        + mm_nt(rises[2], cots[1])
        + mm_nt(back_kgate, init_bf[0])
        + mm_nt(back_kup, init_bf[1])
    ).astype(BF)
    grad_v = (mm_nt(rises[0], cots[2]) + mm_nt(back_proj, init_bf[2])).astype(BF)
    inner = (mm_tn(keys, back_kgate), mm_tn(keys, back_kup), mm_tn(values, back_proj))
    whole = jnp.concatenate([inner[i] + direct[i] for i in range(3)], axis=1)
    rows = inner_buf.shape[1]
    for p in range(inner_buf.shape[0]):
        inner_buf[p] = whole[p * rows : (p + 1) * rows]
    tok_out[:, 0:feat] = grad_k[0:own]
    tok_out[:, feat : 2 * feat] = grad_v[0:own]
    outs[0][...] = inner_buf[place[2]].astype(BF)
    for d in range(1, group):
        out, at = outs[d], 0
        for tok in (grad_k, grad_v):
            at = put(out, at, tok[d * own : (d + 1) * own, :])
        put(out, at, inner_buf[place[2] ^ d].astype(BF))
    for dist in range(group, inner_buf.shape[0]):
        outs[dist][...] = inner_buf[place[2] ^ dist].astype(BF)


def total_of(refs):
    total = refs[0][...].astype(F32)
    for block in refs[1:]:
        total += block[...].astype(F32)
    return total


def tokens_kernel(rate, queries, tok, *refs):
    blocks, (gq, gk, gv) = refs[:-3], refs[-3:]
    _, own, feat = gq.shape
    total = queries[0].astype(F32)
    for j in range(1, queries.shape[0]):
        total += queries[j].astype(F32)
    gq[0] = total.astype(BF)
    sums = [tok[:, i * feat : (i + 1) * feat].astype(F32) for i in range(2)]
    for block in blocks:
        at = 0
        for i in range(2):
            more, at = get(block, at, own, feat)
            sums[i] += more.astype(F32)
    gk[0] = sums[0].astype(BF)
    gv[0] = (rate[...] * sums[1]).astype(BF)


def weights_kernel(group, slab, at, place, inner, *refs):
    blocks, (*outs, buf) = refs[:-4], refs[-4:]
    _, rows, cols = buf.shape
    for d in range(group):
        total = (get(blocks[d - 1], at, rows, cols)[0] if d else inner[...]).astype(F32)
        for far in blocks[group - 1 + d :: group]:
            total += far[...].astype(F32)
        buf[d] = total
    total = [buf[place[1] ^ j] for j in range(group)]
    for i in range(3):
        outs[i][0] = jnp.concatenate([t[:, i * slab : (i + 1) * slab] for t in total], axis=1)


def make_local(seq_n, head_n, group):
    tok_groups = seq_n // group
    groups = [[t * group + j for j in range(group)] for t in range(tok_groups)]

    def move(x, dist, axis="seq", size=seq_n):
        return lax.ppermute(x, axis, [(i, i ^ dist) for i in range(size)])

    def near_all(x):
        return [x] + [move(x, d) for d in range(1, group)]

    def mirror(x):
        return [move(x, e * group) for e in range(1, tok_groups)]

    def local(q, k, v, og, rates, gains, gi, ui, di, gs, us, ds):
        _, rows, hidden = gi.shape
        _, own, feat = q.shape
        slab = hidden // group
        near = group * own
        me = lax.axis_index("seq")
        place = jnp.stack((lax.div(me, group), lax.rem(me, group), me)).astype(jnp.int32)

        (packed,) = copying_call(
            functools.partial(weight_pack_kernel, group, slab),
            (arr((seq_n, rows, 6 * slab), BF),),
            (gs, us, ds, gi, ui, di),
            [pltpu.VMEM((6, rows, hidden), BF)],
        )
        packed, queries = lax.optimization_barrier((packed, q[0]))
        wall = lax.all_to_all(packed, "seq", 0, 0, tiled=True).reshape(seq_n * rows, 6 * slab)
        tokens, kv, gg, rate = call(
            token_pack_kernel,
            (arr((own, 3 * feat), BF), arr((own, 2 * feat), BF), arr((own, feat), F32), arr((own, feat), F32)),
            (q, k, v, og, rates, gains),
            8,
        )
        beside = move(tokens, 1) if group > 1 else None
        rest = range(2, group)
        q_near = [queries, beside][:group] + [move(queries, d) for d in rest]
        kv_near = [kv, beside][:group] + [move(kv, d) for d in rest]

        block = arr((own, feat), BF)
        mflop = 2 * near * feat * slab
        *parts, normed = call(
            functools.partial(forward_kernel, slab, group),
            (*(block,) * group, arr((seq_n * rows, 3 * slab), BF)),
            (wall, *q_near),
            24,
            flops=3 * mflop,
        )
        parts = [parts[0]] + [move(parts[d], d) for d in (*range(2, group), *range(1, min(2, group)))]
        *parts, kv_near = lax.optimization_barrier((*parts, kv_near))
        apply_out, sums = call(
            reduce_kernel, (arr((own, feat), F32), arr((2, own), F32)), (gg, *parts), 16
        )
        sums, queries = lax.optimization_barrier((sums, queries))
        sums = [sums] + [move(sums, d, "head", head_n) for d in range(1, head_n)]
        q_mirror = mirror(queries)
        (od,) = call(functools.partial(delta_kernel, head_n * feat), (block,), (apply_out, gg, *sums), 16)
        od_mirror = mirror(od)
        od_near = near_all(od)
        column = arr((3, seq_n * rows, slab), F32)
        factors, rises, *stats = call(
            functools.partial(key_kernel, slab, group),
            (arr((4, near, slab), F32), arr((3, near, slab), BF), arr((3, slab), F32), column, column),
            (wall, *kv_near),
            24,
            flops=12 * mflop,
        )
        *od_mirror, stats[0] = lax.optimization_barrier((*od_mirror, stats[0]))
        pairs = [
            call(pair_kernel, (arr((own, 2 * feat), BF),), pair, 16)[0] for pair in zip(od_mirror, q_mirror)
        ]
        pairs = [x for m in pairs for x in near_all(m)]
        grad_q, grads = call(
            functools.partial(near_kernel, slab, group),
            (arr((group, own, feat), BF), arr((3, seq_n * rows, slab), F32)),
            (place, normed, *q_near, *od_near),
            24,
            smem=1,
            flops=300 * mflop,
        )

        q_block = (own, feat)
        grad_q = lax.all_to_all(grad_q, "seq", 0, 0, axis_index_groups=groups, tiled=True)
        tok, inner, *sends = call(
            functools.partial(backward_kernel, slab, group, tok_groups),
            (
                arr((own, 2 * feat), BF),
                arr((rows, 3 * slab), BF),
                *(message(*(q_block,) * 2, (rows, 3 * slab)),) * (group - 1),
                *(arr((rows, 3 * slab), BF),) * (seq_n - group),
            ),
            (place, wall, normed, grads, factors, rises, *stats, *kv_near, *pairs),
            40,
            smem=1,
            flops=600 * mflop,
            scratch=[
                pltpu.VMEM((seq_n, rows, 3 * slab), F32),
                pltpu.VMEM((3, seq_n * rows, slab), F32),
            ],
        )
        sends, grad_q = lax.optimization_barrier((sends, grad_q))
        near_got = {d: move(sends[d - 1], d) for d in (*range(2, group), *range(1, min(2, group)))}
        near_got = [near_got[d] for d in range(1, group)]
        far_got = [move(sends[d - 1], d) for d in range(group, seq_n)]
        out_tok = arr((1, own, feat), BF)
        grad_w = arr((1, rows, hidden), F32)
        grads_t = call(tokens_kernel, (out_tok,) * 3, (rate, grad_q, tok, *near_got), 16)
        at = 2 * tiles(feat) * padded(own)
        grads_w = call(
            functools.partial(weights_kernel, group, slab, at),
            (grad_w,) * 3,
            (place, inner, *near_got, *far_got),
            16,
            smem=1,
            scratch=[pltpu.VMEM((group, rows, 3 * slab), F32)],
        )
        return (*grads_t, *grads_w)

    return local


def solution(mesh):
    seq_n = mesh.shape["seq"]
    head_n = mesh.shape["head"]
    group = min(4, seq_n)
    tok = P("head", "seq", None)
    return jax.shard_map(
        make_local(seq_n, head_n, group),
        mesh=mesh,
        in_specs=(tok, tok, tok, tok, P("head", "seq"), P("head", None), tok, tok, tok, tok, tok, tok),
        out_specs=(tok, tok, tok, tok, tok, tok),
        check_vma=False,
    )
```

```python
import functools

import jax
import jax.numpy as jnp
from jax import lax
from jax.experimental import pallas as pl
from jax.experimental.pallas import tpu as pltpu
from jax.sharding import PartitionSpec as P

EPS_COL = 1e-06
EPS_ROOT = 1e-05
BF = jnp.bfloat16
F32 = jnp.float32
LANES = 128
VMEM = pl.BlockSpec(memory_space=pltpu.VMEM)
SMEM = pl.BlockSpec(memory_space=pltpu.SMEM)


def silu_parts(pre_act):
    sigmoid_val = jax.nn.sigmoid(pre_act)
    silu_val = pre_act * sigmoid_val
    silu_slope = sigmoid_val * (1.0 + pre_act * (1.0 - sigmoid_val))
    silu_bend = sigmoid_val * (1.0 - sigmoid_val) * (2.0 + pre_act * (1.0 - 2.0 * sigmoid_val))
    return (silu_val, silu_slope, silu_bend)


def mm(left_op, right_op):
    return jnp.dot(left_op, right_op, preferred_element_type=F32)


def mm_nt(left_op, right_op):
    return lax.dot_general(left_op, right_op, (((1,), (1,)), ((), ())), preferred_element_type=F32)


def mm_tn(left_op, right_op):
    return lax.dot_general(left_op, right_op, (((0,), (0,)), ((), ())), preferred_element_type=F32)


def column_norm(weight):
    return jnp.sqrt(jnp.sum(weight * weight, axis=0, keepdims=True) + EPS_COL)


def flat(x):
    return x.reshape(-1, x.shape[-1])


def call(kernel, outs, args, mib, smem=0, flops=0, scratch=()):
    moved = sum(x.size * x.dtype.itemsize for x in (*args, *outs))
    return pl.pallas_call(
        kernel,
        out_shape=outs,
        in_specs=[SMEM] * smem + [VMEM] * (len(args) - smem),
        out_specs=[VMEM] * len(outs),
        scratch_shapes=scratch,
        compiler_params=pltpu.CompilerParams(vmem_limit_bytes=mib << 20),
        cost_estimate=pl.CostEstimate(flops=flops, bytes_accessed=moved, transcendentals=0),
    )(*args)


def copying_call(kernel, outs, args, buffers):
    return pl.pallas_call(
        kernel,
        out_shape=outs,
        in_specs=[pl.BlockSpec(memory_space=pltpu.HBM)] * len(args),
        out_specs=[VMEM] * len(outs),
        scratch_shapes=[*buffers, pltpu.SemaphoreType.DMA((len(args),))],
        compiler_params=pltpu.CompilerParams(vmem_limit_bytes=56 << 20),
    )(*args)


def arr(shape, dtype):
    return jax.ShapeDtypeStruct(shape, dtype)


def fetch(sources, buffers, sems):
    copies = [pltpu.make_async_copy(s, b, sems.at[i]) for i, (s, b) in enumerate(zip(sources, buffers))]
    for copy in copies:
        copy.start()
    for copy in copies:
        copy.wait()


def padded(rows):
    return -(-rows // 16) * 16


def tiles(cols):
    return -(-cols // LANES)


def put(out, at, value):
    rows, cols = value.shape
    for t in range(tiles(cols)):
        wide = min(LANES, cols - t * LANES)
        out[at : at + rows, 0:wide] = value[:, t * LANES : t * LANES + wide]
        at += padded(rows)
    return at


def get(ref, at, rows, cols):
    parts = []
    for t in range(tiles(cols)):
        wide = min(LANES, cols - t * LANES)
        parts.append(ref[at : at + rows, 0:wide])
        at += padded(rows)
    return jnp.concatenate(parts, axis=1), at


def message(*blocks):
    return arr((sum(tiles(cols) * padded(rows) for rows, cols in blocks), LANES), BF)


def token_pack_kernel(q, k, v, og, rates, gains, all_out, kv_out, gg_out, rate_out):
    tokens, feat = gg_out.shape
    rate = jnp.broadcast_to(rates[...], (feat, tokens)).T
    values = (rate * v[0].astype(F32)).astype(BF)
    all_out[:, 0:feat] = q[0]
    all_out[:, feat : 2 * feat] = k[0]
    all_out[:, 2 * feat : 3 * feat] = values
    kv_out[:, 0:feat] = k[0]
    kv_out[:, feat : 2 * feat] = values
    gg_out[...] = gains[...] * og[0].astype(F32)
    rate_out[...] = rate


def weight_pack_kernel(group, slab, *refs):
    args, (w_out, buf, sems) = refs[:6], refs[6:]
    fetch(args, [buf.at[pl.ds(i, 1)] for i in range(6)], sems)
    for j in range(group):
        cols = pl.ds(j * slab, slab)
        block = jnp.concatenate([buf[i, :, cols] for i in range(6)], axis=1)
        for p in range(j, w_out.shape[0], group):
            w_out[p] = block


def columns(w, slab):
    parts = [w[:, pl.ds(i * slab, slab)].astype(F32) for i in range(6)]
    saved, init = parts[:3], parts[3:]
    return saved, init, [column_norm(x) for x in init], [column_norm(x) for x in saved]


def stack(refs, cols=slice(None)):
    return jnp.concatenate([r[:, cols] for r in refs], axis=0)


def thirds(x, slab):
    return [x[:, pl.ds(i * slab, slab)] for i in range(3)]


def forward_kernel(slab, group, w, *refs):
    queries, parts, normed_out = refs[:group], refs[group:-1], refs[-1]
    own, feat = parts[0].shape
    saved, init, norm_init, norm_saved = columns(w, slab)
    normed = [(saved[i] * (norm_init[i] / norm_saved[i])).astype(BF) for i in range(3)]
    rows = stack(queries, slice(0, feat))
    hidden = (silu_parts(mm(rows, normed[0]))[0] * mm(rows, normed[1])).astype(BF)
    out = mm_nt(hidden, normed[2]).astype(BF)
    for d in range(group):
        parts[d][...] = out[d * own : (d + 1) * own]
    normed_out[...] = jnp.concatenate(normed, axis=1)


def reduce_kernel(gg, *refs):
    parts, (apply_out, sums) = refs[:-2], refs[-2:]
    total = total_of(parts)
    apply_out[...] = total
    sums[0:1, :] = jnp.sum((total * total).T, axis=0, keepdims=True)
    sums[1:2, :] = jnp.sum((total * gg[...]).T, axis=0, keepdims=True)


def delta_kernel(width, apply_out, gg, *refs):
    sums, out = refs[:-1], refs[-1]
    tokens, feat = apply_out.shape
    total = sums[0][...]
    for more in sums[1:]:
        total += more[...]
    square = jnp.broadcast_to(total[0:1, :], (feat, tokens)).T
    gain = jnp.broadcast_to(total[1:2, :], (feat, tokens)).T
    root = jnp.sqrt(square / width + EPS_ROOT)
    out[...] = (gg[...] / root - apply_out[...] * (gain / width) / (root * root * root)).astype(BF)


def pair_kernel(left, right, out):
    feat = left.shape[1]
    out[:, 0:feat] = left[...]
    out[:, feat : 2 * feat] = right[...]


def query_side(rows, delta, normed):
    q_gate = mm(rows, normed[0])
    q_up = mm(rows, normed[1])
    act, slope, _ = silu_parts(q_gate)
    hidden = (act * q_up).astype(BF)
    delta_hidden = mm(delta, normed[2])
    delta_gate = (delta_hidden * q_up * slope).astype(BF)
    delta_up = (delta_hidden * act).astype(BF)
    grads = (mm_tn(rows, delta_gate), mm_tn(rows, delta_up), mm_tn(delta, hidden))
    return delta_gate, delta_up, grads


def near_kernel(slab, group, place, normed_ref, *refs):
    q_near, od_near, (grad_q, grads_out) = refs[:group], refs[group : 2 * group], refs[2 * group :]
    own = od_near[0].shape[0]
    normed = thirds(normed_ref, slab)
    delta_gate, delta_up, grads = query_side(stack(q_near, slice(0, od_near[0].shape[1])), stack(od_near), normed)
    found = (mm_nt(delta_gate, normed[0]) + mm_nt(delta_up, normed[1])).astype(BF)
    for d in range(group):
        grad_q[place[1] ^ d] = found[d * own : (d + 1) * own]
    for i in range(3):
        grads_out[i] = grads[i]


def key_kernel(slab, group, w, *refs):
    kvs, (factors, rises, ratio, minus, plus) = refs[:group], refs[group:]
    feat = w.shape[0]
    saved, start, norm_init, norm_saved = columns(w, slab)
    for i in range(3):
        ratio[i : i + 1, :] = norm_init[i] / norm_saved[i]
        minus[i] = saved[i] * (norm_init[i] / (norm_saved[i] * norm_saved[i] * norm_saved[i]))
        plus[i] = start[i] / (norm_init[i] * norm_saved[i])
    init = [w[:, pl.ds((3 + i) * slab, slab)] for i in range(3)]
    keys = stack(kvs, slice(-2 * feat, -feat))
    values = stack(kvs, slice(-feat, None))
    k_gate = mm(keys, init[0])
    k_up = mm(keys, init[1])
    k_proj = mm(values, init[2])
    k_act, k_slope, k_bend = silu_parts(k_gate)
    rises[0] = (k_act * k_up).astype(BF)
    rises[1] = (k_proj * k_up * k_slope).astype(BF)
    rises[2] = (k_proj * k_act).astype(BF)
    factors[0] = k_act
    factors[1] = k_up * k_slope
    factors[2] = k_proj * k_slope
    factors[3] = k_proj * k_up * k_bend


def backward_kernel(
    slab, group, tok_groups, place, w, normed_ref, grads, factors, rises, ratio, minus, plus, *refs
):
    far = group * (tok_groups - 1)
    kvs, pairs, outs, (inner_buf, sums) = refs[:group], refs[group : group + far], refs[group + far : -2], refs[-2:]
    feat = w.shape[0]
    tok_out, outs = outs[0], outs[1:]
    own = tok_out.shape[0]
    normed = thirds(normed_ref, slab)
    total = [grads[i] for i in range(3)]
    for e in range(tok_groups - 1):
        these = pairs[e * group : (e + 1) * group]
        more = query_side(stack(these, slice(feat, 2 * feat)), stack(these, slice(0, feat)), normed)[2]
        total = [total[i] + more[i] for i in range(3)]
        if tok_groups > 2:
            for i in range(3):
                sums[i] = total[i]
            total = [sums[i] for i in range(3)]

    cots, direct = [], []
    once = jnp.where(place[0] == 0, 1.0, 0.0)
    for i in range(3):
        saved = w[:, pl.ds(i * slab, slab)].astype(F32)
        col_dot = jnp.sum(saved * total[i], axis=0, keepdims=True)
        cot = total[i] * ratio[i : i + 1, :] - minus[i] * col_dot
        cots.append(cot.astype(BF))
        direct.append((cot + plus[i] * col_dot) * once)

    init_bf = [w[:, pl.ds((3 + i) * slab, slab)] for i in range(3)]
    keys = stack(kvs, slice(-2 * feat, -feat))
    values = stack(kvs, slice(-feat, None))
    back_gate = mm(keys, cots[0])
    back_up = mm(keys, cots[1])
    back_hidden = mm(values, cots[2])
    back_proj = (back_gate * factors[1] + back_up * factors[0]).astype(BF)
    back_kup = (back_gate * factors[2] + back_hidden * factors[0]).astype(BF)
    back_kgate = (back_gate * factors[3] + (back_up * factors[2] + back_hidden * factors[1])).astype(BF)
    grad_k = (
        mm_nt(rises[1], cots[0])
        + mm_nt(rises[2], cots[1])
        + mm_nt(back_kgate, init_bf[0])
        + mm_nt(back_kup, init_bf[1])
    ).astype(BF)
    grad_v = (mm_nt(rises[0], cots[2]) + mm_nt(back_proj, init_bf[2])).astype(BF)
    inner = (mm_tn(keys, back_kgate), mm_tn(keys, back_kup), mm_tn(values, back_proj))
    whole = jnp.concatenate([inner[i] + direct[i] for i in range(3)], axis=1)
    rows = inner_buf.shape[1]
    for p in range(inner_buf.shape[0]):
        inner_buf[p] = whole[p * rows : (p + 1) * rows]
    tok_out[:, 0:feat] = grad_k[0:own]
    tok_out[:, feat : 2 * feat] = grad_v[0:own]
    outs[0][...] = inner_buf[place[2]].astype(BF)
    for d in range(1, group):
        out, at = outs[d], 0
        for tok in (grad_k, grad_v):
            at = put(out, at, tok[d * own : (d + 1) * own, :])
        put(out, at, inner_buf[place[2] ^ d].astype(BF))
    for dist in range(group, inner_buf.shape[0]):
        outs[dist][...] = inner_buf[place[2] ^ dist].astype(BF)


def total_of(refs):
    total = refs[0][...].astype(F32)
    for block in refs[1:]:
        total += block[...].astype(F32)
    return total


def tokens_kernel(rate, queries, tok, *refs):
    blocks, (gq, gk, gv) = refs[:-3], refs[-3:]
    _, own, feat = gq.shape
    total = queries[0].astype(F32)
    for j in range(1, queries.shape[0]):
        total += queries[j].astype(F32)
    gq[0] = total.astype(BF)
    sums = [tok[:, i * feat : (i + 1) * feat].astype(F32) for i in range(2)]
    for block in blocks:
        at = 0
        for i in range(2):
            more, at = get(block, at, own, feat)
            sums[i] += more.astype(F32)
    gk[0] = sums[0].astype(BF)
    gv[0] = (rate[...] * sums[1]).astype(BF)


def weights_kernel(group, slab, at, place, inner, *refs):
    blocks, (*outs, buf) = refs[:-4], refs[-4:]
    _, rows, cols = buf.shape
    for d in range(group):
        total = (get(blocks[d - 1], at, rows, cols)[0] if d else inner[...]).astype(F32)
        for far in blocks[group - 1 + d :: group]:
            total += far[...].astype(F32)
        buf[d] = total
    total = [buf[place[1] ^ j] for j in range(group)]
    for i in range(3):
        outs[i][0] = jnp.concatenate([t[:, i * slab : (i + 1) * slab] for t in total], axis=1)


def make_local(seq_n, head_n, group):
    tok_groups = seq_n // group
    groups = [[t * group + j for j in range(group)] for t in range(tok_groups)]

    def move(x, dist, axis="seq", size=seq_n):
        return lax.ppermute(x, axis, [(i, i ^ dist) for i in range(size)])

    def near_all(x):
        return [x] + [move(x, d) for d in range(1, group)]

    def mirror(x):
        return [move(x, e * group) for e in range(1, tok_groups)]

    def local(q, k, v, og, rates, gains, gi, ui, di, gs, us, ds):
        _, rows, hidden = gi.shape
        _, own, feat = q.shape
        slab = hidden // group
        near = group * own
        me = lax.axis_index("seq")
        place = jnp.stack((lax.div(me, group), lax.rem(me, group), me)).astype(jnp.int32)

        (packed,) = copying_call(
            functools.partial(weight_pack_kernel, group, slab),
            (arr((seq_n, rows, 6 * slab), BF),),
            (gs, us, ds, gi, ui, di),
            [pltpu.VMEM((6, rows, hidden), BF)],
        )
        packed, queries = lax.optimization_barrier((packed, q[0]))
        wall = lax.all_to_all(packed, "seq", 0, 0, tiled=True).reshape(seq_n * rows, 6 * slab)
        tokens, kv, gg, rate = call(
            token_pack_kernel,
            (arr((own, 3 * feat), BF), arr((own, 2 * feat), BF), arr((own, feat), F32), arr((own, feat), F32)),
            (q, k, v, og, rates, gains),
            8,
        )
        beside = move(tokens, 1) if group > 1 else None
        rest = range(2, group)
        q_near = [queries, beside][:group] + [move(queries, d) for d in rest]
        kv_near = [kv, beside][:group] + [move(kv, d) for d in rest]

        block = arr((own, feat), BF)
        mflop = 2 * near * feat * slab
        *parts, normed = call(
            functools.partial(forward_kernel, slab, group),
            (*(block,) * group, arr((seq_n * rows, 3 * slab), BF)),
            (wall, *q_near),
            24,
            flops=3 * mflop,
        )
        parts = [parts[0]] + [move(parts[d], d) for d in (*range(2, group), *range(1, min(2, group)))]
        *parts, kv_near = lax.optimization_barrier((*parts, kv_near))
        apply_out, sums = call(
            reduce_kernel, (arr((own, feat), F32), arr((2, own), F32)), (gg, *parts), 16
        )
        sums, queries = lax.optimization_barrier((sums, queries))
        sums = [sums] + [move(sums, d, "head", head_n) for d in range(1, head_n)]
        q_mirror = mirror(queries)
        (od,) = call(functools.partial(delta_kernel, head_n * feat), (block,), (apply_out, gg, *sums), 16)
        od_mirror = mirror(od)
        od_near = near_all(od)
        column = arr((3, seq_n * rows, slab), F32)
        factors, rises, *stats = call(
            functools.partial(key_kernel, slab, group),
            (arr((4, near, slab), F32), arr((3, near, slab), BF), arr((3, slab), F32), column, column),
            (wall, *kv_near),
            16,
            flops=12 * mflop,
        )
        *od_mirror, stats[0] = lax.optimization_barrier((*od_mirror, stats[0]))
        pairs = [
            call(pair_kernel, (arr((own, 2 * feat), BF),), pair, 16)[0] for pair in zip(od_mirror, q_mirror)
        ]
        pairs = [x for m in pairs for x in near_all(m)]
        grad_q, grads = call(
            functools.partial(near_kernel, slab, group),
            (arr((group, own, feat), BF), arr((3, seq_n * rows, slab), F32)),
            (place, normed, *q_near, *od_near),
            12,
            smem=1,
            flops=60 * mflop,
        )

        q_block = (own, feat)
        grad_q = lax.all_to_all(grad_q, "seq", 0, 0, axis_index_groups=groups, tiled=True)
        tok, inner, *sends = call(
            functools.partial(backward_kernel, slab, group, tok_groups),
            (
                arr((own, 2 * feat), BF),
                arr((rows, 3 * slab), BF),
                *(message(*(q_block,) * 2, (rows, 3 * slab)),) * (group - 1),
                *(arr((rows, 3 * slab), BF),) * (seq_n - group),
            ),
            (place, wall, normed, grads, factors, rises, *stats, *kv_near, *pairs),
            24,
            smem=1,
            flops=120 * mflop,
            scratch=[
                pltpu.VMEM((seq_n, rows, 3 * slab), F32),
                pltpu.VMEM((3, seq_n * rows, slab), F32),
            ],
        )
        sends, grad_q = lax.optimization_barrier((sends, grad_q))
        near_got = {d: move(sends[d - 1], d) for d in (*range(2, group), *range(1, min(2, group)))}
        near_got = [near_got[d] for d in range(1, group)]
        far_got = [move(sends[d - 1], d) for d in range(group, seq_n)]
        out_tok = arr((1, own, feat), BF)
        grad_w = arr((1, rows, hidden), F32)
        grads_t = call(tokens_kernel, (out_tok,) * 3, (rate, grad_q, tok, *near_got), 16)
        at = 2 * tiles(feat) * padded(own)
        grads_w = call(
            functools.partial(weights_kernel, group, slab, at),
            (grad_w,) * 3,
            (place, inner, *near_got, *far_got),
            16,
            smem=1,
            scratch=[pltpu.VMEM((group, rows, 3 * slab), F32)],
        )
        return (*grads_t, *grads_w)

    return local


def solution(mesh):
    seq_n = mesh.shape["seq"]
    head_n = mesh.shape["head"]
    group = min(4, seq_n)
    tok = P("head", "seq", None)
    return jax.shard_map(
        make_local(seq_n, head_n, group),
        mesh=mesh,
        in_specs=(tok, tok, tok, tok, P("head", "seq"), P("head", None), tok, tok, tok, tok, tok, tok),
        out_specs=(tok, tok, tok, tok, tok, tok),
        check_vma=False,
    )
```

```python
import functools

import jax
import jax.numpy as jnp
from jax import lax
from jax.experimental import pallas as pl
from jax.experimental.pallas import tpu as pltpu
from jax.sharding import PartitionSpec as P

EPS_COL = 1e-06
EPS_ROOT = 1e-05
BF = jnp.bfloat16
F32 = jnp.float32
LANES = 128
VMEM = pl.BlockSpec(memory_space=pltpu.VMEM)
SMEM = pl.BlockSpec(memory_space=pltpu.SMEM)


def silu_parts(pre_act):
    sigmoid_val = jax.nn.sigmoid(pre_act)
    silu_val = pre_act * sigmoid_val
    silu_slope = sigmoid_val * (1.0 + pre_act * (1.0 - sigmoid_val))
    silu_bend = sigmoid_val * (1.0 - sigmoid_val) * (2.0 + pre_act * (1.0 - 2.0 * sigmoid_val))
    return (silu_val, silu_slope, silu_bend)


def mm(left_op, right_op):
    return jnp.dot(left_op, right_op, preferred_element_type=F32)


def mm_nt(left_op, right_op):
    return lax.dot_general(left_op, right_op, (((1,), (1,)), ((), ())), preferred_element_type=F32)


def mm_tn(left_op, right_op):
    return lax.dot_general(left_op, right_op, (((0,), (0,)), ((), ())), preferred_element_type=F32)


def column_norm(weight):
    return jnp.sqrt(jnp.sum(weight * weight, axis=0, keepdims=True) + EPS_COL)


def flat(x):
    return x.reshape(-1, x.shape[-1])


def call(kernel, outs, args, mib, smem=0, flops=0, scratch=()):
    moved = sum(x.size * x.dtype.itemsize for x in (*args, *outs))
    return pl.pallas_call(
        kernel,
        out_shape=outs,
        in_specs=[SMEM] * smem + [VMEM] * (len(args) - smem),
        out_specs=[VMEM] * len(outs),
        scratch_shapes=scratch,
        compiler_params=pltpu.CompilerParams(vmem_limit_bytes=mib << 20),
        cost_estimate=pl.CostEstimate(flops=flops, bytes_accessed=moved, transcendentals=0),
    )(*args)


def copying_call(kernel, outs, args, buffers):
    return pl.pallas_call(
        kernel,
        out_shape=outs,
        in_specs=[pl.BlockSpec(memory_space=pltpu.HBM)] * len(args),
        out_specs=[VMEM] * len(outs),
        scratch_shapes=[*buffers, pltpu.SemaphoreType.DMA((len(args),))],
        compiler_params=pltpu.CompilerParams(vmem_limit_bytes=56 << 20),
    )(*args)


def arr(shape, dtype):
    return jax.ShapeDtypeStruct(shape, dtype)


def fetch(sources, buffers, sems):
    copies = [pltpu.make_async_copy(s, b, sems.at[i]) for i, (s, b) in enumerate(zip(sources, buffers))]
    for copy in copies:
        copy.start()
    for copy in copies:
        copy.wait()


def padded(rows):
    return -(-rows // 16) * 16


def tiles(cols):
    return -(-cols // LANES)


def put(out, at, value):
    rows, cols = value.shape
    for t in range(tiles(cols)):
        wide = min(LANES, cols - t * LANES)
        out[at : at + rows, 0:wide] = value[:, t * LANES : t * LANES + wide]
        at += padded(rows)
    return at


def get(ref, at, rows, cols):
    parts = []
    for t in range(tiles(cols)):
        wide = min(LANES, cols - t * LANES)
        parts.append(ref[at : at + rows, 0:wide])
        at += padded(rows)
    return jnp.concatenate(parts, axis=1), at


def message(*blocks):
    return arr((sum(tiles(cols) * padded(rows) for rows, cols in blocks), LANES), BF)


def token_pack_kernel(q, k, v, og, rates, gains, all_out, kv_out, gg_out, rate_out):
    tokens, feat = gg_out.shape
    rate = jnp.broadcast_to(rates[...], (feat, tokens)).T
    values = (rate * v[0].astype(F32)).astype(BF)
    all_out[:, 0:feat] = q[0]
    all_out[:, feat : 2 * feat] = k[0]
    all_out[:, 2 * feat : 3 * feat] = values
    kv_out[:, 0:feat] = k[0]
    kv_out[:, feat : 2 * feat] = values
    gg_out[...] = gains[...] * og[0].astype(F32)
    rate_out[...] = rate


def weight_pack_kernel(group, slab, *refs):
    args, (w_out, buf, sems) = refs[:6], refs[6:]
    fetch(args, [buf.at[pl.ds(i, 1)] for i in range(6)], sems)
    for j in range(group):
        cols = pl.ds(j * slab, slab)
        block = jnp.concatenate([buf[i, :, cols] for i in range(6)], axis=1)
        for p in range(j, w_out.shape[0], group):
            w_out[p] = block


def columns(w, slab):
    parts = [w[:, pl.ds(i * slab, slab)].astype(F32) for i in range(6)]
    saved, init = parts[:3], parts[3:]
    return saved, init, [column_norm(x) for x in init], [column_norm(x) for x in saved]


def stack(refs, cols=slice(None)):
    return jnp.concatenate([r[:, cols] for r in refs], axis=0)


def thirds(x, slab):
    return [x[:, pl.ds(i * slab, slab)] for i in range(3)]


def forward_kernel(slab, group, w, *refs):
    queries, parts, normed_out = refs[:group], refs[group:-1], refs[-1]
    own, feat = parts[0].shape
    saved, init, norm_init, norm_saved = columns(w, slab)
    normed = [(saved[i] * (norm_init[i] / norm_saved[i])).astype(BF) for i in range(3)]
    rows = stack(queries, slice(0, feat))
    hidden = (silu_parts(mm(rows, normed[0]))[0] * mm(rows, normed[1])).astype(BF)
    out = mm_nt(hidden, normed[2]).astype(BF)
    for d in range(group):
        parts[d][...] = out[d * own : (d + 1) * own]
    normed_out[...] = jnp.concatenate(normed, axis=1)


def reduce_kernel(gg, *refs):
    parts, (apply_out, sums) = refs[:-2], refs[-2:]
    total = total_of(parts)
    apply_out[...] = total
    sums[0:1, :] = jnp.sum((total * total).T, axis=0, keepdims=True)
    sums[1:2, :] = jnp.sum((total * gg[...]).T, axis=0, keepdims=True)


def delta_kernel(width, apply_out, gg, *refs):
    sums, out = refs[:-1], refs[-1]
    tokens, feat = apply_out.shape
    total = sums[0][...]
    for more in sums[1:]:
        total += more[...]
    square = jnp.broadcast_to(total[0:1, :], (feat, tokens)).T
    gain = jnp.broadcast_to(total[1:2, :], (feat, tokens)).T
    root = jnp.sqrt(square / width + EPS_ROOT)
    out[...] = (gg[...] / root - apply_out[...] * (gain / width) / (root * root * root)).astype(BF)


def pair_kernel(left, right, out):
    feat = left.shape[1]
    out[:, 0:feat] = left[...]
    out[:, feat : 2 * feat] = right[...]


def query_side(rows, delta, normed):
    q_gate = mm(rows, normed[0])
    q_up = mm(rows, normed[1])
    act, slope, _ = silu_parts(q_gate)
    hidden = (act * q_up).astype(BF)
    delta_hidden = mm(delta, normed[2])
    delta_gate = (delta_hidden * q_up * slope).astype(BF)
    delta_up = (delta_hidden * act).astype(BF)
    grads = (mm_tn(rows, delta_gate), mm_tn(rows, delta_up), mm_tn(delta, hidden))
    return delta_gate, delta_up, grads


def near_kernel(slab, group, normed_ref, *refs):
    q_near, od_near, (*grad_qs, grads_out) = refs[:group], refs[group : 2 * group], refs[2 * group :]
    own = od_near[0].shape[0]
    normed = thirds(normed_ref, slab)
    delta_gate, delta_up, grads = query_side(stack(q_near, slice(0, od_near[0].shape[1])), stack(od_near), normed)
    found = (mm_nt(delta_gate, normed[0]) + mm_nt(delta_up, normed[1])).astype(BF)
    for d in range(group):
        grad_qs[d][...] = found[d * own : (d + 1) * own]
    for i in range(3):
        grads_out[i] = grads[i]


def key_kernel(slab, group, w, *refs):
    kvs, (factors, rises, ratio, minus, plus) = refs[:group], refs[group:]
    feat = w.shape[0]
    saved, start, norm_init, norm_saved = columns(w, slab)
    for i in range(3):
        ratio[i : i + 1, :] = norm_init[i] / norm_saved[i]
        minus[i] = saved[i] * (norm_init[i] / (norm_saved[i] * norm_saved[i] * norm_saved[i]))
        plus[i] = start[i] / (norm_init[i] * norm_saved[i])
    init = [w[:, pl.ds((3 + i) * slab, slab)] for i in range(3)]
    keys = stack(kvs, slice(-2 * feat, -feat))
    values = stack(kvs, slice(-feat, None))
    k_gate = mm(keys, init[0])
    k_up = mm(keys, init[1])
    k_proj = mm(values, init[2])
    k_act, k_slope, k_bend = silu_parts(k_gate)
    rises[0] = (k_act * k_up).astype(BF)
    rises[1] = (k_proj * k_up * k_slope).astype(BF)
    rises[2] = (k_proj * k_act).astype(BF)
    factors[0] = k_act
    factors[1] = k_up * k_slope
    factors[2] = k_proj * k_slope
    factors[3] = k_proj * k_up * k_bend


def backward_kernel(
    slab, group, tok_groups, place, w, normed_ref, grads, factors, rises, ratio, minus, plus, *refs
):
    far = group * (tok_groups - 1)
    kvs, pairs, outs, (inner_buf, sums) = refs[:group], refs[group : group + far], refs[group + far : -2], refs[-2:]
    feat = w.shape[0]
    tok_out, outs = outs[0], outs[1:]
    own = tok_out.shape[0]
    normed = thirds(normed_ref, slab)
    total = [grads[i] for i in range(3)]
    for e in range(tok_groups - 1):
        these = pairs[e * group : (e + 1) * group]
        more = query_side(stack(these, slice(feat, 2 * feat)), stack(these, slice(0, feat)), normed)[2]
        total = [total[i] + more[i] for i in range(3)]
        if tok_groups > 2:
            for i in range(3):
                sums[i] = total[i]
            total = [sums[i] for i in range(3)]

    cots, direct = [], []
    once = jnp.where(place[0] == 0, 1.0, 0.0)
    for i in range(3):
        saved = w[:, pl.ds(i * slab, slab)].astype(F32)
        col_dot = jnp.sum(saved * total[i], axis=0, keepdims=True)
        cot = total[i] * ratio[i : i + 1, :] - minus[i] * col_dot
        cots.append(cot.astype(BF))
        direct.append((cot + plus[i] * col_dot) * once)

    init_bf = [w[:, pl.ds((3 + i) * slab, slab)] for i in range(3)]
    keys = stack(kvs, slice(-2 * feat, -feat))
    values = stack(kvs, slice(-feat, None))
    back_gate = mm(keys, cots[0])
    back_up = mm(keys, cots[1])
    back_hidden = mm(values, cots[2])
    back_proj = (back_gate * factors[1] + back_up * factors[0]).astype(BF)
    back_kup = (back_gate * factors[2] + back_hidden * factors[0]).astype(BF)
    back_kgate = (back_gate * factors[3] + (back_up * factors[2] + back_hidden * factors[1])).astype(BF)
    grad_k = (
        mm_nt(rises[1], cots[0])
        + mm_nt(rises[2], cots[1])
        + mm_nt(back_kgate, init_bf[0])
        + mm_nt(back_kup, init_bf[1])
    ).astype(BF)
    grad_v = (mm_nt(rises[0], cots[2]) + mm_nt(back_proj, init_bf[2])).astype(BF)
    inner = (mm_tn(keys, back_kgate), mm_tn(keys, back_kup), mm_tn(values, back_proj))
    whole = jnp.concatenate([inner[i] + direct[i] for i in range(3)], axis=1)
    rows = inner_buf.shape[1]
    for p in range(inner_buf.shape[0]):
        inner_buf[p] = whole[p * rows : (p + 1) * rows]
    tok_out[:, 0:feat] = grad_k[0:own]
    tok_out[:, feat : 2 * feat] = grad_v[0:own]
    outs[0][...] = inner_buf[place[2]].astype(BF)
    for d in range(1, group):
        out, at = outs[d], 0
        for tok in (grad_k, grad_v):
            at = put(out, at, tok[d * own : (d + 1) * own, :])
        put(out, at, inner_buf[place[2] ^ d].astype(BF))
    for dist in range(group, inner_buf.shape[0]):
        outs[dist][...] = inner_buf[place[2] ^ dist].astype(BF)


def total_of(refs):
    total = refs[0][...].astype(F32)
    for block in refs[1:]:
        total += block[...].astype(F32)
    return total


def tokens_kernel(group, rate, tok, *refs):
    queries, blocks, (gq, gk, gv) = refs[:group], refs[group:-3], refs[-3:]
    _, own, feat = gq.shape
    gq[0] = total_of(queries).astype(BF)
    sums = [tok[:, i * feat : (i + 1) * feat].astype(F32) for i in range(2)]
    for block in blocks:
        at = 0
        for i in range(2):
            more, at = get(block, at, own, feat)
            sums[i] += more.astype(F32)
    gk[0] = sums[0].astype(BF)
    gv[0] = (rate[...] * sums[1]).astype(BF)


def weights_kernel(group, slab, at, place, inner, *refs):
    blocks, (*outs, buf) = refs[:-4], refs[-4:]
    _, rows, cols = buf.shape
    for d in range(group):
        total = (get(blocks[d - 1], at, rows, cols)[0] if d else inner[...]).astype(F32)
        for far in blocks[group - 1 + d :: group]:
            total += far[...].astype(F32)
        buf[d] = total
    total = [buf[place[1] ^ j] for j in range(group)]
    for i in range(3):
        outs[i][0] = jnp.concatenate([t[:, i * slab : (i + 1) * slab] for t in total], axis=1)


def make_local(seq_n, head_n, group):
    tok_groups = seq_n // group

    def move(x, dist, axis="seq", size=seq_n):
        return lax.ppermute(x, axis, [(i, i ^ dist) for i in range(size)])

    def near_all(x):
        return [x] + [move(x, d) for d in range(1, group)]

    def mirror(x):
        return [move(x, e * group) for e in range(1, tok_groups)]

    def local(q, k, v, og, rates, gains, gi, ui, di, gs, us, ds):
        _, rows, hidden = gi.shape
        _, own, feat = q.shape
        slab = hidden // group
        near = group * own
        me = lax.axis_index("seq")
        place = jnp.stack((lax.div(me, group), lax.rem(me, group), me)).astype(jnp.int32)

        (packed,) = copying_call(
            functools.partial(weight_pack_kernel, group, slab),
            (arr((seq_n, rows, 6 * slab), BF),),
            (gs, us, ds, gi, ui, di),
            [pltpu.VMEM((6, rows, hidden), BF)],
        )
        packed, queries = lax.optimization_barrier((packed, q[0]))
        wall = lax.all_to_all(packed, "seq", 0, 0, tiled=True).reshape(seq_n * rows, 6 * slab)
        tokens, kv, gg, rate = call(
            token_pack_kernel,
            (arr((own, 3 * feat), BF), arr((own, 2 * feat), BF), arr((own, feat), F32), arr((own, feat), F32)),
            (q, k, v, og, rates, gains),
            8,
        )
        beside = move(tokens, 1) if group > 1 else None
        rest = range(2, group)
        q_near = [queries, beside][:group] + [move(queries, d) for d in rest]
        kv_near = [kv, beside][:group] + [move(kv, d) for d in rest]

        block = arr((own, feat), BF)
        mflop = 2 * near * feat * slab
        *parts, normed = call(
            functools.partial(forward_kernel, slab, group),
            (*(block,) * group, arr((seq_n * rows, 3 * slab), BF)),
            (wall, *q_near),
            24,
            flops=3 * mflop,
        )
        parts = [parts[0]] + [move(parts[d], d) for d in (*range(2, group), *range(1, min(2, group)))]
        *parts, kv_near = lax.optimization_barrier((*parts, kv_near))
        apply_out, sums = call(
            reduce_kernel, (arr((own, feat), F32), arr((2, own), F32)), (gg, *parts), 16
        )
        sums, queries = lax.optimization_barrier((sums, queries))
        sums = [sums] + [move(sums, d, "head", head_n) for d in range(1, head_n)]
        q_mirror = mirror(queries)
        (od,) = call(functools.partial(delta_kernel, head_n * feat), (block,), (apply_out, gg, *sums), 16)
        od_mirror = mirror(od)
        od_near = near_all(od)
        column = arr((3, seq_n * rows, slab), F32)
        factors, rises, *stats = call(
            functools.partial(key_kernel, slab, group),
            (arr((4, near, slab), F32), arr((3, near, slab), BF), arr((3, slab), F32), column, column),
            (wall, *kv_near),
            16,
            flops=12 * mflop,
        )
        *od_mirror, stats[0] = lax.optimization_barrier((*od_mirror, stats[0]))
        pairs = [
            call(pair_kernel, (arr((own, 2 * feat), BF),), pair, 16)[0] for pair in zip(od_mirror, q_mirror)
        ]
        pairs = [x for m in pairs for x in near_all(m)]
        *grad_q, grads = call(
            functools.partial(near_kernel, slab, group),
            (*(block,) * group, arr((3, seq_n * rows, slab), F32)),
            (normed, *q_near, *od_near),
            12,
            flops=60 * mflop,
        )

        q_block = (own, feat)
        grad_q = [grad_q[0]] + [move(grad_q[d], d) for d in (*range(2, group), *range(1, min(2, group)))]
        tok, inner, *sends = call(
            functools.partial(backward_kernel, slab, group, tok_groups),
            (
                arr((own, 2 * feat), BF),
                arr((rows, 3 * slab), BF),
                *(message(*(q_block,) * 2, (rows, 3 * slab)),) * (group - 1),
                *(arr((rows, 3 * slab), BF),) * (seq_n - group),
            ),
            (place, wall, normed, grads, factors, rises, *stats, *kv_near, *pairs),
            24,
            smem=1,
            flops=120 * mflop,
            scratch=[
                pltpu.VMEM((seq_n, rows, 3 * slab), F32),
                pltpu.VMEM((3, seq_n * rows, slab), F32),
            ],
        )
        sends, grad_q = lax.optimization_barrier((sends, grad_q))
        near_got = {d: move(sends[d - 1], d) for d in (*range(2, group), *range(1, min(2, group)))}
        near_got = [near_got[d] for d in range(1, group)]
        far_got = [move(sends[d - 1], d) for d in range(group, seq_n)]
        out_tok = arr((1, own, feat), BF)
        grad_w = arr((1, rows, hidden), F32)
        grads_t = call(
            functools.partial(tokens_kernel, group), (out_tok,) * 3, (rate, tok, *grad_q, *near_got), 16
        )
        at = 2 * tiles(feat) * padded(own)
        grads_w = call(
            functools.partial(weights_kernel, group, slab, at),
            (grad_w,) * 3,
            (place, inner, *near_got, *far_got),
            16,
            smem=1,
            scratch=[pltpu.VMEM((group, rows, 3 * slab), F32)],
        )
        return (*grads_t, *grads_w)

    return local


def solution(mesh):
    seq_n = mesh.shape["seq"]
    head_n = mesh.shape["head"]
    group = min(4, seq_n)
    tok = P("head", "seq", None)
    return jax.shard_map(
        make_local(seq_n, head_n, group),
        mesh=mesh,
        in_specs=(tok, tok, tok, tok, P("head", "seq"), P("head", None), tok, tok, tok, tok, tok, tok),
        out_specs=(tok, tok, tok, tok, tok, tok),
        check_vma=False,
    )
```

```python
import functools

import jax
import jax.numpy as jnp
from jax import lax
from jax.experimental import pallas as pl
from jax.experimental.pallas import tpu as pltpu
from jax.sharding import PartitionSpec as P

EPS_COL = 1e-06
EPS_ROOT = 1e-05
BF = jnp.bfloat16
F32 = jnp.float32
LANES = 128
VMEM = pl.BlockSpec(memory_space=pltpu.VMEM)
SMEM = pl.BlockSpec(memory_space=pltpu.SMEM)


def silu_parts(pre_act):
    sigmoid_val = jax.nn.sigmoid(pre_act)
    silu_val = pre_act * sigmoid_val
    silu_slope = sigmoid_val * (1.0 + pre_act * (1.0 - sigmoid_val))
    silu_bend = sigmoid_val * (1.0 - sigmoid_val) * (2.0 + pre_act * (1.0 - 2.0 * sigmoid_val))
    return (silu_val, silu_slope, silu_bend)


def mm(left_op, right_op):
    return jnp.dot(left_op, right_op, preferred_element_type=F32)


def mm_nt(left_op, right_op):
    return lax.dot_general(left_op, right_op, (((1,), (1,)), ((), ())), preferred_element_type=F32)


def mm_tn(left_op, right_op):
    return lax.dot_general(left_op, right_op, (((0,), (0,)), ((), ())), preferred_element_type=F32)


def column_norm(weight):
    return jnp.sqrt(jnp.sum(weight * weight, axis=0, keepdims=True) + EPS_COL)


def flat(x):
    return x.reshape(-1, x.shape[-1])


def call(kernel, outs, args, mib, smem=0, flops=0, scratch=()):
    moved = sum(x.size * x.dtype.itemsize for x in (*args, *outs))
    return pl.pallas_call(
        kernel,
        out_shape=outs,
        in_specs=[SMEM] * smem + [VMEM] * (len(args) - smem),
        out_specs=[VMEM] * len(outs),
        scratch_shapes=scratch,
        compiler_params=pltpu.CompilerParams(vmem_limit_bytes=mib << 20),
        cost_estimate=pl.CostEstimate(flops=flops, bytes_accessed=moved, transcendentals=0),
    )(*args)


def copying_call(kernel, outs, args, buffers):
    return pl.pallas_call(
        kernel,
        out_shape=outs,
        in_specs=[pl.BlockSpec(memory_space=pltpu.HBM)] * len(args),
        out_specs=[VMEM] * len(outs),
        scratch_shapes=[*buffers, pltpu.SemaphoreType.DMA((len(args),))],
        compiler_params=pltpu.CompilerParams(vmem_limit_bytes=56 << 20),
    )(*args)


def arr(shape, dtype):
    return jax.ShapeDtypeStruct(shape, dtype)


def fetch(sources, buffers, sems):
    copies = [pltpu.make_async_copy(s, b, sems.at[i]) for i, (s, b) in enumerate(zip(sources, buffers))]
    for copy in copies:
        copy.start()
    for copy in copies:
        copy.wait()


def padded(rows):
    return -(-rows // 16) * 16


def tiles(cols):
    return -(-cols // LANES)


def put(out, at, value):
    rows, cols = value.shape
    for t in range(tiles(cols)):
        wide = min(LANES, cols - t * LANES)
        out[at : at + rows, 0:wide] = value[:, t * LANES : t * LANES + wide]
        at += padded(rows)
    return at


def get(ref, at, rows, cols):
    parts = []
    for t in range(tiles(cols)):
        wide = min(LANES, cols - t * LANES)
        parts.append(ref[at : at + rows, 0:wide])
        at += padded(rows)
    return jnp.concatenate(parts, axis=1), at


def message(*blocks):
    return arr((sum(tiles(cols) * padded(rows) for rows, cols in blocks), LANES), BF)


def token_pack_kernel(q, k, v, og, rates, gains, all_out, kv_out, gg_out, rate_out):
    tokens, feat = gg_out.shape
    rate = jnp.broadcast_to(rates[...], (feat, tokens)).T
    values = (rate * v[0].astype(F32)).astype(BF)
    all_out[:, 0:feat] = q[0]
    all_out[:, feat : 2 * feat] = k[0]
    all_out[:, 2 * feat : 3 * feat] = values
    kv_out[:, 0:feat] = k[0]
    kv_out[:, feat : 2 * feat] = values
    gg_out[...] = gains[...] * og[0].astype(F32)
    rate_out[...] = rate


def weight_pack_kernel(group, slab, *refs):
    args, (w_out, buf, sems) = refs[:6], refs[6:]
    fetch(args, [buf.at[pl.ds(i, 1)] for i in range(6)], sems)
    for j in range(group):
        cols = pl.ds(j * slab, slab)
        block = jnp.concatenate([buf[i, :, cols] for i in range(6)], axis=1)
        for p in range(j, w_out.shape[0], group):
            w_out[p] = block


def columns(w, slab):
    parts = [w[:, pl.ds(i * slab, slab)].astype(F32) for i in range(6)]
    saved, init = parts[:3], parts[3:]
    return saved, init, [column_norm(x) for x in init], [column_norm(x) for x in saved]


def stack(refs, cols=slice(None)):
    return jnp.concatenate([r[:, cols] for r in refs], axis=0)


def thirds(x, slab):
    return [x[:, pl.ds(i * slab, slab)] for i in range(3)]


def forward_kernel(slab, group, w, *refs):
    queries, parts, normed_out = refs[:group], refs[group:-1], refs[-1]
    own, feat = parts[0].shape
    saved, init, norm_init, norm_saved = columns(w, slab)
    normed = [(saved[i] * (norm_init[i] / norm_saved[i])).astype(BF) for i in range(3)]
    rows = stack(queries, slice(0, feat))
    hidden = (silu_parts(mm(rows, normed[0]))[0] * mm(rows, normed[1])).astype(BF)
    out = mm_nt(hidden, normed[2]).astype(BF)
    for d in range(group):
        parts[d][...] = out[d * own : (d + 1) * own]
    normed_out[...] = jnp.concatenate(normed, axis=1)


def reduce_kernel(gg, *refs):
    parts, (apply_out, sums) = refs[:-2], refs[-2:]
    total = total_of(parts)
    apply_out[...] = total
    sums[0:1, :] = jnp.sum((total * total).T, axis=0, keepdims=True)
    sums[1:2, :] = jnp.sum((total * gg[...]).T, axis=0, keepdims=True)


def delta_kernel(width, apply_out, gg, *refs):
    sums, out = refs[:-1], refs[-1]
    tokens, feat = apply_out.shape
    total = sums[0][...]
    for more in sums[1:]:
        total += more[...]
    square = jnp.broadcast_to(total[0:1, :], (feat, tokens)).T
    gain = jnp.broadcast_to(total[1:2, :], (feat, tokens)).T
    root = jnp.sqrt(square / width + EPS_ROOT)
    out[...] = (gg[...] / root - apply_out[...] * (gain / width) / (root * root * root)).astype(BF)


def pair_kernel(left, right, out):
    feat = left.shape[1]
    out[:, 0:feat] = left[...]
    out[:, feat : 2 * feat] = right[...]


def query_side(rows, delta, normed):
    q_gate = mm(rows, normed[0])
    q_up = mm(rows, normed[1])
    act, slope, _ = silu_parts(q_gate)
    hidden = (act * q_up).astype(BF)
    delta_hidden = mm(delta, normed[2])
    delta_gate = (delta_hidden * q_up * slope).astype(BF)
    delta_up = (delta_hidden * act).astype(BF)
    grads = (mm_tn(rows, delta_gate), mm_tn(rows, delta_up), mm_tn(delta, hidden))
    return delta_gate, delta_up, grads


def near_kernel(slab, group, normed_ref, *refs):
    q_near, od_near, (*grad_qs, grads_out) = refs[:group], refs[group : 2 * group], refs[2 * group :]
    own = od_near[0].shape[0]
    normed = thirds(normed_ref, slab)
    delta_gate, delta_up, grads = query_side(stack(q_near, slice(0, od_near[0].shape[1])), stack(od_near), normed)
    found = (mm_nt(delta_gate, normed[0]) + mm_nt(delta_up, normed[1])).astype(BF)
    for d in range(group):
        grad_qs[d][...] = found[d * own : (d + 1) * own]
    for i in range(3):
        grads_out[i] = grads[i]


def key_kernel(slab, group, w, *refs):
    kvs, (factors, rises, ratio, minus, plus) = refs[:group], refs[group:]
    feat = w.shape[0]
    saved, start, norm_init, norm_saved = columns(w, slab)
    for i in range(3):
        ratio[i : i + 1, :] = norm_init[i] / norm_saved[i]
        minus[i] = saved[i] * (norm_init[i] / (norm_saved[i] * norm_saved[i] * norm_saved[i]))
        plus[i] = start[i] / (norm_init[i] * norm_saved[i])
    init = [w[:, pl.ds((3 + i) * slab, slab)] for i in range(3)]
    keys = stack(kvs, slice(-2 * feat, -feat))
    values = stack(kvs, slice(-feat, None))
    k_gate = mm(keys, init[0])
    k_up = mm(keys, init[1])
    k_proj = mm(values, init[2])
    k_act, k_slope, k_bend = silu_parts(k_gate)
    rises[0] = (k_act * k_up).astype(BF)
    rises[1] = (k_proj * k_up * k_slope).astype(BF)
    rises[2] = (k_proj * k_act).astype(BF)
    factors[0] = k_act
    factors[1] = k_up * k_slope
    factors[2] = k_proj * k_slope
    factors[3] = k_proj * k_up * k_bend


def backward_kernel(
    slab, group, tok_groups, place, w, normed_ref, grads, factors, rises, ratio, minus, plus, *refs
):
    far = group * (tok_groups - 1)
    kvs, pairs, outs, (inner_buf, sums) = refs[:group], refs[group : group + far], refs[group + far : -2], refs[-2:]
    feat = w.shape[0]
    tok_out, outs = outs[0], outs[1:]
    own = tok_out.shape[0]
    normed = thirds(normed_ref, slab)
    total = [grads[i] for i in range(3)]
    for e in range(tok_groups - 1):
        these = pairs[e * group : (e + 1) * group]
        more = query_side(stack(these, slice(feat, 2 * feat)), stack(these, slice(0, feat)), normed)[2]
        total = [total[i] + more[i] for i in range(3)]
        if tok_groups > 2:
            for i in range(3):
                sums[i] = total[i]
            total = [sums[i] for i in range(3)]

    cots, direct = [], []
    once = jnp.where(place[0] == 0, 1.0, 0.0)
    for i in range(3):
        saved = w[:, pl.ds(i * slab, slab)].astype(F32)
        col_dot = jnp.sum(saved * total[i], axis=0, keepdims=True)
        cot = total[i] * ratio[i : i + 1, :] - minus[i] * col_dot
        cots.append(cot.astype(BF))
        direct.append((cot + plus[i] * col_dot) * once)

    init_bf = [w[:, pl.ds((3 + i) * slab, slab)] for i in range(3)]
    keys = stack(kvs, slice(-2 * feat, -feat))
    values = stack(kvs, slice(-feat, None))
    back_gate = mm(keys, cots[0])
    back_up = mm(keys, cots[1])
    back_hidden = mm(values, cots[2])
    back_proj = (back_gate * factors[1] + back_up * factors[0]).astype(BF)
    back_kup = (back_gate * factors[2] + back_hidden * factors[0]).astype(BF)
    back_kgate = (back_gate * factors[3] + (back_up * factors[2] + back_hidden * factors[1])).astype(BF)
    grad_k = (
        mm_nt(rises[1], cots[0])
        + mm_nt(rises[2], cots[1])
        + mm_nt(back_kgate, init_bf[0])
        + mm_nt(back_kup, init_bf[1])
    ).astype(BF)
    grad_v = (mm_nt(rises[0], cots[2]) + mm_nt(back_proj, init_bf[2])).astype(BF)
    inner = (mm_tn(keys, back_kgate), mm_tn(keys, back_kup), mm_tn(values, back_proj))
    whole = jnp.concatenate([inner[i] + direct[i] for i in range(3)], axis=1)
    rows = inner_buf.shape[1]
    for p in range(inner_buf.shape[0]):
        inner_buf[p] = whole[p * rows : (p + 1) * rows]
    tok_out[:, 0:feat] = grad_k[0:own]
    tok_out[:, feat : 2 * feat] = grad_v[0:own]
    outs[0][...] = inner_buf[place[2]].astype(BF)
    for d in range(1, group):
        out, at = outs[d], 0
        for tok in (grad_k, grad_v):
            at = put(out, at, tok[d * own : (d + 1) * own, :])
        put(out, at, inner_buf[place[2] ^ d].astype(BF))
    for dist, out in zip(far_distances(group, tok_groups), outs[group:]):
        for i in range(2):
            out[i * padded(rows) : i * padded(rows) + rows, :] = inner_buf[place[2] ^ dist ^ i].astype(BF)


def relay_kernel(rows, *refs):
    out, step = refs[-1], padded(rows)
    for i, block in enumerate(refs[:-1]):
        out[i * step : i * step + rows, :] = block[step : step + rows, :]


def far_distances(group, tok_groups):
    return [e * group + d for e in range(1, tok_groups) for d in range(0, group, 2)]


def total_of(refs):
    total = refs[0][...].astype(F32)
    for block in refs[1:]:
        total += block[...].astype(F32)
    return total


def tokens_kernel(group, rate, tok, *refs):
    queries, blocks, (gq, gk, gv) = refs[:group], refs[group:-3], refs[-3:]
    _, own, feat = gq.shape
    gq[0] = total_of(queries).astype(BF)
    sums = [tok[:, i * feat : (i + 1) * feat].astype(F32) for i in range(2)]
    for block in blocks:
        at = 0
        for i in range(2):
            more, at = get(block, at, own, feat)
            sums[i] += more.astype(F32)
    gk[0] = sums[0].astype(BF)
    gv[0] = (rate[...] * sums[1]).astype(BF)


def weights_kernel(group, tok_groups, slab, at, place, relayed, inner, *refs):
    blocks, (*outs, buf) = refs[:-4], refs[-4:]
    _, rows, cols = buf.shape
    step = padded(rows)
    buf[0] = inner[...].astype(F32)
    for d in range(1, group):
        buf[d] = get(blocks[d - 1], at, rows, cols)[0].astype(F32)
    for i, dist in enumerate(far_distances(group, tok_groups)):
        d = dist % group
        buf[d] += blocks[group - 1 + i][0:rows, :].astype(F32)
        buf[d ^ 1] += relayed[i * step : i * step + rows, :].astype(F32)
    total = [buf[place[1] ^ j] for j in range(group)]
    for i in range(3):
        outs[i][0] = jnp.concatenate([t[:, i * slab : (i + 1) * slab] for t in total], axis=1)


def make_local(seq_n, head_n, group):
    tok_groups = seq_n // group

    def move(x, dist, axis="seq", size=seq_n):
        return lax.ppermute(x, axis, [(i, i ^ dist) for i in range(size)])

    def near_all(x):
        return [x] + [move(x, d) for d in range(1, group)]

    def mirror(x):
        return [move(x, e * group) for e in range(1, tok_groups)]

    def local(q, k, v, og, rates, gains, gi, ui, di, gs, us, ds):
        _, rows, hidden = gi.shape
        _, own, feat = q.shape
        slab = hidden // group
        near = group * own
        me = lax.axis_index("seq")
        place = jnp.stack((lax.div(me, group), lax.rem(me, group), me)).astype(jnp.int32)

        (packed,) = copying_call(
            functools.partial(weight_pack_kernel, group, slab),
            (arr((seq_n, rows, 6 * slab), BF),),
            (gs, us, ds, gi, ui, di),
            [pltpu.VMEM((6, rows, hidden), BF)],
        )
        packed, queries = lax.optimization_barrier((packed, q[0]))
        wall = lax.all_to_all(packed, "seq", 0, 0, tiled=True).reshape(seq_n * rows, 6 * slab)
        tokens, kv, gg, rate = call(
            token_pack_kernel,
            (arr((own, 3 * feat), BF), arr((own, 2 * feat), BF), arr((own, feat), F32), arr((own, feat), F32)),
            (q, k, v, og, rates, gains),
            8,
        )
        beside = move(tokens, 1) if group > 1 else None
        rest = range(2, group)
        q_near = [queries, beside][:group] + [move(queries, d) for d in rest]
        kv_near = [kv, beside][:group] + [move(kv, d) for d in rest]

        block = arr((own, feat), BF)
        mflop = 2 * near * feat * slab
        *parts, normed = call(
            functools.partial(forward_kernel, slab, group),
            (*(block,) * group, arr((seq_n * rows, 3 * slab), BF)),
            (wall, *q_near),
            24,
            flops=3 * mflop,
        )
        parts = [parts[0]] + [move(parts[d], d) for d in (*range(2, group), *range(1, min(2, group)))]
        *parts, kv_near = lax.optimization_barrier((*parts, kv_near))
        apply_out, sums = call(
            reduce_kernel, (arr((own, feat), F32), arr((2, own), F32)), (gg, *parts), 16
        )
        sums, queries = lax.optimization_barrier((sums, queries))
        sums = [sums] + [move(sums, d, "head", head_n) for d in range(1, head_n)]
        q_mirror = mirror(queries)
        (od,) = call(functools.partial(delta_kernel, head_n * feat), (block,), (apply_out, gg, *sums), 16)
        od_mirror = mirror(od)
        od_near = near_all(od)
        column = arr((3, seq_n * rows, slab), F32)
        factors, rises, *stats = call(
            functools.partial(key_kernel, slab, group),
            (arr((4, near, slab), F32), arr((3, near, slab), BF), arr((3, slab), F32), column, column),
            (wall, *kv_near),
            16,
            flops=12 * mflop,
        )
        *od_mirror, stats[0] = lax.optimization_barrier((*od_mirror, stats[0]))
        pairs = [
            call(pair_kernel, (arr((own, 2 * feat), BF),), pair, 16)[0] for pair in zip(od_mirror, q_mirror)
        ]
        pairs = [x for m in pairs for x in near_all(m)]
        *grad_q, grads = call(
            functools.partial(near_kernel, slab, group),
            (*(block,) * group, arr((3, seq_n * rows, slab), F32)),
            (normed, *q_near, *od_near),
            12,
            flops=60 * mflop,
        )

        q_block = (own, feat)
        grad_q = [grad_q[0]] + [move(grad_q[d], d) for d in (*range(2, group), *range(1, min(2, group)))]
        far = far_distances(group, tok_groups)
        tok, inner, *sends = call(
            functools.partial(backward_kernel, slab, group, tok_groups),
            (
                arr((own, 2 * feat), BF),
                arr((rows, 3 * slab), BF),
                *(message(*(q_block,) * 2, (rows, 3 * slab)),) * (group - 1),
                *(arr((2 * padded(rows), 3 * slab), BF),) * len(far),
            ),
            (place, wall, normed, grads, factors, rises, *stats, *kv_near, *pairs),
            24,
            smem=1,
            flops=120 * mflop,
            scratch=[
                pltpu.VMEM((seq_n, rows, 3 * slab), F32),
                pltpu.VMEM((3, seq_n * rows, slab), F32),
            ],
        )
        sends, grad_q = lax.optimization_barrier((sends, grad_q))
        near_got = {d: move(sends[d - 1], d) for d in (*range(2, group), *range(1, min(2, group)))}
        near_got = [near_got[d] for d in range(1, group)]
        far_got = [move(x, d) for x, d in zip(sends[group - 1 :], far)]
        (relayed,) = call(
            functools.partial(relay_kernel, rows),
            (arr((len(far) * padded(rows), 3 * slab), BF),),
            far_got,
            16,
        )
        relayed = move(relayed, 1)
        out_tok = arr((1, own, feat), BF)
        grad_w = arr((1, rows, hidden), F32)
        grads_t = call(
            functools.partial(tokens_kernel, group), (out_tok,) * 3, (rate, tok, *grad_q, *near_got), 16
        )
        at = 2 * tiles(feat) * padded(own)
        grads_w = call(
            functools.partial(weights_kernel, group, tok_groups, slab, at),
            (grad_w,) * 3,
            (place, relayed, inner, *near_got, *far_got),
            16,
            smem=1,
            scratch=[pltpu.VMEM((group, rows, 3 * slab), F32)],
        )
        return (*grads_t, *grads_w)

    return local


def solution(mesh):
    seq_n = mesh.shape["seq"]
    head_n = mesh.shape["head"]
    group = min(4, seq_n)
    tok = P("head", "seq", None)
    return jax.shard_map(
        make_local(seq_n, head_n, group),
        mesh=mesh,
        in_specs=(tok, tok, tok, tok, P("head", "seq"), P("head", None), tok, tok, tok, tok, tok, tok),
        out_specs=(tok, tok, tok, tok, tok, tok),
        check_vma=False,
    )
```

```python
import functools

import jax
import jax.numpy as jnp
from jax import lax
from jax.experimental import pallas as pl
from jax.experimental.pallas import tpu as pltpu
from jax.sharding import PartitionSpec as P

EPS_COL = 1e-06
EPS_ROOT = 1e-05
BF = jnp.bfloat16
F32 = jnp.float32
LANES = 128
VMEM = pl.BlockSpec(memory_space=pltpu.VMEM)
SMEM = pl.BlockSpec(memory_space=pltpu.SMEM)


def silu_parts(pre_act):
    sigmoid_val = jax.nn.sigmoid(pre_act)
    silu_val = pre_act * sigmoid_val
    silu_slope = sigmoid_val * (1.0 + pre_act * (1.0 - sigmoid_val))
    silu_bend = sigmoid_val * (1.0 - sigmoid_val) * (2.0 + pre_act * (1.0 - 2.0 * sigmoid_val))
    return (silu_val, silu_slope, silu_bend)


def mm(left_op, right_op):
    return jnp.dot(left_op, right_op, preferred_element_type=F32)


def mm_nt(left_op, right_op):
    return lax.dot_general(left_op, right_op, (((1,), (1,)), ((), ())), preferred_element_type=F32)


def mm_tn(left_op, right_op):
    return lax.dot_general(left_op, right_op, (((0,), (0,)), ((), ())), preferred_element_type=F32)


def column_norm(weight):
    return jnp.sqrt(jnp.sum(weight * weight, axis=0, keepdims=True) + EPS_COL)


def flat(x):
    return x.reshape(-1, x.shape[-1])


def call(kernel, outs, args, mib, smem=0, flops=0, scratch=()):
    moved = sum(x.size * x.dtype.itemsize for x in (*args, *outs))
    return pl.pallas_call(
        kernel,
        out_shape=outs,
        in_specs=[SMEM] * smem + [VMEM] * (len(args) - smem),
        out_specs=[VMEM] * len(outs),
        scratch_shapes=scratch,
        compiler_params=pltpu.CompilerParams(vmem_limit_bytes=mib << 20),
        cost_estimate=pl.CostEstimate(flops=flops, bytes_accessed=moved, transcendentals=0),
    )(*args)


def copying_call(kernel, outs, args, buffers):
    return pl.pallas_call(
        kernel,
        out_shape=outs,
        in_specs=[pl.BlockSpec(memory_space=pltpu.HBM)] * len(args),
        out_specs=[VMEM] * len(outs),
        scratch_shapes=[*buffers, pltpu.SemaphoreType.DMA((len(args),))],
        compiler_params=pltpu.CompilerParams(vmem_limit_bytes=56 << 20),
    )(*args)


def arr(shape, dtype):
    return jax.ShapeDtypeStruct(shape, dtype)


def fetch(sources, buffers, sems):
    copies = [pltpu.make_async_copy(s, b, sems.at[i]) for i, (s, b) in enumerate(zip(sources, buffers))]
    for copy in copies:
        copy.start()
    for copy in copies:
        copy.wait()


def padded(rows):
    return -(-rows // 16) * 16


def tiles(cols):
    return -(-cols // LANES)


def put(out, at, value):
    rows, cols = value.shape
    for t in range(tiles(cols)):
        wide = min(LANES, cols - t * LANES)
        out[at : at + rows, 0:wide] = value[:, t * LANES : t * LANES + wide]
        at += padded(rows)
    return at


def get(ref, at, rows, cols):
    parts = []
    for t in range(tiles(cols)):
        wide = min(LANES, cols - t * LANES)
        parts.append(ref[at : at + rows, 0:wide])
        at += padded(rows)
    return jnp.concatenate(parts, axis=1), at


def message(*blocks):
    return arr((sum(tiles(cols) * padded(rows) for rows, cols in blocks), LANES), BF)


def token_pack_kernel(q, k, v, og, rates, gains, all_out, kv_out, gg_out, rate_out):
    tokens, feat = gg_out.shape
    rate = jnp.broadcast_to(rates[...], (feat, tokens)).T
    values = (rate * v[0].astype(F32)).astype(BF)
    all_out[:, 0:feat] = q[0]
    all_out[:, feat : 2 * feat] = k[0]
    all_out[:, 2 * feat : 3 * feat] = values
    kv_out[:, 0:feat] = k[0]
    kv_out[:, feat : 2 * feat] = values
    gg_out[...] = gains[...] * og[0].astype(F32)
    rate_out[...] = rate


def weight_pack_kernel(group, slab, *refs):
    args, (w_out, buf, sems) = refs[:6], refs[6:]
    fetch(args, [buf.at[pl.ds(i, 1)] for i in range(6)], sems)
    for j in range(group):
        cols = pl.ds(j * slab, slab)
        block = jnp.concatenate([buf[i, :, cols] for i in range(6)], axis=1)
        for p in range(j, w_out.shape[0], group):
            w_out[p] = block


def columns(w, slab):
    parts = [w[:, pl.ds(i * slab, slab)].astype(F32) for i in range(6)]
    saved, init = parts[:3], parts[3:]
    return saved, init, [column_norm(x) for x in init], [column_norm(x) for x in saved]


def stack(refs, cols=slice(None)):
    return jnp.concatenate([r[:, cols] for r in refs], axis=0)


def thirds(x, slab):
    return [x[:, pl.ds(i * slab, slab)] for i in range(3)]


def forward_kernel(slab, group, w, *refs):
    queries, parts, normed_out = refs[:group], refs[group:-1], refs[-1]
    own, feat = parts[0].shape
    saved, init, norm_init, norm_saved = columns(w, slab)
    normed = [(saved[i] * (norm_init[i] / norm_saved[i])).astype(BF) for i in range(3)]
    rows = stack(queries, slice(0, feat))
    hidden = (silu_parts(mm(rows, normed[0]))[0] * mm(rows, normed[1])).astype(BF)
    out = mm_nt(hidden, normed[2]).astype(BF)
    for d in range(group):
        parts[d][...] = out[d * own : (d + 1) * own]
    normed_out[...] = jnp.concatenate(normed, axis=1)


def reduce_kernel(gg, *refs):
    parts, (apply_out, sums) = refs[:-2], refs[-2:]
    total = total_of(parts)
    apply_out[...] = total
    sums[0:1, :] = jnp.sum((total * total).T, axis=0, keepdims=True)
    sums[1:2, :] = jnp.sum((total * gg[...]).T, axis=0, keepdims=True)


def delta_kernel(width, apply_out, gg, *refs):
    sums, out = refs[:-1], refs[-1]
    tokens, feat = apply_out.shape
    total = sums[0][...]
    for more in sums[1:]:
        total += more[...]
    square = jnp.broadcast_to(total[0:1, :], (feat, tokens)).T
    gain = jnp.broadcast_to(total[1:2, :], (feat, tokens)).T
    root = jnp.sqrt(square / width + EPS_ROOT)
    out[...] = (gg[...] / root - apply_out[...] * (gain / width) / (root * root * root)).astype(BF)


def pair_kernel(left, right, out):
    feat = left.shape[1]
    out[:, 0:feat] = left[...]
    out[:, feat : 2 * feat] = right[...]


def query_side(rows, delta, normed):
    q_gate = mm(rows, normed[0])
    q_up = mm(rows, normed[1])
    act, slope, _ = silu_parts(q_gate)
    hidden = (act * q_up).astype(BF)
    delta_hidden = mm(delta, normed[2])
    delta_gate = (delta_hidden * q_up * slope).astype(BF)
    delta_up = (delta_hidden * act).astype(BF)
    grads = (mm_tn(rows, delta_gate), mm_tn(rows, delta_up), mm_tn(delta, hidden))
    return delta_gate, delta_up, grads


def near_kernel(slab, group, normed_ref, *refs):
    q_near, od_near, (*grad_qs, grads_out) = refs[:group], refs[group : 2 * group], refs[2 * group :]
    own = od_near[0].shape[0]
    normed = thirds(normed_ref, slab)
    delta_gate, delta_up, grads = query_side(stack(q_near, slice(0, od_near[0].shape[1])), stack(od_near), normed)
    found = (mm_nt(delta_gate, normed[0]) + mm_nt(delta_up, normed[1])).astype(BF)
    for d in range(group):
        grad_qs[d][...] = found[d * own : (d + 1) * own]
    for i in range(3):
        grads_out[i] = grads[i]


def key_kernel(slab, group, w, *refs):
    kvs, (factors, rises, ratio, minus, plus) = refs[:group], refs[group:]
    feat = w.shape[0]
    saved, start, norm_init, norm_saved = columns(w, slab)
    for i in range(3):
        ratio[i : i + 1, :] = norm_init[i] / norm_saved[i]
        minus[i] = saved[i] * (norm_init[i] / (norm_saved[i] * norm_saved[i] * norm_saved[i]))
        plus[i] = start[i] / (norm_init[i] * norm_saved[i])
    init = [w[:, pl.ds((3 + i) * slab, slab)] for i in range(3)]
    keys = stack(kvs, slice(-2 * feat, -feat))
    values = stack(kvs, slice(-feat, None))
    k_gate = mm(keys, init[0])
    k_up = mm(keys, init[1])
    k_proj = mm(values, init[2])
    k_act, k_slope, k_bend = silu_parts(k_gate)
    rises[0] = (k_act * k_up).astype(BF)
    rises[1] = (k_proj * k_up * k_slope).astype(BF)
    rises[2] = (k_proj * k_act).astype(BF)
    factors[0] = k_act
    factors[1] = k_up * k_slope
    factors[2] = k_proj * k_slope
    factors[3] = k_proj * k_up * k_bend


def backward_kernel(
    slab, group, tok_groups, place, w, normed_ref, grads, factors, rises, ratio, minus, plus, *refs
):
    far = group * (tok_groups - 1)
    kvs, pairs, outs, (inner_buf, sums) = refs[:group], refs[group : group + far], refs[group + far : -2], refs[-2:]
    feat = w.shape[0]
    tok_out, outs = outs[0], outs[1:]
    own = tok_out.shape[0]
    normed = thirds(normed_ref, slab)
    total = [grads[i] for i in range(3)]
    for e in range(tok_groups - 1):
        these = pairs[e * group : (e + 1) * group]
        more = query_side(stack(these, slice(feat, 2 * feat)), stack(these, slice(0, feat)), normed)[2]
        total = [total[i] + more[i] for i in range(3)]
        if tok_groups > 2:
            for i in range(3):
                sums[i] = total[i]
            total = [sums[i] for i in range(3)]

    cots, direct = [], []
    once = jnp.where(place[0] == 0, 1.0, 0.0)
    for i in range(3):
        saved = w[:, pl.ds(i * slab, slab)].astype(F32)
        col_dot = jnp.sum(saved * total[i], axis=0, keepdims=True)
        cot = total[i] * ratio[i : i + 1, :] - minus[i] * col_dot
        cots.append(cot.astype(BF))
        direct.append((cot + plus[i] * col_dot) * once)

    init_bf = [w[:, pl.ds((3 + i) * slab, slab)] for i in range(3)]
    keys = stack(kvs, slice(-2 * feat, -feat))
    values = stack(kvs, slice(-feat, None))
    back_gate = mm(keys, cots[0])
    back_up = mm(keys, cots[1])
    back_hidden = mm(values, cots[2])
    back_proj = (back_gate * factors[1] + back_up * factors[0]).astype(BF)
    back_kup = (back_gate * factors[2] + back_hidden * factors[0]).astype(BF)
    back_kgate = (back_gate * factors[3] + (back_up * factors[2] + back_hidden * factors[1])).astype(BF)
    grad_k = (
        mm_nt(rises[1], cots[0])
        + mm_nt(rises[2], cots[1])
        + mm_nt(back_kgate, init_bf[0])
        + mm_nt(back_kup, init_bf[1])
    ).astype(BF)
    grad_v = (mm_nt(rises[0], cots[2]) + mm_nt(back_proj, init_bf[2])).astype(BF)
    inner = (mm_tn(keys, back_kgate), mm_tn(keys, back_kup), mm_tn(values, back_proj))
    whole = jnp.concatenate([inner[i] + direct[i] for i in range(3)], axis=1)
    rows = inner_buf.shape[1]
    for p in range(inner_buf.shape[0]):
        inner_buf[p] = whole[p * rows : (p + 1) * rows]
    tok_out[:, 0:feat] = grad_k[0:own]
    tok_out[:, feat : 2 * feat] = grad_v[0:own]
    outs[0][...] = inner_buf[place[2]].astype(BF)
    for d in range(1, group):
        out, at = outs[d], 0
        for tok in (grad_k, grad_v):
            at = put(out, at, tok[d * own : (d + 1) * own, :])
        put(out, at, inner_buf[place[2] ^ d].astype(BF))
    for dist, out in zip(far_distances(group, tok_groups), outs[group:]):
        for i in range(2):
            out[i * padded(rows) : i * padded(rows) + rows, :] = inner_buf[place[2] ^ dist ^ i].astype(BF)


def relay_kernel(rows, *refs):
    out, step = refs[-1], padded(rows)
    for i, block in enumerate(refs[:-1]):
        out[i * step : i * step + rows, :] = block[step : step + rows, :]


def far_distances(group, tok_groups):
    return [e * group + d for e in range(1, tok_groups) for d in range(0, group, 2)]


def total_of(refs):
    total = refs[0][...].astype(F32)
    for block in refs[1:]:
        total += block[...].astype(F32)
    return total


def tokens_kernel(group, rate, tok, *refs):
    queries, blocks, (gq, gk, gv) = refs[:group], refs[group:-3], refs[-3:]
    _, own, feat = gq.shape
    gq[0] = total_of(queries).astype(BF)
    sums = [tok[:, i * feat : (i + 1) * feat].astype(F32) for i in range(2)]
    for block in blocks:
        at = 0
        for i in range(2):
            more, at = get(block, at, own, feat)
            sums[i] += more.astype(F32)
    gk[0] = sums[0].astype(BF)
    gv[0] = (rate[...] * sums[1]).astype(BF)


def weights_kernel(group, tok_groups, slab, at, place, relayed, inner, *refs):
    blocks, (*outs, buf) = refs[:-4], refs[-4:]
    _, rows, cols = buf.shape
    step = padded(rows)
    buf[0] = inner[...].astype(F32)
    for d in range(1, group):
        buf[d] = get(blocks[d - 1], at, rows, cols)[0].astype(F32)
    for i, dist in enumerate(far_distances(group, tok_groups)):
        d = dist % group
        buf[d] += blocks[group - 1 + i][0:rows, :].astype(F32)
        buf[d ^ 1] += relayed[i * step : i * step + rows, :].astype(F32)
    total = [buf[place[1] ^ j] for j in range(group)]
    for i in range(3):
        outs[i][0] = jnp.concatenate([t[:, i * slab : (i + 1) * slab] for t in total], axis=1)


def make_local(seq_n, head_n, group):
    tok_groups = seq_n // group

    def move(x, dist, axis="seq", size=seq_n):
        return lax.ppermute(x, axis, [(i, i ^ dist) for i in range(size)])

    def near_all(x):
        return [x] + [move(x, d) for d in range(1, group)]

    def mirror(x):
        return [move(x, e * group) for e in range(1, tok_groups)]

    def local(q, k, v, og, rates, gains, gi, ui, di, gs, us, ds):
        _, rows, hidden = gi.shape
        _, own, feat = q.shape
        slab = hidden // group
        near = group * own
        me = lax.axis_index("seq")
        place = jnp.stack((lax.div(me, group), lax.rem(me, group), me)).astype(jnp.int32)

        (packed,) = copying_call(
            functools.partial(weight_pack_kernel, group, slab),
            (arr((seq_n, rows, 6 * slab), BF),),
            (gs, us, ds, gi, ui, di),
            [pltpu.VMEM((6, rows, hidden), BF)],
        )
        packed, queries = lax.optimization_barrier((packed, q[0]))
        wall = lax.all_to_all(packed, "seq", 0, 0, tiled=True).reshape(seq_n * rows, 6 * slab)
        tokens, kv, gg, rate = call(
            token_pack_kernel,
            (arr((own, 3 * feat), BF), arr((own, 2 * feat), BF), arr((own, feat), F32), arr((own, feat), F32)),
            (q, k, v, og, rates, gains),
            8,
        )
        beside = move(tokens, 1) if group > 1 else None
        rest = range(2, group)
        q_near = [queries, beside][:group] + [move(queries, d) for d in rest]
        kv_near = [kv, beside][:group] + [move(kv, d) for d in rest]

        block = arr((own, feat), BF)
        mflop = 2 * near * feat * slab
        *parts, normed = call(
            functools.partial(forward_kernel, slab, group),
            (*(block,) * group, arr((seq_n * rows, 3 * slab), BF)),
            (wall, *q_near),
            24,
            flops=3 * mflop,
        )
        *parts, queries = lax.optimization_barrier((*parts, queries))
        parts = [parts[0]] + [move(parts[d], d) for d in (*range(2, group), *range(1, min(2, group)))]
        q_mirror = mirror(queries)
        *parts, kv_near = lax.optimization_barrier((*parts, kv_near))
        apply_out, sums = call(
            reduce_kernel, (arr((own, feat), F32), arr((2, own), F32)), (gg, *parts), 16
        )
        sums = [sums] + [move(sums, d, "head", head_n) for d in range(1, head_n)]
        sums, q_mirror = lax.optimization_barrier((sums, q_mirror))
        (od,) = call(functools.partial(delta_kernel, head_n * feat), (block,), (apply_out, gg, *sums), 16)
        od_mirror = mirror(od)
        od_near = near_all(od)
        column = arr((3, seq_n * rows, slab), F32)
        factors, rises, *stats = call(
            functools.partial(key_kernel, slab, group),
            (arr((4, near, slab), F32), arr((3, near, slab), BF), arr((3, slab), F32), column, column),
            (wall, *kv_near),
            16,
            flops=12 * mflop,
        )
        *od_mirror, stats[0] = lax.optimization_barrier((*od_mirror, stats[0]))
        pairs = [
            call(pair_kernel, (arr((own, 2 * feat), BF),), pair, 16)[0] for pair in zip(od_mirror, q_mirror)
        ]
        pairs = [x for m in pairs for x in near_all(m)]
        *grad_q, grads = call(
            functools.partial(near_kernel, slab, group),
            (*(block,) * group, arr((3, seq_n * rows, slab), F32)),
            (normed, *q_near, *od_near),
            12,
            flops=60 * mflop,
        )

        q_block = (own, feat)
        grad_q = [grad_q[0]] + [move(grad_q[d], d) for d in (*range(2, group), *range(1, min(2, group)))]
        far = far_distances(group, tok_groups)
        tok, inner, *sends = call(
            functools.partial(backward_kernel, slab, group, tok_groups),
            (
                arr((own, 2 * feat), BF),
                arr((rows, 3 * slab), BF),
                *(message(*(q_block,) * 2, (rows, 3 * slab)),) * (group - 1),
                *(arr((2 * padded(rows), 3 * slab), BF),) * len(far),
            ),
            (place, wall, normed, grads, factors, rises, *stats, *kv_near, *pairs),
            24,
            smem=1,
            flops=120 * mflop,
            scratch=[
                pltpu.VMEM((seq_n, rows, 3 * slab), F32),
                pltpu.VMEM((3, seq_n * rows, slab), F32),
            ],
        )
        sends, grad_q = lax.optimization_barrier((sends, grad_q))
        near_got = {d: move(sends[d - 1], d) for d in (*range(2, group), *range(1, min(2, group)))}
        near_got = [near_got[d] for d in range(1, group)]
        far_got = [move(x, d) for x, d in zip(sends[group - 1 :], far)]
        (relayed,) = call(
            functools.partial(relay_kernel, rows),
            (arr((len(far) * padded(rows), 3 * slab), BF),),
            far_got,
            16,
            flops=12 * mflop,
        )
        relayed = move(relayed, 1)
        out_tok = arr((1, own, feat), BF)
        grad_w = arr((1, rows, hidden), F32)
        grads_t = call(
            functools.partial(tokens_kernel, group), (out_tok,) * 3, (rate, tok, *grad_q, *near_got), 16
        )
        relayed, grads_t = lax.optimization_barrier((relayed, grads_t))
        at = 2 * tiles(feat) * padded(own)
        grads_w = call(
            functools.partial(weights_kernel, group, tok_groups, slab, at),
            (grad_w,) * 3,
            (place, relayed, inner, *near_got, *far_got),
            16,
            smem=1,
            scratch=[pltpu.VMEM((group, rows, 3 * slab), F32)],
        )
        return (*grads_t, *grads_w)

    return local


def solution(mesh):
    seq_n = mesh.shape["seq"]
    head_n = mesh.shape["head"]
    group = min(4, seq_n)
    tok = P("head", "seq", None)
    return jax.shard_map(
        make_local(seq_n, head_n, group),
        mesh=mesh,
        in_specs=(tok, tok, tok, tok, P("head", "seq"), P("head", None), tok, tok, tok, tok, tok, tok),
        out_specs=(tok, tok, tok, tok, tok, tok),
        check_vma=False,
    )
```

```python
import functools

import jax
import jax.numpy as jnp
from jax import lax
from jax.experimental import pallas as pl
from jax.experimental.pallas import tpu as pltpu
from jax.sharding import PartitionSpec as P

EPS_COL = 1e-06
EPS_ROOT = 1e-05
BF = jnp.bfloat16
F32 = jnp.float32
LANES = 128
VMEM = pl.BlockSpec(memory_space=pltpu.VMEM)
SMEM = pl.BlockSpec(memory_space=pltpu.SMEM)


def silu_parts(pre_act):
    sigmoid_val = jax.nn.sigmoid(pre_act)
    silu_val = pre_act * sigmoid_val
    silu_slope = sigmoid_val * (1.0 + pre_act * (1.0 - sigmoid_val))
    silu_bend = sigmoid_val * (1.0 - sigmoid_val) * (2.0 + pre_act * (1.0 - 2.0 * sigmoid_val))
    return (silu_val, silu_slope, silu_bend)


def mm(left_op, right_op):
    return jnp.dot(left_op, right_op, preferred_element_type=F32)


def mm_nt(left_op, right_op):
    return lax.dot_general(left_op, right_op, (((1,), (1,)), ((), ())), preferred_element_type=F32)


def mm_tn(left_op, right_op):
    return lax.dot_general(left_op, right_op, (((0,), (0,)), ((), ())), preferred_element_type=F32)


def column_norm(weight):
    return jnp.sqrt(jnp.sum(weight * weight, axis=0, keepdims=True) + EPS_COL)


def flat(x):
    return x.reshape(-1, x.shape[-1])


def call(kernel, outs, args, mib, smem=0, flops=0, scratch=()):
    moved = sum(x.size * x.dtype.itemsize for x in (*args, *outs))
    return pl.pallas_call(
        kernel,
        out_shape=outs,
        in_specs=[SMEM] * smem + [VMEM] * (len(args) - smem),
        out_specs=[VMEM] * len(outs),
        scratch_shapes=scratch,
        compiler_params=pltpu.CompilerParams(vmem_limit_bytes=mib << 20),
        cost_estimate=pl.CostEstimate(flops=flops, bytes_accessed=moved, transcendentals=0),
    )(*args)


def copying_call(kernel, outs, args, buffers):
    return pl.pallas_call(
        kernel,
        out_shape=outs,
        in_specs=[pl.BlockSpec(memory_space=pltpu.HBM)] * len(args),
        out_specs=[VMEM] * len(outs),
        scratch_shapes=[*buffers, pltpu.SemaphoreType.DMA((len(args),))],
        compiler_params=pltpu.CompilerParams(vmem_limit_bytes=56 << 20),
    )(*args)


def arr(shape, dtype):
    return jax.ShapeDtypeStruct(shape, dtype)


def padded(rows):
    return -(-rows // 16) * 16


def tiles(cols):
    return -(-cols // LANES)


def put(out, at, value):
    rows, cols = value.shape
    for t in range(tiles(cols)):
        wide = min(LANES, cols - t * LANES)
        out[at : at + rows, 0:wide] = value[:, t * LANES : t * LANES + wide]
        at += padded(rows)
    return at


def get(ref, at, rows, cols):
    parts = []
    for t in range(tiles(cols)):
        wide = min(LANES, cols - t * LANES)
        parts.append(ref[at : at + rows, 0:wide])
        at += padded(rows)
    return jnp.concatenate(parts, axis=1), at


def message(*blocks):
    return arr((sum(tiles(cols) * padded(rows) for rows, cols in blocks), LANES), BF)


def token_pack_kernel(q, k, v, og, rates, gains, all_out, kv_out, gg_out, rate_out):
    tokens, feat = gg_out.shape
    rate = jnp.broadcast_to(rates[...], (feat, tokens)).T
    values = (rate * v[0].astype(F32)).astype(BF)
    all_out[:, 0:feat] = q[0]
    all_out[:, feat : 2 * feat] = k[0]
    all_out[:, 2 * feat : 3 * feat] = values
    kv_out[:, 0:feat] = k[0]
    kv_out[:, feat : 2 * feat] = values
    gg_out[...] = gains[...] * og[0].astype(F32)
    rate_out[...] = rate


def weight_pack_kernel(group, slab, *refs):
    args, (w_out, buf, sems) = refs[:6], refs[6:]
    copies = [pltpu.make_async_copy(args[i], buf.at[pl.ds(i, 1)], sems.at[i]) for i in range(6)]
    for copy in copies:
        copy.start()
    for i, copy in enumerate(copies):
        copy.wait()
        for j in range(group):
            block = buf[i, :, j * slab : (j + 1) * slab]
            for p in range(j, w_out.shape[0], group):
                w_out[p, :, i * slab : (i + 1) * slab] = block


def columns(w, slab):
    parts = [w[:, pl.ds(i * slab, slab)].astype(F32) for i in range(6)]
    saved, init = parts[:3], parts[3:]
    return saved, init, [column_norm(x) for x in init], [column_norm(x) for x in saved]


def stack(refs, cols=slice(None)):
    return jnp.concatenate([r[:, cols] for r in refs], axis=0)


def thirds(x, slab):
    return [x[:, pl.ds(i * slab, slab)] for i in range(3)]


def forward_kernel(slab, group, w, *refs):
    queries, parts, normed_out = refs[:group], refs[group:-1], refs[-1]
    own, feat = parts[0].shape
    saved, init, norm_init, norm_saved = columns(w, slab)
    normed = [(saved[i] * (norm_init[i] / norm_saved[i])).astype(BF) for i in range(3)]
    rows = stack(queries, slice(0, feat))
    hidden = (silu_parts(mm(rows, normed[0]))[0] * mm(rows, normed[1])).astype(BF)
    out = mm_nt(hidden, normed[2]).astype(BF)
    for d in range(group):
        parts[d][...] = out[d * own : (d + 1) * own]
    normed_out[...] = jnp.concatenate(normed, axis=1)


def reduce_kernel(gg, *refs):
    parts, (apply_out, sums) = refs[:-2], refs[-2:]
    total = total_of(parts)
    apply_out[...] = total
    sums[0:1, :] = jnp.sum((total * total).T, axis=0, keepdims=True)
    sums[1:2, :] = jnp.sum((total * gg[...]).T, axis=0, keepdims=True)


def delta_kernel(width, apply_out, gg, *refs):
    sums, out = refs[:-1], refs[-1]
    tokens, feat = apply_out.shape
    total = sums[0][...]
    for more in sums[1:]:
        total += more[...]
    square = jnp.broadcast_to(total[0:1, :], (feat, tokens)).T
    gain = jnp.broadcast_to(total[1:2, :], (feat, tokens)).T
    root = jnp.sqrt(square / width + EPS_ROOT)
    out[...] = (gg[...] / root - apply_out[...] * (gain / width) / (root * root * root)).astype(BF)


def pair_kernel(left, right, out):
    feat = left.shape[1]
    out[:, 0:feat] = left[...]
    out[:, feat : 2 * feat] = right[...]


def query_side(rows, delta, normed):
    q_gate = mm(rows, normed[0])
    q_up = mm(rows, normed[1])
    act, slope, _ = silu_parts(q_gate)
    hidden = (act * q_up).astype(BF)
    delta_hidden = mm(delta, normed[2])
    delta_gate = (delta_hidden * q_up * slope).astype(BF)
    delta_up = (delta_hidden * act).astype(BF)
    grads = (mm_tn(rows, delta_gate), mm_tn(rows, delta_up), mm_tn(delta, hidden))
    return delta_gate, delta_up, grads


def near_kernel(slab, group, normed_ref, *refs):
    q_near, od_near, (*grad_qs, grads_out) = refs[:group], refs[group : 2 * group], refs[2 * group :]
    own = od_near[0].shape[0]
    normed = thirds(normed_ref, slab)
    delta_gate, delta_up, grads = query_side(stack(q_near, slice(0, od_near[0].shape[1])), stack(od_near), normed)
    found = (mm_nt(delta_gate, normed[0]) + mm_nt(delta_up, normed[1])).astype(BF)
    for d in range(group):
        grad_qs[d][...] = found[d * own : (d + 1) * own]
    for i in range(3):
        grads_out[i] = grads[i]


def key_kernel(slab, group, w, *refs):
    kvs, (factors, rises, ratio, minus, plus) = refs[:group], refs[group:]
    feat = w.shape[0]
    saved, start, norm_init, norm_saved = columns(w, slab)
    for i in range(3):
        ratio[i : i + 1, :] = norm_init[i] / norm_saved[i]
        minus[i] = saved[i] * (norm_init[i] / (norm_saved[i] * norm_saved[i] * norm_saved[i]))
        plus[i] = start[i] / (norm_init[i] * norm_saved[i])
    init = [w[:, pl.ds((3 + i) * slab, slab)] for i in range(3)]
    keys = stack(kvs, slice(-2 * feat, -feat))
    values = stack(kvs, slice(-feat, None))
    k_gate = mm(keys, init[0])
    k_up = mm(keys, init[1])
    k_proj = mm(values, init[2])
    k_act, k_slope, k_bend = silu_parts(k_gate)
    rises[0] = (k_act * k_up).astype(BF)
    rises[1] = (k_proj * k_up * k_slope).astype(BF)
    rises[2] = (k_proj * k_act).astype(BF)
    factors[0] = k_act
    factors[1] = k_up * k_slope
    factors[2] = k_proj * k_slope
    factors[3] = k_proj * k_up * k_bend


def backward_kernel(
    slab, group, tok_groups, place, w, normed_ref, grads, factors, rises, ratio, minus, plus, *refs
):
    far = group * (tok_groups - 1)
    kvs, pairs, outs, (inner_buf, sums) = refs[:group], refs[group : group + far], refs[group + far : -2], refs[-2:]
    feat = w.shape[0]
    tok_out, outs = outs[0], outs[1:]
    own = tok_out.shape[0]
    normed = thirds(normed_ref, slab)
    total = [grads[i] for i in range(3)]
    for e in range(tok_groups - 1):
        these = pairs[e * group : (e + 1) * group]
        more = query_side(stack(these, slice(feat, 2 * feat)), stack(these, slice(0, feat)), normed)[2]
        total = [total[i] + more[i] for i in range(3)]
        if tok_groups > 2:
            for i in range(3):
                sums[i] = total[i]
            total = [sums[i] for i in range(3)]

    cots, direct = [], []
    once = jnp.where(place[0] == 0, 1.0, 0.0)
    for i in range(3):
        saved = w[:, pl.ds(i * slab, slab)].astype(F32)
        col_dot = jnp.sum(saved * total[i], axis=0, keepdims=True)
        cot = total[i] * ratio[i : i + 1, :] - minus[i] * col_dot
        cots.append(cot.astype(BF))
        direct.append((cot + plus[i] * col_dot) * once)

    init_bf = [w[:, pl.ds((3 + i) * slab, slab)] for i in range(3)]
    keys = stack(kvs, slice(-2 * feat, -feat))
    values = stack(kvs, slice(-feat, None))
    back_gate = mm(keys, cots[0])
    back_up = mm(keys, cots[1])
    back_hidden = mm(values, cots[2])
    back_proj = (back_gate * factors[1] + back_up * factors[0]).astype(BF)
    back_kup = (back_gate * factors[2] + back_hidden * factors[0]).astype(BF)
    back_kgate = (back_gate * factors[3] + (back_up * factors[2] + back_hidden * factors[1])).astype(BF)
    grad_k = (
        mm_nt(rises[1], cots[0])
        + mm_nt(rises[2], cots[1])
        + mm_nt(back_kgate, init_bf[0])
        + mm_nt(back_kup, init_bf[1])
    ).astype(BF)
    grad_v = (mm_nt(rises[0], cots[2]) + mm_nt(back_proj, init_bf[2])).astype(BF)
    inner = (mm_tn(keys, back_kgate), mm_tn(keys, back_kup), mm_tn(values, back_proj))
    whole = jnp.concatenate([inner[i] + direct[i] for i in range(3)], axis=1)
    rows = inner_buf.shape[1]
    for p in range(inner_buf.shape[0]):
        inner_buf[p] = whole[p * rows : (p + 1) * rows]
    tok_out[:, 0:feat] = grad_k[0:own]
    tok_out[:, feat : 2 * feat] = grad_v[0:own]
    outs[0][...] = inner_buf[place[2]].astype(BF)
    for d in range(1, group):
        out, at = outs[d], 0
        for tok in (grad_k, grad_v):
            at = put(out, at, tok[d * own : (d + 1) * own, :])
        put(out, at, inner_buf[place[2] ^ d].astype(BF))
    for dist, out in zip(far_distances(group, tok_groups), outs[group:]):
        for i in range(2):
            out[i * padded(rows) : i * padded(rows) + rows, :] = inner_buf[place[2] ^ dist ^ i].astype(BF)


def relay_kernel(rows, *refs):
    out, step = refs[-1], padded(rows)
    for i, block in enumerate(refs[:-1]):
        out[i * step : i * step + rows, :] = block[step : step + rows, :]


def far_distances(group, tok_groups):
    return [e * group + d for e in range(1, tok_groups) for d in range(0, group, 2)]


def total_of(refs):
    total = refs[0][...].astype(F32)
    for block in refs[1:]:
        total += block[...].astype(F32)
    return total


def tokens_kernel(group, rate, tok, *refs):
    queries, blocks, (gq, gk, gv) = refs[:group], refs[group:-3], refs[-3:]
    _, own, feat = gq.shape
    gq[0] = total_of(queries).astype(BF)
    sums = [tok[:, i * feat : (i + 1) * feat].astype(F32) for i in range(2)]
    for block in blocks:
        at = 0
        for i in range(2):
            more, at = get(block, at, own, feat)
            sums[i] += more.astype(F32)
    gk[0] = sums[0].astype(BF)
    gv[0] = (rate[...] * sums[1]).astype(BF)


def final_kernel(group, tok_groups, slab, at, place, rate, tok, relayed, inner, *refs):
    queries, blocks, outs, buf = refs[:group], refs[group:-7], refs[-7:-1], refs[-1]
    tokens_kernel(group, rate, tok, *queries, *blocks[: group - 1], *outs[:3])
    _, rows, cols = buf.shape
    step = padded(rows)
    buf[0] = inner[...].astype(F32)
    for d in range(1, group):
        buf[d] = get(blocks[d - 1], at, rows, cols)[0].astype(F32)
    for i, dist in enumerate(far_distances(group, tok_groups)):
        d = dist % group
        buf[d] += blocks[group - 1 + i][0:rows, :].astype(F32)
        buf[d ^ 1] += relayed[i * step : i * step + rows, :].astype(F32)
    total = [buf[place[1] ^ j] for j in range(group)]
    for i in range(3):
        outs[3 + i][0] = jnp.concatenate([t[:, i * slab : (i + 1) * slab] for t in total], axis=1)


def make_local(seq_n, head_n, group):
    tok_groups = seq_n // group

    def move(x, dist, axis="seq", size=seq_n):
        return lax.ppermute(x, axis, [(i, i ^ dist) for i in range(size)])

    def near_all(x):
        return [x] + [move(x, d) for d in range(1, group)]

    def mirror(x):
        return [move(x, e * group) for e in range(1, tok_groups)]

    def local(q, k, v, og, rates, gains, gi, ui, di, gs, us, ds):
        _, rows, hidden = gi.shape
        _, own, feat = q.shape
        slab = hidden // group
        near = group * own
        me = lax.axis_index("seq")
        place = jnp.stack((lax.div(me, group), lax.rem(me, group), me)).astype(jnp.int32)

        (packed,) = copying_call(
            functools.partial(weight_pack_kernel, group, slab),
            (arr((seq_n, rows, 6 * slab), BF),),
            (gs, us, ds, gi, ui, di),
            [pltpu.VMEM((6, rows, hidden), BF)],
        )
        packed, queries = lax.optimization_barrier((packed, q[0]))
        wall = lax.all_to_all(packed, "seq", 0, 0, tiled=True).reshape(seq_n * rows, 6 * slab)
        tokens, kv, gg, rate = call(
            token_pack_kernel,
            (arr((own, 3 * feat), BF), arr((own, 2 * feat), BF), arr((own, feat), F32), arr((own, feat), F32)),
            (q, k, v, og, rates, gains),
            8,
        )
        beside = move(tokens, 1) if group > 1 else None
        rest = range(2, group)
        q_near = [queries, beside][:group] + [move(queries, d) for d in rest]
        kv_near = [kv, beside][:group] + [move(kv, d) for d in rest]

        block = arr((own, feat), BF)
        mflop = 2 * near * feat * slab
        *parts, normed = call(
            functools.partial(forward_kernel, slab, group),
            (*(block,) * group, arr((seq_n * rows, 3 * slab), BF)),
            (wall, *q_near),
            24,
            flops=3 * mflop,
        )
        *parts, queries = lax.optimization_barrier((*parts, queries))
        parts = [parts[0]] + [move(parts[d], d) for d in (*range(2, group), *range(1, min(2, group)))]
        q_mirror = mirror(queries)
        *parts, kv_near = lax.optimization_barrier((*parts, kv_near))
        apply_out, sums = call(
            reduce_kernel, (arr((own, feat), F32), arr((2, own), F32)), (gg, *parts), 16
        )
        sums = [sums] + [move(sums, d, "head", head_n) for d in range(1, head_n)]
        sums, q_mirror = lax.optimization_barrier((sums, q_mirror))
        (od,) = call(functools.partial(delta_kernel, head_n * feat), (block,), (apply_out, gg, *sums), 16)
        od_mirror = mirror(od)
        od_near = near_all(od)
        column = arr((3, seq_n * rows, slab), F32)
        factors, rises, *stats = call(
            functools.partial(key_kernel, slab, group),
            (arr((4, near, slab), F32), arr((3, near, slab), BF), arr((3, slab), F32), column, column),
            (wall, *kv_near),
            16,
            flops=12 * mflop,
        )
        *od_mirror, stats[0] = lax.optimization_barrier((*od_mirror, stats[0]))
        pairs = [
            call(pair_kernel, (arr((own, 2 * feat), BF),), pair, 16)[0] for pair in zip(od_mirror, q_mirror)
        ]
        pairs = [x for m in pairs for x in near_all(m)]
        *grad_q, grads = call(
            functools.partial(near_kernel, slab, group),
            (*(block,) * group, arr((3, seq_n * rows, slab), F32)),
            (normed, *q_near, *od_near),
            12,
            flops=60 * mflop,
        )

        q_block = (own, feat)
        grad_q = [grad_q[0]] + [move(grad_q[d], d) for d in (*range(2, group), *range(1, min(2, group)))]
        far = far_distances(group, tok_groups)
        tok, inner, *sends = call(
            functools.partial(backward_kernel, slab, group, tok_groups),
            (
                arr((own, 2 * feat), BF),
                arr((rows, 3 * slab), BF),
                *(message(*(q_block,) * 2, (rows, 3 * slab)),) * (group - 1),
                *(arr((2 * padded(rows), 3 * slab), BF),) * len(far),
            ),
            (place, wall, normed, grads, factors, rises, *stats, *kv_near, *pairs),
            24,
            smem=1,
            flops=120 * mflop,
            scratch=[
                pltpu.VMEM((seq_n, rows, 3 * slab), F32),
                pltpu.VMEM((3, seq_n * rows, slab), F32),
            ],
        )
        sends, grad_q = lax.optimization_barrier((sends, grad_q))
        near_got = {d: move(sends[d - 1], d) for d in (*range(2, group), *range(1, min(2, group)))}
        near_got = [near_got[d] for d in range(1, group)]
        far_got = [move(x, d) for x, d in zip(sends[group - 1 :], far)]
        (relayed,) = call(
            functools.partial(relay_kernel, rows),
            (arr((len(far) * padded(rows), 3 * slab), BF),),
            far_got,
            16,
            flops=12 * mflop,
        )
        relayed = move(relayed, 1)
        out_tok = arr((1, own, feat), BF)
        grad_w = arr((1, rows, hidden), F32)
        at = 2 * tiles(feat) * padded(own)
        return call(
            functools.partial(final_kernel, group, tok_groups, slab, at),
            (*(out_tok,) * 3, *(grad_w,) * 3),
            (place, rate, tok, relayed, inner, *grad_q, *near_got, *far_got),
            16,
            smem=1,
            scratch=[pltpu.VMEM((group, rows, 3 * slab), F32)],
        )

    return local


def solution(mesh):
    seq_n = mesh.shape["seq"]
    head_n = mesh.shape["head"]
    group = min(4, seq_n)
    tok = P("head", "seq", None)
    return jax.shard_map(
        make_local(seq_n, head_n, group),
        mesh=mesh,
        in_specs=(tok, tok, tok, tok, P("head", "seq"), P("head", None), tok, tok, tok, tok, tok, tok),
        out_specs=(tok, tok, tok, tok, tok, tok),
        check_vma=False,
    )
```

```python
import functools

import jax
import jax.numpy as jnp
from jax import lax
from jax.experimental import pallas as pl
from jax.experimental.pallas import tpu as pltpu
from jax.sharding import PartitionSpec as P

EPS_COL = 1e-06
EPS_ROOT = 1e-05
BF = jnp.bfloat16
F32 = jnp.float32
LANES = 128
VMEM = pl.BlockSpec(memory_space=pltpu.VMEM)
SMEM = pl.BlockSpec(memory_space=pltpu.SMEM)


def silu_parts(pre_act):
    sigmoid_val = jax.nn.sigmoid(pre_act)
    silu_val = pre_act * sigmoid_val
    silu_slope = sigmoid_val * (1.0 + pre_act * (1.0 - sigmoid_val))
    silu_bend = sigmoid_val * (1.0 - sigmoid_val) * (2.0 + pre_act * (1.0 - 2.0 * sigmoid_val))
    return (silu_val, silu_slope, silu_bend)


def mm(left_op, right_op):
    return jnp.dot(left_op, right_op, preferred_element_type=F32)


def mm_nt(left_op, right_op):
    return lax.dot_general(left_op, right_op, (((1,), (1,)), ((), ())), preferred_element_type=F32)


def mm_tn(left_op, right_op):
    return lax.dot_general(left_op, right_op, (((0,), (0,)), ((), ())), preferred_element_type=F32)


def column_norm(weight):
    return jnp.sqrt(jnp.sum(weight * weight, axis=0, keepdims=True) + EPS_COL)


def flat(x):
    return x.reshape(-1, x.shape[-1])


def call(kernel, outs, args, mib, smem=0, flops=0, scratch=()):
    moved = sum(x.size * x.dtype.itemsize for x in (*args, *outs))
    return pl.pallas_call(
        kernel,
        out_shape=outs,
        in_specs=[SMEM] * smem + [VMEM] * (len(args) - smem),
        out_specs=[VMEM] * len(outs),
        scratch_shapes=scratch,
        compiler_params=pltpu.CompilerParams(vmem_limit_bytes=mib << 20),
        cost_estimate=pl.CostEstimate(flops=flops, bytes_accessed=moved, transcendentals=0),
    )(*args)


def copying_call(kernel, outs, args, buffers):
    return pl.pallas_call(
        kernel,
        out_shape=outs,
        in_specs=[pl.BlockSpec(memory_space=pltpu.HBM)] * len(args),
        out_specs=[VMEM] * len(outs),
        scratch_shapes=[*buffers, pltpu.SemaphoreType.DMA((len(args),))],
        compiler_params=pltpu.CompilerParams(vmem_limit_bytes=56 << 20),
    )(*args)


def arr(shape, dtype):
    return jax.ShapeDtypeStruct(shape, dtype)


def fetch(sources, buffers, sems):
    copies = [pltpu.make_async_copy(s, b, sems.at[i]) for i, (s, b) in enumerate(zip(sources, buffers))]
    for copy in copies:
        copy.start()
    for copy in copies:
        copy.wait()


def padded(rows):
    return -(-rows // 16) * 16


def tiles(cols):
    return -(-cols // LANES)


def put(out, at, value):
    rows, cols = value.shape
    for t in range(tiles(cols)):
        wide = min(LANES, cols - t * LANES)
        out[at : at + rows, 0:wide] = value[:, t * LANES : t * LANES + wide]
        at += padded(rows)
    return at


def get(ref, at, rows, cols):
    parts = []
    for t in range(tiles(cols)):
        wide = min(LANES, cols - t * LANES)
        parts.append(ref[at : at + rows, 0:wide])
        at += padded(rows)
    return jnp.concatenate(parts, axis=1), at


def message(*blocks):
    return arr((sum(tiles(cols) * padded(rows) for rows, cols in blocks), LANES), BF)


def token_pack_kernel(q, k, v, og, rates, gains, all_out, kv_out, gg_out, rate_out):
    tokens, feat = gg_out.shape
    rate = jnp.broadcast_to(rates[...], (feat, tokens)).T
    values = (rate * v[0].astype(F32)).astype(BF)
    all_out[:, 0:feat] = q[0]
    all_out[:, feat : 2 * feat] = k[0]
    all_out[:, 2 * feat : 3 * feat] = values
    kv_out[:, 0:feat] = k[0]
    kv_out[:, feat : 2 * feat] = values
    gg_out[...] = gains[...] * og[0].astype(F32)
    rate_out[...] = rate


def weight_pack_kernel(group, slab, *refs):
    args, (w_out, buf, sems) = refs[:6], refs[6:]
    fetch(args, [buf.at[pl.ds(i, 1)] for i in range(6)], sems)
    for j in range(group):
        cols = pl.ds(j * slab, slab)
        block = jnp.concatenate([buf[i, :, cols] for i in range(6)], axis=1)
        for p in range(j, w_out.shape[0], group):
            w_out[p] = block


def columns(w, slab):
    parts = [w[:, pl.ds(i * slab, slab)].astype(F32) for i in range(6)]
    saved, init = parts[:3], parts[3:]
    return saved, init, [column_norm(x) for x in init], [column_norm(x) for x in saved]


def stack(refs, cols=slice(None)):
    return jnp.concatenate([r[:, cols] for r in refs], axis=0)


def thirds(x, slab):
    return [x[:, pl.ds(i * slab, slab)] for i in range(3)]


def forward_kernel(slab, group, w, *refs):
    queries, parts, normed_out = refs[:group], refs[group:-1], refs[-1]
    own, feat = parts[0].shape
    saved, init, norm_init, norm_saved = columns(w, slab)
    normed = [(saved[i] * (norm_init[i] / norm_saved[i])).astype(BF) for i in range(3)]
    rows = stack(queries, slice(0, feat))
    hidden = (silu_parts(mm(rows, normed[0]))[0] * mm(rows, normed[1])).astype(BF)
    out = mm_nt(hidden, normed[2]).astype(BF)
    for d in range(group):
        parts[d][...] = out[d * own : (d + 1) * own]
    normed_out[...] = jnp.concatenate(normed, axis=1)


def reduce_kernel(gg, *refs):
    parts, (apply_out, sums) = refs[:-2], refs[-2:]
    total = total_of(parts)
    apply_out[...] = total
    sums[0:1, :] = jnp.sum((total * total).T, axis=0, keepdims=True)
    sums[1:2, :] = jnp.sum((total * gg[...]).T, axis=0, keepdims=True)


def delta_kernel(width, apply_out, gg, *refs):
    sums, out = refs[:-1], refs[-1]
    tokens, feat = apply_out.shape
    total = sums[0][...]
    for more in sums[1:]:
        total += more[...]
    square = jnp.broadcast_to(total[0:1, :], (feat, tokens)).T
    gain = jnp.broadcast_to(total[1:2, :], (feat, tokens)).T
    root = jnp.sqrt(square / width + EPS_ROOT)
    out[...] = (gg[...] / root - apply_out[...] * (gain / width) / (root * root * root)).astype(BF)


def pair_kernel(left, right, out):
    feat = left.shape[1]
    out[:, 0:feat] = left[...]
    out[:, feat : 2 * feat] = right[...]


def query_side(rows, delta, normed):
    q_gate = mm(rows, normed[0])
    q_up = mm(rows, normed[1])
    act, slope, _ = silu_parts(q_gate)
    hidden = (act * q_up).astype(BF)
    delta_hidden = mm(delta, normed[2])
    delta_gate = (delta_hidden * q_up * slope).astype(BF)
    delta_up = (delta_hidden * act).astype(BF)
    grads = (mm_tn(rows, delta_gate), mm_tn(rows, delta_up), mm_tn(delta, hidden))
    return delta_gate, delta_up, grads


def near_kernel(slab, group, normed_ref, *refs):
    q_near, od_near, (*grad_qs, grads_out) = refs[:group], refs[group : 2 * group], refs[2 * group :]
    own = od_near[0].shape[0]
    normed = thirds(normed_ref, slab)
    delta_gate, delta_up, grads = query_side(stack(q_near, slice(0, od_near[0].shape[1])), stack(od_near), normed)
    found = (mm_nt(delta_gate, normed[0]) + mm_nt(delta_up, normed[1])).astype(BF)
    for d in range(group):
        grad_qs[d][...] = found[d * own : (d + 1) * own]
    for i in range(3):
        grads_out[i] = grads[i]


def key_kernel(slab, group, w, *refs):
    kvs, (factors, rises, ratio, minus, plus) = refs[:group], refs[group:]
    feat = w.shape[0]
    saved, start, norm_init, norm_saved = columns(w, slab)
    for i in range(3):
        ratio[i : i + 1, :] = norm_init[i] / norm_saved[i]
        minus[i] = saved[i] * (norm_init[i] / (norm_saved[i] * norm_saved[i] * norm_saved[i]))
        plus[i] = start[i] / (norm_init[i] * norm_saved[i])
    init = [w[:, pl.ds((3 + i) * slab, slab)] for i in range(3)]
    keys = stack(kvs, slice(-2 * feat, -feat))
    values = stack(kvs, slice(-feat, None))
    k_gate = mm(keys, init[0])
    k_up = mm(keys, init[1])
    k_proj = mm(values, init[2])
    k_act, k_slope, k_bend = silu_parts(k_gate)
    rises[0] = (k_act * k_up).astype(BF)
    rises[1] = (k_proj * k_up * k_slope).astype(BF)
    rises[2] = (k_proj * k_act).astype(BF)
    factors[0] = k_act
    factors[1] = k_up * k_slope
    factors[2] = k_proj * k_slope
    factors[3] = k_proj * k_up * k_bend


def backward_kernel(
    slab, group, tok_groups, place, w, normed_ref, grads, factors, rises, ratio, minus, plus, *refs
):
    far = group * (tok_groups - 1)
    kvs, pairs, outs, (inner_buf, sums) = refs[:group], refs[group : group + far], refs[group + far : -2], refs[-2:]
    feat = w.shape[0]
    tok_out, outs = outs[0], outs[1:]
    own = tok_out.shape[0]
    normed = thirds(normed_ref, slab)
    total = [grads[i] for i in range(3)]
    for e in range(tok_groups - 1):
        these = pairs[e * group : (e + 1) * group]
        more = query_side(stack(these, slice(feat, 2 * feat)), stack(these, slice(0, feat)), normed)[2]
        total = [total[i] + more[i] for i in range(3)]
        if tok_groups > 2:
            for i in range(3):
                sums[i] = total[i]
            total = [sums[i] for i in range(3)]

    cots, direct = [], []
    once = jnp.where(place[0] == 0, 1.0, 0.0)
    for i in range(3):
        saved = w[:, pl.ds(i * slab, slab)].astype(F32)
        col_dot = jnp.sum(saved * total[i], axis=0, keepdims=True)
        cot = total[i] * ratio[i : i + 1, :] - minus[i] * col_dot
        cots.append(cot.astype(BF))
        direct.append((cot + plus[i] * col_dot) * once)

    init_bf = [w[:, pl.ds((3 + i) * slab, slab)] for i in range(3)]
    keys = stack(kvs, slice(-2 * feat, -feat))
    values = stack(kvs, slice(-feat, None))
    back_gate = mm(keys, cots[0])
    back_up = mm(keys, cots[1])
    back_hidden = mm(values, cots[2])
    back_proj = (back_gate * factors[1] + back_up * factors[0]).astype(BF)
    back_kup = (back_gate * factors[2] + back_hidden * factors[0]).astype(BF)
    back_kgate = (back_gate * factors[3] + (back_up * factors[2] + back_hidden * factors[1])).astype(BF)
    grad_k = (
        mm_nt(rises[1], cots[0])
        + mm_nt(rises[2], cots[1])
        + mm_nt(back_kgate, init_bf[0])
        + mm_nt(back_kup, init_bf[1])
    ).astype(BF)
    grad_v = (mm_nt(rises[0], cots[2]) + mm_nt(back_proj, init_bf[2])).astype(BF)
    inner = (mm_tn(keys, back_kgate), mm_tn(keys, back_kup), mm_tn(values, back_proj))
    whole = jnp.concatenate([inner[i] + direct[i] for i in range(3)], axis=1)
    rows = inner_buf.shape[1]
    for p in range(inner_buf.shape[0]):
        inner_buf[p] = whole[p * rows : (p + 1) * rows]
    tok_out[:, 0:feat] = grad_k[0:own]
    tok_out[:, feat : 2 * feat] = grad_v[0:own]
    outs[0][...] = inner_buf[place[2]].astype(BF)
    for d in range(1, group):
        out, at = outs[d], 0
        for tok in (grad_k, grad_v):
            at = put(out, at, tok[d * own : (d + 1) * own, :])
        put(out, at, inner_buf[place[2] ^ d].astype(BF))
    for dist, out in zip(far_distances(group, tok_groups), outs[group:]):
        for i in range(2):
            out[i * padded(rows) : i * padded(rows) + rows, :] = inner_buf[place[2] ^ dist ^ i].astype(BF)


def relay_kernel(rows, *refs):
    out, step = refs[-1], padded(rows)
    for i, block in enumerate(refs[:-1]):
        out[i * step : i * step + rows, :] = block[step : step + rows, :]


def far_distances(group, tok_groups):
    return [e * group + d for e in range(1, tok_groups) for d in range(0, group, 2)]


def total_of(refs):
    total = refs[0][...].astype(F32)
    for block in refs[1:]:
        total += block[...].astype(F32)
    return total


def tokens_kernel(group, rate, tok, *refs):
    queries, blocks, (gq, gk, gv) = refs[:group], refs[group:-3], refs[-3:]
    _, own, feat = gq.shape
    gq[0] = total_of(queries).astype(BF)
    sums = [tok[:, i * feat : (i + 1) * feat].astype(F32) for i in range(2)]
    for block in blocks:
        at = 0
        for i in range(2):
            more, at = get(block, at, own, feat)
            sums[i] += more.astype(F32)
    gk[0] = sums[0].astype(BF)
    gv[0] = (rate[...] * sums[1]).astype(BF)


def weights_kernel(group, tok_groups, slab, at, place, relayed, inner, *refs):
    blocks, (*outs, buf) = refs[:-4], refs[-4:]
    _, rows, cols = buf.shape
    step = padded(rows)
    buf[0] = inner[...].astype(F32)
    for d in range(1, group):
        buf[d] = get(blocks[d - 1], at, rows, cols)[0].astype(F32)
    for i, dist in enumerate(far_distances(group, tok_groups)):
        d = dist % group
        buf[d] += blocks[group - 1 + i][0:rows, :].astype(F32)
        buf[d ^ 1] += relayed[i * step : i * step + rows, :].astype(F32)
    total = [buf[place[1] ^ j] for j in range(group)]
    for i in range(3):
        outs[i][0] = jnp.concatenate([t[:, i * slab : (i + 1) * slab] for t in total], axis=1)


def make_local(seq_n, head_n, group):
    tok_groups = seq_n // group

    def move(x, dist, axis="seq", size=seq_n):
        return lax.ppermute(x, axis, [(i, i ^ dist) for i in range(size)])

    def near_all(x):
        return [x] + [move(x, d) for d in range(1, group)]

    def mirror(x):
        return [move(x, e * group) for e in range(1, tok_groups)]

    def local(q, k, v, og, rates, gains, gi, ui, di, gs, us, ds):
        _, rows, hidden = gi.shape
        _, own, feat = q.shape
        slab = hidden // group
        near = group * own
        me = lax.axis_index("seq")
        place = jnp.stack((lax.div(me, group), lax.rem(me, group), me)).astype(jnp.int32)

        (packed,) = copying_call(
            functools.partial(weight_pack_kernel, group, slab),
            (arr((seq_n, rows, 6 * slab), BF),),
            (gs, us, ds, gi, ui, di),
            [pltpu.VMEM((6, rows, hidden), BF)],
        )
        packed, queries = lax.optimization_barrier((packed, q[0]))
        wall = lax.all_to_all(packed, "seq", 0, 0, tiled=True).reshape(seq_n * rows, 6 * slab)
        tokens, kv, gg, rate = call(
            token_pack_kernel,
            (arr((own, 3 * feat), BF), arr((own, 2 * feat), BF), arr((own, feat), F32), arr((own, feat), F32)),
            (q, k, v, og, rates, gains),
            8,
        )
        beside = move(tokens, 1) if group > 1 else None
        rest = range(2, group)
        q_near = [queries, beside][:group] + [move(queries, d) for d in rest]
        kv_near = [kv, beside][:group] + [move(kv, d) for d in rest]

        block = arr((own, feat), BF)
        mflop = 2 * near * feat * slab
        *parts, normed = call(
            functools.partial(forward_kernel, slab, group),
            (*(block,) * group, arr((seq_n * rows, 3 * slab), BF)),
            (wall, *q_near),
            24,
            flops=20 * mflop,
        )
        *parts, queries = lax.optimization_barrier((*parts, queries))
        parts = [parts[0]] + [move(parts[d], d) for d in (*range(2, group), *range(1, min(2, group)))]
        q_mirror = mirror(queries)
        *parts, kv_near = lax.optimization_barrier((*parts, kv_near))
        apply_out, sums = call(
            reduce_kernel, (arr((own, feat), F32), arr((2, own), F32)), (gg, *parts), 16
        )
        sums = [sums] + [move(sums, d, "head", head_n) for d in range(1, head_n)]
        sums, q_mirror = lax.optimization_barrier((sums, q_mirror))
        (od,) = call(functools.partial(delta_kernel, head_n * feat), (block,), (apply_out, gg, *sums), 16)
        od_mirror = mirror(od)
        od_near = near_all(od)
        column = arr((3, seq_n * rows, slab), F32)
        factors, rises, *stats = call(
            functools.partial(key_kernel, slab, group),
            (arr((4, near, slab), F32), arr((3, near, slab), BF), arr((3, slab), F32), column, column),
            (wall, *kv_near),
            16,
            flops=12 * mflop,
        )
        *od_mirror, stats[0] = lax.optimization_barrier((*od_mirror, stats[0]))
        pairs = [
            call(pair_kernel, (arr((own, 2 * feat), BF),), pair, 16)[0] for pair in zip(od_mirror, q_mirror)
        ]
        pairs = [x for m in pairs for x in near_all(m)]
        *grad_q, grads = call(
            functools.partial(near_kernel, slab, group),
            (*(block,) * group, arr((3, seq_n * rows, slab), F32)),
            (normed, *q_near, *od_near),
            12,
            flops=60 * mflop,
        )

        q_block = (own, feat)
        grad_q = [grad_q[0]] + [move(grad_q[d], d) for d in (*range(2, group), *range(1, min(2, group)))]
        far = far_distances(group, tok_groups)
        tok, inner, *sends = call(
            functools.partial(backward_kernel, slab, group, tok_groups),
            (
                arr((own, 2 * feat), BF),
                arr((rows, 3 * slab), BF),
                *(message(*(q_block,) * 2, (rows, 3 * slab)),) * (group - 1),
                *(arr((2 * padded(rows), 3 * slab), BF),) * len(far),
            ),
            (place, wall, normed, grads, factors, rises, *stats, *kv_near, *pairs),
            24,
            smem=1,
            flops=120 * mflop,
            scratch=[
                pltpu.VMEM((seq_n, rows, 3 * slab), F32),
                pltpu.VMEM((3, seq_n * rows, slab), F32),
            ],
        )
        sends, grad_q = lax.optimization_barrier((sends, grad_q))
        near_got = {d: move(sends[d - 1], d) for d in (*range(2, group), *range(1, min(2, group)))}
        near_got = [near_got[d] for d in range(1, group)]
        far_got = [move(x, d) for x, d in zip(sends[group - 1 :], far)]
        (relayed,) = call(
            functools.partial(relay_kernel, rows),
            (arr((len(far) * padded(rows), 3 * slab), BF),),
            far_got,
            16,
            flops=12 * mflop,
        )
        relayed = move(relayed, 1)
        out_tok = arr((1, own, feat), BF)
        grad_w = arr((1, rows, hidden), F32)
        grads_t = call(
            functools.partial(tokens_kernel, group), (out_tok,) * 3, (rate, tok, *grad_q, *near_got), 16
        )
        relayed, grads_t = lax.optimization_barrier((relayed, grads_t))
        at = 2 * tiles(feat) * padded(own)
        grads_w = call(
            functools.partial(weights_kernel, group, tok_groups, slab, at),
            (grad_w,) * 3,
            (place, relayed, inner, *near_got, *far_got),
            16,
            smem=1,
            scratch=[pltpu.VMEM((group, rows, 3 * slab), F32)],
        )
        return (*grads_t, *grads_w)

    return local


def solution(mesh):
    seq_n = mesh.shape["seq"]
    head_n = mesh.shape["head"]
    group = min(4, seq_n)
    tok = P("head", "seq", None)
    return jax.shard_map(
        make_local(seq_n, head_n, group),
        mesh=mesh,
        in_specs=(tok, tok, tok, tok, P("head", "seq"), P("head", None), tok, tok, tok, tok, tok, tok),
        out_specs=(tok, tok, tok, tok, tok, tok),
        check_vma=False,
    )
```

```python
import functools

import jax
import jax.numpy as jnp
from jax import lax
from jax.experimental import pallas as pl
from jax.experimental.pallas import tpu as pltpu
from jax.sharding import PartitionSpec as P

EPS_COL = 1e-06
EPS_ROOT = 1e-05
BF = jnp.bfloat16
F32 = jnp.float32
LANES = 128
VMEM = pl.BlockSpec(memory_space=pltpu.VMEM)
SMEM = pl.BlockSpec(memory_space=pltpu.SMEM)


def silu_parts(pre_act):
    sigmoid_val = jax.nn.sigmoid(pre_act)
    silu_val = pre_act * sigmoid_val
    silu_slope = sigmoid_val * (1.0 + pre_act * (1.0 - sigmoid_val))
    silu_bend = sigmoid_val * (1.0 - sigmoid_val) * (2.0 + pre_act * (1.0 - 2.0 * sigmoid_val))
    return (silu_val, silu_slope, silu_bend)


def mm(left_op, right_op):
    return jnp.dot(left_op, right_op, preferred_element_type=F32)


def mm_nt(left_op, right_op):
    return lax.dot_general(left_op, right_op, (((1,), (1,)), ((), ())), preferred_element_type=F32)


def mm_tn(left_op, right_op):
    return lax.dot_general(left_op, right_op, (((0,), (0,)), ((), ())), preferred_element_type=F32)


def column_norm(weight):
    return jnp.sqrt(jnp.sum(weight * weight, axis=0, keepdims=True) + EPS_COL)


def flat(x):
    return x.reshape(-1, x.shape[-1])


def call(kernel, outs, args, mib, smem=0, flops=0, scratch=()):
    moved = sum(x.size * x.dtype.itemsize for x in (*args, *outs))
    return pl.pallas_call(
        kernel,
        out_shape=outs,
        in_specs=[SMEM] * smem + [VMEM] * (len(args) - smem),
        out_specs=[VMEM] * len(outs),
        scratch_shapes=scratch,
        compiler_params=pltpu.CompilerParams(vmem_limit_bytes=mib << 20),
        cost_estimate=pl.CostEstimate(flops=flops, bytes_accessed=moved, transcendentals=0),
    )(*args)


def pack_weights(group, slab, args, seq_n):
    _, rows, hidden = args[0].shape
    hbm = pl.BlockSpec(memory_space=pltpu.HBM)
    return pl.pallas_call(
        functools.partial(weight_pack_kernel, group, slab),
        out_shape=arr((seq_n, rows, 6 * slab), BF),
        in_specs=[hbm] * len(args),
        out_specs=hbm,
        scratch_shapes=[
            pltpu.VMEM((6, rows, hidden), BF),
            pltpu.VMEM((group, rows, 6 * slab), BF),
            pltpu.SemaphoreType.DMA((len(args),)),
            pltpu.SemaphoreType.DMA((seq_n,)),
        ],
        compiler_params=pltpu.CompilerParams(vmem_limit_bytes=56 << 20),
    )(*args)


def arr(shape, dtype):
    return jax.ShapeDtypeStruct(shape, dtype)


def fetch(sources, buffers, sems):
    copies = [pltpu.make_async_copy(s, b, sems.at[i]) for i, (s, b) in enumerate(zip(sources, buffers))]
    for copy in copies:
        copy.start()
    for copy in copies:
        copy.wait()


def padded(rows):
    return -(-rows // 16) * 16


def tiles(cols):
    return -(-cols // LANES)


def put(out, at, value):
    rows, cols = value.shape
    for t in range(tiles(cols)):
        wide = min(LANES, cols - t * LANES)
        out[at : at + rows, 0:wide] = value[:, t * LANES : t * LANES + wide]
        at += padded(rows)
    return at


def get(ref, at, rows, cols):
    parts = []
    for t in range(tiles(cols)):
        wide = min(LANES, cols - t * LANES)
        parts.append(ref[at : at + rows, 0:wide])
        at += padded(rows)
    return jnp.concatenate(parts, axis=1), at


def message(*blocks):
    return arr((sum(tiles(cols) * padded(rows) for rows, cols in blocks), LANES), BF)


def token_pack_kernel(q, k, v, og, rates, gains, all_out, kv_out, gg_out, rate_out):
    tokens, feat = gg_out.shape
    rate = jnp.broadcast_to(rates[...], (feat, tokens)).T
    values = (rate * v[0].astype(F32)).astype(BF)
    all_out[:, 0:feat] = q[0]
    all_out[:, feat : 2 * feat] = k[0]
    all_out[:, 2 * feat : 3 * feat] = values
    kv_out[:, 0:feat] = k[0]
    kv_out[:, feat : 2 * feat] = values
    gg_out[...] = gains[...] * og[0].astype(F32)
    rate_out[...] = rate


def weight_pack_kernel(group, slab, *refs):
    args, (w_out, buf, slabs, sems, out_sems) = refs[:6], refs[6:]
    fetch(args, [buf.at[pl.ds(i, 1)] for i in range(6)], sems)
    copies = []
    for j in range(group):
        cols = pl.ds(j * slab, slab)
        slabs[j] = jnp.concatenate([buf[i, :, cols] for i in range(6)], axis=1)
        for p in range(j, w_out.shape[0], group):
            copies.append(pltpu.make_async_copy(slabs.at[j], w_out.at[p], out_sems.at[p]))
            copies[-1].start()
    for copy in copies:
        copy.wait()


def columns(w, slab):
    parts = [w[:, pl.ds(i * slab, slab)].astype(F32) for i in range(6)]
    saved, init = parts[:3], parts[3:]
    return saved, init, [column_norm(x) for x in init], [column_norm(x) for x in saved]


def stack(refs, cols=slice(None)):
    return jnp.concatenate([r[:, cols] for r in refs], axis=0)


def thirds(x, slab):
    return [x[:, pl.ds(i * slab, slab)] for i in range(3)]


def forward_kernel(slab, group, w, *refs):
    queries, parts, normed_out = refs[:group], refs[group:-1], refs[-1]
    own, feat = parts[0].shape
    saved, init, norm_init, norm_saved = columns(w, slab)
    normed = [(saved[i] * (norm_init[i] / norm_saved[i])).astype(BF) for i in range(3)]
    rows = stack(queries, slice(0, feat))
    hidden = (silu_parts(mm(rows, normed[0]))[0] * mm(rows, normed[1])).astype(BF)
    out = mm_nt(hidden, normed[2]).astype(BF)
    for d in range(group):
        parts[d][...] = out[d * own : (d + 1) * own]
    normed_out[...] = jnp.concatenate(normed, axis=1)


def reduce_kernel(gg, *refs):
    parts, (apply_out, sums) = refs[:-2], refs[-2:]
    total = total_of(parts)
    apply_out[...] = total
    sums[0:1, :] = jnp.sum((total * total).T, axis=0, keepdims=True)
    sums[1:2, :] = jnp.sum((total * gg[...]).T, axis=0, keepdims=True)


def delta_kernel(width, apply_out, gg, *refs):
    sums, out = refs[:-1], refs[-1]
    tokens, feat = apply_out.shape
    total = sums[0][...]
    for more in sums[1:]:
        total += more[...]
    square = jnp.broadcast_to(total[0:1, :], (feat, tokens)).T
    gain = jnp.broadcast_to(total[1:2, :], (feat, tokens)).T
    root = jnp.sqrt(square / width + EPS_ROOT)
    out[...] = (gg[...] / root - apply_out[...] * (gain / width) / (root * root * root)).astype(BF)


def pair_kernel(left, right, out):
    feat = left.shape[1]
    out[:, 0:feat] = left[...]
    out[:, feat : 2 * feat] = right[...]


def query_side(rows, delta, normed):
    q_gate = mm(rows, normed[0])
    q_up = mm(rows, normed[1])
    act, slope, _ = silu_parts(q_gate)
    hidden = (act * q_up).astype(BF)
    delta_hidden = mm(delta, normed[2])
    delta_gate = (delta_hidden * q_up * slope).astype(BF)
    delta_up = (delta_hidden * act).astype(BF)
    grads = (mm_tn(rows, delta_gate), mm_tn(rows, delta_up), mm_tn(delta, hidden))
    return delta_gate, delta_up, grads


def near_kernel(slab, group, normed_ref, *refs):
    q_near, od_near, (*grad_qs, grads_out) = refs[:group], refs[group : 2 * group], refs[2 * group :]
    own = od_near[0].shape[0]
    normed = thirds(normed_ref, slab)
    delta_gate, delta_up, grads = query_side(stack(q_near, slice(0, od_near[0].shape[1])), stack(od_near), normed)
    found = (mm_nt(delta_gate, normed[0]) + mm_nt(delta_up, normed[1])).astype(BF)
    for d in range(group):
        grad_qs[d][...] = found[d * own : (d + 1) * own]
    for i in range(3):
        grads_out[i] = grads[i]


def key_kernel(slab, group, w, *refs):
    kvs, (factors, rises, ratio, minus, plus) = refs[:group], refs[group:]
    feat = w.shape[0]
    saved, start, norm_init, norm_saved = columns(w, slab)
    for i in range(3):
        ratio[i : i + 1, :] = norm_init[i] / norm_saved[i]
        minus[i] = saved[i] * (norm_init[i] / (norm_saved[i] * norm_saved[i] * norm_saved[i]))
        plus[i] = start[i] / (norm_init[i] * norm_saved[i])
    init = [w[:, pl.ds((3 + i) * slab, slab)] for i in range(3)]
    keys = stack(kvs, slice(-2 * feat, -feat))
    values = stack(kvs, slice(-feat, None))
    k_gate = mm(keys, init[0])
    k_up = mm(keys, init[1])
    k_proj = mm(values, init[2])
    k_act, k_slope, k_bend = silu_parts(k_gate)
    rises[0] = (k_act * k_up).astype(BF)
    rises[1] = (k_proj * k_up * k_slope).astype(BF)
    rises[2] = (k_proj * k_act).astype(BF)
    factors[0] = k_act
    factors[1] = k_up * k_slope
    factors[2] = k_proj * k_slope
    factors[3] = k_proj * k_up * k_bend


def backward_kernel(
    slab, group, tok_groups, place, w, normed_ref, grads, factors, rises, ratio, minus, plus, *refs
):
    far = group * (tok_groups - 1)
    kvs, pairs, outs, (inner_buf, sums) = refs[:group], refs[group : group + far], refs[group + far : -2], refs[-2:]
    feat = w.shape[0]
    tok_out, outs = outs[0], outs[1:]
    own = tok_out.shape[0]
    normed = thirds(normed_ref, slab)
    total = [grads[i] for i in range(3)]
    for e in range(tok_groups - 1):
        these = pairs[e * group : (e + 1) * group]
        more = query_side(stack(these, slice(feat, 2 * feat)), stack(these, slice(0, feat)), normed)[2]
        total = [total[i] + more[i] for i in range(3)]
        if tok_groups > 2:
            for i in range(3):
                sums[i] = total[i]
            total = [sums[i] for i in range(3)]

    cots, direct = [], []
    once = jnp.where(place[0] == 0, 1.0, 0.0)
    for i in range(3):
        saved = w[:, pl.ds(i * slab, slab)].astype(F32)
        col_dot = jnp.sum(saved * total[i], axis=0, keepdims=True)
        cot = total[i] * ratio[i : i + 1, :] - minus[i] * col_dot
        cots.append(cot.astype(BF))
        direct.append((cot + plus[i] * col_dot) * once)

    init_bf = [w[:, pl.ds((3 + i) * slab, slab)] for i in range(3)]
    keys = stack(kvs, slice(-2 * feat, -feat))
    values = stack(kvs, slice(-feat, None))
    back_gate = mm(keys, cots[0])
    back_up = mm(keys, cots[1])
    back_hidden = mm(values, cots[2])
    back_proj = (back_gate * factors[1] + back_up * factors[0]).astype(BF)
    back_kup = (back_gate * factors[2] + back_hidden * factors[0]).astype(BF)
    back_kgate = (back_gate * factors[3] + (back_up * factors[2] + back_hidden * factors[1])).astype(BF)
    grad_k = (
        mm_nt(rises[1], cots[0])
        + mm_nt(rises[2], cots[1])
        + mm_nt(back_kgate, init_bf[0])
        + mm_nt(back_kup, init_bf[1])
    ).astype(BF)
    grad_v = (mm_nt(rises[0], cots[2]) + mm_nt(back_proj, init_bf[2])).astype(BF)
    inner = (mm_tn(keys, back_kgate), mm_tn(keys, back_kup), mm_tn(values, back_proj))
    whole = jnp.concatenate([inner[i] + direct[i] for i in range(3)], axis=1)
    rows = inner_buf.shape[1]
    for p in range(inner_buf.shape[0]):
        inner_buf[p] = whole[p * rows : (p + 1) * rows]
    tok_out[:, 0:feat] = grad_k[0:own]
    tok_out[:, feat : 2 * feat] = grad_v[0:own]
    outs[0][...] = inner_buf[place[2]].astype(BF)
    for d in range(1, group):
        out, at = outs[d], 0
        for tok in (grad_k, grad_v):
            at = put(out, at, tok[d * own : (d + 1) * own, :])
        put(out, at, inner_buf[place[2] ^ d].astype(BF))
    for dist, out in zip(far_distances(group, tok_groups), outs[group:]):
        for i in range(2):
            out[i * padded(rows) : i * padded(rows) + rows, :] = inner_buf[place[2] ^ dist ^ i].astype(BF)


def relay_kernel(rows, *refs):
    out, step = refs[-1], padded(rows)
    for i, block in enumerate(refs[:-1]):
        out[i * step : i * step + rows, :] = block[step : step + rows, :]


def far_distances(group, tok_groups):
    return [e * group + d for e in range(1, tok_groups) for d in range(0, group, 2)]


def total_of(refs):
    total = refs[0][...].astype(F32)
    for block in refs[1:]:
        total += block[...].astype(F32)
    return total


def tokens_kernel(group, rate, tok, *refs):
    queries, blocks, (gq, gk, gv) = refs[:group], refs[group:-3], refs[-3:]
    _, own, feat = gq.shape
    gq[0] = total_of(queries).astype(BF)
    sums = [tok[:, i * feat : (i + 1) * feat].astype(F32) for i in range(2)]
    for block in blocks:
        at = 0
        for i in range(2):
            more, at = get(block, at, own, feat)
            sums[i] += more.astype(F32)
    gk[0] = sums[0].astype(BF)
    gv[0] = (rate[...] * sums[1]).astype(BF)


def weights_kernel(group, tok_groups, slab, at, place, relayed, inner, *refs):
    blocks, (*outs, buf) = refs[:-4], refs[-4:]
    _, rows, cols = buf.shape
    step = padded(rows)
    buf[0] = inner[...].astype(F32)
    for d in range(1, group):
        buf[d] = get(blocks[d - 1], at, rows, cols)[0].astype(F32)
    for i, dist in enumerate(far_distances(group, tok_groups)):
        d = dist % group
        buf[d] += blocks[group - 1 + i][0:rows, :].astype(F32)
        buf[d ^ 1] += relayed[i * step : i * step + rows, :].astype(F32)
    total = [buf[place[1] ^ j] for j in range(group)]
    for i in range(3):
        outs[i][0] = jnp.concatenate([t[:, i * slab : (i + 1) * slab] for t in total], axis=1)


def make_local(seq_n, head_n, group):
    tok_groups = seq_n // group

    def move(x, dist, axis="seq", size=seq_n):
        return lax.ppermute(x, axis, [(i, i ^ dist) for i in range(size)])

    def near_all(x):
        moved = {d: move(x, d) for d in reversed(range(1, group))}
        return [x] + [moved[d] for d in range(1, group)]

    def mirror(x):
        return [move(x, e * group) for e in range(1, tok_groups)]

    def local(q, k, v, og, rates, gains, gi, ui, di, gs, us, ds):
        _, rows, hidden = gi.shape
        _, own, feat = q.shape
        slab = hidden // group
        near = group * own
        me = lax.axis_index("seq")
        place = jnp.stack((lax.div(me, group), lax.rem(me, group), me)).astype(jnp.int32)

        packed = pack_weights(group, slab, (gs, us, ds, gi, ui, di), seq_n)
        packed, queries = lax.optimization_barrier((packed, q[0]))
        wall = lax.all_to_all(packed, "seq", 0, 0, tiled=True).reshape(seq_n * rows, 6 * slab)
        tokens, kv, gg, rate = call(
            token_pack_kernel,
            (arr((own, 3 * feat), BF), arr((own, 2 * feat), BF), arr((own, feat), F32), arr((own, feat), F32)),
            (q, k, v, og, rates, gains),
            8,
        )
        beside = move(tokens, 1) if group > 1 else None
        rest = range(2, group)
        q_near = [queries, beside][:group] + [move(queries, d) for d in rest]
        kv_near = [kv, beside][:group] + [move(kv, d) for d in rest]

        block = arr((own, feat), BF)
        mflop = 2 * near * feat * slab
        *parts, normed = call(
            functools.partial(forward_kernel, slab, group),
            (*(block,) * group, arr((seq_n * rows, 3 * slab), BF)),
            (wall, *q_near),
            24,
            flops=20 * mflop,
        )
        *parts, queries = lax.optimization_barrier((*parts, queries))
        parts = [parts[0]] + [move(parts[d], d) for d in (*range(2, group), *range(1, min(2, group)))]
        q_mirror = mirror(queries)
        *parts, kv_near = lax.optimization_barrier((*parts, kv_near))
        apply_out, sums = call(
            reduce_kernel, (arr((own, feat), F32), arr((2, own), F32)), (gg, *parts), 16
        )
        sums = [sums] + [move(sums, d, "head", head_n) for d in range(1, head_n)]
        sums, q_mirror = lax.optimization_barrier((sums, q_mirror))
        (od,) = call(functools.partial(delta_kernel, head_n * feat), (block,), (apply_out, gg, *sums), 16)
        od_mirror = mirror(od)
        od_near = near_all(od)
        column = arr((3, seq_n * rows, slab), F32)
        factors, rises, *stats = call(
            functools.partial(key_kernel, slab, group),
            (arr((4, near, slab), F32), arr((3, near, slab), BF), arr((3, slab), F32), column, column),
            (wall, *kv_near),
            16,
            flops=12 * mflop,
        )
        *od_mirror, stats[0] = lax.optimization_barrier((*od_mirror, stats[0]))
        pairs = [
            call(pair_kernel, (arr((own, 2 * feat), BF),), pair, 16)[0] for pair in zip(od_mirror, q_mirror)
        ]
        pairs = [x for m in pairs for x in near_all(m)]
        *grad_q, grads = call(
            functools.partial(near_kernel, slab, group),
            (*(block,) * group, arr((3, seq_n * rows, slab), F32)),
            (normed, *q_near, *od_near),
            12,
            flops=60 * mflop,
        )

        q_block = (own, feat)
        grad_q = [grad_q[0]] + [move(grad_q[d], d) for d in (*range(2, group), *range(1, min(2, group)))]
        far = far_distances(group, tok_groups)
        tok, inner, *sends = call(
            functools.partial(backward_kernel, slab, group, tok_groups),
            (
                arr((own, 2 * feat), BF),
                arr((rows, 3 * slab), BF),
                *(message(*(q_block,) * 2, (rows, 3 * slab)),) * (group - 1),
                *(arr((2 * padded(rows), 3 * slab), BF),) * len(far),
            ),
            (place, wall, normed, grads, factors, rises, *stats, *kv_near, *pairs),
            24,
            smem=1,
            flops=120 * mflop,
            scratch=[
                pltpu.VMEM((seq_n, rows, 3 * slab), F32),
                pltpu.VMEM((3, seq_n * rows, slab), F32),
            ],
        )
        sends, grad_q = lax.optimization_barrier((sends, grad_q))
        near_got = {d: move(sends[d - 1], d) for d in (*range(2, group), *range(1, min(2, group)))}
        near_got = [near_got[d] for d in range(1, group)]
        far_got = [move(x, d) for x, d in zip(sends[group - 1 :], far)]
        (relayed,) = call(
            functools.partial(relay_kernel, rows),
            (arr((len(far) * padded(rows), 3 * slab), BF),),
            far_got,
            16,
            flops=12 * mflop,
        )
        relayed = move(relayed, 1)
        out_tok = arr((1, own, feat), BF)
        grad_w = arr((1, rows, hidden), F32)
        grads_t = call(
            functools.partial(tokens_kernel, group), (out_tok,) * 3, (rate, tok, *grad_q, *near_got), 16
        )
        relayed, grads_t = lax.optimization_barrier((relayed, grads_t))
        at = 2 * tiles(feat) * padded(own)
        grads_w = call(
            functools.partial(weights_kernel, group, tok_groups, slab, at),
            (grad_w,) * 3,
            (place, relayed, inner, *near_got, *far_got),
            16,
            smem=1,
            scratch=[pltpu.VMEM((group, rows, 3 * slab), F32)],
        )
        return (*grads_t, *grads_w)

    return local


def solution(mesh):
    seq_n = mesh.shape["seq"]
    head_n = mesh.shape["head"]
    group = min(4, seq_n)
    tok = P("head", "seq", None)
    return jax.shard_map(
        make_local(seq_n, head_n, group),
        mesh=mesh,
        in_specs=(tok, tok, tok, tok, P("head", "seq"), P("head", None), tok, tok, tok, tok, tok, tok),
        out_specs=(tok, tok, tok, tok, tok, tok),
        check_vma=False,
    )
```

```python
import functools

import jax
import jax.numpy as jnp
from jax import lax
from jax.experimental import pallas as pl
from jax.experimental.pallas import tpu as pltpu
from jax.sharding import PartitionSpec as P

EPS_COL = 1e-06
EPS_ROOT = 1e-05
BF = jnp.bfloat16
F32 = jnp.float32
LANES = 128
VMEM = pl.BlockSpec(memory_space=pltpu.VMEM)
SMEM = pl.BlockSpec(memory_space=pltpu.SMEM)


def silu_parts(pre_act):
    sigmoid_val = jax.nn.sigmoid(pre_act)
    silu_val = pre_act * sigmoid_val
    silu_slope = sigmoid_val * (1.0 + pre_act * (1.0 - sigmoid_val))
    silu_bend = sigmoid_val * (1.0 - sigmoid_val) * (2.0 + pre_act * (1.0 - 2.0 * sigmoid_val))
    return (silu_val, silu_slope, silu_bend)


def mm(left_op, right_op):
    return jnp.dot(left_op, right_op, preferred_element_type=F32)


def mm_nt(left_op, right_op):
    return lax.dot_general(left_op, right_op, (((1,), (1,)), ((), ())), preferred_element_type=F32)


def mm_tn(left_op, right_op):
    return lax.dot_general(left_op, right_op, (((0,), (0,)), ((), ())), preferred_element_type=F32)


def column_norm(weight):
    return jnp.sqrt(jnp.sum(weight * weight, axis=0, keepdims=True) + EPS_COL)


def flat(x):
    return x.reshape(-1, x.shape[-1])


def call(kernel, outs, args, mib, smem=0, flops=0, scratch=()):
    moved = sum(x.size * x.dtype.itemsize for x in (*args, *outs))
    return pl.pallas_call(
        kernel,
        out_shape=outs,
        in_specs=[SMEM] * smem + [VMEM] * (len(args) - smem),
        out_specs=[VMEM] * len(outs),
        scratch_shapes=scratch,
        compiler_params=pltpu.CompilerParams(vmem_limit_bytes=mib << 20),
        cost_estimate=pl.CostEstimate(flops=flops, bytes_accessed=moved, transcendentals=0),
    )(*args)


def copying_call(kernel, outs, args, buffers):
    return pl.pallas_call(
        kernel,
        out_shape=outs,
        in_specs=[pl.BlockSpec(memory_space=pltpu.HBM)] * len(args),
        out_specs=[VMEM] * len(outs),
        scratch_shapes=[*buffers, pltpu.SemaphoreType.DMA((len(args),))],
        compiler_params=pltpu.CompilerParams(vmem_limit_bytes=56 << 20),
    )(*args)


def arr(shape, dtype):
    return jax.ShapeDtypeStruct(shape, dtype)


def fetch(sources, buffers, sems):
    copies = [pltpu.make_async_copy(s, b, sems.at[i]) for i, (s, b) in enumerate(zip(sources, buffers))]
    for copy in copies:
        copy.start()
    for copy in copies:
        copy.wait()


def padded(rows):
    return -(-rows // 16) * 16


def tiles(cols):
    return -(-cols // LANES)


def put(out, at, value):
    rows, cols = value.shape
    for t in range(tiles(cols)):
        wide = min(LANES, cols - t * LANES)
        out[at : at + rows, 0:wide] = value[:, t * LANES : t * LANES + wide]
        at += padded(rows)
    return at


def get(ref, at, rows, cols):
    parts = []
    for t in range(tiles(cols)):
        wide = min(LANES, cols - t * LANES)
        parts.append(ref[at : at + rows, 0:wide])
        at += padded(rows)
    return jnp.concatenate(parts, axis=1), at


def message(*blocks):
    return arr((sum(tiles(cols) * padded(rows) for rows, cols in blocks), LANES), BF)


def token_pack_kernel(q, k, v, og, rates, gains, all_out, kv_out, gg_out, rate_out):
    tokens, feat = gg_out.shape
    rate = jnp.broadcast_to(rates[...], (feat, tokens)).T
    values = (rate * v[0].astype(F32)).astype(BF)
    all_out[:, 0:feat] = q[0]
    all_out[:, feat : 2 * feat] = k[0]
    all_out[:, 2 * feat : 3 * feat] = values
    kv_out[:, 0:feat] = k[0]
    kv_out[:, feat : 2 * feat] = values
    gg_out[...] = gains[...] * og[0].astype(F32)
    rate_out[...] = rate


def weight_pack_kernel(group, slab, *refs):
    args, (w_out, buf, sems) = refs[:6], refs[6:]
    fetch(args, [buf.at[pl.ds(i, 1)] for i in range(6)], sems)
    for j in range(group):
        cols = pl.ds(j * slab, slab)
        block = jnp.concatenate([buf[i, :, cols] for i in range(6)], axis=1)
        for p in range(j, w_out.shape[0], group):
            w_out[p] = block


def columns(w, slab):
    parts = [w[:, pl.ds(i * slab, slab)].astype(F32) for i in range(6)]
    saved, init = parts[:3], parts[3:]
    return saved, init, [column_norm(x) for x in init], [column_norm(x) for x in saved]


def stack(refs, cols=slice(None)):
    return jnp.concatenate([r[:, cols] for r in refs], axis=0)


def thirds(x, slab):
    return [x[:, pl.ds(i * slab, slab)] for i in range(3)]


def forward_kernel(slab, group, w, *refs):
    queries, parts, normed_out = refs[:group], refs[group:-1], refs[-1]
    own, feat = parts[0].shape
    saved, init, norm_init, norm_saved = columns(w, slab)
    normed = [(saved[i] * (norm_init[i] / norm_saved[i])).astype(BF) for i in range(3)]
    rows = stack(queries, slice(0, feat))
    hidden = (silu_parts(mm(rows, normed[0]))[0] * mm(rows, normed[1])).astype(BF)
    out = mm_nt(hidden, normed[2]).astype(BF)
    for d in range(group):
        parts[d][...] = out[d * own : (d + 1) * own]
    normed_out[...] = jnp.concatenate(normed, axis=1)


def reduce_kernel(gg, *refs):
    parts, (apply_out, sums) = refs[:-2], refs[-2:]
    total = total_of(parts)
    apply_out[...] = total
    sums[0:1, :] = jnp.sum((total * total).T, axis=0, keepdims=True)
    sums[1:2, :] = jnp.sum((total * gg[...]).T, axis=0, keepdims=True)


def delta_kernel(width, apply_out, gg, *refs):
    sums, out = refs[:-1], refs[-1]
    tokens, feat = apply_out.shape
    total = sums[0][...]
    for more in sums[1:]:
        total += more[...]
    square = jnp.broadcast_to(total[0:1, :], (feat, tokens)).T
    gain = jnp.broadcast_to(total[1:2, :], (feat, tokens)).T
    root = jnp.sqrt(square / width + EPS_ROOT)
    out[...] = (gg[...] / root - apply_out[...] * (gain / width) / (root * root * root)).astype(BF)


def pair_kernel(left, right, out):
    feat = left.shape[1]
    out[:, 0:feat] = left[...]
    out[:, feat : 2 * feat] = right[...]


def query_side(rows, delta, normed):
    q_gate = mm(rows, normed[0])
    q_up = mm(rows, normed[1])
    act, slope, _ = silu_parts(q_gate)
    hidden = (act * q_up).astype(BF)
    delta_hidden = mm(delta, normed[2])
    delta_gate = (delta_hidden * q_up * slope).astype(BF)
    delta_up = (delta_hidden * act).astype(BF)
    grads = (mm_tn(rows, delta_gate), mm_tn(rows, delta_up), mm_tn(delta, hidden))
    return delta_gate, delta_up, grads


def near_kernel(slab, group, normed_ref, *refs):
    q_near, od_near, (*grad_qs, grads_out) = refs[:group], refs[group : 2 * group], refs[2 * group :]
    own = od_near[0].shape[0]
    normed = thirds(normed_ref, slab)
    delta_gate, delta_up, grads = query_side(stack(q_near, slice(0, od_near[0].shape[1])), stack(od_near), normed)
    found = (mm_nt(delta_gate, normed[0]) + mm_nt(delta_up, normed[1])).astype(BF)
    for d in range(group):
        grad_qs[d][...] = found[d * own : (d + 1) * own]
    for i in range(3):
        grads_out[i] = grads[i]


def key_kernel(slab, group, w, *refs):
    kvs, (factors, rises, ratio, minus, plus) = refs[:group], refs[group:]
    feat = w.shape[0]
    saved, start, norm_init, norm_saved = columns(w, slab)
    for i in range(3):
        ratio[i : i + 1, :] = norm_init[i] / norm_saved[i]
        minus[i] = saved[i] * (norm_init[i] / (norm_saved[i] * norm_saved[i] * norm_saved[i]))
        plus[i] = start[i] / (norm_init[i] * norm_saved[i])
    init = [w[:, pl.ds((3 + i) * slab, slab)] for i in range(3)]
    keys = stack(kvs, slice(-2 * feat, -feat))
    values = stack(kvs, slice(-feat, None))
    k_gate = mm(keys, init[0])
    k_up = mm(keys, init[1])
    k_proj = mm(values, init[2])
    k_act, k_slope, k_bend = silu_parts(k_gate)
    rises[0] = (k_act * k_up).astype(BF)
    rises[1] = (k_proj * k_up * k_slope).astype(BF)
    rises[2] = (k_proj * k_act).astype(BF)
    factors[0] = k_act
    factors[1] = k_up * k_slope
    factors[2] = k_proj * k_slope
    factors[3] = k_proj * k_up * k_bend


def backward_kernel(
    slab, group, tok_groups, place, w, normed_ref, grads, factors, rises, ratio, minus, plus, *refs
):
    far = group * (tok_groups - 1)
    kvs, pairs, outs, (inner_buf, sums) = refs[:group], refs[group : group + far], refs[group + far : -2], refs[-2:]
    feat = w.shape[0]
    tok_out, outs = outs[0], outs[1:]
    own = tok_out.shape[0]
    normed = thirds(normed_ref, slab)
    total = [grads[i] for i in range(3)]
    for e in range(tok_groups - 1):
        these = pairs[e * group : (e + 1) * group]
        more = query_side(stack(these, slice(feat, 2 * feat)), stack(these, slice(0, feat)), normed)[2]
        total = [total[i] + more[i] for i in range(3)]
        if tok_groups > 2:
            for i in range(3):
                sums[i] = total[i]
            total = [sums[i] for i in range(3)]

    cots, direct = [], []
    once = jnp.where(place[0] == 0, 1.0, 0.0)
    for i in range(3):
        saved = w[:, pl.ds(i * slab, slab)].astype(F32)
        col_dot = jnp.sum(saved * total[i], axis=0, keepdims=True)
        cot = total[i] * ratio[i : i + 1, :] - minus[i] * col_dot
        cots.append(cot.astype(BF))
        direct.append((cot + plus[i] * col_dot) * once)

    init_bf = [w[:, pl.ds((3 + i) * slab, slab)] for i in range(3)]
    keys = stack(kvs, slice(-2 * feat, -feat))
    values = stack(kvs, slice(-feat, None))
    back_gate = mm(keys, cots[0])
    back_up = mm(keys, cots[1])
    back_hidden = mm(values, cots[2])
    back_proj = (back_gate * factors[1] + back_up * factors[0]).astype(BF)
    back_kup = (back_gate * factors[2] + back_hidden * factors[0]).astype(BF)
    back_kgate = (back_gate * factors[3] + (back_up * factors[2] + back_hidden * factors[1])).astype(BF)
    grad_k = (
        mm_nt(rises[1], cots[0])
        + mm_nt(rises[2], cots[1])
        + mm_nt(back_kgate, init_bf[0])
        + mm_nt(back_kup, init_bf[1])
    ).astype(BF)
    grad_v = (mm_nt(rises[0], cots[2]) + mm_nt(back_proj, init_bf[2])).astype(BF)
    inner = (mm_tn(keys, back_kgate), mm_tn(keys, back_kup), mm_tn(values, back_proj))
    whole = jnp.concatenate([inner[i] + direct[i] for i in range(3)], axis=1)
    rows = inner_buf.shape[1]
    for p in range(inner_buf.shape[0]):
        inner_buf[p] = whole[p * rows : (p + 1) * rows]
    tok_out[:, 0:feat] = grad_k[0:own]
    tok_out[:, feat : 2 * feat] = grad_v[0:own]
    outs[0][...] = inner_buf[place[2]].astype(BF)
    for d in range(1, group):
        out, at = outs[d], 0
        for tok in (grad_k, grad_v):
            at = put(out, at, tok[d * own : (d + 1) * own, :])
        put(out, at, inner_buf[place[2] ^ d].astype(BF))
    for dist, out in zip(far_distances(group, tok_groups), outs[group:]):
        for i in range(2):
            out[i * padded(rows) : i * padded(rows) + rows, :] = inner_buf[place[2] ^ dist ^ i].astype(BF)


def relay_kernel(rows, *refs):
    out, step = refs[-1], padded(rows)
    for i, block in enumerate(refs[:-1]):
        out[i * step : i * step + rows, :] = block[step : step + rows, :]


def far_distances(group, tok_groups):
    return [e * group + d for e in range(1, tok_groups) for d in range(0, group, 2)]


def total_of(refs):
    total = refs[0][...].astype(F32)
    for block in refs[1:]:
        total += block[...].astype(F32)
    return total


def tokens_kernel(group, rate, tok, *refs):
    queries, blocks, (gq, gk, gv) = refs[:group], refs[group:-3], refs[-3:]
    _, own, feat = gq.shape
    gq[0] = total_of(queries).astype(BF)
    sums = [tok[:, i * feat : (i + 1) * feat].astype(F32) for i in range(2)]
    for block in blocks:
        at = 0
        for i in range(2):
            more, at = get(block, at, own, feat)
            sums[i] += more.astype(F32)
    gk[0] = sums[0].astype(BF)
    gv[0] = (rate[...] * sums[1]).astype(BF)


def weights_kernel(group, tok_groups, slab, at, place, relayed, inner, *refs):
    blocks, (*outs, buf) = refs[:-4], refs[-4:]
    _, rows, cols = buf.shape
    step = padded(rows)
    buf[0] = inner[...].astype(F32)
    for d in range(1, group):
        buf[d] = get(blocks[d - 1], at, rows, cols)[0].astype(F32)
    for i, dist in enumerate(far_distances(group, tok_groups)):
        d = dist % group
        buf[d] += blocks[group - 1 + i][0:rows, :].astype(F32)
        buf[d ^ 1] += relayed[i * step : i * step + rows, :].astype(F32)
    total = [buf[place[1] ^ j] for j in range(group)]
    for i in range(3):
        outs[i][0] = jnp.concatenate([t[:, i * slab : (i + 1) * slab] for t in total], axis=1)


def make_local(seq_n, head_n, group):
    tok_groups = seq_n // group

    def move(x, dist, axis="seq", size=seq_n):
        return lax.ppermute(x, axis, [(i, i ^ dist) for i in range(size)])

    def near_all(x):
        return [x] + [move(x, d) for d in range(1, group)]

    def mirror(x):
        return [move(x, e * group) for e in range(1, tok_groups)]

    def local(q, k, v, og, rates, gains, gi, ui, di, gs, us, ds):
        _, rows, hidden = gi.shape
        _, own, feat = q.shape
        slab = hidden // group
        near = group * own
        me = lax.axis_index("seq")
        place = jnp.stack((lax.div(me, group), lax.rem(me, group), me)).astype(jnp.int32)

        (packed,) = copying_call(
            functools.partial(weight_pack_kernel, group, slab),
            (arr((seq_n, rows, 6 * slab), BF),),
            (gs, us, ds, gi, ui, di),
            [pltpu.VMEM((6, rows, hidden), BF)],
        )
        packed, queries = lax.optimization_barrier((packed, q[0]))
        wall = lax.all_to_all(packed, "seq", 0, 0, tiled=True).reshape(seq_n * rows, 6 * slab)
        tokens, kv, gg, rate = call(
            token_pack_kernel,
            (arr((own, 3 * feat), BF), arr((own, 2 * feat), BF), arr((own, feat), F32), arr((own, feat), F32)),
            (q, k, v, og, rates, gains),
            8,
        )
        beside = move(tokens, 1) if group > 1 else None
        rest = range(2, group)
        q_near = [queries, beside][:group] + [move(queries, d) for d in rest]
        kv_near = [kv, beside][:group] + [move(kv, d) for d in rest]

        block = arr((own, feat), BF)
        mflop = 2 * near * feat * slab
        *parts, normed = call(
            functools.partial(forward_kernel, slab, group),
            (*(block,) * group, arr((seq_n * rows, 3 * slab), BF)),
            (wall, *q_near),
            24,
            flops=20 * mflop,
        )
        *parts, queries = lax.optimization_barrier((*parts, queries))
        parts = [parts[0]] + [move(parts[d], d) for d in range(group - 1, 0, -1)]
        q_mirror = mirror(queries)
        *parts, kv_near = lax.optimization_barrier((*parts, kv_near))
        apply_out, sums = call(
            reduce_kernel, (arr((own, feat), F32), arr((2, own), F32)), (gg, *parts), 16
        )
        sums = [sums] + [move(sums, d, "head", head_n) for d in range(1, head_n)]
        sums, q_mirror = lax.optimization_barrier((sums, q_mirror))
        (od,) = call(functools.partial(delta_kernel, head_n * feat), (block,), (apply_out, gg, *sums), 16)
        od_mirror = mirror(od)
        od_near = near_all(od)
        column = arr((3, seq_n * rows, slab), F32)
        factors, rises, *stats = call(
            functools.partial(key_kernel, slab, group),
            (arr((4, near, slab), F32), arr((3, near, slab), BF), arr((3, slab), F32), column, column),
            (wall, *kv_near),
            16,
            flops=12 * mflop,
        )
        *od_mirror, stats[0] = lax.optimization_barrier((*od_mirror, stats[0]))
        pairs = [
            call(pair_kernel, (arr((own, 2 * feat), BF),), pair, 16)[0] for pair in zip(od_mirror, q_mirror)
        ]
        pairs = [x for m in pairs for x in near_all(m)]
        *grad_q, grads = call(
            functools.partial(near_kernel, slab, group),
            (*(block,) * group, arr((3, seq_n * rows, slab), F32)),
            (normed, *q_near, *od_near),
            12,
            flops=60 * mflop,
        )

        q_block = (own, feat)
        grad_q = [grad_q[0]] + [move(grad_q[d], d) for d in range(group - 1, 0, -1)]
        far = far_distances(group, tok_groups)
        tok, inner, *sends = call(
            functools.partial(backward_kernel, slab, group, tok_groups),
            (
                arr((own, 2 * feat), BF),
                arr((rows, 3 * slab), BF),
                *(message(*(q_block,) * 2, (rows, 3 * slab)),) * (group - 1),
                *(arr((2 * padded(rows), 3 * slab), BF),) * len(far),
            ),
            (place, wall, normed, grads, factors, rises, *stats, *kv_near, *pairs),
            24,
            smem=1,
            flops=120 * mflop,
            scratch=[
                pltpu.VMEM((seq_n, rows, 3 * slab), F32),
                pltpu.VMEM((3, seq_n * rows, slab), F32),
            ],
        )
        sends, grad_q = lax.optimization_barrier((sends, grad_q))
        near_got = {d: move(sends[d - 1], d) for d in range(group - 1, 0, -1)}
        near_got = [near_got[d] for d in range(1, group)]
        far_got = [move(x, d) for x, d in zip(sends[group - 1 :], far)]
        (relayed,) = call(
            functools.partial(relay_kernel, rows),
            (arr((len(far) * padded(rows), 3 * slab), BF),),
            far_got,
            16,
            flops=12 * mflop,
        )
        relayed = move(relayed, 1)
        out_tok = arr((1, own, feat), BF)
        grad_w = arr((1, rows, hidden), F32)
        grads_t = call(
            functools.partial(tokens_kernel, group), (out_tok,) * 3, (rate, tok, *grad_q, *near_got), 16
        )
        relayed, grads_t = lax.optimization_barrier((relayed, grads_t))
        at = 2 * tiles(feat) * padded(own)
        grads_w = call(
            functools.partial(weights_kernel, group, tok_groups, slab, at),
            (grad_w,) * 3,
            (place, relayed, inner, *near_got, *far_got),
            16,
            smem=1,
            scratch=[pltpu.VMEM((group, rows, 3 * slab), F32)],
        )
        return (*grads_t, *grads_w)

    return local


def solution(mesh):
    seq_n = mesh.shape["seq"]
    head_n = mesh.shape["head"]
    group = min(4, seq_n)
    tok = P("head", "seq", None)
    return jax.shard_map(
        make_local(seq_n, head_n, group),
        mesh=mesh,
        in_specs=(tok, tok, tok, tok, P("head", "seq"), P("head", None), tok, tok, tok, tok, tok, tok),
        out_specs=(tok, tok, tok, tok, tok, tok),
        check_vma=False,
    )
```
